32 devices in a mesh: parts: 2 (over y), row: 4 (over z), col: 2 (over x), rhs: 2 (over core).
Axes of the slice: x: 2, y: 2, z: 4, core: 2. Of those that a mesh axis runs over, the one named last changes fastest.
Arguments:
- current: bfloat16 [32, 65536], P('rhs', ('parts', 'row', 'col')), parts along dimension 1, may hold values from -6 to 6
- charge: bfloat16 [32, 8192], P('rhs', ('parts', 'row', 'col')), parts along dimension 1, may hold values from -6 to 6
- rhs_scale: float32 [64], P(('parts', 'rhs')), parts along dimension 0, may hold values from 0.5 to 2
- induct_tiles: bfloat16 [3072, 128, 128], P(('parts', 'row', 'col')), parts along dimension 0, may hold values from -0.21875 to 0.21875
- induct_rows: int32 [3072], P(('parts', 'row', 'col')), parts along dimension 0, may hold values from 0 to 63
- induct_slots: int32 [3072], P(('parts', 'row', 'col')), parts along dimension 0, may hold values from 0 to 31, as said below
- induct_needs: int32 [64, 8], P(('parts', 'row', 'col')), parts along dimension 0, may hold values from 0 to 63
- coeff_tiles: bfloat16 [1536, 128, 128], P(('parts', 'row', 'col')), parts along dimension 0, may hold values from -0.109375 to 0.109375
- coeff_rows: int32 [1536], P(('parts', 'row', 'col')), parts along dimension 0, may hold values from 0 to 7
- coeff_slots: int32 [1536], P(('parts', 'row', 'col')), parts along dimension 0, may hold values from 0 to 15, as said below
- coeff_needs: int32 [64, 4], P(('parts', 'row', 'col')), parts along dimension 0, may hold values from 0 to 7
- link_needs: int32 [64, 16], P(('parts', 'row', 'col')), parts along dimension 0, may hold values from 0 to 7
- end_slots: int32 [512, 2], P(('parts', 'row', 'col')), parts along dimension 0, may hold values from 0 to 63, as said below
- end_offsets: int32 [65536, 2], P(('parts', 'row', 'col')), parts along dimension 0, may hold values from 0 to 127
Outputs:
- seg_out: bfloat16 [32, 65536], P('rhs', ('parts', 'row', 'col')), parts along dimension 1
- pan_out: bfloat16 [32, 8192], P('rhs', ('parts', 'row', 'col')), parts along dimension 1
- potential: bfloat16 [32, 8192], P('rhs', ('parts', 'row', 'col')), parts along dimension 1
The draws below stay inside these ranges and needn't reach their ends.
There are 2 independent parts, one for each index of `parts`. The reference program is written for one: setup_inputs(seed, part) draws one part's arguments, and reference() takes and returns one part's arrays. A program takes and returns all parts, laid end to end along the dimension named above; each array names one. Nothing has to cross between parts.
Inputs may be any that keep to these rules, and one draw needn't show every extreme that they name: `induct_slots`: every slot 0 to 31 of a device is named by one or more of its tiles. `coeff_slots`: every slot 0 to 15 of a device is named by one or more of its tiles. `end_slots`: the 64 ends of a device's segment blocks take its link slots, each once.
All inputs are finite; a program needn't handle non-finite values.
Results may differ from the reference program's by a relative error of at most 0.0044.
Values may be sent and summed in bfloat16 or wider, within the bound.
No kernel may reach another device: no remote copies, remote signals or barrier semaphores. Data moves between devices by JAX's collectives and lax.ppermute only.
A program may use at most 64 MiB of HBM per device.

```python
import math
import jax
import jax.numpy as jnp
from jax import lax

R = 32
BLK = 128
SB_COL = 32
PB_COL = 4
LT = 192
PT = 96
CAPL = 8
CAPP = 4
CAPK = 16
NSEG = 32768
NPAN = 4096
N_ROW = 4
N_COL = 2


def slot_draw(key, slot_count, tile_count):
    dev_count = N_ROW * N_COL
    first_pass = jax.vmap(lambda sub: jax.random.permutation(sub, slot_count))(jax.random.split(key, dev_count))
    more_slots = jax.random.randint(jax.random.fold_in(key, 1), (dev_count, tile_count - slot_count), 0, slot_count)
    return jnp.concatenate([first_pass.astype(jnp.int32), more_slots.astype(jnp.int32)], axis=1).reshape(-1)


def draw_induct_slots(key, part):
    key = jax.random.fold_in(key, 11)
    return slot_draw(key, N_ROW * CAPL, LT)


def draw_coeff_slots(key, part):
    key = jax.random.fold_in(key, 23)
    return slot_draw(key, N_ROW * CAPP, PT)


def draw_end_slots(key, part):
    key = jax.random.fold_in(key, 37)
    dev_count = N_ROW * N_COL
    orders = jax.vmap(lambda sub: jax.random.permutation(sub, 2 * SB_COL))(jax.random.split(key, dev_count))
    return orders.astype(jnp.int32).reshape(dev_count * SB_COL, 2)


def with_ends(values, rng, smallest, high):
    spot = [jax.random.randint(jax.random.fold_in(rng, axis), (), 0, length) for axis, length in enumerate(values.shape)]
    longest = values.shape.index(max(values.shape))
    beside = spot[:longest] + [(spot[longest] + 1) % values.shape[longest]] + spot[longest + 1:]
    return values.at[tuple(spot)].set(smallest).at[tuple(beside)].set(high)


def steps_of(key, dims, pieces, low, largest):
    def one(position, shards_of):
        heights = jax.random.uniform(jax.random.fold_in(jax.random.fold_in(key, 6), position), (shards_of,), jnp.float32, low / len(pieces), largest / len(pieces))
        return jnp.repeat(jnp.exp(heights), dims[position] // shards_of).reshape((-1,) + (1,) * (len(dims) - position - 1))

    loudness = one(*pieces[0])
    for cut in pieces[1:]:
        loudness = loudness * one(*cut)
    return loudness


def noise(key, extent, spread, most, pieces=(), kind=jnp.bfloat16):
    values = spread * jax.random.normal(key, extent, jnp.float32)
    if pieces:
        values = values * steps_of(key, extent, pieces, -0.22, 0.18)
    return jnp.clip(values, -most, most).astype(kind)


def setup_inputs(seed: int = 0, part: int = 0) -> dict:
    seeds = jax.random.split(jax.random.key(seed), 15)
    part_keys = jax.random.split(jax.random.fold_in(seeds[14], part), 15)
    current = noise(part_keys[0], (R, NSEG), 1.0, 6.0, ((0, 2), (1, 8)))
    charge = noise(part_keys[1], (R, NPAN), 1.0, 6.0, ((0, 2), (1, 8)))
    rhs_scale = jnp.clip(jnp.exp(math.log(2.0) - 1.3862944 * jax.random.uniform(part_keys[2], (R,), jnp.float32) ** steps_of(part_keys[2], (R,), ((0, 2),), -0.2, 0.2)), 0.5, 2.0)
    induct_tiles = noise(part_keys[3], (N_ROW * N_COL * LT, BLK, BLK), (LT * BLK // SB_COL) ** -0.5, 0.21875, ((0, 8),))
    induct_rows = with_ends(jax.random.randint(part_keys[4], (N_ROW * N_COL * LT,), 0, SB_COL * N_COL), jax.random.fold_in(part_keys[4], 1), 0, (SB_COL * N_COL) - 1).astype(jnp.int32)
    induct_slots = draw_induct_slots(jax.random.fold_in(jax.random.fold_in(seeds[14], part), 71), part)
    induct_needs = with_ends(jax.random.randint(part_keys[6], (N_ROW * N_COL * N_ROW, CAPL), 0, SB_COL * N_COL), jax.random.fold_in(part_keys[6], 1), 0, (SB_COL * N_COL) - 1).astype(jnp.int32)
    coeff_tiles = noise(part_keys[7], (N_ROW * N_COL * PT, BLK, BLK), (PT * BLK // PB_COL) ** -0.5, 0.109375, ((0, 8),))
    coeff_rows = with_ends(jax.random.randint(part_keys[8], (N_ROW * N_COL * PT,), 0, PB_COL * N_COL), jax.random.fold_in(part_keys[8], 1), 0, (PB_COL * N_COL) - 1).astype(jnp.int32)
    coeff_slots = draw_coeff_slots(jax.random.fold_in(jax.random.fold_in(seeds[14], part), 71), part)
    coeff_needs = with_ends(jax.random.randint(part_keys[10], (N_ROW * N_COL * N_ROW, CAPP), 0, PB_COL * N_COL), jax.random.fold_in(part_keys[10], 1), 0, (PB_COL * N_COL) - 1).astype(jnp.int32)
    link_needs = with_ends(jax.random.randint(part_keys[11], (N_ROW * N_COL * N_ROW, CAPK), 0, PB_COL * N_COL), jax.random.fold_in(part_keys[11], 1), 0, (PB_COL * N_COL) - 1).astype(jnp.int32)
    end_slots = draw_end_slots(jax.random.fold_in(jax.random.fold_in(seeds[14], part), 71), part)
    end_offsets = with_ends(jax.random.randint(part_keys[13], (NSEG, 2), 0, BLK), jax.random.fold_in(part_keys[13], 1), 0, BLK - 1).astype(jnp.int32)
    return dict(current=current, charge=charge, rhs_scale=rhs_scale, induct_tiles=induct_tiles, induct_rows=induct_rows, induct_slots=induct_slots, induct_needs=induct_needs, coeff_tiles=coeff_tiles, coeff_rows=coeff_rows, coeff_slots=coeff_slots, coeff_needs=coeff_needs, link_needs=link_needs, end_slots=end_slots, end_offsets=end_offsets)


def tile_apply(blocks, tile_set, sources, targets, block_count):
    dev_count = N_ROW * N_COL
    tiles_dev = tile_set.reshape(dev_count, -1, BLK, BLK)
    src_dev = sources.reshape(dev_count, -1)
    dst_dev = targets.reshape(dev_count, -1)

    def one_device(running, inputs):
        tile_group, src_set, dst_set = inputs
        picked = jnp.take(blocks, src_set, axis=1).astype(jnp.float32)
        product = jnp.einsum('rta,tab->rtb', picked, tile_group.astype(jnp.float32), precision=lax.Precision.HIGHEST)
        return running.at[:, dst_set].add(product), None

    start = jnp.zeros((R, block_count, BLK), jnp.float32)
    running, _unused = lax.scan(one_device, start, (tiles_dev, src_dev, dst_dev))
    return running


def reference(current, charge, rhs_scale, induct_tiles, induct_rows, induct_slots, induct_needs, coeff_tiles, coeff_rows, coeff_slots, coeff_needs, link_needs, end_slots, end_offsets):
    dev_count = N_ROW * N_COL
    seg_group = SB_COL * N_COL
    pan_group = PB_COL * N_COL
    seg_blocks = dev_count * SB_COL
    pan_blocks = dev_count * PB_COL
    cur_blocks = current.reshape(R, seg_blocks, BLK)
    chg_blocks = charge.reshape(R, pan_blocks, BLK)
    row_of = jnp.arange(dev_count, dtype=jnp.int32) // N_COL
    peer_row = jnp.arange(N_ROW, dtype=jnp.int32)
    ind_global = (peer_row[None, :, None] * seg_group + induct_needs.reshape(dev_count, N_ROW, CAPL)).reshape(dev_count, -1)
    ind_owner = jnp.arange(dev_count * LT, dtype=jnp.int32) // LT
    ind_source = ind_global[ind_owner, induct_slots]
    ind_target = row_of[ind_owner] * seg_group + induct_rows
    field = tile_apply(cur_blocks, induct_tiles, ind_source, ind_target, seg_blocks)
    coe_global = (peer_row[None, :, None] * pan_group + coeff_needs.reshape(dev_count, N_ROW, CAPP)).reshape(dev_count, -1)
    coe_owner = jnp.arange(dev_count * PT, dtype=jnp.int32) // PT
    coe_source = coe_global[coe_owner, coeff_slots]
    coe_target = row_of[coe_owner] * pan_group + coeff_rows
    coeff = tile_apply(chg_blocks, coeff_tiles, coe_source, coe_target, pan_blocks)
    potential = coeff.reshape(R, -1).astype(jnp.bfloat16)
    link_global = (peer_row[None, :, None] * pan_group + link_needs.reshape(dev_count, N_ROW, CAPK)).reshape(dev_count, -1)
    block_owner = jnp.arange(seg_blocks, dtype=jnp.int32) // SB_COL
    end_panel = link_global[block_owner[:, None], end_slots]
    offsets = end_offsets.reshape(seg_blocks, BLK, 2)
    end_signs = jnp.array([1.0, -1.0], jnp.float32)
    values = cur_blocks.astype(jnp.float32)[:, :, :, None] * end_signs
    block_index = jnp.arange(seg_blocks, dtype=jnp.int32)
    end_index = jnp.arange(2, dtype=jnp.int32)
    sum_keys = (block_index[:, None, None] * 2 + end_index[None, None, :]) * BLK + offsets
    end_sums = jax.ops.segment_sum(values.reshape(R, -1).T, sum_keys.reshape(-1), num_segments=seg_blocks * 2 * BLK)
    end_sums = lax.optimization_barrier(end_sums.astype(jnp.bfloat16)).astype(jnp.float32)
    offset_range = jnp.arange(BLK, dtype=jnp.int32)
    destination = (end_panel[:, :, None] * BLK + offset_range[None, None, :]).reshape(-1)
    incoming = jnp.zeros((pan_blocks * BLK, R), jnp.float32).at[destination].add(end_sums)
    pan_out = (rhs_scale[:, None] * charge.astype(jnp.float32) + incoming.T).astype(jnp.bfloat16)
    pot_flat = potential.astype(jnp.float32)
    panel_index = end_panel[:, None, :] * BLK + offsets
    at_ends = pot_flat[:, panel_index]
    seg_out = (field + at_ends[..., 0] - at_ends[..., 1]).reshape(R, -1).astype(jnp.bfloat16)
    return seg_out, pan_out, potential
```

```python
import functools

import jax
import jax.numpy as jnp
from jax import lax
from jax.experimental import pallas as pl
from jax.experimental.pallas import tpu as pltpu
from jax.sharding import PartitionSpec as P

F32 = jnp.float32
BF16 = jnp.bfloat16
VMEM = pl.BlockSpec(memory_space=pltpu.VMEM)
SMEM = pl.BlockSpec(memory_space=pltpu.SMEM)
ANY = pl.BlockSpec(memory_space=pl.ANY)


def shift(x, axis, k):
    n = lax.axis_size(axis)
    if k % n == 0:
        return x
    return lax.ppermute(x, axis, [(i, (i + k) % n) for i in range(n)])


def call(body, name, out_shape, in_specs, scratch=(), limit=16, flops=0, moved=0):
    return pl.pallas_call(
        body,
        out_shape=out_shape,
        in_specs=in_specs,
        out_specs=[VMEM] * len(out_shape),
        scratch_shapes=list(scratch),
        compiler_params=pltpu.CompilerParams(vmem_limit_bytes=limit * 2**20),
        cost_estimate=pl.CostEstimate(flops=flops, bytes_accessed=moved, transcendentals=0),
        name=name,
    )


def wrapped(x, n):
    return lax.rem(x + n, n)


def one_hot_rows(off_ref, k, width):
    levels = lax.broadcasted_iota(jnp.int32, (width, width), 0)
    span = pl.ds(pl.multiple_of(k * width, width), width)
    to_hot = jnp.where(levels == off_ref[0:1, span], 1.0, 0.0).astype(BF16)
    from_hot = jnp.where(levels == off_ref[1:2, span], -1.0, 0.0).astype(BF16)
    return jnp.concatenate([to_hot, from_hot], axis=0)


def ends_body(n_row, n_col, seg_own, pan_own, cap, slots, links, cur, off, own, *rest):
    sends, acc = rest[:-1], rest[-1]
    width = cur.shape[1] // seg_own
    pan_group = pan_own * n_col
    r, c = lax.axis_index("row"), lax.axis_index("col")
    acc[...] = jnp.zeros_like(acc)

    def block(k):
        span = pl.ds(pl.multiple_of(k * width, width), width)
        hot = one_hot_rows(off, k, width)
        sums = lax.dot_general(cur[:, span], hot, (((1,), (1,)), ((), ())), preferred_element_type=F32)
        return sums.astype(BF16).astype(F32)

    unroll = 4

    def step(i, carry):
        got = [block(i * unroll + u) for u in range(unroll)]
        for u in range(unroll):
            for e in range(2):
                slot = slots[e, i * unroll + u]
                p = lax.div(slot, cap)
                b = links[p, slot - p * cap]
                place = wrapped(p - r, n_row) * pan_group + b
                acc[place] += got[u][:, e * width : (e + 1) * width]
        return carry

    lax.fori_loop(0, seg_own // unroll, step, 0)
    for k in range(n_row):
        own[k] = acc[pl.ds(k * pan_group + c * pan_own, pan_own)]
        for j in range(1, n_col):
            there = lax.rem(c + j, n_col)
            sends[j - 1][k] = acc[pl.ds(k * pan_group + there * pan_own, pan_own)].astype(BF16)


def pick_body(n_row, n_col, seg_own, pan_own, cap_l, cap_p, *refs):
    asked = refs[:n_row]
    cur = refs[n_row : n_row + n_col]
    chg = refs[n_row + n_col : n_row + 2 * n_col]
    outs = refs[n_row + 2 * n_col :]
    width = cur[0].shape[1] // seg_own
    r, c = lax.axis_index("row"), lax.axis_index("col")

    def block(parts, own_blocks, b):
        owner = lax.div(b, own_blocks)
        j = wrapped(owner - c, n_col)
        span = pl.ds(pl.multiple_of((b - owner * own_blocks) * width, width), width)
        value = parts[0][:, span]
        for q in range(1, n_col):
            value = jnp.where(j == q, parts[q][:, span], value)
        return value

    for k in range(n_row):
        for s in range(cap_l):
            outs[k][s] = block(cur, seg_own, asked[k][r, s])
        for s in range(cap_p):
            outs[k][cap_l + s] = block(chg, pan_own, asked[k][r, cap_l + s])


def tile_copies(tiles, held, sems):
    chunks = sems.shape[0]
    size = tiles.shape[0] // chunks
    spans = [pl.ds(q * size, size) for q in range(chunks)]
    return [pltpu.make_async_copy(tiles.at[s], held.at[s], sems.at[q]) for q, s in enumerate(spans)]


def multiply(copies, held, src, slots, rows, acc, unroll):
    size = held.shape[0] // len(copies)
    for q, copy in enumerate(copies):
        copy.wait()

        def step(i, carry):
            at = [q * size + i * unroll + u for u in range(unroll)]
            got = [jnp.dot(src[slots[t]], held[t], preferred_element_type=F32) for t in at]
            for t, value in zip(at, got):
                acc[rows[t]] += value
            return carry

        lax.fori_loop(0, size // unroll, step, 0)


def coeff_body(n_row, n_col, cap_l, cap_p, slots, rows, *refs):
    got = refs[:n_row]
    ends_own = refs[n_row]
    ends_in = refs[n_row + 1 : n_row + n_col]
    tiles = refs[n_row + n_col]
    part, end_keep, *end_sends = refs[n_row + n_col + 1 : -3]
    src, held, sems = refs[-3:]
    r = lax.axis_index("row")
    copies = tile_copies(tiles, held, sems)
    for copy in copies:
        copy.start()
    for k in range(n_row):
        src[pl.ds(lax.rem(r + k, n_row) * cap_p, cap_p)] = got[k][pl.ds(cap_l, cap_p)]
        total = ends_own[k]
        for more in ends_in:
            total += more[k].astype(F32)
        if k == 0:
            end_keep[...] = total
        else:
            end_sends[k - 1][...] = total.astype(BF16)
    part[...] = jnp.zeros_like(part)
    multiply(copies, held, src, slots, rows, part, 8)


def induct_body(n_row, n_col, seg_own, cap_l, slots, rows, *refs):
    got = refs[:n_row]
    tiles = refs[n_row]
    own, *sends = refs[n_row + 1 : -4]
    src, held, acc, sems = refs[-4:]
    r, c = lax.axis_index("row"), lax.axis_index("col")
    copies = tile_copies(tiles, held, sems)
    for copy in copies:
        copy.start()
    for k in range(n_row):
        src[pl.ds(lax.rem(r + k, n_row) * cap_l, cap_l)] = got[k][pl.ds(0, cap_l)]
    acc[...] = jnp.zeros_like(acc)
    multiply(copies, held, src, slots, rows, acc, 8)
    own[...] = acc[pl.ds(c * seg_own, seg_own)]
    for j in range(1, n_col):
        sends[j - 1][...] = acc[pl.ds(lax.rem(c + j, n_col) * seg_own, seg_own)].astype(BF16)


def final_body(n_row, n_col, seg_own, pan_own, cap, slots, links, off, charge, scale, *refs):
    field_own, end_own = refs[0], refs[1]
    field_in = refs[2 : 1 + n_col]
    end_in = refs[1 + n_col : n_col + n_row]
    pots = refs[n_col + n_row : n_col + 2 * n_row]
    seg_out, pan_out, pot_out, held = refs[n_col + 2 * n_row :]
    width = charge.shape[1] // pan_own
    pan_group = pan_own * n_col
    r, c = lax.axis_index("row"), lax.axis_index("col")
    for k in range(n_row):
        held[pl.ds(lax.rem(r + k, n_row) * pan_group, pan_group)] = pots[k][...]
    for q in range(pan_own):
        span = slice(q * width, (q + 1) * width)
        total = end_own[q]
        for more in end_in:
            total += more[q].astype(F32)
        pan_out[:, span] = (scale[...] * charge[:, span].astype(F32) + total).astype(BF16)
        pot_out[:, span] = pots[0][c * pan_own + q]

    def block(k):
        ends = []
        for e in range(2):
            slot = slots[e, k]
            p = lax.div(slot, cap)
            ends.append(held[p * pan_group + links[p, slot - p * cap]])
        drops = jnp.dot(
            jnp.concatenate(ends, axis=1), one_hot_rows(off, k, width), preferred_element_type=F32
        )
        total = field_own[k]
        for more in field_in:
            total += more[k].astype(F32)
        return (total + drops).astype(BF16)

    unroll = 4

    def step(i, carry):
        for u in range(unroll):
            k = i * unroll + u
            seg_out[:, pl.ds(pl.multiple_of(k * width, width), width)] = block(k)
        return carry

    lax.fori_loop(0, seg_own // unroll, step, 0)


def shards(
    current,
    charge,
    rhs_scale,
    induct_tiles,
    induct_rows,
    induct_slots,
    induct_needs,
    coeff_tiles,
    coeff_rows,
    coeff_slots,
    coeff_needs,
    link_needs,
    end_slots,
    end_offsets,
):
    n_row = lax.axis_size("row")
    n_col = lax.axis_size("col")
    width = induct_tiles.shape[1]
    rhs = current.shape[0]
    seg_own = current.shape[1] // width
    pan_own = charge.shape[1] // width
    seg_group, pan_group = seg_own * n_col, pan_own * n_col
    cap_l, cap_p, cap_k = induct_needs.shape[1], coeff_needs.shape[1], link_needs.shape[1]
    slots_t, off_t = end_slots.T, end_offsets.T

    def like(blocks, dtype):
        return jax.ShapeDtypeStruct((*blocks, rhs, width), dtype)

    needs = jnp.concatenate([induct_needs, coeff_needs], axis=1)
    asked = [shift(needs, "row", k) for k in range(n_row)]
    cur = [shift(current, "col", -j) for j in range(n_col)]
    chg = [shift(charge, "col", -j) for j in range(n_col)]

    ends_own, *ends_out = call(
        functools.partial(ends_body, n_row, n_col, seg_own, pan_own, cap_k),
        "end_sums",
        [like((n_row, pan_own), F32)] + [like((n_row, pan_own), BF16)] * (n_col - 1),
        [SMEM, SMEM, VMEM, VMEM],
        [pltpu.VMEM((n_row * pan_group, rhs, width), F32)],
        flops=2 * 10**9,
        moved=2**18,
    )(slots_t, link_needs, current, off_t)

    picked = call(
        functools.partial(pick_body, n_row, n_col, seg_own, pan_own, cap_l, cap_p),
        "pick_blocks",
        [like((cap_l + cap_p,), BF16)] * n_row,
        [SMEM] * n_row + [VMEM] * (2 * n_col),
        moved=2**20,
    )(*asked, *cur, *chg)
    got = [shift(x, "row", -k) for k, x in enumerate(picked)]
    ends_in = [shift(x, "col", j + 1) for j, x in enumerate(ends_out)]

    pt = coeff_tiles.shape[0]
    part, end_keep, *end_sends = call(
        functools.partial(coeff_body, n_row, n_col, cap_l, cap_p),
        "coeff_tiles",
        [like((pan_group,), F32), like((pan_own,), F32)] + [like((pan_own,), BF16)] * (n_row - 1),
        [SMEM, SMEM] + [VMEM] * (n_row + n_col) + [ANY],
        [
            pltpu.VMEM((n_row * cap_p, rhs, width), BF16),
            pltpu.VMEM(coeff_tiles.shape, BF16),
            pltpu.SemaphoreType.DMA((4,)),
        ],
        flops=2 * 10**9,
        moved=coeff_tiles.size * 2,
    )(coeff_slots, coeff_rows, *got, ends_own, *ends_in, coeff_tiles)
    parts = [shift(part, "col", j) for j in range(n_col)]
    end_in = [shift(x, "row", k + 1) for k, x in enumerate(end_sends)]

    field_own, *field_out = call(
        functools.partial(induct_body, n_row, n_col, seg_own, cap_l),
        "induct_tiles",
        [like((seg_own,), F32)] + [like((seg_own,), BF16)] * (n_col - 1),
        [SMEM, SMEM] + [VMEM] * n_row + [ANY],
        [
            pltpu.VMEM((n_row * cap_l, rhs, width), BF16),
            pltpu.VMEM(induct_tiles.shape, BF16),
            pltpu.VMEM((seg_group, rhs, width), F32),
            pltpu.SemaphoreType.DMA((8,)),
        ],
        flops=4 * 10**9,
        moved=induct_tiles.size * 2,
    )(induct_slots, induct_rows, *got, induct_tiles)
    field_in = [shift(x, "col", j + 1) for j, x in enumerate(field_out)]

    potential = parts[0]
    for more in parts[1:]:
        potential = potential + more
    potential = potential.astype(BF16)
    pots = [shift(potential, "row", -k) for k in range(n_row)]

    return tuple(
        call(
            functools.partial(final_body, n_row, n_col, seg_own, pan_own, cap_k),
            "outputs",
            [jax.ShapeDtypeStruct(x.shape, BF16) for x in (current, charge, charge)],
            [SMEM, SMEM] + [VMEM] * (3 + n_col + 2 * n_row),
            [pltpu.VMEM((n_row * pan_group, rhs, width), BF16)],
            flops=2 * 10**9,
            moved=2**20,
        )(
            slots_t,
            link_needs,
            off_t,
            charge,
            rhs_scale[:, None],
            field_own,
            end_keep,
            *field_in,
            *end_in,
            *pots,
        )
    )


def solution(mesh):
    blocks = P(("parts", "row", "col"))
    matrix = P(("parts", "row", "col"), None)
    tiles = P(("parts", "row", "col"), None, None)
    values = P("rhs", ("parts", "row", "col"))
    return jax.shard_map(
        shards,
        mesh=mesh,
        in_specs=(
            values,
            values,
            P(("parts", "rhs")),
            tiles,
            blocks,
            blocks,
            matrix,
            tiles,
            blocks,
            blocks,
            matrix,
            matrix,
            matrix,
            matrix,
        ),
        out_specs=(values, values, values),
        check_vma=False,
    )
```

```python
import functools

import jax
import jax.numpy as jnp
from jax import lax
from jax.experimental import pallas as pl
from jax.experimental.pallas import tpu as pltpu
from jax.sharding import PartitionSpec as P

F32 = jnp.float32
BF16 = jnp.bfloat16
VMEM = pl.BlockSpec(memory_space=pltpu.VMEM)
SMEM = pl.BlockSpec(memory_space=pltpu.SMEM)
ANY = pl.BlockSpec(memory_space=pl.ANY)


def shift(x, axis, k):
    n = lax.axis_size(axis)
    if k % n == 0:
        return x
    return lax.ppermute(x, axis, [(i, (i + k) % n) for i in range(n)])


def call(body, name, out_shape, in_specs, scratch=(), limit=16, flops=0, moved=0):
    return pl.pallas_call(
        body,
        out_shape=out_shape,
        in_specs=in_specs,
        out_specs=[VMEM] * len(out_shape),
        scratch_shapes=list(scratch),
        compiler_params=pltpu.CompilerParams(vmem_limit_bytes=limit * 2**20),
        cost_estimate=pl.CostEstimate(flops=flops, bytes_accessed=moved, transcendentals=0),
        name=name,
    )


def in_hbm(*arrays):
    return [pltpu.with_memory_space_constraint(x, pltpu.HBM) for x in arrays]


def wrapped(x, n):
    return lax.rem(x + n, n)


def one_hot_rows(off_ref, k, width):
    levels = lax.broadcasted_iota(jnp.int32, (width, width), 0)
    span = pl.ds(pl.multiple_of(k * width, width), width)
    to_hot = jnp.where(levels == off_ref[0:1, span], 1.0, 0.0).astype(BF16)
    from_hot = jnp.where(levels == off_ref[1:2, span], -1.0, 0.0).astype(BF16)
    return jnp.concatenate([to_hot, from_hot], axis=0)


def ends_body(n_row, n_col, seg_own, pan_own, cap, slots, links, cur, off, own, *rest):
    sends, acc = rest[:-1], rest[-1]
    width = cur.shape[1] // seg_own
    pan_group = pan_own * n_col
    r, c = lax.axis_index("row"), lax.axis_index("col")
    acc[...] = jnp.zeros_like(acc)

    def block(k):
        span = pl.ds(pl.multiple_of(k * width, width), width)
        hot = one_hot_rows(off, k, width)
        sums = lax.dot_general(cur[:, span], hot, (((1,), (1,)), ((), ())), preferred_element_type=F32)
        return sums.astype(BF16).astype(F32)

    unroll = 4

    def step(i, carry):
        got = [block(i * unroll + u) for u in range(unroll)]
        for u in range(unroll):
            for e in range(2):
                slot = slots[e, i * unroll + u]
                p = lax.div(slot, cap)
                b = links[p, slot - p * cap]
                place = wrapped(p - r, n_row) * pan_group + b
                acc[place] += got[u][:, e * width : (e + 1) * width]
        return carry

    lax.fori_loop(0, seg_own // unroll, step, 0)
    for k in range(n_row):
        here = pl.ds(k * pan_own, pan_own)
        own[here] = acc[pl.ds(k * pan_group + c * pan_own, pan_own)]
        for j in range(1, n_col):
            there = lax.rem(c + j, n_col)
            sends[j - 1][here] = acc[pl.ds(k * pan_group + there * pan_own, pan_own)].astype(BF16)


def pick_body(n_row, n_col, seg_own, pan_own, cap_l, cap_p, *refs):
    asked = refs[:n_row]
    cur = refs[n_row : n_row + n_col]
    chg = refs[n_row + n_col : n_row + 2 * n_col]
    outs = refs[n_row + 2 * n_col :]
    width = cur[0].shape[1] // seg_own
    r, c = lax.axis_index("row"), lax.axis_index("col")

    def block(parts, own_blocks, b):
        owner = lax.div(b, own_blocks)
        j = wrapped(owner - c, n_col)
        span = pl.ds(pl.multiple_of((b - owner * own_blocks) * width, width), width)
        value = parts[0][:, span]
        for q in range(1, n_col):
            value = jnp.where(j == q, parts[q][:, span], value)
        return value

    for k in range(n_row):
        for s in range(cap_l):
            outs[k][s] = block(cur, seg_own, asked[k][r, s])
        for s in range(cap_p):
            outs[k][cap_l + s] = block(chg, pan_own, asked[k][r, cap_l + s])


def tile_copies(tiles, held, sems):
    chunks = sems.shape[0]
    size = tiles.shape[0] // chunks
    spans = [pl.ds(q * size, size) for q in range(chunks)]
    return [pltpu.make_async_copy(tiles.at[s], held.at[s], sems.at[q]) for q, s in enumerate(spans)]


def multiply(held, first, count, src, slots, rows, acc, unroll, paired):
    def products(t):
        if not paired:
            return [jnp.dot(src[slots[t]], held[t], preferred_element_type=F32)]
        left = jnp.concatenate([src[slots[t]], src[slots[t + 1]]], axis=0)
        both = jnp.dot(left, jnp.concatenate([held[t], held[t + 1]], axis=1), preferred_element_type=F32)
        rhs, width = src.shape[1:]
        return [both[:rhs, :width], both[rhs:, width:]]

    def step(i, carry):
        start = first + i * unroll
        got = []
        for u in range(0, unroll, 2 if paired else 1):
            got += products(start + u)
        for u, value in enumerate(got):
            acc[rows[start + u]] += value
        return carry

    lax.fori_loop(0, count // unroll, step, 0)


def coeff_body(n_row, n_col, cap_l, cap_p, slots, rows, *refs):
    got = refs[:n_row]
    ends_out = refs[n_row : n_row + n_col - 1]
    tiles = refs[n_row + n_col - 1]
    part, *messages = refs[n_row + n_col : -1]
    src = refs[-1]
    r = lax.axis_index("row")
    for k in range(n_row):
        src[pl.ds(lax.rem(r + k, n_row) * cap_p, cap_p)] = got[k][pl.ds(cap_l, cap_p)]
    part[...] = jnp.zeros_like(part)
    multiply(tiles, 0, tiles.shape[0], src, slots, rows, part, 8, False)
    high = part[...].astype(BF16)
    low = (part[...] - high.astype(F32)).astype(BF16)
    pan_group = part.shape[0]
    for message, ends in zip(messages, ends_out):
        count = ends.shape[0]
        message[pl.ds(0, count)] = ends[...]
        message[pl.ds(count, pan_group)] = high
        message[pl.ds(count + pan_group, pan_group)] = low


def panels_body(n_row, n_col, pan_own, part, ends_own, *refs):
    arrived = refs[: n_col - 1]
    pot, end_keep, *messages = refs[n_col - 1 :]
    pan_group = part.shape[0]
    count = n_row * pan_own
    total = part[...]
    for x in arrived:
        high, low = x[pl.ds(count, pan_group)], x[pl.ds(count + pan_group, pan_group)]
        total += high.astype(F32) + low.astype(F32)
    rounded = total.astype(BF16)
    pot[...] = rounded
    for k in range(n_row):
        here = pl.ds(k * pan_own, pan_own)
        sums = ends_own[here]
        for x in arrived:
            sums += x[here].astype(F32)
        if k == 0:
            end_keep[...] = sums
        else:
            messages[k - 1][pl.ds(0, pan_own)] = sums.astype(BF16)
            messages[k - 1][pl.ds(pan_own, pan_group)] = rounded


def induct_body(n_row, n_col, seg_own, cap_l, slots, rows, *refs):
    got = refs[:n_row]
    tiles = refs[n_row]
    own, *sends = refs[n_row + 1 : -4]
    src, held, acc, sems = refs[-4:]
    r, c = lax.axis_index("row"), lax.axis_index("col")
    copies = tile_copies(tiles, held, sems)
    for copy in copies:
        copy.start()
    for k in range(n_row):
        src[pl.ds(lax.rem(r + k, n_row) * cap_l, cap_l)] = got[k][pl.ds(0, cap_l)]
    acc[...] = jnp.zeros_like(acc)
    size = tiles.shape[0] // len(copies)
    for q, copy in enumerate(copies):
        copy.wait()
        multiply(held, q * size, size, src, slots, rows, acc, 8, True)
    own[...] = acc[pl.ds(c * seg_own, seg_own)]
    for j in range(1, n_col):
        sends[j - 1][...] = acc[pl.ds(lax.rem(c + j, n_col) * seg_own, seg_own)].astype(BF16)


def final_body(n_row, n_col, seg_own, pan_own, cap, slots, links, off, charge, scale, *refs):
    field_own, end_own, pot = refs[:3]
    field_in = refs[3 : 2 + n_col]
    arrived = refs[2 + n_col : 1 + n_col + n_row]
    seg_out, pan_out, pot_out, held = refs[1 + n_col + n_row :]
    width = charge.shape[1] // pan_own
    pan_group = pan_own * n_col
    r, c = lax.axis_index("row"), lax.axis_index("col")
    held[pl.ds(r * pan_group, pan_group)] = pot[...]
    for k, x in enumerate(arrived):
        sender = wrapped(r - (k + 1), n_row)
        held[pl.ds(sender * pan_group, pan_group)] = x[pl.ds(pan_own, pan_group)]
    for q in range(pan_own):
        span = slice(q * width, (q + 1) * width)
        total = end_own[q]
        for x in arrived:
            total += x[q].astype(F32)
        pan_out[:, span] = (scale[...] * charge[:, span].astype(F32) + total).astype(BF16)
        pot_out[:, span] = pot[c * pan_own + q]

    def block(k):
        ends = []
        for e in range(2):
            slot = slots[e, k]
            p = lax.div(slot, cap)
            ends.append(held[p * pan_group + links[p, slot - p * cap]])
        drops = jnp.dot(
            jnp.concatenate(ends, axis=1), one_hot_rows(off, k, width), preferred_element_type=F32
        )
        total = field_own[k]
        for more in field_in:
            total += more[k].astype(F32)
        return (total + drops).astype(BF16)

    unroll = 4

    def step(i, carry):
        for u in range(unroll):
            k = i * unroll + u
            seg_out[:, pl.ds(pl.multiple_of(k * width, width), width)] = block(k)
        return carry

    lax.fori_loop(0, seg_own // unroll, step, 0)


def shards(
    current,
    charge,
    rhs_scale,
    induct_tiles,
    induct_rows,
    induct_slots,
    induct_needs,
    coeff_tiles,
    coeff_rows,
    coeff_slots,
    coeff_needs,
    link_needs,
    end_slots,
    end_offsets,
):
    n_row = lax.axis_size("row")
    n_col = lax.axis_size("col")
    width = induct_tiles.shape[1]
    rhs = current.shape[0]
    seg_own = current.shape[1] // width
    pan_own = charge.shape[1] // width
    seg_group, pan_group = seg_own * n_col, pan_own * n_col
    cap_l, cap_p, cap_k = induct_needs.shape[1], coeff_needs.shape[1], link_needs.shape[1]
    slots_t, off_t = end_slots.T, end_offsets.T

    def like(blocks, dtype):
        return jax.ShapeDtypeStruct((*blocks, rhs, width), dtype)

    needs = jnp.concatenate([induct_needs, coeff_needs], axis=1)
    asked = [shift(needs, "row", k) for k in range(n_row)]
    cur = [shift(current, "col", -j) for j in range(n_col)]
    chg = [shift(charge, "col", -j) for j in range(n_col)]

    ends_own, *ends_out = call(
        functools.partial(ends_body, n_row, n_col, seg_own, pan_own, cap_k),
        "end_sums",
        [like((n_row * pan_own,), F32)] + [like((n_row * pan_own,), BF16)] * (n_col - 1),
        [SMEM, SMEM, VMEM, VMEM],
        [pltpu.VMEM((n_row * pan_group, rhs, width), F32)],
        flops=2 * 10**9,
        moved=2**18,
    )(*in_hbm(slots_t, link_needs, current, off_t))

    picked = call(
        functools.partial(pick_body, n_row, n_col, seg_own, pan_own, cap_l, cap_p),
        "pick_blocks",
        [like((cap_l + cap_p,), BF16)] * n_row,
        [SMEM] * n_row + [VMEM] * (2 * n_col),
        moved=2**20,
    )(*asked, *in_hbm(cur[0]), *cur[1:], *in_hbm(chg[0]), *chg[1:])
    got = [shift(x, "row", -k) for k, x in enumerate(picked)]

    message = like((n_row * pan_own + 2 * pan_group,), BF16)
    part, *col_messages = call(
        functools.partial(coeff_body, n_row, n_col, cap_l, cap_p),
        "coeff_tiles",
        [like((pan_group,), F32)] + [message] * (n_col - 1),
        [SMEM, SMEM] + [VMEM] * (n_row + n_col),
        [pltpu.VMEM((n_row * cap_p, rhs, width), BF16)],
        flops=2 * 10**9,
        moved=coeff_tiles.size * 2,
    )(coeff_slots, coeff_rows, *got, *ends_out, coeff_tiles)
    from_col = [shift(x, "col", j + 1) for j, x in enumerate(col_messages)]

    field_own, *field_out = call(
        functools.partial(induct_body, n_row, n_col, seg_own, cap_l),
        "induct_tiles",
        [like((seg_own,), F32)] + [like((seg_own,), BF16)] * (n_col - 1),
        [SMEM, SMEM] + [VMEM] * n_row + [ANY],
        [
            pltpu.VMEM((n_row * cap_l, rhs, width), BF16),
            pltpu.VMEM(induct_tiles.shape, BF16),
            pltpu.VMEM((seg_group, rhs, width), F32),
            pltpu.SemaphoreType.DMA((8,)),
        ],
        flops=4 * 10**9,
        moved=induct_tiles.size * 2,
    )(induct_slots, induct_rows, *got, induct_tiles)
    field_in = [shift(x, "col", j + 1) for j, x in enumerate(field_out)]

    pot, end_keep, *row_messages = call(
        functools.partial(panels_body, n_row, n_col, pan_own),
        "panel_sums",
        [like((pan_group,), BF16), like((pan_own,), F32)] + [like((pan_own + pan_group,), BF16)] * (n_row - 1),
        [VMEM] * (1 + n_col),
        moved=2**18,
    )(part, ends_own, *from_col)
    from_row = [shift(x, "row", k + 1) for k, x in enumerate(row_messages)]

    return tuple(
        call(
            functools.partial(final_body, n_row, n_col, seg_own, pan_own, cap_k),
            "outputs",
            [jax.ShapeDtypeStruct(x.shape, BF16) for x in (current, charge, charge)],
            [SMEM, SMEM] + [VMEM] * (4 + n_col + n_row),
            [pltpu.VMEM((n_row * pan_group, rhs, width), BF16)],
            flops=2 * 10**9,
            moved=2**20,
        )(
            slots_t,
            link_needs,
            off_t,
            charge,
            rhs_scale[:, None],
            field_own,
            end_keep,
            pot,
            *field_in,
            *from_row,
        )
    )


def solution(mesh):
    blocks = P(("parts", "row", "col"))
    matrix = P(("parts", "row", "col"), None)
    tiles = P(("parts", "row", "col"), None, None)
    values = P("rhs", ("parts", "row", "col"))
    return jax.shard_map(
        shards,
        mesh=mesh,
        in_specs=(
            values,
            values,
            P(("parts", "rhs")),
            tiles,
            blocks,
            blocks,
            matrix,
            tiles,
            blocks,
            blocks,
            matrix,
            matrix,
            matrix,
            matrix,
        ),
        out_specs=(values, values, values),
        check_vma=False,
    )
```

```python
import functools

import jax
import jax.numpy as jnp
from jax import lax
from jax.experimental import pallas as pl
from jax.experimental.pallas import tpu as pltpu
from jax.sharding import PartitionSpec as P

F32 = jnp.float32
BF16 = jnp.bfloat16
VMEM = pl.BlockSpec(memory_space=pltpu.VMEM)
SMEM = pl.BlockSpec(memory_space=pltpu.SMEM)
ANY = pl.BlockSpec(memory_space=pl.ANY)


def exchange(x, axis, k):
    if k == 0:
        return x
    return lax.ppermute(x, axis, [(i, i ^ k) for i in range(lax.axis_size(axis))])


def exchange_all(first, others, axis):
    n = lax.axis_size(axis)
    got = {0: first}
    for k in reversed(range(1, n)):
        got[k] = exchange(others[k - 1], axis, k)
    return [got[k] for k in range(n)]


def call(body, name, out_shape, in_specs, scratch=(), flops=0, moved=0):
    return pl.pallas_call(
        body,
        out_shape=out_shape,
        in_specs=in_specs,
        out_specs=[VMEM] * len(out_shape),
        scratch_shapes=list(scratch),
        compiler_params=pltpu.CompilerParams(vmem_limit_bytes=16 * 2**20),
        cost_estimate=pl.CostEstimate(flops=flops, bytes_accessed=moved, transcendentals=0),
        name=name,
    )


def in_hbm(*arrays):
    return [pltpu.with_memory_space_constraint(x, pltpu.HBM) for x in arrays]


def pack_body(pan_own, charge, needs, message, wide):
    width = charge.shape[1] // pan_own
    for q in range(pan_own):
        message[q] = charge[:, q * width : (q + 1) * width]
    wide[...] = jnp.zeros_like(wide)
    wide[: needs.shape[0], : needs.shape[1]] = needs[...]
    message[pan_own] = wide[...].astype(F32).astype(BF16)


def ends_body(n_row, n_col, seg_own, pan_own, cap, slots, links, cur, off, own, *rest):
    sends, (blocks, hots, acc) = rest[: n_col - 1], rest[n_col - 1 :]
    width = cur.shape[1] // seg_own
    pan_group = pan_own * n_col
    r, c = lax.axis_index("row"), lax.axis_index("col")
    acc[...] = jnp.zeros_like(acc)
    levels = lax.broadcasted_iota(jnp.int32, (width, width), 0)

    def block(k):
        span = pl.ds(pl.multiple_of(k * width, width), width)
        value = cur[:, span]
        blocks[k] = value
        to_hot = jnp.where(levels == off[0:1, span], 1.0, 0.0).astype(BF16)
        from_hot = jnp.where(levels == off[1:2, span], -1.0, 0.0).astype(BF16)
        hot = jnp.concatenate([to_hot, from_hot], axis=0)
        hots[k] = hot
        sums = lax.dot_general(value, hot, (((1,), (1,)), ((), ())), preferred_element_type=F32)
        return sums.astype(BF16).astype(F32)

    unroll = 8

    def step(i, carry):
        got = [block(i * unroll + u) for u in range(unroll)]
        for u in range(unroll):
            for e in range(2):
                slot = slots[e, i * unroll + u]
                p = lax.div(slot, cap)
                b = links[p, slot - p * cap]
                acc[lax.bitwise_xor(p, r) * pan_group + b] += got[u][:, e * width : (e + 1) * width]
        return carry

    lax.fori_loop(0, seg_own // unroll, step, 0)
    for k in range(n_row):
        here = pl.ds(k * pan_own, pan_own)
        own[here] = acc[pl.ds(k * pan_group + c * pan_own, pan_own)]
        for j in range(1, n_col):
            there = lax.bitwise_xor(c, j)
            sends[j - 1][here] = acc[pl.ds(k * pan_group + there * pan_own, pan_own)].astype(BF16)


def relay_body(n_row, n_col, pan_own, *refs):
    packs = refs[:n_row][::-1]
    ends = refs[n_row : n_row + n_col - 1]
    asked, *messages = refs[n_row + n_col - 1 :]
    r = lax.axis_index("row")
    rhs, width = packs[0].shape[1:]
    mine = lax.broadcasted_iota(jnp.int32, (rhs, width), 0) == r
    for k in range(n_row):
        needs = packs[k][pan_own].astype(F32)
        asked[k : k + 1, :] = jnp.sum(jnp.where(mine, needs, 0.0), axis=0, keepdims=True).astype(jnp.int32)
        for message in messages:
            message[pl.ds(k * pan_own, pan_own)] = packs[k][pl.ds(0, pan_own)]
    for message, sums in zip(messages, ends):
        message[pl.ds(n_row * pan_own, n_row * pan_own)] = sums[...]


def pick_body(n_row, n_col, cap, asked, own, *refs):
    peers, outs = refs[: n_col - 1], refs[n_col - 1 :]
    seg_own, _, width = own.shape
    c = lax.axis_index("col")
    for k in range(n_row):
        for s in range(cap):
            b = asked[k, s]
            holder = lax.div(b, seg_own)
            b = b - holder * seg_own
            j = lax.bitwise_xor(holder, c)
            value = own[b]
            span = pl.ds(pl.multiple_of(b * width, width), width)
            for q, peer in enumerate(peers):
                value = jnp.where(j == q + 1, peer[:, span], value)
            outs[n_row - 1 - k][s] = value


def multiply(tiles, src, source, rows, acc):
    rhs, width = src.shape[1:]
    unroll = min(32, tiles.shape[0])

    def step(i, carry):
        start = i * unroll
        got = []
        for u in range(0, unroll, 2):
            t = start + u
            left = jnp.concatenate([src[source(t)], src[source(t + 1)]], axis=0)
            right = jnp.concatenate([tiles[t], tiles[t + 1]], axis=1)
            both = jnp.dot(left, right, preferred_element_type=F32)
            got += [both[:rhs, :width], both[rhs:, width:]]
        for u, value in enumerate(got):
            acc[rows[start + u]] += value
        return carry

    lax.fori_loop(0, tiles.shape[0] // unroll, step, 0)


def coeff_body(n_row, n_col, pan_own, slots, rows, needs, *refs):
    packs = refs[:n_row][::-1]
    from_col = refs[n_row : n_row + n_col - 1]
    tiles, part, message, src, named = refs[n_row + n_col - 1 :]
    r, c = lax.axis_index("row"), lax.axis_index("col")
    pan_group = pan_own * n_col
    cap = needs.shape[1]
    for k in range(n_row):
        first = lax.bitwise_xor(r, k) * pan_group
        src[pl.ds(first + c * pan_own, pan_own)] = packs[k][pl.ds(0, pan_own)]
        for j, x in enumerate(from_col):
            there = first + lax.bitwise_xor(c, j + 1) * pan_own
            src[pl.ds(there, pan_own)] = x[pl.ds(k * pan_own, pan_own)]
    for p in range(n_row):
        for s in range(cap):
            named[p * cap + s] = p * pan_group + needs[p, s]
    part[...] = jnp.zeros_like(part)
    multiply(tiles, src, lambda t: named[slots[t]], rows, part)
    high = part[...].astype(BF16)
    message[pl.ds(0, pan_group)] = high
    message[pl.ds(pan_group, pan_group)] = (part[...] - high.astype(F32)).astype(BF16)


def induct_body(n_row, n_col, seg_own, slots, rows, _after, *refs):
    got = refs[:n_row][::-1]
    tiles = refs[n_row]
    own, *sends = refs[n_row + 1 : -2]
    src, acc = refs[-2:]
    cap = got[0].shape[0]
    r, c = lax.axis_index("row"), lax.axis_index("col")
    for k in range(n_row):
        src[pl.ds(lax.bitwise_xor(r, k) * cap, cap)] = got[k][...]
    acc[...] = jnp.zeros_like(acc)
    multiply(tiles, src, lambda t: slots[t], rows, acc)
    own[...] = acc[pl.ds(c * seg_own, seg_own)]
    for j in range(1, n_col):
        sends[j - 1][...] = acc[pl.ds(lax.bitwise_xor(c, j) * seg_own, seg_own)].astype(BF16)


def panels_body(n_row, n_col, pan_own, part, ends_own, *refs):
    parts = refs[: n_col - 1]
    relayed = refs[n_col - 1 : 2 * n_col - 2]
    pot, end_keep, *messages = refs[2 * n_col - 2 :]
    pan_group = part.shape[0]
    total = part[...]
    for x in parts:
        total += x[pl.ds(0, pan_group)].astype(F32) + x[pl.ds(pan_group, pan_group)].astype(F32)
    rounded = total.astype(BF16)
    pot[...] = rounded
    for k in range(n_row):
        sums = ends_own[pl.ds(k * pan_own, pan_own)]
        for x in relayed:
            sums += x[pl.ds((n_row + k) * pan_own, pan_own)].astype(F32)
        if k == 0:
            end_keep[...] = sums
        else:
            messages[n_row - 1 - k][pl.ds(0, pan_own)] = sums.astype(BF16)
            messages[n_row - 1 - k][pl.ds(pan_own, pan_group)] = rounded


def final_body(n_row, n_col, pan_own, cap, slots, links, hots, charge, scale, *refs):
    field_own, end_own, pot = refs[:3]
    field_in = refs[3 : 2 + n_col]
    arrived = refs[2 + n_col : 1 + n_col + n_row][::-1]
    seg_out, pan_out, pot_out, held = refs[1 + n_col + n_row :]
    width = charge.shape[1] // pan_own
    pan_group = pan_own * n_col
    r, c = lax.axis_index("row"), lax.axis_index("col")
    held[pl.ds(r * pan_group, pan_group)] = pot[...]
    for k, x in enumerate(arrived):
        sender = lax.bitwise_xor(r, k + 1)
        held[pl.ds(sender * pan_group, pan_group)] = x[pl.ds(pan_own, pan_group)]
    for q in range(pan_own):
        span = slice(q * width, (q + 1) * width)
        total = end_own[q]
        for x in arrived:
            total += x[q].astype(F32)
        pan_out[:, span] = (scale[...] * charge[:, span].astype(F32) + total).astype(BF16)
        pot_out[:, span] = pot[c * pan_own + q]

    def block(k):
        ends = []
        for e in range(2):
            slot = slots[e, k]
            p = lax.div(slot, cap)
            ends.append(held[p * pan_group + links[p, slot - p * cap]])
        drops = jnp.dot(jnp.concatenate(ends, axis=1), hots[k], preferred_element_type=F32)
        total = field_own[k]
        for x in field_in:
            total += x[k].astype(F32)
        return (total + drops).astype(BF16)

    unroll = 16

    def step(i, carry):
        got = [block(i * unroll + u) for u in range(unroll)]
        for u, value in enumerate(got):
            first = pl.multiple_of((i * unroll + u) * width, width)
            seg_out[:, pl.ds(first, width)] = value
        return carry

    lax.fori_loop(0, hots.shape[0] // unroll, step, 0)


def shards(
    current,
    charge,
    rhs_scale,
    induct_tiles,
    induct_rows,
    induct_slots,
    induct_needs,
    coeff_tiles,
    coeff_rows,
    coeff_slots,
    coeff_needs,
    link_needs,
    end_slots,
    end_offsets,
):
    n_row = lax.axis_size("row")
    n_col = lax.axis_size("col")
    width = induct_tiles.shape[1]
    rhs = current.shape[0]
    seg_own = current.shape[1] // width
    pan_own = charge.shape[1] // width
    seg_group, pan_group = seg_own * n_col, pan_own * n_col
    cap_l, cap_p, cap_k = induct_needs.shape[1], coeff_needs.shape[1], link_needs.shape[1]
    slots_t, off_t = end_slots.T, end_offsets.T

    def like(blocks, dtype):
        return jax.ShapeDtypeStruct((blocks, rhs, width), dtype)

    cur = exchange_all(current, [current] * (n_col - 1), "col")
    (pack,) = call(
        functools.partial(pack_body, pan_own),
        "pack_charges",
        [like(pan_own + 1, BF16)],
        [VMEM] * 2,
        [pltpu.VMEM((rhs, width), jnp.int32)],
        moved=2**16,
    )(*in_hbm(charge, induct_needs))
    packs = exchange_all(pack, [pack] * (n_row - 1), "row")

    rows_own = n_row * pan_own
    ends_own, *rest = call(
        functools.partial(ends_body, n_row, n_col, seg_own, pan_own, cap_k),
        "end_sums",
        [like(rows_own, F32)]
        + [like(rows_own, BF16)] * (n_col - 1)
        + [like(seg_own, BF16), jax.ShapeDtypeStruct((seg_own, 2 * width, width), BF16)],
        [SMEM, SMEM, VMEM, VMEM],
        [pltpu.VMEM((n_row * pan_group, rhs, width), F32)],
        flops=2 * 10**9,
        moved=2**18,
    )(*in_hbm(slots_t, link_needs, current, off_t))
    ends_out, (own_blocks, hots) = rest[: n_col - 1], rest[n_col - 1 :]

    asked, *relays = call(
        functools.partial(relay_body, n_row, n_col, pan_own),
        "relay_charges",
        [jax.ShapeDtypeStruct((n_row, width), jnp.int32)] + [like(2 * rows_own, BF16)] * (n_col - 1),
        [VMEM] * (n_row + n_col - 1),
        moved=2**16,
    )(*packs[::-1], *ends_out)
    relayed = exchange_all(None, relays, "col")[1:]

    *picks, own_picks = call(
        functools.partial(pick_body, n_row, n_col, cap_l),
        "pick_blocks",
        [like(cap_l, BF16)] * n_row,
        [SMEM] + [VMEM] * n_col,
        moved=2**18,
    )(asked, own_blocks, *cur[1:])
    got = exchange_all(own_picks, picks[::-1], "row")

    part, message = call(
        functools.partial(coeff_body, n_row, n_col, pan_own),
        "coeff_tiles",
        [like(pan_group, F32), like(2 * pan_group, BF16)],
        [SMEM] * 3 + [VMEM] * (n_row + n_col),
        [
            pltpu.VMEM((n_row * pan_group, rhs, width), BF16),
            pltpu.SMEM((n_row * cap_p,), jnp.int32),
        ],
        flops=2 * 10**9,
        moved=coeff_tiles.size * 2,
    )(coeff_slots, coeff_rows, coeff_needs, *packs[::-1], *relayed, coeff_tiles)
    parts = exchange_all(None, [message] * (n_col - 1), "col")[1:]

    field_own, *field_out = call(
        functools.partial(induct_body, n_row, n_col, seg_own),
        "induct_tiles",
        [like(seg_own, F32)] + [like(seg_own, BF16)] * (n_col - 1),
        [SMEM, SMEM, ANY] + [VMEM] * (n_row + 1),
        [
            pltpu.VMEM((n_row * cap_l, rhs, width), BF16),
            pltpu.VMEM((seg_group, rhs, width), F32),
        ],
        flops=4 * 10**9,
        moved=induct_tiles.size * 2,
    )(induct_slots, induct_rows, part, *got[::-1], induct_tiles)
    field_in = exchange_all(None, field_out, "col")[1:]

    pot, end_keep, *row_messages = call(
        functools.partial(panels_body, n_row, n_col, pan_own),
        "panel_sums",
        [like(pan_group, BF16), like(pan_own, F32)] + [like(pan_own + pan_group, BF16)] * (n_row - 1),
        [VMEM] * (2 * n_col),
        flops=5 * 10**9,
        moved=2**18,
    )(part, ends_own, *parts, *relayed)
    arrived = exchange_all(None, row_messages[::-1], "row")[1:]

    return tuple(
        call(
            functools.partial(final_body, n_row, n_col, pan_own, cap_k),
            "outputs",
            [jax.ShapeDtypeStruct(x.shape, BF16) for x in (current, charge, charge)],
            [SMEM, SMEM] + [VMEM] * (4 + n_col + n_row),
            [pltpu.VMEM((n_row * pan_group, rhs, width), BF16)],
            flops=2 * 10**9,
            moved=2**20,
        )(
            slots_t,
            link_needs,
            hots,
            charge,
            rhs_scale[:, None],
            field_own,
            end_keep,
            pot,
            *field_in,
            *arrived[::-1],
        )
    )


def solution(mesh):
    blocks = P(("parts", "row", "col"))
    matrix = P(("parts", "row", "col"), None)
    tiles = P(("parts", "row", "col"), None, None)
    values = P("rhs", ("parts", "row", "col"))
    return jax.shard_map(
        shards,
        mesh=mesh,
        in_specs=(
            values,
            values,
            P(("parts", "rhs")),
            tiles,
            blocks,
            blocks,
            matrix,
            tiles,
            blocks,
            blocks,
            matrix,
            matrix,
            matrix,
            matrix,
        ),
        out_specs=(values, values, values),
        check_vma=False,
    )
```

```python
import functools

import jax
import jax.numpy as jnp
from jax import lax
from jax.experimental import pallas as pl
from jax.experimental.pallas import tpu as pltpu
from jax.sharding import PartitionSpec as P

F32 = jnp.float32
BF16 = jnp.bfloat16
VMEM = pl.BlockSpec(memory_space=pltpu.VMEM)
SMEM = pl.BlockSpec(memory_space=pltpu.SMEM)
ANY = pl.BlockSpec(memory_space=pl.ANY)


def exchange(x, axis, k):
    if k == 0:
        return x
    return lax.ppermute(x, axis, [(i, i ^ k) for i in range(lax.axis_size(axis))])


def exchange_all(others, axis):
    return [exchange(x, axis, k + 1) for k, x in enumerate(others)]


def bits_of(n):
    return [1 << i for i in range(n.bit_length() - 1)]


def gather_plan(bits):
    known = [[0]]
    for bit in bits:
        known.append(known[-1] + [s ^ bit for s in known[-1]])
    return known


def scatter_plan(n, bits):
    left, plan = list(range(n)), []
    for bit in bits:
        plan.append(([k for k in left if not k & bit], [k for k in left if k & bit]))
        left = plan[-1][0]
    return plan


def swap_plan(n, bits):
    at = {(k, 0): (0, k) for k in range(n)}
    hops = []
    for i, bit in enumerate(bits):
        sent = sorted(pair for pair in at if pair[0] & bit)
        hops.append([at.pop(pair) for pair in sent])
        for place, (k, s) in enumerate(sent):
            at[(k ^ bit, s ^ bit)] = (i + 1, place)
    return hops, [at[(0, s)] for s in range(n)]


def call(body, name, out_shape, in_specs, scratch=(), flops=0, moved=0):
    return pl.pallas_call(
        body,
        out_shape=out_shape,
        in_specs=in_specs,
        out_specs=[VMEM] * len(out_shape),
        scratch_shapes=list(scratch),
        compiler_params=pltpu.CompilerParams(vmem_limit_bytes=16 * 2**20),
        cost_estimate=pl.CostEstimate(flops=flops, bytes_accessed=moved, transcendentals=0),
        name=name,
    )


def in_hbm(*arrays):
    return [pltpu.with_memory_space_constraint(x, pltpu.HBM) for x in arrays]


def stage_body(pan_own, seg_own, charge, needs, cur, off, slots, links, message, blocks, off_out, slots_out, links_out, wide):
    width = charge.shape[1] // pan_own
    for q in range(pan_own):
        message[q] = charge[:, q * width : (q + 1) * width]
    wide[...] = jnp.zeros_like(wide)
    wide[: needs.shape[0], : needs.shape[1]] = needs[...]
    message[pan_own] = wide[...].astype(F32).astype(BF16)
    for k in range(seg_own):
        blocks[k] = cur[:, k * width : (k + 1) * width]
    off_out[...] = off[...]
    slots_out[...] = slots[...]
    links_out[...] = links[...]


def join_body(*refs):
    out, first = refs[-1], 0
    for x in refs[:-1]:
        out[pl.ds(first, x.shape[0])] = x[...]
        first += x.shape[0]


def ends_body(n_row, n_col, pan_own, cap, slots, links, blocks, off, own, *rest):
    sends, (hots, acc) = rest[: n_col - 1], rest[n_col - 1 :]
    seg_own, _, width = blocks.shape
    pan_group = pan_own * n_col
    r, c = lax.axis_index("row"), lax.axis_index("col")
    acc[...] = jnp.zeros_like(acc)
    levels = lax.broadcasted_iota(jnp.int32, (width, width), 0)

    def block(k):
        span = pl.ds(pl.multiple_of(k * width, width), width)
        to_hot = jnp.where(levels == off[0:1, span], 1.0, 0.0).astype(BF16)
        from_hot = jnp.where(levels == off[1:2, span], -1.0, 0.0).astype(BF16)
        hot = jnp.concatenate([to_hot, from_hot], axis=0)
        hots[k] = hot
        sums = lax.dot_general(blocks[k], hot, (((1,), (1,)), ((), ())), preferred_element_type=F32)
        return sums.astype(BF16).astype(F32)

    unroll = 16

    def step(i, carry):
        got = [block(i * unroll + u) for u in range(unroll)]
        for u in range(unroll):
            for e in range(2):
                slot = slots[e, i * unroll + u]
                p = lax.div(slot, cap)
                b = links[p, slot - p * cap]
                acc[lax.bitwise_xor(p, r) * pan_group + b] += got[u][:, e * width : (e + 1) * width]
        return carry

    lax.fori_loop(0, seg_own // unroll, step, 0)
    for k in range(n_row):
        here = pl.ds(k * pan_own, pan_own)
        own[here] = acc[pl.ds(k * pan_group + c * pan_own, pan_own)]
        for j in range(1, n_col):
            there = lax.bitwise_xor(c, j)
            sends[j - 1][here] = acc[pl.ds(k * pan_group + there * pan_own, pan_own)].astype(BF16)


def pack_of(packs, size, k):
    own, *arrived = packs
    if k == 0:
        return own, 0
    hop = k.bit_length() - 1
    return arrived[hop], (k - (1 << hop)) * size


def relay_body(n_row, n_col, pan_own, *refs):
    hops = n_row.bit_length()
    packs = refs[:hops]
    ends = refs[hops : hops + n_col - 1]
    asked, *messages = refs[hops + n_col - 1 :]
    r = lax.axis_index("row")
    rhs, width = packs[0].shape[1:]
    mine = lax.broadcasted_iota(jnp.int32, (rhs, width), 0) == r
    for k in range(n_row):
        pack, first = pack_of(packs, pan_own + 1, k)
        needs = pack[first + pan_own].astype(F32)
        asked[k : k + 1, :] = jnp.sum(jnp.where(mine, needs, 0.0), axis=0, keepdims=True).astype(jnp.int32)
        for message in messages:
            message[pl.ds(k * pan_own, pan_own)] = pack[pl.ds(first, pan_own)]
    for message, sums in zip(messages, ends):
        message[pl.ds(n_row * pan_own, n_row * pan_own)] = sums[...]


def pick_body(n_row, n_col, cap, asked, own, *refs):
    peers, (keep, send) = refs[: n_col - 1], refs[n_col - 1 :]
    seg_own, _, width = own.shape
    c = lax.axis_index("col")
    for k in range(n_row):
        out = keep if k < n_row // 2 else send
        for s in range(cap):
            b = asked[k, s]
            holder = lax.div(b, seg_own)
            b = b - holder * seg_own
            j = lax.bitwise_xor(holder, c)
            value = own[b]
            span = pl.ds(pl.multiple_of(b * width, width), width)
            for q, peer in enumerate(peers):
                value = jnp.where(j == q + 1, peer[:, span], value)
            out[k % (n_row // 2) * cap + s] = value


def forward_body(cap, places, _after, *refs):
    held, out = refs[:-1], refs[-1]
    for i, (holder, place) in enumerate(places):
        out[pl.ds(i * cap, cap)] = held[holder][pl.ds(place * cap, cap)]


def multiply(tiles, src, source, rows, acc):
    rhs, width = src.shape[1:]
    unroll = min(32, tiles.shape[0])

    def step(i, carry):
        start = i * unroll
        got = []
        for u in range(0, unroll, 2):
            t = start + u
            left = jnp.concatenate([src[source(t)], src[source(t + 1)]], axis=0)
            right = jnp.concatenate([tiles[t], tiles[t + 1]], axis=1)
            both = jnp.dot(left, right, preferred_element_type=F32)
            got += [both[:rhs, :width], both[rhs:, width:]]
        for u, value in enumerate(got):
            acc[rows[start + u]] += value
        return carry

    lax.fori_loop(0, tiles.shape[0] // unroll, step, 0)


def coeff_body(n_row, n_col, pan_own, slots, rows, needs, _after, *refs):
    hops = n_row.bit_length()
    packs = refs[:hops]
    from_col = refs[hops : hops + n_col - 1]
    tiles, part, message, src, named = refs[hops + n_col - 1 :]
    r, c = lax.axis_index("row"), lax.axis_index("col")
    pan_group = pan_own * n_col
    cap = needs.shape[1]
    for k in range(n_row):
        first = lax.bitwise_xor(r, k) * pan_group
        pack, at = pack_of(packs, pan_own + 1, k)
        src[pl.ds(first + c * pan_own, pan_own)] = pack[pl.ds(at, pan_own)]
        for j, x in enumerate(from_col):
            there = first + lax.bitwise_xor(c, j + 1) * pan_own
            src[pl.ds(there, pan_own)] = x[pl.ds(k * pan_own, pan_own)]
    for p in range(n_row):
        for s in range(cap):
            named[p * cap + s] = p * pan_group + needs[p, s]
    part[...] = jnp.zeros_like(part)
    multiply(tiles, src, lambda t: named[slots[t]], rows, part)
    high = part[...].astype(BF16)
    message[pl.ds(0, pan_group)] = high
    message[pl.ds(pan_group, pan_group)] = (part[...] - high.astype(F32)).astype(BF16)


def induct_body(n_row, n_col, seg_own, places, cap, slots, rows, _after, *refs):
    hops = n_row.bit_length()
    held = refs[:hops]
    tiles = refs[hops]
    own, *sends = refs[hops + 1 : -2]
    src, acc = refs[-2:]
    r, c = lax.axis_index("row"), lax.axis_index("col")
    for k, (holder, place) in enumerate(places):
        src[pl.ds(lax.bitwise_xor(r, k) * cap, cap)] = held[holder][pl.ds(place * cap, cap)]
    acc[...] = jnp.zeros_like(acc)
    multiply(tiles, src, lambda t: slots[t], rows, acc)
    own[...] = acc[pl.ds(c * seg_own, seg_own)]
    for j in range(1, n_col):
        sends[j - 1][...] = acc[pl.ds(lax.bitwise_xor(c, j) * seg_own, seg_own)].astype(BF16)


def panels_body(n_row, n_col, pan_own, _after, part, ends_own, *refs):
    parts = refs[: n_col - 1]
    relayed = refs[n_col - 1 : 2 * n_col - 2]
    pot, keep, message = refs[2 * n_col - 2 :]
    pan_group = part.shape[0]
    total = part[...]
    for x in parts:
        total += x[pl.ds(0, pan_group)].astype(F32) + x[pl.ds(pan_group, pan_group)].astype(F32)
    rounded = total.astype(BF16)
    pot[...] = rounded
    half = n_row // 2
    for k in range(n_row):
        sums = ends_own[pl.ds(k * pan_own, pan_own)]
        for x in relayed:
            sums += x[pl.ds((n_row + k) * pan_own, pan_own)].astype(F32)
        here = pl.ds(k % half * pan_own, pan_own)
        if k < half:
            keep[here] = sums
        else:
            message[here] = sums.astype(BF16)
    message[pl.ds(half * pan_own, pan_group)] = rounded


def pass_body(stay, go, pan_own, _after, sums, pot, *refs):
    arrived, (keep, message) = refs[:-2], refs[-2:]
    pan_group = pot.shape[0]

    def total(k):
        here = pl.ds(k * pan_own, pan_own)
        return sums[here] + arrived[-1][here].astype(F32)

    for i, k in enumerate(stay):
        keep[pl.ds(i * pan_own, pan_own)] = total(k)
    for i, k in enumerate(go):
        message[pl.ds(i * pan_own, pan_own)] = total(k).astype(BF16)
    first = len(go) * pan_own
    message[pl.ds(first, pan_group)] = pot[...]
    first += pan_group
    for i, x in enumerate(arrived):
        count = pan_group << i
        message[pl.ds(first, count)] = x[pl.ds(x.shape[0] - count, count)]
        first += count


def final_body(n_row, n_col, pan_own, cap, slots, links, hots, charge, scale, *refs):
    field_own, end_own, pot = refs[:3]
    field_in = refs[3 : 2 + n_col]
    arrived, (seg_out, pan_out, pot_out, held) = refs[2 + n_col : -4], refs[-4:]
    width = charge.shape[1] // pan_own
    pan_group = pan_own * n_col
    r, c = lax.axis_index("row"), lax.axis_index("col")
    known = gather_plan(bits_of(n_row)[::-1])
    held[pl.ds(r * pan_group, pan_group)] = pot[...]
    for i, x in enumerate(arrived):
        first = x.shape[0] - (pan_group << i)
        for k in known[i + 1][1 << i :]:
            sender = lax.bitwise_xor(r, k)
            held[pl.ds(sender * pan_group, pan_group)] = x[pl.ds(first, pan_group)]
            first += pan_group
    for q in range(pan_own):
        span = slice(q * width, (q + 1) * width)
        total = end_own[q] + arrived[-1][q].astype(F32)
        pan_out[:, span] = (scale[...] * charge[:, span].astype(F32) + total).astype(BF16)
        pot_out[:, span] = pot[c * pan_own + q]

    def block(k):
        ends = []
        for e in range(2):
            slot = slots[e, k]
            p = lax.div(slot, cap)
            ends.append(held[p * pan_group + links[p, slot - p * cap]])
        drops = jnp.dot(jnp.concatenate(ends, axis=1), hots[k], preferred_element_type=F32)
        total = field_own[k]
        for x in field_in:
            total += x[k].astype(F32)
        return (total + drops).astype(BF16)

    unroll = min(32, hots.shape[0])

    def step(i, carry):
        got = [block(i * unroll + u) for u in range(unroll)]
        for u, value in enumerate(got):
            first = pl.multiple_of((i * unroll + u) * width, width)
            seg_out[:, pl.ds(first, width)] = value
        return carry

    lax.fori_loop(0, hots.shape[0] // unroll, step, 0)


def shards(
    current,
    charge,
    rhs_scale,
    induct_tiles,
    induct_rows,
    induct_slots,
    induct_needs,
    coeff_tiles,
    coeff_rows,
    coeff_slots,
    coeff_needs,
    link_needs,
    end_slots,
    end_offsets,
):
    n_row = lax.axis_size("row")
    n_col = lax.axis_size("col")
    width = induct_tiles.shape[1]
    rhs = current.shape[0]
    seg_own = current.shape[1] // width
    pan_own = charge.shape[1] // width
    seg_group, pan_group = seg_own * n_col, pan_own * n_col
    cap_l, cap_p, cap_k = induct_needs.shape[1], coeff_needs.shape[1], link_needs.shape[1]
    slots_t, off_t = end_slots.T, end_offsets.T

    def like(blocks, dtype):
        return jax.ShapeDtypeStruct((blocks, rhs, width), dtype)

    bits = bits_of(n_row)
    half = n_row // 2

    message, own_blocks, off_v, slots_v, links_v = call(
        functools.partial(stage_body, pan_own, seg_own),
        "stage_inputs",
        [like(pan_own + 1, BF16), like(seg_own, BF16)]
        + [jax.ShapeDtypeStruct(x.shape, jnp.int32) for x in (off_t, slots_t, link_needs)],
        [VMEM] * 6,
        [pltpu.VMEM((rhs, width), jnp.int32)],
        moved=2**18,
    )(*in_hbm(charge, induct_needs, current, off_t, slots_t, link_needs))
    packs = [message]
    for i, bit in enumerate(bits):
        packs.append(exchange(message, "row", bit))
        if i < len(bits) - 1:
            (message,) = call(
                join_body,
                "join_packs",
                [like(message.shape[0] * 2, BF16)],
                [VMEM] * len(packs),
                moved=2**16,
            )(*packs)
    cur = exchange_all([current] * (n_col - 1), "col")

    rows_own = n_row * pan_own
    ends_own, *rest = call(
        functools.partial(ends_body, n_row, n_col, pan_own, cap_k),
        "end_sums",
        [like(rows_own, F32)]
        + [like(rows_own, BF16)] * (n_col - 1)
        + [jax.ShapeDtypeStruct((seg_own, 2 * width, width), BF16)],
        [SMEM, SMEM, VMEM, VMEM],
        [pltpu.VMEM((n_row * pan_group, rhs, width), F32)],
        flops=2 * 10**9,
        moved=2**18,
    )(slots_v, links_v, own_blocks, off_v)
    ends_out, (hots,) = rest[: n_col - 1], rest[n_col - 1 :]

    asked, *relays = call(
        functools.partial(relay_body, n_row, n_col, pan_own),
        "relay_charges",
        [jax.ShapeDtypeStruct((n_row, width), jnp.int32)] + [like(2 * rows_own, BF16)] * (n_col - 1),
        [VMEM] * (len(packs) + n_col - 1),
        moved=2**16,
    )(*packs, *ends_out)
    relayed = exchange_all(relays, "col")

    picks, message = call(
        functools.partial(pick_body, n_row, n_col, cap_l),
        "pick_blocks",
        [like(half * cap_l, BF16)] * 2,
        [SMEM] + [VMEM] * n_col,
        moved=2**18,
    )(asked, own_blocks, *cur)

    part, part_message = call(
        functools.partial(coeff_body, n_row, n_col, pan_own),
        "coeff_tiles",
        [like(pan_group, F32), like(2 * pan_group, BF16)],
        [SMEM] * 3 + [ANY] + [VMEM] * (len(packs) + n_col),
        [
            pltpu.VMEM((n_row * pan_group, rhs, width), BF16),
            pltpu.SMEM((n_row * cap_p,), jnp.int32),
        ],
        flops=2 * 10**9,
        moved=coeff_tiles.size * 2,
    )(coeff_slots, coeff_rows, coeff_needs, picks, *packs, *relayed, coeff_tiles)
    parts = exchange_all([part_message] * (n_col - 1), "col")

    hops, places = swap_plan(n_row, bits[::-1])
    held = [picks, exchange(message, "row", bits[-1])]
    for bit, hop in zip(bits[-2::-1], hops[1:]):
        (message,) = call(
            functools.partial(forward_body, cap_l, hop),
            "forward_blocks",
            [like(half * cap_l, BF16)],
            [ANY] + [VMEM] * len(held),
            moved=2**16,
        )(part, *held)
        held.append(exchange(message, "row", bit))

    plan = scatter_plan(n_row, bits[::-1])
    pot, sums, end_message = call(
        functools.partial(panels_body, n_row, n_col, pan_own),
        "panel_sums",
        [like(pan_group, BF16), like(half * pan_own, F32), like(half * pan_own + pan_group, BF16)],
        [ANY] + [VMEM] * (2 * n_col),
        flops=10**9,
        moved=2**18,
    )(message, part, ends_own, *parts, *relayed)

    field_own, *field_out = call(
        functools.partial(induct_body, n_row, n_col, seg_own, places, cap_l),
        "induct_tiles",
        [like(seg_own, F32)] + [like(seg_own, BF16)] * (n_col - 1),
        [SMEM, SMEM, ANY] + [VMEM] * (len(held) + 1),
        [
            pltpu.VMEM((n_row * cap_l, rhs, width), BF16),
            pltpu.VMEM((seg_group, rhs, width), F32),
        ],
        flops=4 * 10**9,
        moved=induct_tiles.size * 2,
    )(induct_slots, induct_rows, pot, *held, induct_tiles)
    field_in = exchange_all(field_out, "col")

    arrived = [exchange(end_message, "row", bits[-1])]
    for i, bit in enumerate(bits[-2::-1]):
        stay, go = plan[i + 1]
        known = 2 << i
        sums, end_message = call(
            functools.partial(pass_body, stay, go, pan_own),
            "pass_sums",
            [like(len(stay) * pan_own, F32), like(len(go) * pan_own + known * pan_group, BF16)],
            [ANY] + [VMEM] * (2 + len(arrived)),
            moved=2**18,
        )(field_own, sums, pot, *arrived)
        arrived.append(exchange(end_message, "row", bit))

    return tuple(
        call(
            functools.partial(final_body, n_row, n_col, pan_own, cap_k),
            "outputs",
            [jax.ShapeDtypeStruct(x.shape, BF16) for x in (current, charge, charge)],
            [SMEM, SMEM] + [VMEM] * (5 + n_col + len(arrived)),
            [pltpu.VMEM((n_row * pan_group, rhs, width), BF16)],
            flops=2 * 10**9,
            moved=2**20,
        )(
            slots_v,
            links_v,
            hots,
            charge,
            rhs_scale[:, None],
            field_own,
            sums,
            pot,
            *field_in,
            *arrived,
        )
    )


def solution(mesh):
    blocks = P(("parts", "row", "col"))
    matrix = P(("parts", "row", "col"), None)
    tiles = P(("parts", "row", "col"), None, None)
    values = P("rhs", ("parts", "row", "col"))
    return jax.shard_map(
        shards,
        mesh=mesh,
        in_specs=(
            values,
            values,
            P(("parts", "rhs")),
            tiles,
            blocks,
            blocks,
            matrix,
            tiles,
            blocks,
            blocks,
            matrix,
            matrix,
            matrix,
            matrix,
        ),
        out_specs=(values, values, values),
        check_vma=False,
    )
```

```python
import functools

import jax
import jax.numpy as jnp
from jax import lax
from jax.experimental import pallas as pl
from jax.experimental.pallas import tpu as pltpu
from jax.sharding import PartitionSpec as P

F32 = jnp.float32
BF16 = jnp.bfloat16
VMEM = pl.BlockSpec(memory_space=pltpu.VMEM)
SMEM = pl.BlockSpec(memory_space=pltpu.SMEM)
ANY = pl.BlockSpec(memory_space=pl.ANY)


def exchange(x, axis, k):
    if k == 0:
        return x
    return lax.ppermute(x, axis, [(i, i ^ k) for i in range(lax.axis_size(axis))])


def exchange_all(first, others, axis):
    n = lax.axis_size(axis)
    got = {0: first}
    for k in reversed(range(1, n)):
        got[k] = exchange(others[k - 1], axis, k)
    return [got[k] for k in range(n)]


def call(body, name, out_shape, in_specs, scratch=(), flops=0, moved=0):
    return pl.pallas_call(
        body,
        out_shape=out_shape,
        in_specs=in_specs,
        out_specs=[VMEM] * len(out_shape),
        scratch_shapes=list(scratch),
        compiler_params=pltpu.CompilerParams(vmem_limit_bytes=16 * 2**20),
        cost_estimate=pl.CostEstimate(flops=flops, bytes_accessed=moved, transcendentals=0),
        name=name,
    )


def in_hbm(*arrays):
    return [pltpu.with_memory_space_constraint(x, pltpu.HBM) for x in arrays]


def stage_body(pan_own, seg_own, charge, needs, cur, off, slots, links, message, blocks, off_out, slots_out, links_out, wide):
    width = charge.shape[1] // pan_own
    for q in range(pan_own):
        message[q] = charge[:, q * width : (q + 1) * width]
    wide[...] = jnp.zeros_like(wide)
    wide[: needs.shape[0], : needs.shape[1]] = needs[...]
    message[pan_own] = wide[...].astype(F32).astype(BF16)
    for k in range(seg_own):
        blocks[k] = cur[:, k * width : (k + 1) * width]
    off_out[...] = off[...]
    slots_out[...] = slots[...]
    links_out[...] = links[...]


def ends_body(n_row, n_col, pan_own, cap, slots, links, blocks, off, own, *rest):
    sends, acc = rest[:-1], rest[-1]
    seg_own, _, width = blocks.shape
    pan_group = pan_own * n_col
    r, c = lax.axis_index("row"), lax.axis_index("col")
    acc[...] = jnp.zeros_like(acc)
    levels = lax.broadcasted_iota(jnp.int32, (width, width), 0)

    def block(k):
        span = pl.ds(pl.multiple_of(k * width, width), width)
        to_hot = jnp.where(levels == off[0:1, span], 1.0, 0.0).astype(BF16)
        from_hot = jnp.where(levels == off[1:2, span], -1.0, 0.0).astype(BF16)
        hot = jnp.concatenate([to_hot, from_hot], axis=0)
        sums = lax.dot_general(blocks[k], hot, (((1,), (1,)), ((), ())), preferred_element_type=F32)
        return sums.astype(BF16).astype(F32)

    unroll = 16

    def step(i, carry):
        got = [block(i * unroll + u) for u in range(unroll)]
        for u in range(unroll):
            for e in range(2):
                slot = slots[e, i * unroll + u]
                p = lax.div(slot, cap)
                b = links[p, slot - p * cap]
                acc[lax.bitwise_xor(p, r) * pan_group + b] += got[u][:, e * width : (e + 1) * width]
        return carry

    lax.fori_loop(0, seg_own // unroll, step, 0)
    for k in range(n_row):
        here = pl.ds(k * pan_own, pan_own)
        own[here] = acc[pl.ds(k * pan_group + c * pan_own, pan_own)]
        for j in range(1, n_col):
            there = lax.bitwise_xor(c, j)
            sends[j - 1][here] = acc[pl.ds(k * pan_group + there * pan_own, pan_own)].astype(BF16)


def relay_body(n_row, n_col, pan_own, *refs):
    packs = refs[:n_row]
    ends = refs[n_row : n_row + n_col - 1]
    asked, *messages = refs[n_row + 2 * n_col - 2 :]
    r = lax.axis_index("row")
    rhs, width = packs[0].shape[1:]
    mine = lax.broadcasted_iota(jnp.int32, (rhs, width), 0) == r
    for k in range(n_row):
        needs = packs[k][pan_own].astype(F32)
        asked[k : k + 1, :] = jnp.sum(jnp.where(mine, needs, 0.0), axis=0, keepdims=True).astype(jnp.int32)
        for message in messages:
            message[pl.ds(k * pan_own, pan_own)] = packs[k][pl.ds(0, pan_own)]
    for message, sums in zip(messages, ends):
        message[pl.ds(n_row * pan_own, n_row * pan_own)] = sums[...]


def pick_body(n_row, n_col, cap, asked, own, *refs):
    peers, outs = refs[: n_col - 1], refs[n_col - 1 :]
    seg_own, _, width = own.shape
    c = lax.axis_index("col")
    for k in range(n_row):
        for s in range(cap):
            b = asked[k, s]
            holder = lax.div(b, seg_own)
            b = b - holder * seg_own
            j = lax.bitwise_xor(holder, c)
            value = own[b]
            span = pl.ds(pl.multiple_of(b * width, width), width)
            for q, peer in enumerate(peers):
                value = jnp.where(j == q + 1, peer[:, span], value)
            outs[n_row - 1 - k][s] = value


def multiply(tiles, src, source, rows, acc):
    rhs, width = src.shape[1:]
    unroll = min(32, tiles.shape[0])

    def step(i, carry):
        start = i * unroll
        got = []
        for u in range(0, unroll, 2):
            t = start + u
            left = jnp.concatenate([src[source(t)], src[source(t + 1)]], axis=0)
            right = jnp.concatenate([tiles[t], tiles[t + 1]], axis=1)
            both = jnp.dot(left, right, preferred_element_type=F32)
            got += [both[:rhs, :width], both[rhs:, width:]]
        for u, value in enumerate(got):
            acc[rows[start + u]] += value
        return carry

    lax.fori_loop(0, tiles.shape[0] // unroll, step, 0)


def coeff_body(n_row, n_col, pan_own, slots, rows, needs, *refs):
    packs = refs[:n_row]
    from_col = refs[n_row : n_row + n_col - 1]
    tiles, part, message, src, named = refs[n_row + n_col - 1 :]
    r, c = lax.axis_index("row"), lax.axis_index("col")
    pan_group = pan_own * n_col
    cap = needs.shape[1]
    for k in range(n_row):
        first = lax.bitwise_xor(r, k) * pan_group
        src[pl.ds(first + c * pan_own, pan_own)] = packs[k][pl.ds(0, pan_own)]
        for j, x in enumerate(from_col):
            there = first + lax.bitwise_xor(c, j + 1) * pan_own
            src[pl.ds(there, pan_own)] = x[pl.ds(k * pan_own, pan_own)]
    for p in range(n_row):
        for s in range(cap):
            named[p * cap + s] = p * pan_group + needs[p, s]
    part[...] = jnp.zeros_like(part)
    multiply(tiles, src, lambda t: named[slots[t]], rows, part)
    high = part[...].astype(BF16)
    message[pl.ds(0, pan_group)] = high
    message[pl.ds(pan_group, pan_group)] = (part[...] - high.astype(F32)).astype(BF16)


def induct_body(n_row, n_col, seg_own, slots, rows, _after, *refs):
    got = refs[:n_row][::-1]
    tiles = refs[n_row]
    own, *sends = refs[n_row + 1 : -2]
    src, acc = refs[-2:]
    cap = got[0].shape[0]
    r, c = lax.axis_index("row"), lax.axis_index("col")
    for k in range(n_row):
        src[pl.ds(lax.bitwise_xor(r, k) * cap, cap)] = got[k][...]
    acc[...] = jnp.zeros_like(acc)
    multiply(tiles, src, lambda t: slots[t], rows, acc)
    own[...] = acc[pl.ds(c * seg_own, seg_own)]
    for j in range(1, n_col):
        sends[j - 1][...] = acc[pl.ds(lax.bitwise_xor(c, j) * seg_own, seg_own)].astype(BF16)


def panels_body(n_row, n_col, pan_own, part, ends_own, *refs):
    parts = refs[: n_col - 1]
    relayed = refs[n_col - 1 : 2 * n_col - 2]
    pot, end_keep, *messages = refs[2 * n_col - 2 :]
    pan_group = part.shape[0]
    total = part[...]
    for x in parts:
        total += x[pl.ds(0, pan_group)].astype(F32) + x[pl.ds(pan_group, pan_group)].astype(F32)
    rounded = total.astype(BF16)
    pot[...] = rounded
    for k in range(n_row):
        sums = ends_own[pl.ds(k * pan_own, pan_own)]
        for x in relayed:
            sums += x[pl.ds((n_row + k) * pan_own, pan_own)].astype(F32)
        if k == 0:
            end_keep[...] = sums
        else:
            messages[n_row - 1 - k][pl.ds(0, pan_own)] = sums.astype(BF16)
            messages[n_row - 1 - k][pl.ds(pan_own, pan_group)] = rounded


def final_body(n_row, n_col, pan_own, cap, slots, links, off, charge, scale, *refs):
    field_own, end_own, pot = refs[:3]
    field_in = refs[3 : 2 + n_col]
    arrived = refs[2 + n_col : 1 + n_col + n_row][::-1]
    seg_out, pan_out, pot_out, held = refs[1 + n_col + n_row :]
    seg_own, rhs, width = field_own.shape
    pan_group = pan_own * n_col
    r, c = lax.axis_index("row"), lax.axis_index("col")
    held[pl.ds(r * pan_group, pan_group)] = pot[...].astype(F32)
    for k, x in enumerate(arrived):
        sender = lax.bitwise_xor(r, k + 1)
        held[pl.ds(sender * pan_group, pan_group)] = x[pl.ds(pan_own, pan_group)].astype(F32)
    for q in range(pan_own):
        span = slice(q * width, (q + 1) * width)
        total = end_own[q]
        for x in arrived:
            total += x[q].astype(F32)
        pan_out[:, span] = (scale[...] * charge[:, span].astype(F32) + total).astype(BF16)
        pot_out[:, span] = pot[c * pan_own + q]

    def at_end(e, k, span):
        slot = slots[e, k]
        p = lax.div(slot, cap)
        values = held[p * pan_group + links[p, slot - p * cap]]
        lanes = jnp.broadcast_to(off[e : e + 1, span], (rhs, width))
        return jnp.take_along_axis(values, lanes, axis=1, mode="promise_in_bounds")

    unroll = 8

    def step(i, carry):
        for u in range(unroll):
            k = i * unroll + u
            span = pl.ds(pl.multiple_of(k * width, width), width)
            total = field_own[k]
            for x in field_in:
                total += x[k].astype(F32)
            seg_out[:, span] = (total + at_end(0, k, span) - at_end(1, k, span)).astype(BF16)
        return carry

    lax.fori_loop(0, seg_own // unroll, step, 0)


def shards(
    current,
    charge,
    rhs_scale,
    induct_tiles,
    induct_rows,
    induct_slots,
    induct_needs,
    coeff_tiles,
    coeff_rows,
    coeff_slots,
    coeff_needs,
    link_needs,
    end_slots,
    end_offsets,
):
    n_row = lax.axis_size("row")
    n_col = lax.axis_size("col")
    width = induct_tiles.shape[1]
    rhs = current.shape[0]
    seg_own = current.shape[1] // width
    pan_own = charge.shape[1] // width
    seg_group, pan_group = seg_own * n_col, pan_own * n_col
    cap_l, cap_p, cap_k = induct_needs.shape[1], coeff_needs.shape[1], link_needs.shape[1]
    slots_t, off_t = end_slots.T, end_offsets.T

    def like(blocks, dtype):
        return jax.ShapeDtypeStruct((blocks, rhs, width), dtype)

    cur = exchange_all(current, [current] * (n_col - 1), "col")
    pack, own_blocks, off_v, slots_v, links_v = call(
        functools.partial(stage_body, pan_own, seg_own),
        "stage_inputs",
        [like(pan_own + 1, BF16), like(seg_own, BF16)]
        + [jax.ShapeDtypeStruct(x.shape, jnp.int32) for x in (off_t, slots_t, link_needs)],
        [VMEM] * 6,
        [pltpu.VMEM((rhs, width), jnp.int32)],
        moved=2**18,
    )(*in_hbm(charge, induct_needs, current, off_t, slots_t, link_needs))
    packs = exchange_all(pack, [pack] * (n_row - 1), "row")

    rows_own = n_row * pan_own
    ends_own, *ends_out = call(
        functools.partial(ends_body, n_row, n_col, pan_own, cap_k),
        "end_sums",
        [like(rows_own, F32)] + [like(rows_own, BF16)] * (n_col - 1),
        [SMEM, SMEM, VMEM, VMEM],
        [pltpu.VMEM((n_row * pan_group, rhs, width), F32)],
        flops=2 * 10**9,
        moved=2**18,
    )(slots_v, links_v, own_blocks, off_v)

    asked, *relays = call(
        functools.partial(relay_body, n_row, n_col, pan_own),
        "relay_charges",
        [jax.ShapeDtypeStruct((n_row, width), jnp.int32)] + [like(2 * rows_own, BF16)] * (n_col - 1),
        [VMEM] * (n_row + n_col - 1) + [ANY] * (n_col - 1),
        moved=2**16,
    )(*packs, *ends_out, *cur[1:])
    relayed = exchange_all(None, relays, "col")[1:]

    *picks, own_picks = call(
        functools.partial(pick_body, n_row, n_col, cap_l),
        "pick_blocks",
        [like(cap_l, BF16)] * n_row,
        [SMEM] + [VMEM] * n_col,
        moved=2**18,
    )(asked, own_blocks, *cur[1:])
    got = exchange_all(own_picks, picks[::-1], "row")

    part, message = call(
        functools.partial(coeff_body, n_row, n_col, pan_own),
        "coeff_tiles",
        [like(pan_group, F32), like(2 * pan_group, BF16)],
        [SMEM] * 3 + [VMEM] * (n_row + n_col),
        [
            pltpu.VMEM((n_row * pan_group, rhs, width), BF16),
            pltpu.SMEM((n_row * cap_p,), jnp.int32),
        ],
        flops=2 * 10**9,
        moved=coeff_tiles.size * 2,
    )(coeff_slots, coeff_rows, coeff_needs, *packs, *relayed, coeff_tiles)
    parts = exchange_all(None, [message] * (n_col - 1), "col")[1:]

    field_own, *field_out = call(
        functools.partial(induct_body, n_row, n_col, seg_own),
        "induct_tiles",
        [like(seg_own, F32)] + [like(seg_own, BF16)] * (n_col - 1),
        [SMEM, SMEM, ANY] + [VMEM] * (n_row + 1),
        [
            pltpu.VMEM((n_row * cap_l, rhs, width), BF16),
            pltpu.VMEM((seg_group, rhs, width), F32),
        ],
        flops=4 * 10**9,
        moved=induct_tiles.size * 2,
    )(induct_slots, induct_rows, part, *got[::-1], induct_tiles)
    field_in = exchange_all(None, field_out, "col")[1:]

    pot, end_keep, *row_messages = call(
        functools.partial(panels_body, n_row, n_col, pan_own),
        "panel_sums",
        [like(pan_group, BF16), like(pan_own, F32)] + [like(pan_own + pan_group, BF16)] * (n_row - 1),
        [VMEM] * (2 * n_col),
        flops=5 * 10**9,
        moved=2**18,
    )(part, ends_own, *parts, *relayed)
    arrived = exchange_all(None, row_messages[::-1], "row")[1:]

    return tuple(
        call(
            functools.partial(final_body, n_row, n_col, pan_own, cap_k),
            "outputs",
            [jax.ShapeDtypeStruct(x.shape, BF16) for x in (current, charge, charge)],
            [SMEM, SMEM] + [VMEM] * (4 + n_col + n_row),
            [pltpu.VMEM((n_row * pan_group, rhs, width), F32)],
            flops=10**9,
            moved=2**20,
        )(
            slots_v,
            links_v,
            off_v,
            charge,
            rhs_scale[:, None],
            field_own,
            end_keep,
            pot,
            *field_in,
            *arrived[::-1],
        )
    )


def solution(mesh):
    blocks = P(("parts", "row", "col"))
    matrix = P(("parts", "row", "col"), None)
    tiles = P(("parts", "row", "col"), None, None)
    values = P("rhs", ("parts", "row", "col"))
    return jax.shard_map(
        shards,
        mesh=mesh,
        in_specs=(
            values,
            values,
            P(("parts", "rhs")),
            tiles,
            blocks,
            blocks,
            matrix,
            tiles,
            blocks,
            blocks,
            matrix,
            matrix,
            matrix,
            matrix,
        ),
        out_specs=(values, values, values),
        check_vma=False,
    )
```

```python
import functools

import jax
import jax.numpy as jnp
from jax import lax
from jax.experimental import pallas as pl
from jax.experimental.pallas import tpu as pltpu
from jax.sharding import PartitionSpec as P

F32 = jnp.float32
BF16 = jnp.bfloat16
VMEM = pl.BlockSpec(memory_space=pltpu.VMEM)
SMEM = pl.BlockSpec(memory_space=pltpu.SMEM)
ANY = pl.BlockSpec(memory_space=pl.ANY)


def exchange(x, axis, k):
    if k == 0:
        return x
    return lax.ppermute(x, axis, [(i, i ^ k) for i in range(lax.axis_size(axis))])


def exchange_all(first, others, axis):
    n = lax.axis_size(axis)
    got = {0: first}
    for k in reversed(range(1, n)):
        got[k] = exchange(others[k - 1], axis, k)
    return [got[k] for k in range(n)]


def call(body, name, out_shape, in_specs, scratch=(), flops=0, moved=0, out_specs=None):
    return pl.pallas_call(
        body,
        out_shape=out_shape,
        in_specs=in_specs,
        out_specs=out_specs or [VMEM] * len(out_shape),
        scratch_shapes=list(scratch),
        compiler_params=pltpu.CompilerParams(vmem_limit_bytes=16 * 2**20),
        cost_estimate=pl.CostEstimate(flops=flops, bytes_accessed=moved, transcendentals=0),
        name=name,
    )


def in_hbm(*arrays):
    return [pltpu.with_memory_space_constraint(x, pltpu.HBM) for x in arrays]


def pack_body(pan_own, charge, needs, message, wide):
    width = charge.shape[1] // pan_own
    for q in range(pan_own):
        message[q] = charge[:, q * width : (q + 1) * width]
    wide[...] = jnp.zeros_like(wide)
    wide[: needs.shape[0], : needs.shape[1]] = needs[...]
    message[pan_own] = wide[...].astype(F32).astype(BF16)


def ends_body(n_row, n_col, pan_own, cap, n_tables, *refs):
    sources, rest = refs[: n_tables + 2], refs[n_tables + 2 :]
    tables, (off, blocks, own) = rest[:n_tables], rest[n_tables : n_tables + 3]
    sends, (cur, acc, sems) = rest[n_tables + 3 : -3], rest[-3:]
    copies = [
        pltpu.make_async_copy(source, target, sems.at[i])
        for i, (source, target) in enumerate(zip(sources, (*tables, off, cur)))
    ]
    for copy in copies[::-1]:
        copy.start()
    slots, links = tables[:2]
    seg_own, _, width = blocks.shape
    pan_group = pan_own * n_col
    r, c = lax.axis_index("row"), lax.axis_index("col")
    acc[...] = jnp.zeros_like(acc)
    levels = lax.broadcasted_iota(jnp.int32, (width, width), 0)
    for copy in copies[::-1]:
        copy.wait()

    def block(k):
        span = pl.ds(pl.multiple_of(k * width, width), width)
        to_hot = jnp.where(levels == off[0:1, span], 1.0, 0.0).astype(BF16)
        from_hot = jnp.where(levels == off[1:2, span], -1.0, 0.0).astype(BF16)
        hot = jnp.concatenate([to_hot, from_hot], axis=0)
        value = cur[:, span]
        blocks[k] = value
        sums = lax.dot_general(value, hot, (((1,), (1,)), ((), ())), preferred_element_type=F32)
        return sums.astype(BF16).astype(F32)

    unroll = 16

    def step(i, carry):
        got = [block(i * unroll + u) for u in range(unroll)]
        for u in range(unroll):
            for e in range(2):
                slot = slots[e, i * unroll + u]
                p = lax.div(slot, cap)
                b = links[p, slot - p * cap]
                acc[lax.bitwise_xor(p, r) * pan_group + b] += got[u][:, e * width : (e + 1) * width]
        return carry

    lax.fori_loop(0, seg_own // unroll, step, 0)
    for k in range(n_row):
        here = pl.ds(k * pan_own, pan_own)
        own[here] = acc[pl.ds(k * pan_group + c * pan_own, pan_own)]
        for j in range(1, n_col):
            there = lax.bitwise_xor(c, j)
            sends[j - 1][here] = acc[pl.ds(k * pan_group + there * pan_own, pan_own)].astype(BF16)


def relay_body(n_row, n_col, pan_own, *refs):
    packs = refs[:n_row]
    ends = refs[n_row : n_row + n_col - 1]
    asked, *messages = refs[n_row + 2 * n_col - 2 :]
    r = lax.axis_index("row")
    rhs, width = packs[0].shape[1:]
    mine = lax.broadcasted_iota(jnp.int32, (rhs, width), 0) == r
    for k in range(n_row):
        needs = packs[k][pan_own].astype(F32)
        asked[k : k + 1, :] = jnp.sum(jnp.where(mine, needs, 0.0), axis=0, keepdims=True).astype(jnp.int32)
        for message in messages:
            message[pl.ds(k * pan_own, pan_own)] = packs[k][pl.ds(0, pan_own)]
    for message, sums in zip(messages, ends):
        message[pl.ds(n_row * pan_own, n_row * pan_own)] = sums[...]


def pick_body(n_row, n_col, cap, asked, own, *refs):
    peers, outs = refs[: n_col - 1], refs[n_col - 1 :]
    seg_own, _, width = own.shape
    c = lax.axis_index("col")
    for k in range(n_row):
        for s in range(cap):
            b = asked[k, s]
            holder = lax.div(b, seg_own)
            b = b - holder * seg_own
            j = lax.bitwise_xor(holder, c)
            value = own[b]
            span = pl.ds(pl.multiple_of(b * width, width), width)
            for q, peer in enumerate(peers):
                value = jnp.where(j == q + 1, peer[:, span], value)
            outs[n_row - 1 - k][s] = value


def multiply(tiles, src, source, rows, acc):
    rhs, width = src.shape[1:]
    unroll = min(32, tiles.shape[0])

    def step(i, carry):
        start = i * unroll
        got = []
        for u in range(0, unroll, 2):
            t = start + u
            left = jnp.concatenate([src[source(t)], src[source(t + 1)]], axis=0)
            right = jnp.concatenate([tiles[t], tiles[t + 1]], axis=1)
            both = jnp.dot(left, right, preferred_element_type=F32)
            got += [both[:rhs, :width], both[rhs:, width:]]
        for u, value in enumerate(got):
            acc[rows[start + u]] += value
        return carry

    lax.fori_loop(0, tiles.shape[0] // unroll, step, 0)


def coeff_body(n_row, n_col, pan_own, slots, rows, needs, *refs):
    packs = refs[:n_row]
    from_col = refs[n_row : n_row + n_col - 1]
    tiles, part, message, src, named = refs[n_row + n_col - 1 :]
    r, c = lax.axis_index("row"), lax.axis_index("col")
    pan_group = pan_own * n_col
    cap = needs.shape[1]
    for k in range(n_row):
        first = lax.bitwise_xor(r, k) * pan_group
        src[pl.ds(first + c * pan_own, pan_own)] = packs[k][pl.ds(0, pan_own)]
        for j, x in enumerate(from_col):
            there = first + lax.bitwise_xor(c, j + 1) * pan_own
            src[pl.ds(there, pan_own)] = x[pl.ds(k * pan_own, pan_own)]
    for p in range(n_row):
        for s in range(cap):
            named[p * cap + s] = p * pan_group + needs[p, s]
    part[...] = jnp.zeros_like(part)
    multiply(tiles, src, lambda t: named[slots[t]], rows, part)
    high = part[...].astype(BF16)
    message[pl.ds(0, pan_group)] = high
    message[pl.ds(pan_group, pan_group)] = (part[...] - high.astype(F32)).astype(BF16)


def induct_body(n_row, n_col, seg_own, slots, rows, _after, *refs):
    got = refs[:n_row][::-1]
    tiles = refs[n_row]
    own, *sends = refs[n_row + 1 : -2]
    src, acc = refs[-2:]
    cap = got[0].shape[0]
    r, c = lax.axis_index("row"), lax.axis_index("col")
    for k in range(n_row):
        src[pl.ds(lax.bitwise_xor(r, k) * cap, cap)] = got[k][...]
    acc[...] = jnp.zeros_like(acc)
    multiply(tiles, src, lambda t: slots[t], rows, acc)
    own[...] = acc[pl.ds(c * seg_own, seg_own)]
    for j in range(1, n_col):
        sends[j - 1][...] = acc[pl.ds(lax.bitwise_xor(c, j) * seg_own, seg_own)].astype(BF16)


def panels_body(n_row, n_col, pan_own, part, ends_own, *refs):
    parts = refs[: n_col - 1]
    relayed = refs[n_col - 1 : 2 * n_col - 2]
    pot, end_keep, *messages = refs[2 * n_col - 2 :]
    pan_group = part.shape[0]
    total = part[...]
    for x in parts:
        total += x[pl.ds(0, pan_group)].astype(F32) + x[pl.ds(pan_group, pan_group)].astype(F32)
    rounded = total.astype(BF16)
    pot[...] = rounded
    for k in range(n_row):
        sums = ends_own[pl.ds(k * pan_own, pan_own)]
        for x in relayed:
            sums += x[pl.ds((n_row + k) * pan_own, pan_own)].astype(F32)
        if k == 0:
            end_keep[...] = sums
        else:
            messages[n_row - 1 - k][pl.ds(0, pan_own)] = sums.astype(BF16)
            messages[n_row - 1 - k][pl.ds(pan_own, pan_group)] = rounded


def base_body(n_col, pan_own, charge, scale, field_own, end_own, pot, *refs):
    field_in, (field, panels, pot_out) = refs[: n_col - 1], refs[n_col - 1 :]
    width = pot.shape[2]
    c = lax.axis_index("col")
    total = field_own[...]
    for x in field_in:
        total += x[...].astype(F32)
    field[...] = total
    for q in range(pan_own):
        span = slice(q * width, (q + 1) * width)
        panels[q] = scale[...] * charge[:, span].astype(F32) + end_own[q]
        pot_out[:, span] = pot[c * pan_own + q]


def final_body(n_row, n_col, pan_own, cap, slots, links, off, field, panels, pot, *refs):
    arrived, (seg_out, pan_out, held, seg, sems) = refs[: n_row - 1][::-1], refs[n_row - 1 :]
    seg_own, rhs, width = field.shape
    pan_group = pan_own * n_col
    r = lax.axis_index("row")
    held[pl.ds(r * pan_group, pan_group)] = pot[...].astype(F32)
    for k, x in enumerate(arrived):
        sender = lax.bitwise_xor(r, k + 1)
        held[pl.ds(sender * pan_group, pan_group)] = x[pl.ds(pan_own, pan_group)].astype(F32)

    def at_end(e, k, span):
        slot = slots[e, k]
        p = lax.div(slot, cap)
        values = held[p * pan_group + links[p, slot - p * cap]]
        lanes = jnp.broadcast_to(off[e : e + 1, span], (rhs, width))
        return jnp.take_along_axis(values, lanes, axis=1, mode="promise_in_bounds")

    chunks = sems.shape[0]
    size = seg_own // chunks
    copies = []
    for i in range(chunks):
        for k in range(i * size, (i + 1) * size):
            span = pl.ds(k * width, width)
            seg[:, span] = (field[k] + at_end(0, k, span) - at_end(1, k, span)).astype(BF16)
        part = pl.ds(i * size * width, size * width)
        copies.append(pltpu.make_async_copy(seg.at[:, part], seg_out.at[:, part], sems.at[i]))
        copies[i].start()
    for q in range(pan_own):
        total = panels[q]
        for x in arrived:
            total += x[q].astype(F32)
        pan_out[:, q * width : (q + 1) * width] = total.astype(BF16)
    for copy in copies:
        copy.wait()


def shards(
    current,
    charge,
    rhs_scale,
    induct_tiles,
    induct_rows,
    induct_slots,
    induct_needs,
    coeff_tiles,
    coeff_rows,
    coeff_slots,
    coeff_needs,
    link_needs,
    end_slots,
    end_offsets,
):
    n_row = lax.axis_size("row")
    n_col = lax.axis_size("col")
    width = induct_tiles.shape[1]
    rhs = current.shape[0]
    seg_own = current.shape[1] // width
    pan_own = charge.shape[1] // width
    seg_group, pan_group = seg_own * n_col, pan_own * n_col
    cap_l, cap_p, cap_k = induct_needs.shape[1], coeff_needs.shape[1], link_needs.shape[1]
    slots_t, off_t = end_slots.T, end_offsets.T

    def like(blocks, dtype):
        return jax.ShapeDtypeStruct((blocks, rhs, width), dtype)

    cur = exchange_all(current, [current] * (n_col - 1), "col")
    (pack,) = call(
        functools.partial(pack_body, pan_own),
        "pack_charges",
        [like(pan_own + 1, BF16)],
        [VMEM] * 2,
        [pltpu.VMEM((rhs, width), jnp.int32)],
        moved=2**16,
    )(*in_hbm(charge, induct_needs))
    packs = exchange_all(pack, [pack] * (n_row - 1), "row")

    rows_own = n_row * pan_own
    scalars = [slots_t, link_needs, induct_slots, induct_rows, coeff_slots, coeff_rows, coeff_needs]
    n_tables = len(scalars)
    outs = call(
        functools.partial(ends_body, n_row, n_col, pan_own, cap_k, n_tables),
        "end_sums",
        [pltpu.SMEM(x.shape, jnp.int32) for x in scalars]
        + [jax.ShapeDtypeStruct(off_t.shape, jnp.int32), like(seg_own, BF16), like(rows_own, F32)]
        + [like(rows_own, BF16)] * (n_col - 1),
        [ANY] * (n_tables + 2),
        [
            pltpu.VMEM(current.shape, BF16),
            pltpu.VMEM((n_row * pan_group, rhs, width), F32),
            pltpu.SemaphoreType.DMA((n_tables + 2,)),
        ],
        flops=5 * 10**8,
        moved=2**18,
        out_specs=[SMEM] * n_tables + [VMEM] * (2 + n_col),
    )(*in_hbm(*scalars, off_t, current))
    slots_s, links_s, induct_slots, induct_rows, coeff_slots, coeff_rows, coeff_needs = outs[:n_tables]
    off_v, own_blocks, ends_own, *ends_out = outs[n_tables:]

    asked, *relays = call(
        functools.partial(relay_body, n_row, n_col, pan_own),
        "relay_charges",
        [jax.ShapeDtypeStruct((n_row, width), jnp.int32)] + [like(2 * rows_own, BF16)] * (n_col - 1),
        [VMEM] * (n_row + n_col - 1) + [ANY] * (n_col - 1),
        moved=2**16,
    )(*packs, *ends_out, *cur[1:])
    relayed = exchange_all(None, relays, "col")[1:]

    *picks, own_picks = call(
        functools.partial(pick_body, n_row, n_col, cap_l),
        "pick_blocks",
        [like(cap_l, BF16)] * n_row,
        [SMEM] + [VMEM] * n_col,
        moved=2**18,
    )(asked, own_blocks, *cur[1:])
    got = exchange_all(own_picks, picks[::-1], "row")

    part, message = call(
        functools.partial(coeff_body, n_row, n_col, pan_own),
        "coeff_tiles",
        [like(pan_group, F32), like(2 * pan_group, BF16)],
        [SMEM] * 3 + [VMEM] * (n_row + n_col),
        [
            pltpu.VMEM((n_row * pan_group, rhs, width), BF16),
            pltpu.SMEM((n_row * cap_p,), jnp.int32),
        ],
        flops=2 * 10**9,
        moved=coeff_tiles.size * 2,
    )(coeff_slots, coeff_rows, coeff_needs, *packs, *relayed, coeff_tiles)
    parts = exchange_all(None, [message] * (n_col - 1), "col")[1:]

    field_own, *field_out = call(
        functools.partial(induct_body, n_row, n_col, seg_own),
        "induct_tiles",
        [like(seg_own, F32)] + [like(seg_own, BF16)] * (n_col - 1),
        [SMEM, SMEM, ANY] + [VMEM] * (n_row + 1),
        [
            pltpu.VMEM((n_row * cap_l, rhs, width), BF16),
            pltpu.VMEM((seg_group, rhs, width), F32),
        ],
        flops=4 * 10**9,
        moved=induct_tiles.size * 2,
    )(induct_slots, induct_rows, part, *got[::-1], induct_tiles)
    field_in = exchange_all(None, field_out, "col")[1:]

    pot, end_keep, *row_messages = call(
        functools.partial(panels_body, n_row, n_col, pan_own),
        "panel_sums",
        [like(pan_group, BF16), like(pan_own, F32)] + [like(pan_own + pan_group, BF16)] * (n_row - 1),
        [VMEM] * (2 * n_col),
        flops=5 * 10**9,
        moved=2**18,
    )(part, ends_own, *parts, *relayed)
    arrived = exchange_all(None, row_messages[::-1], "row")[1:]

    field, panels, pot_out = call(
        functools.partial(base_body, n_col, pan_own),
        "base_sums",
        [like(seg_own, F32), like(pan_own, F32), jax.ShapeDtypeStruct(charge.shape, BF16)],
        [VMEM] * (4 + n_col),
        flops=10**9,
        moved=2**20,
    )(charge, rhs_scale[:, None], field_own, end_keep, pot, *field_in)

    seg_out, pan_out = call(
        functools.partial(final_body, n_row, n_col, pan_own, cap_k),
        "outputs",
        [jax.ShapeDtypeStruct(x.shape, BF16) for x in (current, charge)],
        [SMEM, SMEM] + [VMEM] * (3 + n_row),
        [
            pltpu.VMEM((n_row * pan_group, rhs, width), F32),
            pltpu.VMEM(current.shape, BF16),
            pltpu.SemaphoreType.DMA((4,)),
        ],
        flops=10**9,
        moved=2**20,
        out_specs=[ANY, VMEM],
    )(slots_s, links_s, off_v, field, panels, pot, *arrived[::-1])
    return (seg_out, pan_out, pot_out)


def solution(mesh):
    blocks = P(("parts", "row", "col"))
    matrix = P(("parts", "row", "col"), None)
    tiles = P(("parts", "row", "col"), None, None)
    values = P("rhs", ("parts", "row", "col"))
    return jax.shard_map(
        shards,
        mesh=mesh,
        in_specs=(
            values,
            values,
            P(("parts", "rhs")),
            tiles,
            blocks,
            blocks,
            matrix,
            tiles,
            blocks,
            blocks,
            matrix,
            matrix,
            matrix,
            matrix,
        ),
        out_specs=(values, values, values),
        check_vma=False,
    )
```

```python
import functools

import jax
import jax.numpy as jnp
from jax import lax
from jax.experimental import pallas as pl
from jax.experimental.pallas import tpu as pltpu
from jax.sharding import PartitionSpec as P

F32 = jnp.float32
BF16 = jnp.bfloat16
VMEM = pl.BlockSpec(memory_space=pltpu.VMEM)
SMEM = pl.BlockSpec(memory_space=pltpu.SMEM)
ANY = pl.BlockSpec(memory_space=pl.ANY)


def exchange(x, axis, k):
    if k == 0:
        return x
    return lax.ppermute(x, axis, [(i, i ^ k) for i in range(lax.axis_size(axis))])


def exchange_all(first, others, axis):
    n = lax.axis_size(axis)
    got = {0: first}
    for k in reversed(range(1, n)):
        got[k] = exchange(others[k - 1], axis, k)
    return [got[k] for k in range(n)]


def call(body, name, out_shape, in_specs, scratch=(), flops=0, moved=0, out_specs=None):
    return pl.pallas_call(
        body,
        out_shape=out_shape,
        in_specs=in_specs,
        out_specs=out_specs or [VMEM] * len(out_shape),
        scratch_shapes=list(scratch),
        compiler_params=pltpu.CompilerParams(vmem_limit_bytes=16 * 2**20),
        cost_estimate=pl.CostEstimate(flops=flops, bytes_accessed=moved, transcendentals=0),
        name=name,
    )


def in_hbm(*arrays):
    return [pltpu.with_memory_space_constraint(x, pltpu.HBM) for x in arrays]


def pack_body(pan_own, charge, needs, message, wide):
    width = charge.shape[1] // pan_own
    for q in range(pan_own):
        message[q] = charge[:, q * width : (q + 1) * width]
    wide[...] = jnp.zeros_like(wide)
    wide[: needs.shape[0], : needs.shape[1]] = needs[...]
    message[pan_own] = wide[...].astype(F32).astype(BF16)


def ends_body(n_row, n_col, pan_own, cap, n_moved, *refs):
    sources, targets = refs[: n_moved + 2], refs[n_moved + 2 : 2 * n_moved + 2]
    (holder, lanes, blocks, own, *sends), (cur, off, acc, sems) = refs[2 * n_moved + 2 : -4], refs[-4:]
    copies = [
        pltpu.make_async_copy(source, target, sems.at[i])
        for i, (source, target) in enumerate(zip(sources, (cur, off, *targets)))
    ]
    for copy in copies:
        copy.start()
    slots, links = targets[:2]
    seg_own, _, width = blocks.shape
    pan_group = pan_own * n_col
    r, c = lax.axis_index("row"), lax.axis_index("col")
    acc[...] = jnp.zeros_like(acc)
    levels = lax.broadcasted_iota(jnp.int32, (width, width), 0)
    for copy in copies[:4]:
        copy.wait()

    def block(k):
        span = pl.ds(pl.multiple_of(k * width, width), width)
        for e in range(2):
            lanes[pl.ds(2 * k + e, 1), :] = off[e : e + 1, span]
        to_hot = jnp.where(levels == off[0:1, span], 1.0, 0.0).astype(BF16)
        from_hot = jnp.where(levels == off[1:2, span], -1.0, 0.0).astype(BF16)
        hot = jnp.concatenate([to_hot, from_hot], axis=0)
        value = cur[:, span]
        blocks[k] = value
        sums = lax.dot_general(value, hot, (((1,), (1,)), ((), ())), preferred_element_type=F32)
        return sums.astype(BF16).astype(F32)

    unroll = 16

    def step(i, carry):
        got = [block(i * unroll + u) for u in range(unroll)]
        for u in range(unroll):
            for e in range(2):
                slot = slots[e, i * unroll + u]
                holder[slot] = 2 * (i * unroll + u) + e
                p = lax.div(slot, cap)
                b = links[p, slot - p * cap]
                acc[lax.bitwise_xor(p, r) * pan_group + b] += got[u][:, e * width : (e + 1) * width]
        return carry

    lax.fori_loop(0, seg_own // unroll, step, 0)
    for k in range(n_row):
        here = pl.ds(k * pan_own, pan_own)
        own[here] = acc[pl.ds(k * pan_group + c * pan_own, pan_own)]
        for j in range(1, n_col):
            there = lax.bitwise_xor(c, j)
            sends[j - 1][here] = acc[pl.ds(k * pan_group + there * pan_own, pan_own)].astype(BF16)
    for copy in copies[4:]:
        copy.wait()


def relay_body(n_row, n_col, pan_own, *refs):
    packs = refs[:n_row]
    ends = refs[n_row : n_row + n_col - 1]
    asked, *messages = refs[n_row + 2 * n_col - 2 :]
    r = lax.axis_index("row")
    rhs, width = packs[0].shape[1:]
    mine = lax.broadcasted_iota(jnp.int32, (rhs, width), 0) == r
    for k in range(n_row):
        needs = packs[k][pan_own].astype(F32)
        asked[k : k + 1, :] = jnp.sum(jnp.where(mine, needs, 0.0), axis=0, keepdims=True).astype(jnp.int32)
        for message in messages:
            message[pl.ds(k * pan_own, pan_own)] = packs[k][pl.ds(0, pan_own)]
    for message, sums in zip(messages, ends):
        message[pl.ds(n_row * pan_own, n_row * pan_own)] = sums[...]


def pick_body(n_row, n_col, cap, asked, own, *refs):
    peers, outs = refs[: n_col - 1], refs[n_col - 1 :]
    seg_own, _, width = own.shape
    c = lax.axis_index("col")
    for k in range(n_row):
        for s in range(cap):
            b = asked[k, s]
            holder = lax.div(b, seg_own)
            b = b - holder * seg_own
            j = lax.bitwise_xor(holder, c)
            value = own[b]
            span = pl.ds(pl.multiple_of(b * width, width), width)
            for q, peer in enumerate(peers):
                value = jnp.where(j == q + 1, peer[:, span], value)
            outs[n_row - 1 - k][s] = value


def multiply(tiles, src, source, rows, acc):
    rhs, width = src.shape[1:]
    unroll = min(32, tiles.shape[0])

    def step(i, carry):
        start = i * unroll
        got = []
        for u in range(0, unroll, 2):
            t = start + u
            left = jnp.concatenate([src[source(t)], src[source(t + 1)]], axis=0)
            right = jnp.concatenate([tiles[t], tiles[t + 1]], axis=1)
            both = jnp.dot(left, right, preferred_element_type=F32)
            got += [both[:rhs, :width], both[rhs:, width:]]
        for u, value in enumerate(got):
            acc[rows[start + u]] += value
        return carry

    lax.fori_loop(0, tiles.shape[0] // unroll, step, 0)


def coeff_body(n_row, n_col, pan_own, slots, rows, needs, *refs):
    packs = refs[:n_row]
    from_col = refs[n_row : n_row + n_col - 1]
    tiles, part, message, src, named = refs[n_row + n_col - 1 :]
    r, c = lax.axis_index("row"), lax.axis_index("col")
    pan_group = pan_own * n_col
    cap = needs.shape[1]
    for k in range(n_row):
        first = lax.bitwise_xor(r, k) * pan_group
        src[pl.ds(first + c * pan_own, pan_own)] = packs[k][pl.ds(0, pan_own)]
        for j, x in enumerate(from_col):
            there = first + lax.bitwise_xor(c, j + 1) * pan_own
            src[pl.ds(there, pan_own)] = x[pl.ds(k * pan_own, pan_own)]
    for p in range(n_row):
        for s in range(cap):
            named[p * cap + s] = p * pan_group + needs[p, s]
    part[...] = jnp.zeros_like(part)
    multiply(tiles, src, lambda t: named[slots[t]], rows, part)
    high = part[...].astype(BF16)
    message[pl.ds(0, pan_group)] = high
    message[pl.ds(pan_group, pan_group)] = (part[...] - high.astype(F32)).astype(BF16)


def induct_body(n_row, n_col, seg_own, slots, rows, _after, *refs):
    got = refs[:n_row][::-1]
    tiles = refs[n_row]
    own, *sends = refs[n_row + 1 : -2]
    src, acc = refs[-2:]
    cap = got[0].shape[0]
    r, c = lax.axis_index("row"), lax.axis_index("col")
    for k in range(n_row):
        src[pl.ds(lax.bitwise_xor(r, k) * cap, cap)] = got[k][...]
    acc[...] = jnp.zeros_like(acc)
    multiply(tiles, src, lambda t: slots[t], rows, acc)
    own[...] = acc[pl.ds(c * seg_own, seg_own)]
    for j in range(1, n_col):
        sends[j - 1][...] = acc[pl.ds(lax.bitwise_xor(c, j) * seg_own, seg_own)].astype(BF16)


def panels_body(n_row, n_col, pan_own, part, ends_own, *refs):
    parts = refs[: n_col - 1]
    relayed = refs[n_col - 1 : 2 * n_col - 2]
    pot, end_keep, *messages = refs[2 * n_col - 2 :]
    pan_group = part.shape[0]
    total = part[...]
    for x in parts:
        total += x[pl.ds(0, pan_group)].astype(F32) + x[pl.ds(pan_group, pan_group)].astype(F32)
    rounded = total.astype(BF16)
    pot[...] = rounded
    for k in range(n_row):
        sums = ends_own[pl.ds(k * pan_own, pan_own)]
        for x in relayed:
            sums += x[pl.ds((n_row + k) * pan_own, pan_own)].astype(F32)
        if k == 0:
            end_keep[...] = sums
        else:
            messages[n_row - 1 - k][pl.ds(0, pan_own)] = sums.astype(BF16)
            messages[n_row - 1 - k][pl.ds(pan_own, pan_group)] = rounded


def add_drops(p, pots, first, links, holder, lanes, field):
    cap = links.shape[1]
    ends, drops = [], []
    for s in range(cap):
        j = holder[p * cap + s]
        values = pots[first + links[p, s]].astype(F32)
        at = jnp.broadcast_to(lanes[pl.ds(j, 1), :], values.shape)
        drop = jnp.take_along_axis(values, at, axis=1, mode="promise_in_bounds")
        k = lax.div(j, 2)
        drops.append(drop * (1 - 2 * (j - 2 * k)).astype(F32))
        ends.append(k)
    for k, drop in zip(ends, drops):
        field[k] += drop


def base_body(n_col, pan_own, links, holder, scale, lanes, pack, field_own, end_own, pot, *refs):
    field_in, (field, panels, pot_out) = refs[: n_col - 1], refs[n_col - 1 :]
    rhs, width = pot.shape[1:]
    r, c = lax.axis_index("row"), lax.axis_index("col")
    total = field_own[...]
    for x in field_in:
        total += x[...].astype(F32)
    field[...] = total
    row = lax.broadcasted_iota(jnp.int32, (rhs, width), 0)
    factor = jnp.zeros((rhs, width), F32)
    for i in range(rhs):
        factor = jnp.where(row == i, scale[i], factor)
    for q in range(pan_own):
        panels[q] = factor * pack[q].astype(F32) + end_own[q]
        pot_out[:, q * width : (q + 1) * width] = pot[c * pan_own + q]
    add_drops(r, pot, 0, links, holder, lanes, field)


def drops_body(k, pan_own, links, holder, lanes, message, field_in, field):
    field[...] = field_in[...]
    p = lax.bitwise_xor(lax.axis_index("row"), k)
    add_drops(p, message, pan_own, links, holder, lanes, field)


def final_body(n_row, pan_own, links, holder, lanes, field_in, panels, *refs):
    arrived, (seg_out, pan_out, field, seg, sems) = refs[: n_row - 1], refs[n_row - 1 :]
    seg_own, _, width = field.shape
    field[...] = field_in[...]
    p = lax.bitwise_xor(lax.axis_index("row"), 1)
    add_drops(p, arrived[0], pan_own, links, holder, lanes, field)
    chunks = sems.shape[0]
    size = seg_own // chunks
    copies = []
    for i in range(chunks):
        for k in range(i * size, (i + 1) * size):
            seg[:, k * width : (k + 1) * width] = field[k].astype(BF16)
        part = pl.ds(i * size * width, size * width)
        copies.append(pltpu.make_async_copy(seg.at[:, part], seg_out.at[:, part], sems.at[i]))
        copies[i].start()
    for q in range(pan_own):
        total = panels[q]
        for x in arrived:
            total += x[q].astype(F32)
        pan_out[:, q * width : (q + 1) * width] = total.astype(BF16)
    for copy in copies:
        copy.wait()


def shards(
    current,
    charge,
    rhs_scale,
    induct_tiles,
    induct_rows,
    induct_slots,
    induct_needs,
    coeff_tiles,
    coeff_rows,
    coeff_slots,
    coeff_needs,
    link_needs,
    end_slots,
    end_offsets,
):
    n_row = lax.axis_size("row")
    n_col = lax.axis_size("col")
    width = induct_tiles.shape[1]
    rhs = current.shape[0]
    seg_own = current.shape[1] // width
    pan_own = charge.shape[1] // width
    seg_group, pan_group = seg_own * n_col, pan_own * n_col
    cap_l, cap_p, cap_k = induct_needs.shape[1], coeff_needs.shape[1], link_needs.shape[1]
    slots_t, off_t = end_slots.T, end_offsets.T

    def like(blocks, dtype):
        return jax.ShapeDtypeStruct((blocks, rhs, width), dtype)

    cur = exchange_all(current, [current] * (n_col - 1), "col")
    (pack,) = call(
        functools.partial(pack_body, pan_own),
        "pack_charges",
        [like(pan_own + 1, BF16)],
        [VMEM] * 2,
        [pltpu.VMEM((rhs, width), jnp.int32)],
        moved=2**16,
    )(*in_hbm(charge, induct_needs))
    packs = exchange_all(pack, [pack] * (n_row - 1), "row")

    rows_own = n_row * pan_own
    scalars = [slots_t, link_needs, coeff_slots, coeff_rows, coeff_needs, induct_slots, induct_rows, rhs_scale]
    moved = [*scalars, coeff_tiles]
    outs = call(
        functools.partial(ends_body, n_row, n_col, pan_own, cap_k, len(moved)),
        "end_sums",
        [pltpu.SMEM(x.shape, x.dtype) for x in scalars]
        + [jax.ShapeDtypeStruct(coeff_tiles.shape, BF16)]
        + [pltpu.SMEM((2 * seg_own,), jnp.int32), jax.ShapeDtypeStruct((2 * seg_own, width), jnp.int32)]
        + [like(seg_own, BF16), like(rows_own, F32)]
        + [like(rows_own, BF16)] * (n_col - 1),
        [ANY] * (len(moved) + 2),
        [
            pltpu.VMEM(current.shape, BF16),
            pltpu.VMEM(off_t.shape, jnp.int32),
            pltpu.VMEM((n_row * pan_group, rhs, width), F32),
            pltpu.SemaphoreType.DMA((len(moved) + 2,)),
        ],
        flops=5 * 10**8,
        moved=2**18,
        out_specs=[SMEM] * len(scalars) + [VMEM, SMEM] + [VMEM] * (2 + n_col),
    )(*in_hbm(current, off_t, *moved))
    _, links_s, coeff_slots, coeff_rows, coeff_needs, induct_slots, induct_rows, scale, coeff_tiles = outs[: len(moved)]
    holder, lanes, own_blocks, ends_own, *ends_out = outs[len(moved) :]

    asked, *relays = call(
        functools.partial(relay_body, n_row, n_col, pan_own),
        "relay_charges",
        [jax.ShapeDtypeStruct((n_row, width), jnp.int32)] + [like(2 * rows_own, BF16)] * (n_col - 1),
        [VMEM] * (n_row + n_col - 1) + [ANY] * (n_col - 1),
        moved=2**16,
    )(*packs, *ends_out, *cur[1:])
    relayed = exchange_all(None, relays, "col")[1:]

    *picks, own_picks = call(
        functools.partial(pick_body, n_row, n_col, cap_l),
        "pick_blocks",
        [like(cap_l, BF16)] * n_row,
        [SMEM] + [VMEM] * n_col,
        moved=2**18,
    )(asked, own_blocks, *cur[1:])
    got = exchange_all(own_picks, picks[::-1], "row")

    part, message = call(
        functools.partial(coeff_body, n_row, n_col, pan_own),
        "coeff_tiles",
        [like(pan_group, F32), like(2 * pan_group, BF16)],
        [SMEM] * 3 + [VMEM] * (n_row + n_col),
        [
            pltpu.VMEM((n_row * pan_group, rhs, width), BF16),
            pltpu.SMEM((n_row * cap_p,), jnp.int32),
        ],
        flops=2 * 10**9,
        moved=coeff_tiles.size * 2,
    )(coeff_slots, coeff_rows, coeff_needs, *packs, *relayed, coeff_tiles)
    parts = exchange_all(None, [message] * (n_col - 1), "col")[1:]

    field_own, *field_out = call(
        functools.partial(induct_body, n_row, n_col, seg_own),
        "induct_tiles",
        [like(seg_own, F32)] + [like(seg_own, BF16)] * (n_col - 1),
        [SMEM, SMEM, ANY] + [VMEM] * (n_row + 1),
        [
            pltpu.VMEM((n_row * cap_l, rhs, width), BF16),
            pltpu.VMEM((seg_group, rhs, width), F32),
        ],
        flops=4 * 10**9,
        moved=induct_tiles.size * 2,
    )(induct_slots, induct_rows, part, *got[::-1], induct_tiles)
    field_in = exchange_all(None, field_out, "col")[1:]

    pot, end_keep, *row_messages = call(
        functools.partial(panels_body, n_row, n_col, pan_own),
        "panel_sums",
        [like(pan_group, BF16), like(pan_own, F32)] + [like(pan_own + pan_group, BF16)] * (n_row - 1),
        [VMEM] * (2 * n_col),
        flops=5 * 10**9,
        moved=2**18,
    )(part, ends_own, *parts, *relayed)
    arrived = exchange_all(None, row_messages[::-1], "row")[1:]

    field, panels, pot_out = call(
        functools.partial(base_body, n_col, pan_own),
        "base_sums",
        [like(seg_own, F32), like(pan_own, F32), jax.ShapeDtypeStruct(charge.shape, BF16)],
        [SMEM] * 3 + [VMEM] * (4 + n_col),
        flops=10**9,
        moved=2**20,
    )(links_s, holder, scale, lanes, pack, field_own, end_keep, pot, *field_in)

    for k in reversed(range(2, n_row)):
        (field,) = call(
            functools.partial(drops_body, k, pan_own),
            "add_drops",
            [like(seg_own, F32)],
            [SMEM] * 2 + [VMEM] * 3,
            flops=10**8,
            moved=2**20,
        )(links_s, holder, lanes, arrived[k - 1], field)

    seg_out, pan_out = call(
        functools.partial(final_body, n_row, pan_own),
        "outputs",
        [jax.ShapeDtypeStruct(x.shape, BF16) for x in (current, charge)],
        [SMEM] * 2 + [VMEM] * (2 + n_row),
        [
            pltpu.VMEM((seg_own, rhs, width), F32),
            pltpu.VMEM(current.shape, BF16),
            pltpu.SemaphoreType.DMA((4,)),
        ],
        flops=10**9,
        moved=2**20,
        out_specs=[ANY, VMEM],
    )(links_s, holder, lanes, field, panels, *arrived)
    return (seg_out, pan_out, pot_out)


def solution(mesh):
    blocks = P(("parts", "row", "col"))
    matrix = P(("parts", "row", "col"), None)
    tiles = P(("parts", "row", "col"), None, None)
    values = P("rhs", ("parts", "row", "col"))
    return jax.shard_map(
        shards,
        mesh=mesh,
        in_specs=(
            values,
            values,
            P(("parts", "rhs")),
            tiles,
            blocks,
            blocks,
            matrix,
            tiles,
            blocks,
            blocks,
            matrix,
            matrix,
            matrix,
            matrix,
        ),
        out_specs=(values, values, values),
        check_vma=False,
    )
```

```python
import functools

import jax
import jax.numpy as jnp
from jax import lax
from jax.experimental import pallas as pl
from jax.experimental.pallas import tpu as pltpu
from jax.sharding import PartitionSpec as P

F32 = jnp.float32
BF16 = jnp.bfloat16
VMEM = pl.BlockSpec(memory_space=pltpu.VMEM)
SMEM = pl.BlockSpec(memory_space=pltpu.SMEM)
ANY = pl.BlockSpec(memory_space=pl.ANY)


def exchange(x, axis, k):
    if k == 0:
        return x
    return lax.ppermute(x, axis, [(i, i ^ k) for i in range(lax.axis_size(axis))])


def exchange_all(first, others, axis):
    n = lax.axis_size(axis)
    got = {0: first}
    for k in reversed(range(1, n)):
        got[k] = exchange(others[k - 1], axis, k)
    return [got[k] for k in range(n)]


def call(body, name, out_shape, in_specs, scratch=(), flops=0, moved=0, out_specs=None):
    return pl.pallas_call(
        body,
        out_shape=out_shape,
        in_specs=in_specs,
        out_specs=out_specs or [VMEM] * len(out_shape),
        scratch_shapes=list(scratch),
        compiler_params=pltpu.CompilerParams(vmem_limit_bytes=16 * 2**20),
        cost_estimate=pl.CostEstimate(flops=flops, bytes_accessed=moved, transcendentals=0),
        name=name,
    )


def in_hbm(*arrays):
    return [pltpu.with_memory_space_constraint(x, pltpu.HBM) for x in arrays]


def pack_body(pan_own, charge, needs, message, wide):
    width = charge.shape[1] // pan_own
    for q in range(pan_own):
        message[q] = charge[:, q * width : (q + 1) * width]
    wide[...] = jnp.zeros_like(wide)
    wide[: needs.shape[0], : needs.shape[1]] = needs[...]
    message[pan_own] = wide[...].astype(F32).astype(BF16)


def ends_body(n_row, n_col, pan_own, cap, n_moved, *refs):
    sources, targets = refs[: n_moved + 2], refs[n_moved + 2 : 2 * n_moved + 2]
    (holder, lanes, blocks, own, *sends), (cur, off, acc, sems) = refs[2 * n_moved + 2 : -4], refs[-4:]
    copies = [
        pltpu.make_async_copy(source, target, sems.at[i])
        for i, (source, target) in enumerate(zip(sources, (cur, off, *targets)))
    ]
    for copy in copies:
        copy.start()
    slots, links = targets[:2]
    seg_own, _, width = blocks.shape
    pan_group = pan_own * n_col
    r, c = lax.axis_index("row"), lax.axis_index("col")
    acc[...] = jnp.zeros_like(acc)
    levels = lax.broadcasted_iota(jnp.int32, (width, width), 0)
    for copy in copies[:4]:
        copy.wait()

    def block(k):
        span = pl.ds(pl.multiple_of(k * width, width), width)
        for e in range(2):
            lanes[pl.ds(2 * k + e, 1), :] = off[e : e + 1, span]
        to_hot = jnp.where(levels == off[0:1, span], 1.0, 0.0).astype(BF16)
        from_hot = jnp.where(levels == off[1:2, span], -1.0, 0.0).astype(BF16)
        hot = jnp.concatenate([to_hot, from_hot], axis=0)
        value = cur[:, span]
        blocks[k] = value
        sums = lax.dot_general(value, hot, (((1,), (1,)), ((), ())), preferred_element_type=F32)
        return sums.astype(BF16).astype(F32)

    unroll = 16

    def step(i, carry):
        got = [block(i * unroll + u) for u in range(unroll)]
        for u in range(unroll):
            for e in range(2):
                slot = slots[e, i * unroll + u]
                holder[slot] = 2 * (i * unroll + u) + e
                p = lax.div(slot, cap)
                b = links[p, slot - p * cap]
                acc[lax.bitwise_xor(p, r) * pan_group + b] += got[u][:, e * width : (e + 1) * width]
        return carry

    lax.fori_loop(0, seg_own // unroll, step, 0)
    for k in range(n_row):
        here = pl.ds(k * pan_own, pan_own)
        own[here] = acc[pl.ds(k * pan_group + c * pan_own, pan_own)]
        for j in range(1, n_col):
            there = lax.bitwise_xor(c, j)
            sends[j - 1][here] = acc[pl.ds(k * pan_group + there * pan_own, pan_own)].astype(BF16)
    for copy in copies[4:]:
        copy.wait()


def relay_body(n_row, n_col, pan_own, *refs):
    packs = refs[:n_row]
    ends = refs[n_row : n_row + n_col - 1]
    asked, *messages = refs[n_row + 2 * n_col - 2 :]
    r = lax.axis_index("row")
    rhs, width = packs[0].shape[1:]
    mine = lax.broadcasted_iota(jnp.int32, (rhs, width), 0) == r
    for k in range(n_row):
        needs = packs[k][pan_own].astype(F32)
        asked[k : k + 1, :] = jnp.sum(jnp.where(mine, needs, 0.0), axis=0, keepdims=True).astype(jnp.int32)
        for message in messages:
            message[pl.ds(k * pan_own, pan_own)] = packs[k][pl.ds(0, pan_own)]
    for message, sums in zip(messages, ends):
        message[pl.ds(n_row * pan_own, n_row * pan_own)] = sums[...]


def pick_body(n_row, n_col, cap, asked, own, *refs):
    peers, outs = refs[: n_col - 1], refs[n_col - 1 :]
    seg_own, _, width = own.shape
    c = lax.axis_index("col")
    for k in range(n_row):
        for s in range(cap):
            b = asked[k, s]
            holder = lax.div(b, seg_own)
            b = b - holder * seg_own
            j = lax.bitwise_xor(holder, c)
            value = own[b]
            span = pl.ds(pl.multiple_of(b * width, width), width)
            for q, peer in enumerate(peers):
                value = jnp.where(j == q + 1, peer[:, span], value)
            outs[n_row - 1 - k][s] = value


def multiply(tiles, src, source, rows, acc):
    rhs, width = src.shape[1:]
    unroll = min(32, tiles.shape[0])

    def step(i, carry):
        start = i * unroll
        got = []
        for u in range(0, unroll, 2):
            t = start + u
            left = jnp.concatenate([src[source(t)], src[source(t + 1)]], axis=0)
            right = jnp.concatenate([tiles[t], tiles[t + 1]], axis=1)
            both = jnp.dot(left, right, preferred_element_type=F32)
            got += [both[:rhs, :width], both[rhs:, width:]]
        for u, value in enumerate(got):
            acc[rows[start + u]] += value
        return carry

    lax.fori_loop(0, tiles.shape[0] // unroll, step, 0)


def coeff_body(n_row, n_col, pan_own, slots, rows, needs, *refs):
    packs = refs[:n_row]
    from_col = refs[n_row : n_row + n_col - 1]
    tiles, part, message, src, named = refs[n_row + n_col - 1 :]
    r, c = lax.axis_index("row"), lax.axis_index("col")
    pan_group = pan_own * n_col
    cap = needs.shape[1]
    for k in range(n_row):
        first = lax.bitwise_xor(r, k) * pan_group
        src[pl.ds(first + c * pan_own, pan_own)] = packs[k][pl.ds(0, pan_own)]
        for j, x in enumerate(from_col):
            there = first + lax.bitwise_xor(c, j + 1) * pan_own
            src[pl.ds(there, pan_own)] = x[pl.ds(k * pan_own, pan_own)]
    for p in range(n_row):
        for s in range(cap):
            named[p * cap + s] = p * pan_group + needs[p, s]
    part[...] = jnp.zeros_like(part)
    multiply(tiles, src, lambda t: named[slots[t]], rows, part)
    high = part[...].astype(BF16)
    message[pl.ds(0, pan_group)] = high
    message[pl.ds(pan_group, pan_group)] = (part[...] - high.astype(F32)).astype(BF16)


def induct_body(n_row, n_col, seg_own, slots, rows, _after, *refs):
    got = refs[:n_row][::-1]
    tiles = refs[n_row]
    own, *sends = refs[n_row + 1 : -2]
    src, acc = refs[-2:]
    cap = got[0].shape[0]
    r, c = lax.axis_index("row"), lax.axis_index("col")
    for k in range(n_row):
        src[pl.ds(lax.bitwise_xor(r, k) * cap, cap)] = got[k][...]
    acc[...] = jnp.zeros_like(acc)
    multiply(tiles, src, lambda t: slots[t], rows, acc)
    own[...] = acc[pl.ds(c * seg_own, seg_own)]
    for j in range(1, n_col):
        sends[j - 1][...] = acc[pl.ds(lax.bitwise_xor(c, j) * seg_own, seg_own)].astype(BF16)


def panels_body(n_row, n_col, pan_own, part, ends_own, *refs):
    parts = refs[: n_col - 1]
    relayed = refs[n_col - 1 : 2 * n_col - 2]
    pot, end_keep, *messages = refs[2 * n_col - 2 :]
    pan_group = part.shape[0]
    total = part[...]
    for x in parts:
        total += x[pl.ds(0, pan_group)].astype(F32) + x[pl.ds(pan_group, pan_group)].astype(F32)
    rounded = total.astype(BF16)
    pot[...] = rounded
    for k in range(n_row):
        sums = ends_own[pl.ds(k * pan_own, pan_own)]
        for x in relayed:
            sums += x[pl.ds((n_row + k) * pan_own, pan_own)].astype(F32)
        if k == 0:
            end_keep[...] = sums
        else:
            messages[n_row - 1 - k][pl.ds(0, pan_own)] = sums.astype(BF16)
            messages[n_row - 1 - k][pl.ds(pan_own, pan_group)] = rounded


def add_drops(p, pots, first, links, holder, lanes, field):
    cap = links.shape[1]
    ends, drops = [], []
    for s in range(cap):
        j = holder[p * cap + s]
        values = pots[first + links[p, s]].astype(F32)
        at = jnp.broadcast_to(lanes[pl.ds(j, 1), :], values.shape)
        drop = jnp.take_along_axis(values, at, axis=1, mode="promise_in_bounds")
        k = lax.div(j, 2)
        drops.append(drop * (1 - 2 * (j - 2 * k)).astype(F32))
        ends.append(k)
    for k, drop in zip(ends, drops):
        field[k] += drop


def base_body(n_col, pan_own, links, holder, scale, lanes, pack, field_own, end_own, pot, *refs):
    field_in, (field, panels, pot_out) = refs[: n_col - 1], refs[n_col - 1 :]
    rhs, width = pot.shape[1:]
    r, c = lax.axis_index("row"), lax.axis_index("col")
    total = field_own[...]
    for x in field_in:
        total += x[...].astype(F32)
    field[...] = total
    row = lax.broadcasted_iota(jnp.int32, (rhs, width), 0)
    factor = jnp.zeros((rhs, width), F32)
    for i in range(rhs):
        factor = jnp.where(row == i, scale[i], factor)
    for q in range(pan_own):
        panels[q] = factor * pack[q].astype(F32) + end_own[q]
        pot_out[:, q * width : (q + 1) * width] = pot[c * pan_own + q]
    add_drops(r, pot, 0, links, holder, lanes, field)


def drops_body(k, pan_own, links, holder, lanes, message, field_in, field):
    field[...] = field_in[...]
    p = lax.bitwise_xor(lax.axis_index("row"), k)
    add_drops(p, message, pan_own, links, holder, lanes, field)


def final_body(n_row, pan_own, links, holder, lanes, field_in, panels, *refs):
    arrived, (seg_out, pan_out, field, seg, pan, sems) = refs[: n_row - 1], refs[n_row - 1 :]
    seg_own, _, width = field.shape
    field[...] = field_in[...]
    p = lax.bitwise_xor(lax.axis_index("row"), 1)
    add_drops(p, arrived[0], pan_own, links, holder, lanes, field)
    for q in range(pan_own):
        total = panels[q]
        for x in arrived:
            total += x[q].astype(F32)
        pan[:, q * width : (q + 1) * width] = total.astype(BF16)
    chunks = sems.shape[0] - 1
    copies = [pltpu.make_async_copy(pan, pan_out, sems.at[chunks])]
    copies[0].start()
    size = seg_own // chunks
    for i in range(chunks):
        for k in range(i * size, (i + 1) * size):
            seg[:, k * width : (k + 1) * width] = field[k].astype(BF16)
        part = pl.ds(i * size * width, size * width)
        copies.append(pltpu.make_async_copy(seg.at[:, part], seg_out.at[:, part], sems.at[i]))
        copies[-1].start()
    for copy in copies:
        copy.wait()


def shards(
    current,
    charge,
    rhs_scale,
    induct_tiles,
    induct_rows,
    induct_slots,
    induct_needs,
    coeff_tiles,
    coeff_rows,
    coeff_slots,
    coeff_needs,
    link_needs,
    end_slots,
    end_offsets,
):
    n_row = lax.axis_size("row")
    n_col = lax.axis_size("col")
    width = induct_tiles.shape[1]
    rhs = current.shape[0]
    seg_own = current.shape[1] // width
    pan_own = charge.shape[1] // width
    seg_group, pan_group = seg_own * n_col, pan_own * n_col
    cap_l, cap_p, cap_k = induct_needs.shape[1], coeff_needs.shape[1], link_needs.shape[1]
    slots_t, off_t = end_slots.T, end_offsets.T

    def like(blocks, dtype):
        return jax.ShapeDtypeStruct((blocks, rhs, width), dtype)

    cur = exchange_all(current, [current] * (n_col - 1), "col")
    (pack,) = call(
        functools.partial(pack_body, pan_own),
        "pack_charges",
        [like(pan_own + 1, BF16)],
        [VMEM] * 2,
        [pltpu.VMEM((rhs, width), jnp.int32)],
        moved=2**16,
    )(*in_hbm(charge, induct_needs))
    packs = exchange_all(pack, [pack] * (n_row - 1), "row")

    rows_own = n_row * pan_own
    scalars = [slots_t, link_needs, coeff_slots, coeff_rows, coeff_needs, induct_slots, induct_rows, rhs_scale]
    moved = [*scalars, coeff_tiles]
    outs = call(
        functools.partial(ends_body, n_row, n_col, pan_own, cap_k, len(moved)),
        "end_sums",
        [pltpu.SMEM(x.shape, x.dtype) for x in scalars]
        + [jax.ShapeDtypeStruct(coeff_tiles.shape, BF16)]
        + [pltpu.SMEM((2 * seg_own,), jnp.int32), jax.ShapeDtypeStruct((2 * seg_own, width), jnp.int32)]
        + [like(seg_own, BF16), like(rows_own, F32)]
        + [like(rows_own, BF16)] * (n_col - 1),
        [ANY] * (len(moved) + 2),
        [
            pltpu.VMEM(current.shape, BF16),
            pltpu.VMEM(off_t.shape, jnp.int32),
            pltpu.VMEM((n_row * pan_group, rhs, width), F32),
            pltpu.SemaphoreType.DMA((len(moved) + 2,)),
        ],
        flops=5 * 10**8,
        moved=2**18,
        out_specs=[SMEM] * len(scalars) + [VMEM, SMEM] + [VMEM] * (2 + n_col),
    )(*in_hbm(current, off_t, *moved))
    _, links_s, coeff_slots, coeff_rows, coeff_needs, induct_slots, induct_rows, scale, coeff_tiles = outs[: len(moved)]
    holder, lanes, own_blocks, ends_own, *ends_out = outs[len(moved) :]

    asked, *relays = call(
        functools.partial(relay_body, n_row, n_col, pan_own),
        "relay_charges",
        [jax.ShapeDtypeStruct((n_row, width), jnp.int32)] + [like(2 * rows_own, BF16)] * (n_col - 1),
        [VMEM] * (n_row + n_col - 1) + [ANY] * (n_col - 1),
        moved=2**16,
    )(*packs, *ends_out, *cur[1:])
    relayed = exchange_all(None, relays, "col")[1:]

    *picks, own_picks = call(
        functools.partial(pick_body, n_row, n_col, cap_l),
        "pick_blocks",
        [like(cap_l, BF16)] * n_row,
        [VMEM] * (1 + n_col),
        moved=2**18,
    )(asked, own_blocks, *cur[1:])
    got = exchange_all(own_picks, picks[::-1], "row")

    part, message = call(
        functools.partial(coeff_body, n_row, n_col, pan_own),
        "coeff_tiles",
        [like(pan_group, F32), like(2 * pan_group, BF16)],
        [SMEM] * 3 + [VMEM] * (n_row + n_col),
        [
            pltpu.VMEM((n_row * pan_group, rhs, width), BF16),
            pltpu.SMEM((n_row * cap_p,), jnp.int32),
        ],
        flops=2 * 10**9,
        moved=coeff_tiles.size * 2,
    )(coeff_slots, coeff_rows, coeff_needs, *packs, *relayed, coeff_tiles)
    parts = exchange_all(None, [message] * (n_col - 1), "col")[1:]

    field_own, *field_out = call(
        functools.partial(induct_body, n_row, n_col, seg_own),
        "induct_tiles",
        [like(seg_own, F32)] + [like(seg_own, BF16)] * (n_col - 1),
        [SMEM, SMEM, ANY] + [VMEM] * (n_row + 1),
        [
            pltpu.VMEM((n_row * cap_l, rhs, width), BF16),
            pltpu.VMEM((seg_group, rhs, width), F32),
        ],
        flops=4 * 10**9,
        moved=induct_tiles.size * 2,
    )(induct_slots, induct_rows, part, *got[::-1], induct_tiles)
    field_in = exchange_all(None, field_out, "col")[1:]

    pot, end_keep, *row_messages = call(
        functools.partial(panels_body, n_row, n_col, pan_own),
        "panel_sums",
        [like(pan_group, BF16), like(pan_own, F32)] + [like(pan_own + pan_group, BF16)] * (n_row - 1),
        [VMEM] * (2 * n_col),
        flops=5 * 10**9,
        moved=2**18,
    )(part, ends_own, *parts, *relayed)
    arrived = exchange_all(None, row_messages[::-1], "row")[1:]

    field, panels, pot_out = call(
        functools.partial(base_body, n_col, pan_own),
        "base_sums",
        [like(seg_own, F32), like(pan_own, F32), jax.ShapeDtypeStruct(charge.shape, BF16)],
        [SMEM] * 3 + [VMEM] * (4 + n_col),
        flops=10**9,
        moved=2**20,
    )(links_s, holder, scale, lanes, pack, field_own, end_keep, pot, *field_in)

    for k in reversed(range(2, n_row)):
        (field,) = call(
            functools.partial(drops_body, k, pan_own),
            "add_drops",
            [like(seg_own, F32)],
            [SMEM] * 2 + [VMEM] * 3,
            flops=10**8,
            moved=2**20,
        )(links_s, holder, lanes, arrived[k - 1], field)

    seg_out, pan_out = call(
        functools.partial(final_body, n_row, pan_own),
        "outputs",
        [jax.ShapeDtypeStruct(x.shape, BF16) for x in (current, charge)],
        [SMEM] * 2 + [VMEM] * (2 + n_row),
        [
            pltpu.VMEM((seg_own, rhs, width), F32),
            pltpu.VMEM(current.shape, BF16),
            pltpu.VMEM(charge.shape, BF16),
            pltpu.SemaphoreType.DMA((3,)),
        ],
        flops=10**9,
        moved=2**20,
        out_specs=[ANY, ANY],
    )(links_s, holder, lanes, field, panels, *arrived)
    return (seg_out, pan_out, pot_out)


def solution(mesh):
    blocks = P(("parts", "row", "col"))
    matrix = P(("parts", "row", "col"), None)
    tiles = P(("parts", "row", "col"), None, None)
    values = P("rhs", ("parts", "row", "col"))
    return jax.shard_map(
        shards,
        mesh=mesh,
        in_specs=(
            values,
            values,
            P(("parts", "rhs")),
            tiles,
            blocks,
            blocks,
            matrix,
            tiles,
            blocks,
            blocks,
            matrix,
            matrix,
            matrix,
            matrix,
        ),
        out_specs=(values, values, values),
        check_vma=False,
    )
```

```python
import functools

import jax
import jax.numpy as jnp
from jax import lax
from jax.experimental import pallas as pl
from jax.experimental.pallas import tpu as pltpu
from jax.sharding import PartitionSpec as P

F32 = jnp.float32
BF16 = jnp.bfloat16
VMEM = pl.BlockSpec(memory_space=pltpu.VMEM)
SMEM = pl.BlockSpec(memory_space=pltpu.SMEM)
ANY = pl.BlockSpec(memory_space=pl.ANY)


def exchange(x, axis, k):
    if k == 0:
        return x
    return lax.ppermute(x, axis, [(i, i ^ k) for i in range(lax.axis_size(axis))])


def exchange_all(first, others, axis):
    n = lax.axis_size(axis)
    got = {0: first}
    for k in reversed(range(1, n)):
        got[k] = exchange(others[k - 1], axis, k)
    return [got[k] for k in range(n)]


def call(body, name, out_shape, in_specs, scratch=(), flops=0, moved=0, out_specs=None):
    return pl.pallas_call(
        body,
        out_shape=out_shape,
        in_specs=in_specs,
        out_specs=out_specs or [VMEM] * len(out_shape),
        scratch_shapes=list(scratch),
        compiler_params=pltpu.CompilerParams(vmem_limit_bytes=16 * 2**20),
        cost_estimate=pl.CostEstimate(flops=flops, bytes_accessed=moved, transcendentals=0),
        name=name,
    )


def in_hbm(*arrays):
    return [pltpu.with_memory_space_constraint(x, pltpu.HBM) for x in arrays]


def pack_body(pan_own, charge, needs, message, wide):
    width = charge.shape[1] // pan_own
    for q in range(pan_own):
        message[q] = charge[:, q * width : (q + 1) * width]
    wide[...] = jnp.zeros_like(wide)
    wide[: needs.shape[0], : needs.shape[1]] = needs[...]
    message[pan_own] = wide[...].astype(F32).astype(BF16)


def join_body(pan_own, own, *refs):
    others, message = refs[:-1], refs[-1]
    c = lax.axis_index("col")
    width = own.shape[2]
    message[pl.ds(c * pan_own, pan_own)] = own[pl.ds(0, pan_own)]
    for j, x in enumerate(others):
        first = lax.bitwise_xor(c, j + 1) * pan_own
        for q in range(pan_own):
            message[first + q] = x[:, q * width : (q + 1) * width]
    message[message.shape[0] - 1] = own[pan_own]


def ends_body(n_row, n_col, pan_own, cap, n_moved, *refs):
    sources, targets = refs[: n_moved + 2], refs[n_moved + 2 : 2 * n_moved + 2]
    (holder, lanes, blocks, own, *sends), (cur, off, acc, sems) = refs[2 * n_moved + 2 : -4], refs[-4:]
    copies = [
        pltpu.make_async_copy(source, target, sems.at[i])
        for i, (source, target) in enumerate(zip(sources, (cur, off, *targets)))
    ]
    for copy in copies:
        copy.start()
    slots, links = targets[:2]
    seg_own, _, width = blocks.shape
    pan_group = pan_own * n_col
    r, c = lax.axis_index("row"), lax.axis_index("col")
    acc[...] = jnp.zeros_like(acc)
    levels = lax.broadcasted_iota(jnp.int32, (width, width), 0)
    for copy in copies[:4]:
        copy.wait()

    def block(k):
        span = pl.ds(pl.multiple_of(k * width, width), width)
        for e in range(2):
            lanes[pl.ds(2 * k + e, 1), :] = off[e : e + 1, span]
        to_hot = jnp.where(levels == off[0:1, span], 1.0, 0.0).astype(BF16)
        from_hot = jnp.where(levels == off[1:2, span], -1.0, 0.0).astype(BF16)
        hot = jnp.concatenate([to_hot, from_hot], axis=0)
        value = cur[:, span]
        blocks[k] = value
        sums = lax.dot_general(value, hot, (((1,), (1,)), ((), ())), preferred_element_type=F32)
        return sums.astype(BF16).astype(F32)

    unroll = 16

    def step(i, carry):
        got = [block(i * unroll + u) for u in range(unroll)]
        for u in range(unroll):
            for e in range(2):
                slot = slots[e, i * unroll + u]
                holder[slot] = 2 * (i * unroll + u) + e
                p = lax.div(slot, cap)
                b = links[p, slot - p * cap]
                acc[lax.bitwise_xor(p, r) * pan_group + b] += got[u][:, e * width : (e + 1) * width]
        return carry

    lax.fori_loop(0, seg_own // unroll, step, 0)
    for k in range(n_row):
        here = pl.ds(k * pan_own, pan_own)
        own[here] = acc[pl.ds(k * pan_group + c * pan_own, pan_own)]
        for j in range(1, n_col):
            there = lax.bitwise_xor(c, j)
            sends[j - 1][here] = acc[pl.ds(k * pan_group + there * pan_own, pan_own)].astype(BF16)
    for copy in copies[4:]:
        copy.wait()


def pick_body(n_row, n_col, cap, _after, *refs):
    packs, own, peers = refs[:n_row][::-1], refs[n_row], refs[n_row + 1 : n_row + n_col]
    outs, asked = refs[n_row + n_col : -1], refs[-1]
    seg_own, rhs, width = own.shape
    r, c = lax.axis_index("row"), lax.axis_index("col")
    mine = lax.broadcasted_iota(jnp.int32, (rhs, width), 0) == r
    for k in range(n_row):
        needs = packs[k][packs[k].shape[0] - 1].astype(F32)
        asked[k : k + 1, :] = jnp.sum(jnp.where(mine, needs, 0.0), axis=0, keepdims=True).astype(jnp.int32)
    for k in range(n_row):
        for s in range(cap):
            b = asked[k, s]
            holder = lax.div(b, seg_own)
            b = b - holder * seg_own
            j = lax.bitwise_xor(holder, c)
            value = own[b]
            span = pl.ds(pl.multiple_of(b * width, width), width)
            for q, peer in enumerate(peers):
                value = jnp.where(j == q + 1, peer[:, span], value)
            outs[n_row - 1 - k][s] = value


def multiply(tiles, src, source, rows, acc):
    rhs, width = src.shape[1:]
    unroll = min(32, tiles.shape[0])

    def step(i, carry):
        start = i * unroll
        got = []
        for u in range(0, unroll, 2):
            t = start + u
            left = jnp.concatenate([src[source(t)], src[source(t + 1)]], axis=0)
            right = jnp.concatenate([tiles[t], tiles[t + 1]], axis=1)
            both = jnp.dot(left, right, preferred_element_type=F32)
            got += [both[:rhs, :width], both[rhs:, width:]]
        for u, value in enumerate(got):
            acc[rows[start + u]] += value
        return carry

    lax.fori_loop(0, tiles.shape[0] // unroll, step, 0)


def coeff_body(n_row, n_col, pan_own, slots, rows, needs, *refs):
    packs = refs[:n_row][::-1]
    ends = refs[n_row : n_row + n_col - 1]
    tiles, part, *messages = refs[n_row + n_col - 1 : -2]
    src, named = refs[-2:]
    r = lax.axis_index("row")
    pan_group = pan_own * n_col
    cap = needs.shape[1]
    for k in range(n_row):
        src[pl.ds(lax.bitwise_xor(r, k) * pan_group, pan_group)] = packs[k][pl.ds(0, pan_group)]
    for p in range(n_row):
        for s in range(cap):
            named[p * cap + s] = p * pan_group + needs[p, s]
    part[...] = jnp.zeros_like(part)
    multiply(tiles, src, lambda t: named[slots[t]], rows, part)
    high = part[...].astype(BF16)
    low = (part[...] - high.astype(F32)).astype(BF16)
    for message, sums in zip(messages, ends):
        message[pl.ds(0, pan_group)] = high
        message[pl.ds(pan_group, pan_group)] = low
        message[pl.ds(2 * pan_group, sums.shape[0])] = sums[...]


def induct_body(n_row, n_col, seg_own, order, slots, rows, _after, *refs):
    got = {k: refs[i] for i, k in enumerate(order)}
    tiles = refs[n_row]
    own, *sends = refs[n_row + 1 : -2]
    src, acc = refs[-2:]
    cap = got[0].shape[0]
    r, c = lax.axis_index("row"), lax.axis_index("col")
    for k in range(n_row):
        src[pl.ds(lax.bitwise_xor(r, k) * cap, cap)] = got[k][...]
    acc[...] = jnp.zeros_like(acc)
    multiply(tiles, src, lambda t: slots[t], rows, acc)
    own[...] = acc[pl.ds(c * seg_own, seg_own)]
    for j in range(1, n_col):
        sends[j - 1][...] = acc[pl.ds(lax.bitwise_xor(c, j) * seg_own, seg_own)].astype(BF16)


def panels_body(n_row, n_col, pan_own, part, ends_own, *refs):
    parts = refs[: n_col - 1]
    pot, end_keep, *messages = refs[n_col - 1 :]
    pan_group = part.shape[0]
    total = part[...]
    for x in parts:
        total += x[pl.ds(0, pan_group)].astype(F32) + x[pl.ds(pan_group, pan_group)].astype(F32)
    rounded = total.astype(BF16)
    pot[...] = rounded
    for k in range(n_row):
        sums = ends_own[pl.ds(k * pan_own, pan_own)]
        for x in parts:
            sums += x[pl.ds(2 * pan_group + k * pan_own, pan_own)].astype(F32)
        if k == 0:
            end_keep[...] = sums
        else:
            messages[n_row - 1 - k][pl.ds(0, pan_own)] = sums.astype(BF16)
            messages[n_row - 1 - k][pl.ds(pan_own, pan_group)] = rounded


def hold_body(_after, message, out):
    out[...] = message[...]


def add_drops(p, pots, first, links, holder, lanes, field):
    cap = links.shape[1]
    ends, drops = [], []
    for s in range(cap):
        j = holder[p * cap + s]
        values = pots[first + links[p, s]].astype(F32)
        at = jnp.broadcast_to(lanes[pl.ds(j, 1), :], values.shape)
        drop = jnp.take_along_axis(values, at, axis=1, mode="promise_in_bounds")
        k = lax.div(j, 2)
        drops.append(drop * (1 - 2 * (j - 2 * k)).astype(F32))
        ends.append(k)
    for k, drop in zip(ends, drops):
        field[k] += drop


def base_body(pan_own, links, holder, scale, lanes, pack, field_own, end_own, pot, field, panels, pot_out):
    rhs, width = pot.shape[1:]
    r, c = lax.axis_index("row"), lax.axis_index("col")
    field[...] = field_own[...]
    row = lax.broadcasted_iota(jnp.int32, (rhs, width), 0)
    factor = jnp.zeros((rhs, width), F32)
    for i in range(rhs):
        factor = jnp.where(row == i, scale[i], factor)
    for q in range(pan_own):
        panels[q] = factor * pack[c * pan_own + q].astype(F32) + end_own[q]
        pot_out[:, q * width : (q + 1) * width] = pot[c * pan_own + q]
    add_drops(r, pot, 0, links, holder, lanes, field)


def drops_body(k, pan_own, links, holder, lanes, message, field_in, field):
    field[...] = field_in[...]
    p = lax.bitwise_xor(lax.axis_index("row"), k)
    add_drops(p, message, pan_own, links, holder, lanes, field)


def final_body(n_row, n_col, pan_own, links, holder, lanes, field_own, panels, *refs):
    arrived, field_in = refs[: n_row - 1], refs[n_row - 1 : n_row + n_col - 2]
    seg_out, pan_out, field, seg, pan, sems = refs[n_row + n_col - 2 :]
    seg_own, _, width = field.shape
    total = field_own[...]
    for x in field_in:
        total += x[...].astype(F32)
    field[...] = total
    p = lax.bitwise_xor(lax.axis_index("row"), 1)
    add_drops(p, arrived[0], pan_own, links, holder, lanes, field)
    for q in range(pan_own):
        total = panels[q]
        for x in arrived:
            total += x[q].astype(F32)
        pan[:, q * width : (q + 1) * width] = total.astype(BF16)
    chunks = sems.shape[0] - 1
    copies = [pltpu.make_async_copy(pan, pan_out, sems.at[chunks])]
    copies[0].start()
    size = seg_own // chunks
    for i in range(chunks):
        for k in range(i * size, (i + 1) * size):
            seg[:, k * width : (k + 1) * width] = field[k].astype(BF16)
        part = pl.ds(i * size * width, size * width)
        copies.append(pltpu.make_async_copy(seg.at[:, part], seg_out.at[:, part], sems.at[i]))
        copies[-1].start()
    for copy in copies:
        copy.wait()


def shards(
    current,
    charge,
    rhs_scale,
    induct_tiles,
    induct_rows,
    induct_slots,
    induct_needs,
    coeff_tiles,
    coeff_rows,
    coeff_slots,
    coeff_needs,
    link_needs,
    end_slots,
    end_offsets,
):
    n_row = lax.axis_size("row")
    n_col = lax.axis_size("col")
    width = induct_tiles.shape[1]
    rhs = current.shape[0]
    seg_own = current.shape[1] // width
    pan_own = charge.shape[1] // width
    seg_group, pan_group = seg_own * n_col, pan_own * n_col
    cap_l, cap_p, cap_k = induct_needs.shape[1], coeff_needs.shape[1], link_needs.shape[1]
    slots_t, off_t = end_slots.T, end_offsets.T

    def like(blocks, dtype):
        return jax.ShapeDtypeStruct((blocks, rhs, width), dtype)

    charges = exchange_all(charge, [charge] * (n_col - 1), "col")
    cur = exchange_all(current, [current] * (n_col - 1), "col")
    (pack,) = call(
        functools.partial(pack_body, pan_own),
        "pack_charges",
        [like(pan_own + 1, BF16)],
        [VMEM] * 2,
        [pltpu.VMEM((rhs, width), jnp.int32)],
        moved=2**16,
    )(*in_hbm(charge, induct_needs))
    (pack,) = call(
        functools.partial(join_body, pan_own),
        "join_charges",
        [like(pan_group + 1, BF16)],
        [VMEM] * n_col,
        moved=2**16,
    )(pack, *charges[1:])
    packs = exchange_all(pack, [pack] * (n_row - 1), "row")

    rows_own = n_row * pan_own
    scalars = [slots_t, link_needs, coeff_slots, coeff_rows, coeff_needs, induct_slots, induct_rows, rhs_scale]
    moved = [*scalars, coeff_tiles]
    outs = call(
        functools.partial(ends_body, n_row, n_col, pan_own, cap_k, len(moved)),
        "end_sums",
        [pltpu.SMEM(x.shape, x.dtype) for x in scalars]
        + [jax.ShapeDtypeStruct(coeff_tiles.shape, BF16)]
        + [pltpu.SMEM((2 * seg_own,), jnp.int32), jax.ShapeDtypeStruct((2 * seg_own, width), jnp.int32)]
        + [like(seg_own, BF16), like(rows_own, F32)]
        + [like(rows_own, BF16)] * (n_col - 1),
        [ANY] * (len(moved) + 2),
        [
            pltpu.VMEM(current.shape, BF16),
            pltpu.VMEM(off_t.shape, jnp.int32),
            pltpu.VMEM((n_row * pan_group, rhs, width), F32),
            pltpu.SemaphoreType.DMA((len(moved) + 2,)),
        ],
        flops=5 * 10**8,
        moved=2**18,
        out_specs=[SMEM] * len(scalars) + [VMEM, SMEM] + [VMEM] * (2 + n_col),
    )(*in_hbm(current, off_t, *moved))
    _, links_s, coeff_slots, coeff_rows, coeff_needs, induct_slots, induct_rows, scale, coeff_tiles = outs[: len(moved)]
    holder, lanes, own_blocks, ends_own, *ends_out = outs[len(moved) :]

    part, *messages = call(
        functools.partial(coeff_body, n_row, n_col, pan_own),
        "coeff_tiles",
        [like(pan_group, F32)] + [like(2 * pan_group + rows_own, BF16)] * (n_col - 1),
        [SMEM] * 3 + [VMEM] * (n_row + n_col),
        [
            pltpu.VMEM((n_row * pan_group, rhs, width), BF16),
            pltpu.SMEM((n_row * cap_p,), jnp.int32),
        ],
        flops=10**9,
        moved=coeff_tiles.size * 2,
    )(coeff_slots, coeff_rows, coeff_needs, *packs[::-1], *ends_out, coeff_tiles)
    parts = exchange_all(None, messages, "col")[1:]

    *picks, own_picks = call(
        functools.partial(pick_body, n_row, n_col, cap_l),
        "pick_blocks",
        [like(cap_l, BF16)] * n_row,
        [ANY] + [VMEM] * (n_row + n_col),
        [pltpu.VMEM((n_row, width), jnp.int32)],
        moved=2**18,
    )(part, *packs[::-1], own_blocks, *cur[1:])
    got = exchange_all(own_picks, picks[::-1], "row")

    pot, end_keep, *row_messages = call(
        functools.partial(panels_body, n_row, n_col, pan_own),
        "panel_sums",
        [like(pan_group, BF16), like(pan_own, F32)] + [like(pan_own + pan_group, BF16)] * (n_row - 1),
        [VMEM] * (1 + n_col),
        flops=10**9,
        moved=2**18,
    )(part, ends_own, *parts)

    order = [*range(n_row - 2, -1, -1), n_row - 1]
    field_own, *field_out = call(
        functools.partial(induct_body, n_row, n_col, seg_own, order),
        "induct_tiles",
        [like(seg_own, F32)] + [like(seg_own, BF16)] * (n_col - 1),
        [SMEM, SMEM, ANY] + [VMEM] * (n_row + 1),
        [
            pltpu.VMEM((n_row * cap_l, rhs, width), BF16),
            pltpu.VMEM((seg_group, rhs, width), F32),
        ],
        flops=10**8,
        moved=2**16,
    )(induct_slots, induct_rows, pot, *[got[k] for k in order], induct_tiles)
    field_in = exchange_all(None, field_out, "col")[1:]

    (row_messages[-1],) = call(
        hold_body,
        "hold_near",
        [like(pan_own + pan_group, BF16)],
        [ANY, VMEM],
        moved=2**16,
    )(field_own, row_messages[-1])
    arrived = exchange_all(None, row_messages[::-1], "row")[1:]

    field, panels, pot_out = call(
        functools.partial(base_body, pan_own),
        "base_sums",
        [like(seg_own, F32), like(pan_own, F32), jax.ShapeDtypeStruct(charge.shape, BF16)],
        [SMEM] * 3 + [VMEM] * 5,
        flops=0,
        moved=0,
    )(links_s, holder, scale, lanes, pack, field_own, end_keep, pot)

    for k in reversed(range(2, n_row)):
        (field,) = call(
            functools.partial(drops_body, k, pan_own),
            "add_drops",
            [like(seg_own, F32)],
            [SMEM] * 2 + [VMEM] * 3,
            flops=11 * 10**8 if k == 2 else 0,
            moved=0,
        )(links_s, holder, lanes, arrived[k - 1], field)

    seg_out, pan_out = call(
        functools.partial(final_body, n_row, n_col, pan_own),
        "outputs",
        [jax.ShapeDtypeStruct(x.shape, BF16) for x in (current, charge)],
        [SMEM] * 2 + [VMEM] * (1 + n_row + n_col),
        [
            pltpu.VMEM((seg_own, rhs, width), F32),
            pltpu.VMEM(current.shape, BF16),
            pltpu.VMEM(charge.shape, BF16),
            pltpu.SemaphoreType.DMA((3,)),
        ],
        flops=10**9,
        moved=2**20,
        out_specs=[ANY, ANY],
    )(links_s, holder, lanes, field, panels, *arrived, *field_in)
    return (seg_out, pan_out, pot_out)


def solution(mesh):
    blocks = P(("parts", "row", "col"))
    matrix = P(("parts", "row", "col"), None)
    tiles = P(("parts", "row", "col"), None, None)
    values = P("rhs", ("parts", "row", "col"))
    return jax.shard_map(
        shards,
        mesh=mesh,
        in_specs=(
            values,
            values,
            P(("parts", "rhs")),
            tiles,
            blocks,
            blocks,
            matrix,
            tiles,
            blocks,
            blocks,
            matrix,
            matrix,
            matrix,
            matrix,
        ),
        out_specs=(values, values, values),
        check_vma=False,
    )
```

```python
import functools

import jax
import jax.numpy as jnp
from jax import lax
from jax.experimental import pallas as pl
from jax.experimental.pallas import tpu as pltpu
from jax.sharding import PartitionSpec as P

F32 = jnp.float32
BF16 = jnp.bfloat16
VMEM = pl.BlockSpec(memory_space=pltpu.VMEM)
SMEM = pl.BlockSpec(memory_space=pltpu.SMEM)
ANY = pl.BlockSpec(memory_space=pl.ANY)


def exchange(x, axis, k):
    if k == 0:
        return x
    return lax.ppermute(x, axis, [(i, i ^ k) for i in range(lax.axis_size(axis))])


def exchange_all(first, others, axis):
    n = lax.axis_size(axis)
    got = {0: first}
    for k in reversed(range(1, n)):
        got[k] = exchange(others[k - 1], axis, k)
    return [got[k] for k in range(n)]


def call(body, name, out_shape, in_specs, scratch=(), flops=0, moved=0, out_specs=None):
    return pl.pallas_call(
        body,
        out_shape=out_shape,
        in_specs=in_specs,
        out_specs=out_specs or [VMEM] * len(out_shape),
        scratch_shapes=list(scratch),
        compiler_params=pltpu.CompilerParams(vmem_limit_bytes=16 * 2**20),
        cost_estimate=pl.CostEstimate(flops=flops, bytes_accessed=moved, transcendentals=0),
        name=name,
    )


def in_hbm(*arrays):
    return [pltpu.with_memory_space_constraint(x, pltpu.HBM) for x in arrays]


def pack_body(pan_own, charge, needs, message, wide):
    width = charge.shape[1] // pan_own
    for q in range(pan_own):
        message[q] = charge[:, q * width : (q + 1) * width]
    wide[...] = jnp.zeros_like(wide)
    wide[: needs.shape[0], : needs.shape[1]] = needs[...]
    message[pan_own] = wide[...].astype(F32).astype(BF16)


def ends_body(n_row, n_col, pan_own, cap, n_moved, *refs):
    sources, targets = refs[: n_moved + 2], refs[n_moved + 2 : 2 * n_moved + 2]
    (holder, lanes, blocks, own, *sends), (cur, off, acc, sems) = refs[2 * n_moved + 2 : -4], refs[-4:]
    copies = [
        pltpu.make_async_copy(source, target, sems.at[i])
        for i, (source, target) in enumerate(zip(sources, (cur, off, *targets)))
    ]
    for copy in copies:
        copy.start()
    slots, links = targets[:2]
    seg_own, _, width = blocks.shape
    pan_group = pan_own * n_col
    r, c = lax.axis_index("row"), lax.axis_index("col")
    acc[...] = jnp.zeros_like(acc)
    levels = lax.broadcasted_iota(jnp.int32, (width, width), 0)
    for copy in copies[:4]:
        copy.wait()

    def block(k):
        span = pl.ds(pl.multiple_of(k * width, width), width)
        for e in range(2):
            lanes[pl.ds(2 * k + e, 1), :] = off[e : e + 1, span]
        to_hot = jnp.where(levels == off[0:1, span], 1.0, 0.0).astype(BF16)
        from_hot = jnp.where(levels == off[1:2, span], -1.0, 0.0).astype(BF16)
        hot = jnp.concatenate([to_hot, from_hot], axis=0)
        value = cur[:, span]
        blocks[k] = value
        sums = lax.dot_general(value, hot, (((1,), (1,)), ((), ())), preferred_element_type=F32)
        return sums.astype(BF16).astype(F32)

    unroll = 16

    def step(i, carry):
        got = [block(i * unroll + u) for u in range(unroll)]
        for u in range(unroll):
            for e in range(2):
                slot = slots[e, i * unroll + u]
                holder[slot] = 2 * (i * unroll + u) + e
                p = lax.div(slot, cap)
                b = links[p, slot - p * cap]
                acc[lax.bitwise_xor(p, r) * pan_group + b] += got[u][:, e * width : (e + 1) * width]
        return carry

    lax.fori_loop(0, seg_own // unroll, step, 0)
    for k in range(n_row):
        here = pl.ds(k * pan_own, pan_own)
        own[here] = acc[pl.ds(k * pan_group + c * pan_own, pan_own)]
        for j in range(1, n_col):
            there = lax.bitwise_xor(c, j)
            sends[j - 1][here] = acc[pl.ds(k * pan_group + there * pan_own, pan_own)].astype(BF16)
    for copy in copies[4:]:
        copy.wait()


def relay_body(n_row, n_col, pan_own, *refs):
    packs = refs[:n_row]
    ends = refs[n_row : n_row + n_col - 1]
    asked, *messages = refs[n_row + 2 * n_col - 2 :]
    r = lax.axis_index("row")
    rhs, width = packs[0].shape[1:]
    mine = lax.broadcasted_iota(jnp.int32, (rhs, width), 0) == r
    for k in range(n_row):
        needs = packs[k][pan_own].astype(F32)
        asked[k : k + 1, :] = jnp.sum(jnp.where(mine, needs, 0.0), axis=0, keepdims=True).astype(jnp.int32)
        for message in messages:
            message[pl.ds(k * pan_own, pan_own)] = packs[k][pl.ds(0, pan_own)]
    for message, sums in zip(messages, ends):
        message[pl.ds(n_row * pan_own, n_row * pan_own)] = sums[...]


def pick_body(n_row, n_col, cap, asked, own, *refs):
    peers, outs = refs[: n_col - 1], refs[n_col - 1 :]
    seg_own, _, width = own.shape
    c = lax.axis_index("col")
    for k in range(n_row):
        for s in range(cap):
            b = asked[k, s]
            holder = lax.div(b, seg_own)
            b = b - holder * seg_own
            j = lax.bitwise_xor(holder, c)
            value = own[b]
            span = pl.ds(pl.multiple_of(b * width, width), width)
            for q, peer in enumerate(peers):
                value = jnp.where(j == q + 1, peer[:, span], value)
            outs[n_row - 1 - k][s] = value


def multiply(tiles, src, source, rows, acc):
    rhs, width = src.shape[1:]
    count = tiles.shape[0]
    run = max(d for d in range(8, 97, 8) if count % d == 0)

    def products(start):
        got = []
        for t in (start, start + 2, start + 4, start + 6):
            left = jnp.concatenate([src[source(t)], src[source(t + 1)]], axis=0)
            right = jnp.concatenate([tiles[t], tiles[t + 1]], axis=1)
            both = jnp.dot(left, right, preferred_element_type=F32)
            got += [both[:rhs, :width], both[rhs:, width:]]
        return got

    def add(start, got):
        for u, value in enumerate(got):
            acc[rows[start + u]] += value

    def step(i, carry):
        start = i * run
        waiting = products(start)
        for first in range(8, run, 8):
            ahead = products(start + first)
            add(start + first - 8, waiting)
            waiting = ahead
        add(start + run - 8, waiting)
        return carry

    lax.fori_loop(0, count // run, step, 0)


def coeff_body(n_row, n_col, pan_own, slots, rows, needs, *refs):
    packs = refs[:n_row]
    from_col = refs[n_row : n_row + n_col - 1]
    tiles, part, message, src, named = refs[n_row + n_col - 1 :]
    r, c = lax.axis_index("row"), lax.axis_index("col")
    pan_group = pan_own * n_col
    cap = needs.shape[1]
    for k in range(n_row):
        first = lax.bitwise_xor(r, k) * pan_group
        src[pl.ds(first + c * pan_own, pan_own)] = packs[k][pl.ds(0, pan_own)]
        for j, x in enumerate(from_col):
            there = first + lax.bitwise_xor(c, j + 1) * pan_own
            src[pl.ds(there, pan_own)] = x[pl.ds(k * pan_own, pan_own)]
    for p in range(n_row):
        for s in range(cap):
            named[p * cap + s] = p * pan_group + needs[p, s]
    part[...] = jnp.zeros_like(part)
    multiply(tiles, src, lambda t: named[slots[t]], rows, part)
    high = part[...].astype(BF16)
    message[pl.ds(0, pan_group)] = high
    message[pl.ds(pan_group, pan_group)] = (part[...] - high.astype(F32)).astype(BF16)


def induct_body(n_row, n_col, seg_own, slots, rows, _after, *refs):
    got = refs[:n_row][::-1]
    tiles = refs[n_row]
    own, *sends = refs[n_row + 1 : -2]
    src, acc = refs[-2:]
    cap = got[0].shape[0]
    r, c = lax.axis_index("row"), lax.axis_index("col")
    for k in range(n_row):
        src[pl.ds(lax.bitwise_xor(r, k) * cap, cap)] = got[k][...]
    acc[...] = jnp.zeros_like(acc)
    multiply(tiles, src, lambda t: slots[t], rows, acc)
    own[...] = acc[pl.ds(c * seg_own, seg_own)]
    for j in range(1, n_col):
        sends[j - 1][...] = acc[pl.ds(lax.bitwise_xor(c, j) * seg_own, seg_own)].astype(BF16)


def panels_body(n_row, n_col, pan_own, part, ends_own, *refs):
    parts = refs[: n_col - 1]
    relayed = refs[n_col - 1 : 2 * n_col - 2]
    pot, end_keep, *messages = refs[2 * n_col - 2 :]
    pan_group = part.shape[0]
    total = part[...]
    for x in parts:
        total += x[pl.ds(0, pan_group)].astype(F32) + x[pl.ds(pan_group, pan_group)].astype(F32)
    rounded = total.astype(BF16)
    pot[...] = rounded
    for k in range(n_row):
        sums = ends_own[pl.ds(k * pan_own, pan_own)]
        for x in relayed:
            sums += x[pl.ds((n_row + k) * pan_own, pan_own)].astype(F32)
        if k == 0:
            end_keep[...] = sums
        else:
            messages[n_row - 1 - k][pl.ds(0, pan_own)] = sums.astype(BF16)
            messages[n_row - 1 - k][pl.ds(pan_own, pan_group)] = rounded


def add_drops(p, pots, first, links, holder, lanes, field):
    cap = links.shape[1]
    ends, drops = [], []
    for s in range(cap):
        j = holder[p * cap + s]
        values = pots[first + links[p, s]].astype(F32)
        at = jnp.broadcast_to(lanes[pl.ds(j, 1), :], values.shape)
        drop = jnp.take_along_axis(values, at, axis=1, mode="promise_in_bounds")
        k = lax.div(j, 2)
        drops.append(drop * (1 - 2 * (j - 2 * k)).astype(F32))
        ends.append(k)
    for k, drop in zip(ends, drops):
        field[k] += drop


def base_body(n_col, pan_own, links, holder, scale, lanes, pack, field_own, end_own, pot, *refs):
    field_in, (field, panels, pot_out) = refs[: n_col - 1], refs[n_col - 1 :]
    rhs, width = pot.shape[1:]
    r, c = lax.axis_index("row"), lax.axis_index("col")
    total = field_own[...]
    for x in field_in:
        total += x[...].astype(F32)
    field[...] = total
    row = lax.broadcasted_iota(jnp.int32, (rhs, width), 0)
    factor = jnp.zeros((rhs, width), F32)
    for i in range(rhs):
        factor = jnp.where(row == i, scale[i], factor)
    for q in range(pan_own):
        panels[q] = factor * pack[q].astype(F32) + end_own[q]
        pot_out[:, q * width : (q + 1) * width] = pot[c * pan_own + q]
    add_drops(r, pot, 0, links, holder, lanes, field)


def drops_body(k, pan_own, links, holder, lanes, message, field_in, field):
    field[...] = field_in[...]
    p = lax.bitwise_xor(lax.axis_index("row"), k)
    add_drops(p, message, pan_own, links, holder, lanes, field)


def final_body(n_row, pan_own, links, holder, lanes, field_in, panels, *refs):
    arrived, (seg_out, pan_out, field, seg, pan, sems) = refs[: n_row - 1], refs[n_row - 1 :]
    seg_own, _, width = field.shape
    field[...] = field_in[...]
    p = lax.bitwise_xor(lax.axis_index("row"), 1)
    add_drops(p, arrived[0], pan_own, links, holder, lanes, field)
    for q in range(pan_own):
        total = panels[q]
        for x in arrived:
            total += x[q].astype(F32)
        pan[:, q * width : (q + 1) * width] = total.astype(BF16)
    chunks = sems.shape[0] - 1
    copies = [pltpu.make_async_copy(pan, pan_out, sems.at[chunks])]
    copies[0].start()
    size = seg_own // chunks
    for i in range(chunks):
        for k in range(i * size, (i + 1) * size):
            seg[:, k * width : (k + 1) * width] = field[k].astype(BF16)
        part = pl.ds(i * size * width, size * width)
        copies.append(pltpu.make_async_copy(seg.at[:, part], seg_out.at[:, part], sems.at[i]))
        copies[-1].start()
    for copy in copies:
        copy.wait()


def shards(
    current,
    charge,
    rhs_scale,
    induct_tiles,
    induct_rows,
    induct_slots,
    induct_needs,
    coeff_tiles,
    coeff_rows,
    coeff_slots,
    coeff_needs,
    link_needs,
    end_slots,
    end_offsets,
):
    n_row = lax.axis_size("row")
    n_col = lax.axis_size("col")
    width = induct_tiles.shape[1]
    rhs = current.shape[0]
    seg_own = current.shape[1] // width
    pan_own = charge.shape[1] // width
    seg_group, pan_group = seg_own * n_col, pan_own * n_col
    cap_l, cap_p, cap_k = induct_needs.shape[1], coeff_needs.shape[1], link_needs.shape[1]
    slots_t, off_t = end_slots.T, end_offsets.T

    def like(blocks, dtype):
        return jax.ShapeDtypeStruct((blocks, rhs, width), dtype)

    cur = exchange_all(current, [current] * (n_col - 1), "col")
    (pack,) = call(
        functools.partial(pack_body, pan_own),
        "pack_charges",
        [like(pan_own + 1, BF16)],
        [VMEM] * 2,
        [pltpu.VMEM((rhs, width), jnp.int32)],
        moved=2**16,
    )(*in_hbm(charge, induct_needs))
    packs = exchange_all(pack, [pack] * (n_row - 1), "row")

    rows_own = n_row * pan_own
    scalars = [slots_t, link_needs, coeff_slots, coeff_rows, coeff_needs, induct_slots, induct_rows, rhs_scale]
    moved = [*scalars, coeff_tiles]
    outs = call(
        functools.partial(ends_body, n_row, n_col, pan_own, cap_k, len(moved)),
        "end_sums",
        [pltpu.SMEM(x.shape, x.dtype) for x in scalars]
        + [jax.ShapeDtypeStruct(coeff_tiles.shape, BF16)]
        + [pltpu.SMEM((2 * seg_own,), jnp.int32), jax.ShapeDtypeStruct((2 * seg_own, width), jnp.int32)]
        + [like(seg_own, BF16), like(rows_own, F32)]
        + [like(rows_own, BF16)] * (n_col - 1),
        [ANY] * (len(moved) + 2),
        [
            pltpu.VMEM(current.shape, BF16),
            pltpu.VMEM(off_t.shape, jnp.int32),
            pltpu.VMEM((n_row * pan_group, rhs, width), F32),
            pltpu.SemaphoreType.DMA((len(moved) + 2,)),
        ],
        flops=5 * 10**8,
        moved=2**18,
        out_specs=[SMEM] * len(scalars) + [VMEM, SMEM] + [VMEM] * (2 + n_col),
    )(*in_hbm(current, off_t, *moved))
    _, links_s, coeff_slots, coeff_rows, coeff_needs, induct_slots, induct_rows, scale, coeff_tiles = outs[: len(moved)]
    holder, lanes, own_blocks, ends_own, *ends_out = outs[len(moved) :]

    asked, *relays = call(
        functools.partial(relay_body, n_row, n_col, pan_own),
        "relay_charges",
        [jax.ShapeDtypeStruct((n_row, width), jnp.int32)] + [like(2 * rows_own, BF16)] * (n_col - 1),
        [VMEM] * (n_row + n_col - 1) + [ANY] * (n_col - 1),
        moved=2**16,
    )(*packs, *ends_out, *cur[1:])
    relayed = exchange_all(None, relays, "col")[1:]

    *picks, own_picks = call(
        functools.partial(pick_body, n_row, n_col, cap_l),
        "pick_blocks",
        [like(cap_l, BF16)] * n_row,
        [VMEM] * (1 + n_col),
        moved=2**18,
    )(asked, own_blocks, *cur[1:])
    got = exchange_all(own_picks, picks[::-1], "row")

    part, message = call(
        functools.partial(coeff_body, n_row, n_col, pan_own),
        "coeff_tiles",
        [like(pan_group, F32), like(2 * pan_group, BF16)],
        [SMEM] * 3 + [VMEM] * (n_row + n_col),
        [
            pltpu.VMEM((n_row * pan_group, rhs, width), BF16),
            pltpu.SMEM((n_row * cap_p,), jnp.int32),
        ],
        flops=2 * 10**9,
        moved=coeff_tiles.size * 2,
    )(coeff_slots, coeff_rows, coeff_needs, *packs, *relayed, coeff_tiles)
    parts = exchange_all(None, [message] * (n_col - 1), "col")[1:]

    field_own, *field_out = call(
        functools.partial(induct_body, n_row, n_col, seg_own),
        "induct_tiles",
        [like(seg_own, F32)] + [like(seg_own, BF16)] * (n_col - 1),
        [SMEM, SMEM, ANY] + [VMEM] * (n_row + 1),
        [
            pltpu.VMEM((n_row * cap_l, rhs, width), BF16),
            pltpu.VMEM((seg_group, rhs, width), F32),
        ],
        flops=4 * 10**9,
        moved=induct_tiles.size * 2,
    )(induct_slots, induct_rows, part, *got[::-1], induct_tiles)
    field_in = exchange_all(None, field_out, "col")[1:]

    pot, end_keep, *row_messages = call(
        functools.partial(panels_body, n_row, n_col, pan_own),
        "panel_sums",
        [like(pan_group, BF16), like(pan_own, F32)] + [like(pan_own + pan_group, BF16)] * (n_row - 1),
        [VMEM] * (2 * n_col),
        flops=5 * 10**9,
        moved=2**18,
    )(part, ends_own, *parts, *relayed)
    arrived = exchange_all(None, row_messages[::-1], "row")[1:]

    field, panels, pot_out = call(
        functools.partial(base_body, n_col, pan_own),
        "base_sums",
        [like(seg_own, F32), like(pan_own, F32), jax.ShapeDtypeStruct(charge.shape, BF16)],
        [SMEM] * 3 + [VMEM] * (4 + n_col),
        flops=10**9,
        moved=2**20,
    )(links_s, holder, scale, lanes, pack, field_own, end_keep, pot, *field_in)

    for k in reversed(range(2, n_row)):
        (field,) = call(
            functools.partial(drops_body, k, pan_own),
            "add_drops",
            [like(seg_own, F32)],
            [SMEM] * 2 + [VMEM] * 3,
            flops=10**8,
            moved=2**20,
        )(links_s, holder, lanes, arrived[k - 1], field)

    seg_out, pan_out = call(
        functools.partial(final_body, n_row, pan_own),
        "outputs",
        [jax.ShapeDtypeStruct(x.shape, BF16) for x in (current, charge)],
        [SMEM] * 2 + [VMEM] * (2 + n_row),
        [
            pltpu.VMEM((seg_own, rhs, width), F32),
            pltpu.VMEM(current.shape, BF16),
            pltpu.VMEM(charge.shape, BF16),
            pltpu.SemaphoreType.DMA((3,)),
        ],
        flops=10**9,
        moved=2**20,
        out_specs=[ANY, ANY],
    )(links_s, holder, lanes, field, panels, *arrived)
    return (seg_out, pan_out, pot_out)


def solution(mesh):
    blocks = P(("parts", "row", "col"))
    matrix = P(("parts", "row", "col"), None)
    tiles = P(("parts", "row", "col"), None, None)
    values = P("rhs", ("parts", "row", "col"))
    return jax.shard_map(
        shards,
        mesh=mesh,
        in_specs=(
            values,
            values,
            P(("parts", "rhs")),
            tiles,
            blocks,
            blocks,
            matrix,
            tiles,
            blocks,
            blocks,
            matrix,
            matrix,
            matrix,
            matrix,
        ),
        out_specs=(values, values, values),
        check_vma=False,
    )
```

```python
import functools

import jax
import jax.numpy as jnp
from jax import lax
from jax.experimental import pallas as pl
from jax.experimental.pallas import tpu as pltpu
from jax.sharding import PartitionSpec as P

F32 = jnp.float32
BF16 = jnp.bfloat16
VMEM = pl.BlockSpec(memory_space=pltpu.VMEM)
SMEM = pl.BlockSpec(memory_space=pltpu.SMEM)
ANY = pl.BlockSpec(memory_space=pl.ANY)


def exchange(x, axis, k):
    if k == 0:
        return x
    return lax.ppermute(x, axis, [(i, i ^ k) for i in range(lax.axis_size(axis))])


def exchange_all(first, others, axis):
    n = lax.axis_size(axis)
    got = {0: first}
    for k in reversed(range(1, n)):
        got[k] = exchange(others[k - 1], axis, k)
    return [got[k] for k in range(n)]


def call(body, name, out_shape, in_specs, scratch=(), flops=0, moved=0, out_specs=None):
    return pl.pallas_call(
        body,
        out_shape=out_shape,
        in_specs=in_specs,
        out_specs=out_specs or [VMEM] * len(out_shape),
        scratch_shapes=list(scratch),
        compiler_params=pltpu.CompilerParams(vmem_limit_bytes=16 * 2**20),
        cost_estimate=pl.CostEstimate(flops=flops, bytes_accessed=moved, transcendentals=0),
        name=name,
    )


def in_hbm(*arrays):
    return [pltpu.with_memory_space_constraint(x, pltpu.HBM) for x in arrays]


def pack_body(pan_own, charge, needs, message, wide):
    width = charge.shape[1] // pan_own
    for q in range(pan_own):
        message[q] = charge[:, q * width : (q + 1) * width]
    wide[...] = jnp.zeros_like(wide)
    wide[: needs.shape[0], : needs.shape[1]] = needs[...]
    message[pan_own] = wide[...].astype(F32).astype(BF16)


def join_body(pan_own, own, *refs):
    others, message = refs[:-1], refs[-1]
    c = lax.axis_index("col")
    width = own.shape[2]
    message[pl.ds(c * pan_own, pan_own)] = own[pl.ds(0, pan_own)]
    for j, x in enumerate(others):
        first = lax.bitwise_xor(c, j + 1) * pan_own
        for q in range(pan_own):
            message[first + q] = x[:, q * width : (q + 1) * width]
    message[message.shape[0] - 1] = own[pan_own]


def ends_body(n_row, n_col, pan_own, cap, n_moved, *refs):
    sources, targets = refs[: n_moved + 2], refs[n_moved + 2 : 2 * n_moved + 2]
    (holder, lanes, blocks, own, *sends), (cur, off, acc, sems) = refs[2 * n_moved + 2 : -4], refs[-4:]
    copies = [
        pltpu.make_async_copy(source, target, sems.at[i])
        for i, (source, target) in enumerate(zip(sources, (cur, off, *targets)))
    ]
    for copy in copies:
        copy.start()
    slots, links = targets[:2]
    seg_own, _, width = blocks.shape
    pan_group = pan_own * n_col
    r, c = lax.axis_index("row"), lax.axis_index("col")
    acc[...] = jnp.zeros_like(acc)
    levels = lax.broadcasted_iota(jnp.int32, (width, width), 0)
    for copy in copies[:4]:
        copy.wait()

    def block(k):
        span = pl.ds(pl.multiple_of(k * width, width), width)
        for e in range(2):
            lanes[pl.ds(2 * k + e, 1), :] = off[e : e + 1, span]
        to_hot = jnp.where(levels == off[0:1, span], 1.0, 0.0).astype(BF16)
        from_hot = jnp.where(levels == off[1:2, span], -1.0, 0.0).astype(BF16)
        hot = jnp.concatenate([to_hot, from_hot], axis=0)
        value = cur[:, span]
        blocks[k] = value
        sums = lax.dot_general(value, hot, (((1,), (1,)), ((), ())), preferred_element_type=F32)
        return sums.astype(BF16).astype(F32)

    unroll = 16

    def step(i, carry):
        got = [block(i * unroll + u) for u in range(unroll)]
        for u in range(unroll):
            for e in range(2):
                slot = slots[e, i * unroll + u]
                holder[slot] = 2 * (i * unroll + u) + e
                p = lax.div(slot, cap)
                b = links[p, slot - p * cap]
                acc[lax.bitwise_xor(p, r) * pan_group + b] += got[u][:, e * width : (e + 1) * width]
        return carry

    lax.fori_loop(0, seg_own // unroll, step, 0)
    for k in range(n_row):
        here = pl.ds(k * pan_own, pan_own)
        own[here] = acc[pl.ds(k * pan_group + c * pan_own, pan_own)]
        for j in range(1, n_col):
            there = lax.bitwise_xor(c, j)
            sends[j - 1][here] = acc[pl.ds(k * pan_group + there * pan_own, pan_own)].astype(BF16)
    for copy in copies[4:]:
        copy.wait()


def pick_body(n_row, n_col, cap, _after, *refs):
    packs, own, peers = refs[:n_row][::-1], refs[n_row], refs[n_row + 1 : n_row + n_col]
    outs, asked = refs[n_row + n_col : -1], refs[-1]
    seg_own, rhs, width = own.shape
    r, c = lax.axis_index("row"), lax.axis_index("col")
    mine = lax.broadcasted_iota(jnp.int32, (rhs, width), 0) == r
    for k in range(n_row):
        needs = packs[k][packs[k].shape[0] - 1].astype(F32)
        asked[k : k + 1, :] = jnp.sum(jnp.where(mine, needs, 0.0), axis=0, keepdims=True).astype(jnp.int32)
    for k in range(n_row):
        for s in range(cap):
            b = asked[k, s]
            holder = lax.div(b, seg_own)
            b = b - holder * seg_own
            j = lax.bitwise_xor(holder, c)
            value = own[b]
            span = pl.ds(pl.multiple_of(b * width, width), width)
            for q, peer in enumerate(peers):
                value = jnp.where(j == q + 1, peer[:, span], value)
            outs[n_row - 1 - k][s] = value


def multiply(tiles, src, source, rows, acc):
    rhs, width = src.shape[1:]
    count = tiles.shape[0]
    run = max(d for d in range(8, 97, 8) if count % d == 0)

    def products(start):
        got = []
        for t in (start, start + 2, start + 4, start + 6):
            left = jnp.concatenate([src[source(t)], src[source(t + 1)]], axis=0)
            right = jnp.concatenate([tiles[t], tiles[t + 1]], axis=1)
            both = jnp.dot(left, right, preferred_element_type=F32)
            got += [both[:rhs, :width], both[rhs:, width:]]
        return got

    def add(start, got):
        for u, value in enumerate(got):
            acc[rows[start + u]] += value

    def step(i, carry):
        start = i * run
        waiting = products(start)
        for first in range(8, run, 8):
            ahead = products(start + first)
            add(start + first - 8, waiting)
            waiting = ahead
        add(start + run - 8, waiting)
        return carry

    lax.fori_loop(0, count // run, step, 0)


def coeff_body(n_row, n_col, pan_own, slots, rows, needs, *refs):
    packs = refs[:n_row][::-1]
    ends = refs[n_row : n_row + n_col - 1]
    tiles, part, *messages = refs[n_row + n_col - 1 : -2]
    src, named = refs[-2:]
    r = lax.axis_index("row")
    pan_group = pan_own * n_col
    cap = needs.shape[1]
    for k in range(n_row):
        src[pl.ds(lax.bitwise_xor(r, k) * pan_group, pan_group)] = packs[k][pl.ds(0, pan_group)]
    for p in range(n_row):
        for s in range(cap):
            named[p * cap + s] = p * pan_group + needs[p, s]
    part[...] = jnp.zeros_like(part)
    multiply(tiles, src, lambda t: named[slots[t]], rows, part)
    high = part[...].astype(BF16)
    low = (part[...] - high.astype(F32)).astype(BF16)
    for message, sums in zip(messages, ends):
        message[pl.ds(0, pan_group)] = high
        message[pl.ds(pan_group, pan_group)] = low
        message[pl.ds(2 * pan_group, sums.shape[0])] = sums[...]


def induct_body(n_row, n_col, seg_own, order, slots, rows, _after, *refs):
    got = {k: refs[i] for i, k in enumerate(order)}
    tiles = refs[n_row]
    own, *sends = refs[n_row + 1 : -2]
    src, acc = refs[-2:]
    cap = got[0].shape[0]
    r, c = lax.axis_index("row"), lax.axis_index("col")
    for k in range(n_row):
        src[pl.ds(lax.bitwise_xor(r, k) * cap, cap)] = got[k][...]
    acc[...] = jnp.zeros_like(acc)
    multiply(tiles, src, lambda t: slots[t], rows, acc)
    own[...] = acc[pl.ds(c * seg_own, seg_own)]
    for j in range(1, n_col):
        sends[j - 1][...] = acc[pl.ds(lax.bitwise_xor(c, j) * seg_own, seg_own)].astype(BF16)


def panels_body(n_row, n_col, pan_own, part, ends_own, *refs):
    parts = refs[: n_col - 1]
    pot, end_keep, *messages = refs[n_col - 1 :]
    pan_group = part.shape[0]
    total = part[...]
    for x in parts:
        total += x[pl.ds(0, pan_group)].astype(F32) + x[pl.ds(pan_group, pan_group)].astype(F32)
    rounded = total.astype(BF16)
    pot[...] = rounded
    for k in range(n_row):
        sums = ends_own[pl.ds(k * pan_own, pan_own)]
        for x in parts:
            sums += x[pl.ds(2 * pan_group + k * pan_own, pan_own)].astype(F32)
        if k == 0:
            end_keep[...] = sums
        else:
            messages[n_row - 1 - k][pl.ds(0, pan_own)] = sums.astype(BF16)
            messages[n_row - 1 - k][pl.ds(pan_own, pan_group)] = rounded


def hold_body(_after, message, out):
    out[...] = message[...]


def add_drops(p, pots, first, links, holder, lanes, field):
    cap = links.shape[1]
    ends, drops = [], []
    for s in range(cap):
        j = holder[p * cap + s]
        values = pots[first + links[p, s]].astype(F32)
        at = jnp.broadcast_to(lanes[pl.ds(j, 1), :], values.shape)
        drop = jnp.take_along_axis(values, at, axis=1, mode="promise_in_bounds")
        k = lax.div(j, 2)
        drops.append(drop * (1 - 2 * (j - 2 * k)).astype(F32))
        ends.append(k)
    for k, drop in zip(ends, drops):
        field[k] += drop


def base_body(pan_own, links, holder, scale, lanes, pack, field_own, end_own, pot, field, panels, pot_out):
    rhs, width = pot.shape[1:]
    r, c = lax.axis_index("row"), lax.axis_index("col")
    field[...] = field_own[...]
    row = lax.broadcasted_iota(jnp.int32, (rhs, width), 0)
    factor = jnp.zeros((rhs, width), F32)
    for i in range(rhs):
        factor = jnp.where(row == i, scale[i], factor)
    for q in range(pan_own):
        panels[q] = factor * pack[c * pan_own + q].astype(F32) + end_own[q]
        pot_out[:, q * width : (q + 1) * width] = pot[c * pan_own + q]
    add_drops(r, pot, 0, links, holder, lanes, field)


def drops_body(k, pan_own, links, holder, lanes, message, field_in, field):
    field[...] = field_in[...]
    p = lax.bitwise_xor(lax.axis_index("row"), k)
    add_drops(p, message, pan_own, links, holder, lanes, field)


def final_body(n_row, n_col, pan_own, links, holder, lanes, field_own, panels, *refs):
    arrived, field_in = refs[: n_row - 1], refs[n_row - 1 : n_row + n_col - 2]
    seg_out, pan_out, field, seg, pan, sems = refs[n_row + n_col - 2 :]
    seg_own, _, width = field.shape
    total = field_own[...]
    for x in field_in:
        total += x[...].astype(F32)
    field[...] = total
    p = lax.bitwise_xor(lax.axis_index("row"), 1)
    add_drops(p, arrived[0], pan_own, links, holder, lanes, field)
    for q in range(pan_own):
        total = panels[q]
        for x in arrived:
            total += x[q].astype(F32)
        pan[:, q * width : (q + 1) * width] = total.astype(BF16)
    chunks = sems.shape[0] - 1
    copies = [pltpu.make_async_copy(pan, pan_out, sems.at[chunks])]
    copies[0].start()
    size = seg_own // chunks
    for i in range(chunks):
        for k in range(i * size, (i + 1) * size):
            seg[:, k * width : (k + 1) * width] = field[k].astype(BF16)
        part = pl.ds(i * size * width, size * width)
        copies.append(pltpu.make_async_copy(seg.at[:, part], seg_out.at[:, part], sems.at[i]))
        copies[-1].start()
    for copy in copies:
        copy.wait()


def shards(
    current,
    charge,
    rhs_scale,
    induct_tiles,
    induct_rows,
    induct_slots,
    induct_needs,
    coeff_tiles,
    coeff_rows,
    coeff_slots,
    coeff_needs,
    link_needs,
    end_slots,
    end_offsets,
):
    n_row = lax.axis_size("row")
    n_col = lax.axis_size("col")
    width = induct_tiles.shape[1]
    rhs = current.shape[0]
    seg_own = current.shape[1] // width
    pan_own = charge.shape[1] // width
    seg_group, pan_group = seg_own * n_col, pan_own * n_col
    cap_l, cap_p, cap_k = induct_needs.shape[1], coeff_needs.shape[1], link_needs.shape[1]
    slots_t, off_t = end_slots.T, end_offsets.T

    def like(blocks, dtype):
        return jax.ShapeDtypeStruct((blocks, rhs, width), dtype)

    charges = exchange_all(charge, [charge] * (n_col - 1), "col")
    cur = exchange_all(current, [current] * (n_col - 1), "col")
    (pack,) = call(
        functools.partial(pack_body, pan_own),
        "pack_charges",
        [like(pan_own + 1, BF16)],
        [VMEM] * 2,
        [pltpu.VMEM((rhs, width), jnp.int32)],
        moved=2**16,
    )(*in_hbm(charge, induct_needs))
    (pack,) = call(
        functools.partial(join_body, pan_own),
        "join_charges",
        [like(pan_group + 1, BF16)],
        [VMEM] * n_col,
        moved=2**16,
    )(pack, *charges[1:])
    packs = exchange_all(pack, [pack] * (n_row - 1), "row")

    rows_own = n_row * pan_own
    scalars = [slots_t, link_needs, coeff_slots, coeff_rows, coeff_needs, induct_slots, induct_rows, rhs_scale]
    moved = [*scalars, coeff_tiles]
    outs = call(
        functools.partial(ends_body, n_row, n_col, pan_own, cap_k, len(moved)),
        "end_sums",
        [pltpu.SMEM(x.shape, x.dtype) for x in scalars]
        + [jax.ShapeDtypeStruct(coeff_tiles.shape, BF16)]
        + [pltpu.SMEM((2 * seg_own,), jnp.int32), jax.ShapeDtypeStruct((2 * seg_own, width), jnp.int32)]
        + [like(seg_own, BF16), like(rows_own, F32)]
        + [like(rows_own, BF16)] * (n_col - 1),
        [ANY] * (len(moved) + 2),
        [
            pltpu.VMEM(current.shape, BF16),
            pltpu.VMEM(off_t.shape, jnp.int32),
            pltpu.VMEM((n_row * pan_group, rhs, width), F32),
            pltpu.SemaphoreType.DMA((len(moved) + 2,)),
        ],
        flops=5 * 10**8,
        moved=2**18,
        out_specs=[SMEM] * len(scalars) + [VMEM, SMEM] + [VMEM] * (2 + n_col),
    )(*in_hbm(current, off_t, *moved))
    _, links_s, coeff_slots, coeff_rows, coeff_needs, induct_slots, induct_rows, scale, coeff_tiles = outs[: len(moved)]
    holder, lanes, own_blocks, ends_own, *ends_out = outs[len(moved) :]

    part, *messages = call(
        functools.partial(coeff_body, n_row, n_col, pan_own),
        "coeff_tiles",
        [like(pan_group, F32)] + [like(2 * pan_group + rows_own, BF16)] * (n_col - 1),
        [SMEM] * 3 + [VMEM] * (n_row + n_col),
        [
            pltpu.VMEM((n_row * pan_group, rhs, width), BF16),
            pltpu.SMEM((n_row * cap_p,), jnp.int32),
        ],
        flops=10**9,
        moved=coeff_tiles.size * 2,
    )(coeff_slots, coeff_rows, coeff_needs, *packs[::-1], *ends_out, coeff_tiles)
    parts = exchange_all(None, messages, "col")[1:]

    *picks, own_picks = call(
        functools.partial(pick_body, n_row, n_col, cap_l),
        "pick_blocks",
        [like(cap_l, BF16)] * n_row,
        [ANY] + [VMEM] * (n_row + n_col),
        [pltpu.VMEM((n_row, width), jnp.int32)],
        moved=2**18,
    )(part, *packs[::-1], own_blocks, *cur[1:])
    got = exchange_all(own_picks, picks[::-1], "row")

    pot, end_keep, *row_messages = call(
        functools.partial(panels_body, n_row, n_col, pan_own),
        "panel_sums",
        [like(pan_group, BF16), like(pan_own, F32)] + [like(pan_own + pan_group, BF16)] * (n_row - 1),
        [VMEM] * (1 + n_col),
        flops=10**9,
        moved=2**18,
    )(part, ends_own, *parts)

    order = [*range(n_row - 2, -1, -1), n_row - 1]
    field_own, *field_out = call(
        functools.partial(induct_body, n_row, n_col, seg_own, order),
        "induct_tiles",
        [like(seg_own, F32)] + [like(seg_own, BF16)] * (n_col - 1),
        [SMEM, SMEM, ANY] + [VMEM] * (n_row + 1),
        [
            pltpu.VMEM((n_row * cap_l, rhs, width), BF16),
            pltpu.VMEM((seg_group, rhs, width), F32),
        ],
        flops=10**8,
        moved=2**16,
    )(induct_slots, induct_rows, pot, *[got[k] for k in order], induct_tiles)
    field_in = exchange_all(None, field_out, "col")[1:]

    (row_messages[-1],) = call(
        hold_body,
        "hold_near",
        [like(pan_own + pan_group, BF16)],
        [ANY, VMEM],
        moved=2**16,
    )(field_own, row_messages[-1])
    arrived = exchange_all(None, row_messages[::-1], "row")[1:]

    field, panels, pot_out = call(
        functools.partial(base_body, pan_own),
        "base_sums",
        [like(seg_own, F32), like(pan_own, F32), jax.ShapeDtypeStruct(charge.shape, BF16)],
        [SMEM] * 3 + [VMEM] * 5,
        flops=0,
        moved=0,
    )(links_s, holder, scale, lanes, pack, field_own, end_keep, pot)

    for k in reversed(range(2, n_row)):
        (field,) = call(
            functools.partial(drops_body, k, pan_own),
            "add_drops",
            [like(seg_own, F32)],
            [SMEM] * 2 + [VMEM] * 3,
            flops=11 * 10**8 if k == 2 else 0,
            moved=0,
        )(links_s, holder, lanes, arrived[k - 1], field)

    seg_out, pan_out = call(
        functools.partial(final_body, n_row, n_col, pan_own),
        "outputs",
        [jax.ShapeDtypeStruct(x.shape, BF16) for x in (current, charge)],
        [SMEM] * 2 + [VMEM] * (1 + n_row + n_col),
        [
            pltpu.VMEM((seg_own, rhs, width), F32),
            pltpu.VMEM(current.shape, BF16),
            pltpu.VMEM(charge.shape, BF16),
            pltpu.SemaphoreType.DMA((3,)),
        ],
        flops=10**9,
        moved=2**20,
        out_specs=[ANY, ANY],
    )(links_s, holder, lanes, field, panels, *arrived, *field_in)
    return (seg_out, pan_out, pot_out)


def solution(mesh):
    blocks = P(("parts", "row", "col"))
    matrix = P(("parts", "row", "col"), None)
    tiles = P(("parts", "row", "col"), None, None)
    values = P("rhs", ("parts", "row", "col"))
    return jax.shard_map(
        shards,
        mesh=mesh,
        in_specs=(
            values,
            values,
            P(("parts", "rhs")),
            tiles,
            blocks,
            blocks,
            matrix,
            tiles,
            blocks,
            blocks,
            matrix,
            matrix,
            matrix,
            matrix,
        ),
        out_specs=(values, values, values),
        check_vma=False,
    )
```

```python
import functools

import jax
import jax.numpy as jnp
from jax import lax
from jax.experimental import pallas as pl
from jax.experimental.pallas import tpu as pltpu
from jax.sharding import PartitionSpec as P

F32 = jnp.float32
BF16 = jnp.bfloat16
VMEM = pl.BlockSpec(memory_space=pltpu.VMEM)
SMEM = pl.BlockSpec(memory_space=pltpu.SMEM)
ANY = pl.BlockSpec(memory_space=pl.ANY)


def exchange(x, axis, k):
    if k == 0:
        return x
    return lax.ppermute(x, axis, [(i, i ^ k) for i in range(lax.axis_size(axis))])


def exchange_all(first, others, axis):
    n = lax.axis_size(axis)
    got = {0: first}
    for k in reversed(range(1, n)):
        got[k] = exchange(others[k - 1], axis, k)
    return [got[k] for k in range(n)]


def call(body, name, out_shape, in_specs, scratch=(), flops=0, moved=0, out_specs=None):
    return pl.pallas_call(
        body,
        out_shape=out_shape,
        in_specs=in_specs,
        out_specs=out_specs or [VMEM] * len(out_shape),
        scratch_shapes=list(scratch),
        compiler_params=pltpu.CompilerParams(vmem_limit_bytes=16 * 2**20),
        cost_estimate=pl.CostEstimate(flops=flops, bytes_accessed=moved, transcendentals=0),
        name=name,
    )


def in_hbm(*arrays):
    return [pltpu.with_memory_space_constraint(x, pltpu.HBM) for x in arrays]


def pack_body(pan_own, charge, needs, message, wide):
    width = charge.shape[1] // pan_own
    for q in range(pan_own):
        message[q] = charge[:, q * width : (q + 1) * width]
    wide[...] = jnp.zeros_like(wide)
    wide[: needs.shape[0], : needs.shape[1]] = needs[...]
    message[pan_own] = wide[...].astype(F32).astype(BF16)


def join_body(pan_own, own, *refs):
    others, message = refs[:-1], refs[-1]
    c = lax.axis_index("col")
    width = own.shape[2]
    message[pl.ds(c * pan_own, pan_own)] = own[pl.ds(0, pan_own)]
    for j, x in enumerate(others):
        first = lax.bitwise_xor(c, j + 1) * pan_own
        for q in range(pan_own):
            message[first + q] = x[:, q * width : (q + 1) * width]
    message[message.shape[0] - 1] = own[pan_own]


def ends_body(n_row, n_col, pan_own, cap, n_moved, *refs):
    sources, targets = refs[: n_moved + 2], refs[n_moved + 2 : 2 * n_moved + 2]
    (holder, lanes, blocks, own, *sends), (cur, off, acc, sems) = refs[2 * n_moved + 2 : -4], refs[-4:]
    copies = [
        pltpu.make_async_copy(source, target, sems.at[i])
        for i, (source, target) in enumerate(zip(sources, (cur, off, *targets)))
    ]
    for copy in copies:
        copy.start()
    slots, links = targets[:2]
    seg_own, _, width = blocks.shape
    pan_group = pan_own * n_col
    r, c = lax.axis_index("row"), lax.axis_index("col")
    acc[...] = jnp.zeros_like(acc)
    levels = lax.broadcasted_iota(jnp.int32, (width, width), 0)
    for copy in copies[:4]:
        copy.wait()

    def block(k):
        span = pl.ds(pl.multiple_of(k * width, width), width)
        for e in range(2):
            lanes[pl.ds(2 * k + e, 1), :] = off[e : e + 1, span]
        to_hot = jnp.where(levels == off[0:1, span], 1.0, 0.0).astype(BF16)
        from_hot = jnp.where(levels == off[1:2, span], -1.0, 0.0).astype(BF16)
        hot = jnp.concatenate([to_hot, from_hot], axis=0)
        value = cur[:, span]
        blocks[k] = value
        sums = lax.dot_general(value, hot, (((1,), (1,)), ((), ())), preferred_element_type=F32)
        return sums.astype(BF16).astype(F32)

    unroll = 16

    def step(i, carry):
        got = [block(i * unroll + u) for u in range(unroll)]
        for u in range(unroll):
            for e in range(2):
                slot = slots[e, i * unroll + u]
                holder[slot] = 2 * (i * unroll + u) + e
                p = lax.div(slot, cap)
                b = links[p, slot - p * cap]
                acc[lax.bitwise_xor(p, r) * pan_group + b] += got[u][:, e * width : (e + 1) * width]
        return carry

    lax.fori_loop(0, seg_own // unroll, step, 0)
    for k in range(n_row):
        here = pl.ds(k * pan_own, pan_own)
        own[here] = acc[pl.ds(k * pan_group + c * pan_own, pan_own)]
        for j in range(1, n_col):
            there = lax.bitwise_xor(c, j)
            sends[j - 1][here] = acc[pl.ds(k * pan_group + there * pan_own, pan_own)].astype(BF16)
    for copy in copies[4:]:
        copy.wait()


def pick_body(n_row, n_col, cap, _after, *refs):
    packs, own, peers = refs[:n_row][::-1], refs[n_row], refs[n_row + 1 : n_row + n_col]
    outs, asked = refs[n_row + n_col : -1], refs[-1]
    seg_own, rhs, width = own.shape
    r, c = lax.axis_index("row"), lax.axis_index("col")
    mine = lax.broadcasted_iota(jnp.int32, (rhs, width), 0) == r
    for k in range(n_row):
        needs = packs[k][packs[k].shape[0] - 1].astype(F32)
        asked[k : k + 1, :] = jnp.sum(jnp.where(mine, needs, 0.0), axis=0, keepdims=True).astype(jnp.int32)
    for k in range(n_row):
        for s in range(cap):
            b = asked[k, s]
            holder = lax.div(b, seg_own)
            b = b - holder * seg_own
            j = lax.bitwise_xor(holder, c)
            value = own[b]
            span = pl.ds(pl.multiple_of(b * width, width), width)
            for q, peer in enumerate(peers):
                value = jnp.where(j == q + 1, peer[:, span], value)
            outs[n_row - 1 - k][s] = value


def products(tiles, src, source, start, side):
    rhs, width = src.shape[1:]
    got = []
    none = jnp.zeros((side * rhs, width), BF16)
    for offset in range(0, 8, side * side):
        first = start + offset
        bands, lefts = [], []
        for i in range(side):
            row = [first + i * side + j for j in range(side)]
            bands.append(jnp.concatenate([tiles[t] for t in row], axis=1))
            own = jnp.concatenate([src[source(t)] for t in row], axis=0)
            lefts.append(jnp.concatenate([own if j == i else none for j in range(side)], axis=1))
        left, right = jnp.concatenate(lefts, axis=0), jnp.concatenate(bands, axis=0)
        whole = jnp.dot(left, right, preferred_element_type=F32)
        for i in range(side):
            for j in range(side):
                at = (i * side + j) * rhs
                got.append(whole[at : at + rhs, j * width : (j + 1) * width])
    return got


def multiply(tiles, src, source, rows, acc, side):
    count = tiles.shape[0]
    run = max(d for d in range(8, 97, 8) if count % d == 0)

    def add(start, got):
        for u, value in enumerate(got):
            acc[rows[start + u]] += value

    def step(i, carry):
        start = i * run
        waiting = products(tiles, src, source, start, side)
        for first in range(8, run, 8):
            ahead = products(tiles, src, source, start + first, side)
            add(start + first - 8, waiting)
            waiting = ahead
        add(start + run - 8, waiting)
        return carry

    lax.fori_loop(0, count // run, step, 0)


def coeff_body(n_row, n_col, pan_own, slots, rows, needs, *refs):
    packs = refs[:n_row][::-1]
    ends = refs[n_row : n_row + n_col - 1]
    tiles, part, *messages = refs[n_row + n_col - 1 : -2]
    src, named = refs[-2:]
    r = lax.axis_index("row")
    pan_group = pan_own * n_col
    cap = needs.shape[1]
    for k in range(n_row):
        src[pl.ds(lax.bitwise_xor(r, k) * pan_group, pan_group)] = packs[k][pl.ds(0, pan_group)]
    for p in range(n_row):
        for s in range(cap):
            named[p * cap + s] = p * pan_group + needs[p, s]
    part[...] = jnp.zeros_like(part)
    multiply(tiles, src, lambda t: named[slots[t]], rows, part, 1)
    high = part[...].astype(BF16)
    low = (part[...] - high.astype(F32)).astype(BF16)
    for message, sums in zip(messages, ends):
        message[pl.ds(0, pan_group)] = high
        message[pl.ds(pan_group, pan_group)] = low
        message[pl.ds(2 * pan_group, sums.shape[0])] = sums[...]


def induct_body(n_row, n_col, seg_own, order, slots, rows, _after, *refs):
    got = {k: refs[i] for i, k in enumerate(order)}
    tiles = refs[n_row]
    own, *sends = refs[n_row + 1 : -2]
    src, acc = refs[-2:]
    cap = got[0].shape[0]
    r, c = lax.axis_index("row"), lax.axis_index("col")
    for k in range(n_row):
        src[pl.ds(lax.bitwise_xor(r, k) * cap, cap)] = got[k][...]
    acc[...] = jnp.zeros_like(acc)
    multiply(tiles, src, lambda t: slots[t], rows, acc, 2)
    own[...] = acc[pl.ds(c * seg_own, seg_own)]
    for j in range(1, n_col):
        sends[j - 1][...] = acc[pl.ds(lax.bitwise_xor(c, j) * seg_own, seg_own)].astype(BF16)


def panels_body(n_row, n_col, pan_own, part, ends_own, *refs):
    parts = refs[: n_col - 1]
    pot, end_keep, *messages = refs[n_col - 1 :]
    pan_group = part.shape[0]
    total = part[...]
    for x in parts:
        total += x[pl.ds(0, pan_group)].astype(F32) + x[pl.ds(pan_group, pan_group)].astype(F32)
    rounded = total.astype(BF16)
    pot[...] = rounded
    for k in range(n_row):
        sums = ends_own[pl.ds(k * pan_own, pan_own)]
        for x in parts:
            sums += x[pl.ds(2 * pan_group + k * pan_own, pan_own)].astype(F32)
        if k == 0:
            end_keep[...] = sums
        else:
            messages[n_row - 1 - k][pl.ds(0, pan_own)] = sums.astype(BF16)
            messages[n_row - 1 - k][pl.ds(pan_own, pan_group)] = rounded


def hold_body(_after, message, out):
    out[...] = message[...]


def add_drops(p, pots, first, links, holder, lanes, field):
    cap = links.shape[1]
    ends, drops = [], []
    for s in range(cap):
        j = holder[p * cap + s]
        values = pots[first + links[p, s]].astype(F32)
        at = jnp.broadcast_to(lanes[pl.ds(j, 1), :], values.shape)
        drop = jnp.take_along_axis(values, at, axis=1, mode="promise_in_bounds")
        k = lax.div(j, 2)
        drops.append(drop * (1 - 2 * (j - 2 * k)).astype(F32))
        ends.append(k)
    for k, drop in zip(ends, drops):
        field[k] += drop


def base_body(pan_own, links, holder, scale, lanes, pack, field_own, end_own, pot, field, panels, pot_out):
    rhs, width = pot.shape[1:]
    r, c = lax.axis_index("row"), lax.axis_index("col")
    field[...] = field_own[...]
    row = lax.broadcasted_iota(jnp.int32, (rhs, width), 0)
    factor = jnp.zeros((rhs, width), F32)
    for i in range(rhs):
        factor = jnp.where(row == i, scale[i], factor)
    for q in range(pan_own):
        panels[q] = factor * pack[c * pan_own + q].astype(F32) + end_own[q]
        pot_out[:, q * width : (q + 1) * width] = pot[c * pan_own + q]
    add_drops(r, pot, 0, links, holder, lanes, field)


def drops_body(k, pan_own, links, holder, lanes, message, field_in, field):
    field[...] = field_in[...]
    p = lax.bitwise_xor(lax.axis_index("row"), k)
    add_drops(p, message, pan_own, links, holder, lanes, field)


def final_body(n_row, n_col, pan_own, links, holder, lanes, field_own, panels, *refs):
    arrived, field_in = refs[: n_row - 1], refs[n_row - 1 : n_row + n_col - 2]
    seg_out, pan_out, field, seg, pan, sems = refs[n_row + n_col - 2 :]
    seg_own, _, width = field.shape
    total = field_own[...]
    for x in field_in:
        total += x[...].astype(F32)
    field[...] = total
    p = lax.bitwise_xor(lax.axis_index("row"), 1)
    add_drops(p, arrived[0], pan_own, links, holder, lanes, field)
    for q in range(pan_own):
        total = panels[q]
        for x in arrived:
            total += x[q].astype(F32)
        pan[:, q * width : (q + 1) * width] = total.astype(BF16)
    chunks = sems.shape[0] - 1
    copies = [pltpu.make_async_copy(pan, pan_out, sems.at[chunks])]
    copies[0].start()
    size = seg_own // chunks
    for i in range(chunks):
        for k in range(i * size, (i + 1) * size):
            seg[:, k * width : (k + 1) * width] = field[k].astype(BF16)
        part = pl.ds(i * size * width, size * width)
        copies.append(pltpu.make_async_copy(seg.at[:, part], seg_out.at[:, part], sems.at[i]))
        copies[-1].start()
    for copy in copies:
        copy.wait()


def shards(
    current,
    charge,
    rhs_scale,
    induct_tiles,
    induct_rows,
    induct_slots,
    induct_needs,
    coeff_tiles,
    coeff_rows,
    coeff_slots,
    coeff_needs,
    link_needs,
    end_slots,
    end_offsets,
):
    n_row = lax.axis_size("row")
    n_col = lax.axis_size("col")
    width = induct_tiles.shape[1]
    rhs = current.shape[0]
    seg_own = current.shape[1] // width
    pan_own = charge.shape[1] // width
    seg_group, pan_group = seg_own * n_col, pan_own * n_col
    cap_l, cap_p, cap_k = induct_needs.shape[1], coeff_needs.shape[1], link_needs.shape[1]
    slots_t, off_t = end_slots.T, end_offsets.T

    def like(blocks, dtype):
        return jax.ShapeDtypeStruct((blocks, rhs, width), dtype)

    charges = exchange_all(charge, [charge] * (n_col - 1), "col")
    cur = exchange_all(current, [current] * (n_col - 1), "col")
    (pack,) = call(
        functools.partial(pack_body, pan_own),
        "pack_charges",
        [like(pan_own + 1, BF16)],
        [VMEM] * 2,
        [pltpu.VMEM((rhs, width), jnp.int32)],
        moved=2**16,
    )(*in_hbm(charge, induct_needs))
    (pack,) = call(
        functools.partial(join_body, pan_own),
        "join_charges",
        [like(pan_group + 1, BF16)],
        [VMEM] * n_col,
        moved=2**16,
    )(pack, *charges[1:])
    packs = exchange_all(pack, [pack] * (n_row - 1), "row")

    rows_own = n_row * pan_own
    scalars = [slots_t, link_needs, coeff_slots, coeff_rows, coeff_needs, induct_slots, induct_rows, rhs_scale]
    moved = [*scalars, coeff_tiles]
    outs = call(
        functools.partial(ends_body, n_row, n_col, pan_own, cap_k, len(moved)),
        "end_sums",
        [pltpu.SMEM(x.shape, x.dtype) for x in scalars]
        + [jax.ShapeDtypeStruct(coeff_tiles.shape, BF16)]
        + [pltpu.SMEM((2 * seg_own,), jnp.int32), jax.ShapeDtypeStruct((2 * seg_own, width), jnp.int32)]
        + [like(seg_own, BF16), like(rows_own, F32)]
        + [like(rows_own, BF16)] * (n_col - 1),
        [ANY] * (len(moved) + 2),
        [
            pltpu.VMEM(current.shape, BF16),
            pltpu.VMEM(off_t.shape, jnp.int32),
            pltpu.VMEM((n_row * pan_group, rhs, width), F32),
            pltpu.SemaphoreType.DMA((len(moved) + 2,)),
        ],
        flops=5 * 10**8,
        moved=2**18,
        out_specs=[SMEM] * len(scalars) + [VMEM, SMEM] + [VMEM] * (2 + n_col),
    )(*in_hbm(current, off_t, *moved))
    _, links_s, coeff_slots, coeff_rows, coeff_needs, induct_slots, induct_rows, scale, coeff_tiles = outs[: len(moved)]
    holder, lanes, own_blocks, ends_own, *ends_out = outs[len(moved) :]

    part, *messages = call(
        functools.partial(coeff_body, n_row, n_col, pan_own),
        "coeff_tiles",
        [like(pan_group, F32)] + [like(2 * pan_group + rows_own, BF16)] * (n_col - 1),
        [SMEM] * 3 + [VMEM] * (n_row + n_col),
        [
            pltpu.VMEM((n_row * pan_group, rhs, width), BF16),
            pltpu.SMEM((n_row * cap_p,), jnp.int32),
        ],
        flops=10**9,
        moved=coeff_tiles.size * 2,
    )(coeff_slots, coeff_rows, coeff_needs, *packs[::-1], *ends_out, coeff_tiles)
    parts = exchange_all(None, messages, "col")[1:]

    *picks, own_picks = call(
        functools.partial(pick_body, n_row, n_col, cap_l),
        "pick_blocks",
        [like(cap_l, BF16)] * n_row,
        [ANY] + [VMEM] * (n_row + n_col),
        [pltpu.VMEM((n_row, width), jnp.int32)],
        moved=2**18,
    )(part, *packs[::-1], own_blocks, *cur[1:])
    got = exchange_all(own_picks, picks[::-1], "row")

    pot, end_keep, *row_messages = call(
        functools.partial(panels_body, n_row, n_col, pan_own),
        "panel_sums",
        [like(pan_group, BF16), like(pan_own, F32)] + [like(pan_own + pan_group, BF16)] * (n_row - 1),
        [VMEM] * (1 + n_col),
        flops=10**9,
        moved=2**18,
    )(part, ends_own, *parts)

    order = [*range(n_row - 2, -1, -1), n_row - 1]
    field_own, *field_out = call(
        functools.partial(induct_body, n_row, n_col, seg_own, order),
        "induct_tiles",
        [like(seg_own, F32)] + [like(seg_own, BF16)] * (n_col - 1),
        [SMEM, SMEM, ANY] + [VMEM] * (n_row + 1),
        [
            pltpu.VMEM((n_row * cap_l, rhs, width), BF16),
            pltpu.VMEM((seg_group, rhs, width), F32),
        ],
        flops=10**8,
        moved=2**16,
    )(induct_slots, induct_rows, pot, *[got[k] for k in order], induct_tiles)
    field_in = exchange_all(None, field_out, "col")[1:]

    (row_messages[-1],) = call(
        hold_body,
        "hold_near",
        [like(pan_own + pan_group, BF16)],
        [ANY, VMEM],
        moved=2**16,
    )(field_own, row_messages[-1])
    arrived = exchange_all(None, row_messages[::-1], "row")[1:]

    field, panels, pot_out = call(
        functools.partial(base_body, pan_own),
        "base_sums",
        [like(seg_own, F32), like(pan_own, F32), jax.ShapeDtypeStruct(charge.shape, BF16)],
        [SMEM] * 3 + [VMEM] * 5,
        flops=0,
        moved=0,
    )(links_s, holder, scale, lanes, pack, field_own, end_keep, pot)

    for k in reversed(range(2, n_row)):
        (field,) = call(
            functools.partial(drops_body, k, pan_own),
            "add_drops",
            [like(seg_own, F32)],
            [SMEM] * 2 + [VMEM] * 3,
            flops=11 * 10**8 if k == 2 else 0,
            moved=0,
        )(links_s, holder, lanes, arrived[k - 1], field)

    seg_out, pan_out = call(
        functools.partial(final_body, n_row, n_col, pan_own),
        "outputs",
        [jax.ShapeDtypeStruct(x.shape, BF16) for x in (current, charge)],
        [SMEM] * 2 + [VMEM] * (1 + n_row + n_col),
        [
            pltpu.VMEM((seg_own, rhs, width), F32),
            pltpu.VMEM(current.shape, BF16),
            pltpu.VMEM(charge.shape, BF16),
            pltpu.SemaphoreType.DMA((3,)),
        ],
        flops=10**9,
        moved=2**20,
        out_specs=[ANY, ANY],
    )(links_s, holder, lanes, field, panels, *arrived, *field_in)
    return (seg_out, pan_out, pot_out)


def solution(mesh):
    blocks = P(("parts", "row", "col"))
    matrix = P(("parts", "row", "col"), None)
    tiles = P(("parts", "row", "col"), None, None)
    values = P("rhs", ("parts", "row", "col"))
    return jax.shard_map(
        shards,
        mesh=mesh,
        in_specs=(
            values,
            values,
            P(("parts", "rhs")),
            tiles,
            blocks,
            blocks,
            matrix,
            tiles,
            blocks,
            blocks,
            matrix,
            matrix,
            matrix,
            matrix,
        ),
        out_specs=(values, values, values),
        check_vma=False,
    )
```

```python
import functools

import jax
import jax.numpy as jnp
from jax import lax
from jax.experimental import pallas as pl
from jax.experimental.pallas import tpu as pltpu
from jax.sharding import PartitionSpec as P

F32 = jnp.float32
BF16 = jnp.bfloat16
VMEM = pl.BlockSpec(memory_space=pltpu.VMEM)
SMEM = pl.BlockSpec(memory_space=pltpu.SMEM)
ANY = pl.BlockSpec(memory_space=pl.ANY)


def exchange(x, axis, k):
    if k == 0:
        return x
    return lax.ppermute(x, axis, [(i, i ^ k) for i in range(lax.axis_size(axis))])


def exchange_all(first, others, axis):
    n = lax.axis_size(axis)
    got = {0: first}
    for k in reversed(range(1, n)):
        got[k] = exchange(others[k - 1], axis, k)
    return [got[k] for k in range(n)]


def call(body, name, out_shape, in_specs, scratch=(), flops=0, moved=0, out_specs=None):
    return pl.pallas_call(
        body,
        out_shape=out_shape,
        in_specs=in_specs,
        out_specs=out_specs or [VMEM] * len(out_shape),
        scratch_shapes=list(scratch),
        compiler_params=pltpu.CompilerParams(vmem_limit_bytes=16 * 2**20),
        cost_estimate=pl.CostEstimate(flops=flops, bytes_accessed=moved, transcendentals=0),
        name=name,
    )


def in_hbm(*arrays):
    return [pltpu.with_memory_space_constraint(x, pltpu.HBM) for x in arrays]


def pack_body(pan_own, charge, needs, message, wide):
    width = charge.shape[1] // pan_own
    for q in range(pan_own):
        message[q] = charge[:, q * width : (q + 1) * width]
    wide[...] = jnp.zeros_like(wide)
    wide[: needs.shape[0], : needs.shape[1]] = needs[...]
    message[pan_own] = wide[...].astype(F32).astype(BF16)


def join_body(pan_own, own, *refs):
    others, message = refs[:-1], refs[-1]
    c = lax.axis_index("col")
    width = own.shape[2]
    message[pl.ds(c * pan_own, pan_own)] = own[pl.ds(0, pan_own)]
    for j, x in enumerate(others):
        first = lax.bitwise_xor(c, j + 1) * pan_own
        for q in range(pan_own):
            message[first + q] = x[:, q * width : (q + 1) * width]
    message[message.shape[0] - 1] = own[pan_own]


def ends_body(n_row, n_col, pan_own, cap, n_moved, *refs):
    sources, targets = refs[: n_moved + 2], refs[n_moved + 2 : 2 * n_moved + 2]
    (holder, lanes, blocks, own, *sends), (cur, off, acc, sems) = refs[2 * n_moved + 2 : -4], refs[-4:]
    copies = [
        pltpu.make_async_copy(source, target, sems.at[i])
        for i, (source, target) in enumerate(zip(sources, (cur, off, *targets)))
    ]
    for copy in copies:
        copy.start()
    slots, links = targets[:2]
    seg_own, _, width = blocks.shape
    pan_group = pan_own * n_col
    r, c = lax.axis_index("row"), lax.axis_index("col")
    acc[...] = jnp.zeros_like(acc)
    levels = lax.broadcasted_iota(jnp.int32, (width, width), 0)
    for copy in copies[:4]:
        copy.wait()

    def block(k):
        span = pl.ds(pl.multiple_of(k * width, width), width)
        for e in range(2):
            lanes[pl.ds(2 * k + e, 1), :] = off[e : e + 1, span]
        to_hot = jnp.where(levels == off[0:1, span], 1.0, 0.0).astype(BF16)
        from_hot = jnp.where(levels == off[1:2, span], -1.0, 0.0).astype(BF16)
        hot = jnp.concatenate([to_hot, from_hot], axis=0)
        value = cur[:, span]
        blocks[k] = value
        sums = lax.dot_general(value, hot, (((1,), (1,)), ((), ())), preferred_element_type=F32)
        return sums.astype(BF16).astype(F32)

    unroll = 16

    def step(i, carry):
        got = [block(i * unroll + u) for u in range(unroll)]
        for u in range(unroll):
            for e in range(2):
                slot = slots[e, i * unroll + u]
                holder[slot] = 2 * (i * unroll + u) + e
                p = lax.div(slot, cap)
                b = links[p, slot - p * cap]
                acc[lax.bitwise_xor(p, r) * pan_group + b] += got[u][:, e * width : (e + 1) * width]
        return carry

    lax.fori_loop(0, seg_own // unroll, step, 0)
    for k in range(n_row):
        here = pl.ds(k * pan_own, pan_own)
        own[here] = acc[pl.ds(k * pan_group + c * pan_own, pan_own)]
        for j in range(1, n_col):
            there = lax.bitwise_xor(c, j)
            sends[j - 1][here] = acc[pl.ds(k * pan_group + there * pan_own, pan_own)].astype(BF16)
    for copy in copies[4:]:
        copy.wait()


def pick_body(n_row, n_col, cap, partners, _after, *refs):
    packs = {k: refs[i] for i, k in enumerate([*partners, 0])}
    own, peers = refs[n_row], refs[n_row + 1 : n_row + n_col]
    outs, asked = refs[n_row + n_col : -1], refs[-1]
    seg_own, rhs, width = own.shape
    r, c = lax.axis_index("row"), lax.axis_index("col")
    mine = lax.broadcasted_iota(jnp.int32, (rhs, width), 0) == r
    for k in range(n_row):
        needs = packs[k][packs[k].shape[0] - 1].astype(F32)
        asked[k : k + 1, :] = jnp.sum(jnp.where(mine, needs, 0.0), axis=0, keepdims=True).astype(jnp.int32)
    for k in range(n_row):
        for s in range(cap):
            b = asked[k, s]
            holder = lax.div(b, seg_own)
            b = b - holder * seg_own
            j = lax.bitwise_xor(holder, c)
            value = own[b]
            span = pl.ds(pl.multiple_of(b * width, width), width)
            for q, peer in enumerate(peers):
                value = jnp.where(j == q + 1, peer[:, span], value)
            outs[n_row - 1 - k][s] = value


def multiply(tiles, src, source, rows, acc):
    rhs, width = src.shape[1:]
    count = tiles.shape[0]
    run = max(d for d in range(8, 97, 8) if count % d == 0)

    def products(start):
        got = []
        for t in (start, start + 2, start + 4, start + 6):
            left = jnp.concatenate([src[source(t)], src[source(t + 1)]], axis=0)
            right = jnp.concatenate([tiles[t], tiles[t + 1]], axis=1)
            both = jnp.dot(left, right, preferred_element_type=F32)
            got += [both[:rhs, :width], both[rhs:, width:]]
        return got

    def add(start, got):
        for u, value in enumerate(got):
            acc[rows[start + u]] += value

    def step(i, carry):
        start = i * run
        waiting = products(start)
        for first in range(8, run, 8):
            ahead = products(start + first)
            add(start + first - 8, waiting)
            waiting = ahead
        add(start + run - 8, waiting)
        return carry

    lax.fori_loop(0, count // run, step, 0)


def coeff_body(n_row, n_col, pan_own, partners, slots, rows, needs, *refs):
    packs = {k: refs[i] for i, k in enumerate([*partners, 0])}
    ends = refs[n_row : n_row + n_col - 1]
    tiles, part, *messages = refs[n_row + n_col - 1 : -2]
    src, named = refs[-2:]
    r = lax.axis_index("row")
    pan_group = pan_own * n_col
    cap = needs.shape[1]
    for k in range(n_row):
        src[pl.ds(lax.bitwise_xor(r, k) * pan_group, pan_group)] = packs[k][pl.ds(0, pan_group)]
    for p in range(n_row):
        for s in range(cap):
            named[p * cap + s] = p * pan_group + needs[p, s]
    part[...] = jnp.zeros_like(part)
    multiply(tiles, src, lambda t: named[slots[t]], rows, part)
    high = part[...].astype(BF16)
    low = (part[...] - high.astype(F32)).astype(BF16)
    for message, sums in zip(messages, ends):
        message[pl.ds(0, pan_group)] = high
        message[pl.ds(pan_group, pan_group)] = low
        message[pl.ds(2 * pan_group, sums.shape[0])] = sums[...]


def induct_body(n_row, n_col, seg_own, order, slots, rows, _after, *refs):
    got = {k: refs[i] for i, k in enumerate(order)}
    tiles = refs[n_row]
    own, *sends = refs[n_row + 1 : -2]
    src, acc = refs[-2:]
    cap = got[0].shape[0]
    r, c = lax.axis_index("row"), lax.axis_index("col")
    for k in range(n_row):
        src[pl.ds(lax.bitwise_xor(r, k) * cap, cap)] = got[k][...]
    acc[...] = jnp.zeros_like(acc)
    multiply(tiles, src, lambda t: slots[t], rows, acc)
    own[...] = acc[pl.ds(c * seg_own, seg_own)]
    for j in range(1, n_col):
        sends[j - 1][...] = acc[pl.ds(lax.bitwise_xor(c, j) * seg_own, seg_own)].astype(BF16)


def panels_body(n_row, n_col, pan_own, part, ends_own, *refs):
    parts = refs[: n_col - 1]
    pot, end_keep, *messages = refs[n_col - 1 :]
    pan_group = part.shape[0]
    total = part[...]
    for x in parts:
        total += x[pl.ds(0, pan_group)].astype(F32) + x[pl.ds(pan_group, pan_group)].astype(F32)
    rounded = total.astype(BF16)
    pot[...] = rounded
    for k in range(n_row):
        sums = ends_own[pl.ds(k * pan_own, pan_own)]
        for x in parts:
            sums += x[pl.ds(2 * pan_group + k * pan_own, pan_own)].astype(F32)
        if k == 0:
            end_keep[...] = sums
        else:
            messages[n_row - 1 - k][pl.ds(0, pan_own)] = sums.astype(BF16)
            messages[n_row - 1 - k][pl.ds(pan_own, pan_group)] = rounded


def hold_body(_after, message, out):
    out[...] = message[...]


def add_drops(p, pots, first, links, holder, lanes, field):
    cap = links.shape[1]
    ends, drops = [], []
    for s in range(cap):
        j = holder[p * cap + s]
        values = pots[first + links[p, s]].astype(F32)
        at = jnp.broadcast_to(lanes[pl.ds(j, 1), :], values.shape)
        drop = jnp.take_along_axis(values, at, axis=1, mode="promise_in_bounds")
        k = lax.div(j, 2)
        drops.append(drop * (1 - 2 * (j - 2 * k)).astype(F32))
        ends.append(k)
    for k, drop in zip(ends, drops):
        field[k] += drop


def base_body(pan_own, links, holder, scale, lanes, pack, field_own, end_own, pot, field, panels, pot_out):
    rhs, width = pot.shape[1:]
    r, c = lax.axis_index("row"), lax.axis_index("col")
    field[...] = field_own[...]
    row = lax.broadcasted_iota(jnp.int32, (rhs, width), 0)
    factor = jnp.zeros((rhs, width), F32)
    for i in range(rhs):
        factor = jnp.where(row == i, scale[i], factor)
    for q in range(pan_own):
        panels[q] = factor * pack[c * pan_own + q].astype(F32) + end_own[q]
        pot_out[:, q * width : (q + 1) * width] = pot[c * pan_own + q]
    add_drops(r, pot, 0, links, holder, lanes, field)


def drops_body(k, pan_own, links, holder, lanes, message, field_in, field):
    field[...] = field_in[...]
    p = lax.bitwise_xor(lax.axis_index("row"), k)
    add_drops(p, message, pan_own, links, holder, lanes, field)


def final_body(n_row, n_col, pan_own, links, holder, lanes, field_own, panels, *refs):
    arrived, field_in = refs[: n_row - 1], refs[n_row - 1 : n_row + n_col - 2]
    seg_out, pan_out, field, seg, pan, sems = refs[n_row + n_col - 2 :]
    seg_own, _, width = field.shape
    total = field_own[...]
    for x in field_in:
        total += x[...].astype(F32)
    field[...] = total
    p = lax.bitwise_xor(lax.axis_index("row"), 1)
    add_drops(p, arrived[0], pan_own, links, holder, lanes, field)
    for q in range(pan_own):
        total = panels[q]
        for x in arrived:
            total += x[q].astype(F32)
        pan[:, q * width : (q + 1) * width] = total.astype(BF16)
    chunks = sems.shape[0] - 1
    copies = [pltpu.make_async_copy(pan, pan_out, sems.at[chunks])]
    copies[0].start()
    size = seg_own // chunks
    for i in range(chunks):
        for k in range(i * size, (i + 1) * size):
            seg[:, k * width : (k + 1) * width] = field[k].astype(BF16)
        part = pl.ds(i * size * width, size * width)
        copies.append(pltpu.make_async_copy(seg.at[:, part], seg_out.at[:, part], sems.at[i]))
        copies[-1].start()
    for copy in copies:
        copy.wait()


def shards(
    current,
    charge,
    rhs_scale,
    induct_tiles,
    induct_rows,
    induct_slots,
    induct_needs,
    coeff_tiles,
    coeff_rows,
    coeff_slots,
    coeff_needs,
    link_needs,
    end_slots,
    end_offsets,
):
    n_row = lax.axis_size("row")
    n_col = lax.axis_size("col")
    width = induct_tiles.shape[1]
    rhs = current.shape[0]
    seg_own = current.shape[1] // width
    pan_own = charge.shape[1] // width
    seg_group, pan_group = seg_own * n_col, pan_own * n_col
    cap_l, cap_p, cap_k = induct_needs.shape[1], coeff_needs.shape[1], link_needs.shape[1]
    slots_t, off_t = end_slots.T, end_offsets.T

    partners = [*reversed(range(1, n_row))]
    partners[:2] = partners[1::-1]

    def like(blocks, dtype):
        return jax.ShapeDtypeStruct((blocks, rhs, width), dtype)

    charges = exchange_all(charge, [charge] * (n_col - 1), "col")
    cur = exchange_all(current, [current] * (n_col - 1), "col")
    (pack,) = call(
        functools.partial(pack_body, pan_own),
        "pack_charges",
        [like(pan_own + 1, BF16)],
        [VMEM] * 2,
        [pltpu.VMEM((rhs, width), jnp.int32)],
        moved=2**16,
    )(*in_hbm(charge, induct_needs))
    (pack,) = call(
        functools.partial(join_body, pan_own),
        "join_charges",
        [like(pan_group + 1, BF16)],
        [VMEM] * n_col,
        moved=2**16,
    )(pack, *charges[1:])
    packs = exchange_all(pack, [pack] * (n_row - 1), "row")

    rows_own = n_row * pan_own
    scalars = [slots_t, link_needs, coeff_slots, coeff_rows, coeff_needs, induct_slots, induct_rows, rhs_scale]
    moved = [*scalars, coeff_tiles]
    outs = call(
        functools.partial(ends_body, n_row, n_col, pan_own, cap_k, len(moved)),
        "end_sums",
        [pltpu.SMEM(x.shape, x.dtype) for x in scalars]
        + [jax.ShapeDtypeStruct(coeff_tiles.shape, BF16)]
        + [pltpu.SMEM((2 * seg_own,), jnp.int32), jax.ShapeDtypeStruct((2 * seg_own, width), jnp.int32)]
        + [like(seg_own, BF16), like(rows_own, F32)]
        + [like(rows_own, BF16)] * (n_col - 1),
        [ANY] * (len(moved) + 2),
        [
            pltpu.VMEM(current.shape, BF16),
            pltpu.VMEM(off_t.shape, jnp.int32),
            pltpu.VMEM((n_row * pan_group, rhs, width), F32),
            pltpu.SemaphoreType.DMA((len(moved) + 2,)),
        ],
        flops=5 * 10**8,
        moved=2**18,
        out_specs=[SMEM] * len(scalars) + [VMEM, SMEM] + [VMEM] * (2 + n_col),
    )(*in_hbm(current, off_t, *moved))
    _, links_s, coeff_slots, coeff_rows, coeff_needs, induct_slots, induct_rows, scale, coeff_tiles = outs[: len(moved)]
    holder, lanes, own_blocks, ends_own, *ends_out = outs[len(moved) :]

    part, *messages = call(
        functools.partial(coeff_body, n_row, n_col, pan_own, partners),
        "coeff_tiles",
        [like(pan_group, F32)] + [like(2 * pan_group + rows_own, BF16)] * (n_col - 1),
        [SMEM] * 3 + [VMEM] * (n_row + n_col),
        [
            pltpu.VMEM((n_row * pan_group, rhs, width), BF16),
            pltpu.SMEM((n_row * cap_p,), jnp.int32),
        ],
        flops=10**9,
        moved=coeff_tiles.size * 2,
    )(coeff_slots, coeff_rows, coeff_needs, *[packs[k] for k in partners], packs[0], *ends_out, coeff_tiles)
    parts = exchange_all(None, messages, "col")[1:]

    *picks, own_picks = call(
        functools.partial(pick_body, n_row, n_col, cap_l, partners),
        "pick_blocks",
        [like(cap_l, BF16)] * n_row,
        [ANY] + [VMEM] * (n_row + n_col),
        [pltpu.VMEM((n_row, width), jnp.int32)],
        moved=2**18,
    )(part, *[packs[k] for k in partners], packs[0], own_blocks, *cur[1:])
    got = exchange_all(own_picks, picks[::-1], "row")

    pot, end_keep, *row_messages = call(
        functools.partial(panels_body, n_row, n_col, pan_own),
        "panel_sums",
        [like(pan_group, BF16), like(pan_own, F32)] + [like(pan_own + pan_group, BF16)] * (n_row - 1),
        [VMEM] * (1 + n_col),
        flops=10**9,
        moved=2**18,
    )(part, ends_own, *parts)

    order = [*partners[1:], 0, partners[0]]
    field_own, *field_out = call(
        functools.partial(induct_body, n_row, n_col, seg_own, order),
        "induct_tiles",
        [like(seg_own, F32)] + [like(seg_own, BF16)] * (n_col - 1),
        [SMEM, SMEM, ANY] + [VMEM] * (n_row + 1),
        [
            pltpu.VMEM((n_row * cap_l, rhs, width), BF16),
            pltpu.VMEM((seg_group, rhs, width), F32),
        ],
        flops=10**8,
        moved=2**16,
    )(induct_slots, induct_rows, pot, *[got[k] for k in order], induct_tiles)
    field_in = exchange_all(None, field_out, "col")[1:]

    (row_messages[-1],) = call(
        hold_body,
        "hold_near",
        [like(pan_own + pan_group, BF16)],
        [ANY, VMEM],
        moved=2**16,
    )(field_own, row_messages[-1])
    arrived = exchange_all(None, row_messages[::-1], "row")[1:]

    field, panels, pot_out = call(
        functools.partial(base_body, pan_own),
        "base_sums",
        [like(seg_own, F32), like(pan_own, F32), jax.ShapeDtypeStruct(charge.shape, BF16)],
        [SMEM] * 3 + [VMEM] * 5,
        flops=0,
        moved=0,
    )(links_s, holder, scale, lanes, pack, field_own, end_keep, pot)

    for k in reversed(range(2, n_row)):
        (field,) = call(
            functools.partial(drops_body, k, pan_own),
            "add_drops",
            [like(seg_own, F32)],
            [SMEM] * 2 + [VMEM] * 3,
            flops=11 * 10**8 if k == 2 else 0,
            moved=0,
        )(links_s, holder, lanes, arrived[k - 1], field)

    seg_out, pan_out = call(
        functools.partial(final_body, n_row, n_col, pan_own),
        "outputs",
        [jax.ShapeDtypeStruct(x.shape, BF16) for x in (current, charge)],
        [SMEM] * 2 + [VMEM] * (1 + n_row + n_col),
        [
            pltpu.VMEM((seg_own, rhs, width), F32),
            pltpu.VMEM(current.shape, BF16),
            pltpu.VMEM(charge.shape, BF16),
            pltpu.SemaphoreType.DMA((3,)),
        ],
        flops=10**9,
        moved=2**20,
        out_specs=[ANY, ANY],
    )(links_s, holder, lanes, field, panels, *arrived, *field_in)
    return (seg_out, pan_out, pot_out)


def solution(mesh):
    blocks = P(("parts", "row", "col"))
    matrix = P(("parts", "row", "col"), None)
    tiles = P(("parts", "row", "col"), None, None)
    values = P("rhs", ("parts", "row", "col"))
    return jax.shard_map(
        shards,
        mesh=mesh,
        in_specs=(
            values,
            values,
            P(("parts", "rhs")),
            tiles,
            blocks,
            blocks,
            matrix,
            tiles,
            blocks,
            blocks,
            matrix,
            matrix,
            matrix,
            matrix,
        ),
        out_specs=(values, values, values),
        check_vma=False,
    )
```

```python
import functools

import jax
import jax.numpy as jnp
from jax import lax
from jax.experimental import pallas as pl
from jax.experimental.pallas import tpu as pltpu
from jax.sharding import PartitionSpec as P

F32 = jnp.float32
BF16 = jnp.bfloat16
VMEM = pl.BlockSpec(memory_space=pltpu.VMEM)
SMEM = pl.BlockSpec(memory_space=pltpu.SMEM)
ANY = pl.BlockSpec(memory_space=pl.ANY)


def exchange(x, axis, k):
    if k == 0:
        return x
    return lax.ppermute(x, axis, [(i, i ^ k) for i in range(lax.axis_size(axis))])


def exchange_all(first, others, axis):
    n = lax.axis_size(axis)
    got = {0: first}
    for k in reversed(range(1, n)):
        got[k] = exchange(others[k - 1], axis, k)
    return [got[k] for k in range(n)]


def call(body, name, out_shape, in_specs, scratch=(), flops=0, moved=0, out_specs=None):
    return pl.pallas_call(
        body,
        out_shape=out_shape,
        in_specs=in_specs,
        out_specs=out_specs or [VMEM] * len(out_shape),
        scratch_shapes=list(scratch),
        compiler_params=pltpu.CompilerParams(vmem_limit_bytes=16 * 2**20),
        cost_estimate=pl.CostEstimate(flops=flops, bytes_accessed=moved, transcendentals=0),
        name=name,
    )


def in_hbm(*arrays):
    return [pltpu.with_memory_space_constraint(x, pltpu.HBM) for x in arrays]


def pack_body(pan_own, charge, needs, message, wide):
    width = charge.shape[1] // pan_own
    for q in range(pan_own):
        message[q] = charge[:, q * width : (q + 1) * width]
    wide[...] = jnp.zeros_like(wide)
    wide[: needs.shape[0], : needs.shape[1]] = needs[...]
    message[pan_own] = wide[...].astype(F32).astype(BF16)


def join_body(pan_own, own, *refs):
    others, message = refs[:-1], refs[-1]
    c = lax.axis_index("col")
    width = own.shape[2]
    message[pl.ds(c * pan_own, pan_own)] = own[pl.ds(0, pan_own)]
    for j, x in enumerate(others):
        first = lax.bitwise_xor(c, j + 1) * pan_own
        for q in range(pan_own):
            message[first + q] = x[:, q * width : (q + 1) * width]
    message[message.shape[0] - 1] = own[pan_own]


def ends_body(n_row, n_col, pan_own, cap, n_moved, *refs):
    sources, targets = refs[: n_moved + 2], refs[n_moved + 2 : 2 * n_moved + 2]
    (holder, lanes, blocks, own, *sends), (cur, off, acc, sems) = refs[2 * n_moved + 2 : -4], refs[-4:]
    copies = [
        pltpu.make_async_copy(source, target, sems.at[i])
        for i, (source, target) in enumerate(zip(sources, (cur, off, *targets)))
    ]
    for copy in copies:
        copy.start()
    slots, links = targets[:2]
    seg_own, _, width = blocks.shape
    pan_group = pan_own * n_col
    r, c = lax.axis_index("row"), lax.axis_index("col")
    acc[...] = jnp.zeros_like(acc)
    levels = lax.broadcasted_iota(jnp.int32, (width, width), 0)
    for copy in copies[:4]:
        copy.wait()

    def block(k):
        span = pl.ds(pl.multiple_of(k * width, width), width)
        for e in range(2):
            lanes[pl.ds(2 * k + e, 1), :] = off[e : e + 1, span]
        to_hot = jnp.where(levels == off[0:1, span], 1.0, 0.0).astype(BF16)
        from_hot = jnp.where(levels == off[1:2, span], -1.0, 0.0).astype(BF16)
        hot = jnp.concatenate([to_hot, from_hot], axis=0)
        value = cur[:, span]
        blocks[k] = value
        sums = lax.dot_general(value, hot, (((1,), (1,)), ((), ())), preferred_element_type=F32)
        return sums.astype(BF16).astype(F32)

    unroll = 16

    def step(i, carry):
        got = [block(i * unroll + u) for u in range(unroll)]
        for u in range(unroll):
            for e in range(2):
                slot = slots[e, i * unroll + u]
                holder[slot] = 2 * (i * unroll + u) + e
                p = lax.div(slot, cap)
                b = links[p, slot - p * cap]
                acc[lax.bitwise_xor(p, r) * pan_group + b] += got[u][:, e * width : (e + 1) * width]
        return carry

    lax.fori_loop(0, seg_own // unroll, step, 0)
    for k in range(n_row):
        here = pl.ds(k * pan_own, pan_own)
        own[here] = acc[pl.ds(k * pan_group + c * pan_own, pan_own)]
        for j in range(1, n_col):
            there = lax.bitwise_xor(c, j)
            sends[j - 1][here] = acc[pl.ds(k * pan_group + there * pan_own, pan_own)].astype(BF16)
    for copy in copies[4:]:
        copy.wait()


def pick_body(n_row, n_col, cap, partners, _after, *refs):
    packs = {k: refs[i] for i, k in enumerate([*partners, 0])}
    own, peers = refs[n_row], refs[n_row + 1 : n_row + n_col]
    outs, asked = refs[n_row + n_col : -1], refs[-1]
    seg_own, rhs, width = own.shape
    r, c = lax.axis_index("row"), lax.axis_index("col")
    mine = lax.broadcasted_iota(jnp.int32, (rhs, width), 0) == r
    for k in range(n_row):
        needs = packs[k][packs[k].shape[0] - 1].astype(F32)
        asked[k : k + 1, :] = jnp.sum(jnp.where(mine, needs, 0.0), axis=0, keepdims=True).astype(jnp.int32)
    for k in range(n_row):
        for s in range(cap):
            b = asked[k, s]
            holder = lax.div(b, seg_own)
            b = b - holder * seg_own
            j = lax.bitwise_xor(holder, c)
            value = own[b]
            span = pl.ds(pl.multiple_of(b * width, width), width)
            for q, peer in enumerate(peers):
                value = jnp.where(j == q + 1, peer[:, span], value)
            outs[n_row - 1 - k][s] = value


def multiply(tiles, src, source, rows, acc):
    rhs, width = src.shape[1:]
    count = tiles.shape[0]
    run = max(d for d in range(8, 97, 8) if count % d == 0)

    def products(start):
        got = []
        for t in (start, start + 2, start + 4, start + 6):
            left = jnp.concatenate([src[source(t)], src[source(t + 1)]], axis=0)
            right = jnp.concatenate([tiles[t], tiles[t + 1]], axis=1)
            both = jnp.dot(left, right, preferred_element_type=F32)
            got += [both[:rhs, :width], both[rhs:, width:]]
        return got

    def add(start, got):
        for u, value in enumerate(got):
            acc[rows[start + u]] += value

    def step(i, carry):
        start = i * run
        waiting = products(start)
        for first in range(8, run, 8):
            ahead = products(start + first)
            add(start + first - 8, waiting)
            waiting = ahead
        add(start + run - 8, waiting)
        return carry

    lax.fori_loop(0, count // run, step, 0)


def coeff_body(n_row, n_col, pan_own, partners, slots, rows, needs, *refs):
    packs = {k: refs[i] for i, k in enumerate([*partners, 0])}
    ends = refs[n_row : n_row + n_col - 1]
    tiles, part, *messages = refs[n_row + n_col - 1 : -2]
    src, named = refs[-2:]
    r = lax.axis_index("row")
    pan_group = pan_own * n_col
    cap = needs.shape[1]
    for k in range(n_row):
        src[pl.ds(lax.bitwise_xor(r, k) * pan_group, pan_group)] = packs[k][pl.ds(0, pan_group)]
    for p in range(n_row):
        for s in range(cap):
            named[p * cap + s] = p * pan_group + needs[p, s]
    part[...] = jnp.zeros_like(part)
    multiply(tiles, src, lambda t: named[slots[t]], rows, part)
    high = part[...].astype(BF16)
    low = (part[...] - high.astype(F32)).astype(BF16)
    for message, sums in zip(messages, ends):
        message[pl.ds(0, pan_group)] = high
        message[pl.ds(pan_group, pan_group)] = low
        message[pl.ds(2 * pan_group, sums.shape[0])] = sums[...]


def induct_body(n_row, n_col, seg_own, order, slots, rows, _after, *refs):
    got = {k: refs[i] for i, k in enumerate(order)}
    tiles = refs[n_row]
    own, *sends = refs[n_row + 1 : -2]
    src, acc = refs[-2:]
    cap = got[0].shape[0]
    r, c = lax.axis_index("row"), lax.axis_index("col")
    for k in range(n_row):
        src[pl.ds(lax.bitwise_xor(r, k) * cap, cap)] = got[k][...]
    acc[...] = jnp.zeros_like(acc)
    multiply(tiles, src, lambda t: slots[t], rows, acc)
    own[...] = acc[pl.ds(c * seg_own, seg_own)]
    for j in range(1, n_col):
        sends[j - 1][...] = acc[pl.ds(lax.bitwise_xor(c, j) * seg_own, seg_own)].astype(BF16)


def panels_body(n_row, n_col, pan_own, part, ends_own, *refs):
    parts = refs[: n_col - 1]
    pot, end_keep, *messages = refs[n_col - 1 :]
    pan_group = part.shape[0]
    total = part[...]
    for x in parts:
        total += x[pl.ds(0, pan_group)].astype(F32) + x[pl.ds(pan_group, pan_group)].astype(F32)
    rounded = total.astype(BF16)
    pot[...] = rounded
    for k in range(n_row):
        sums = ends_own[pl.ds(k * pan_own, pan_own)]
        for x in parts:
            sums += x[pl.ds(2 * pan_group + k * pan_own, pan_own)].astype(F32)
        if k == 0:
            end_keep[...] = sums
        else:
            messages[n_row - 1 - k][pl.ds(0, pan_own)] = sums.astype(BF16)
            messages[n_row - 1 - k][pl.ds(pan_own, pan_group)] = rounded


def hold_body(_after, message, out):
    out[...] = message[...]


def add_drops(p, pots, first, links, holder, lanes, field):
    cap = links.shape[1]
    ends, drops = [], []
    for s in range(cap):
        j = holder[p * cap + s]
        values = pots[first + links[p, s]].astype(F32)
        at = jnp.broadcast_to(lanes[pl.ds(j, 1), :], values.shape)
        drop = jnp.take_along_axis(values, at, axis=1, mode="promise_in_bounds")
        k = lax.div(j, 2)
        drops.append(drop * (1 - 2 * (j - 2 * k)).astype(F32))
        ends.append(k)
    for k, drop in zip(ends, drops):
        field[k] += drop


def base_body(pan_own, links, holder, scale, lanes, pack, field_own, end_own, pot, field, panels, pot_out):
    rhs, width = pot.shape[1:]
    r, c = lax.axis_index("row"), lax.axis_index("col")
    field[...] = field_own[...]
    row = lax.broadcasted_iota(jnp.int32, (rhs, width), 0)
    factor = jnp.zeros((rhs, width), F32)
    for i in range(rhs):
        factor = jnp.where(row == i, scale[i], factor)
    for q in range(pan_own):
        panels[q] = factor * pack[c * pan_own + q].astype(F32) + end_own[q]
        pot_out[:, q * width : (q + 1) * width] = pot[c * pan_own + q]
    add_drops(r, pot, 0, links, holder, lanes, field)


def drops_body(k, pan_own, links, holder, lanes, message, field_in, field):
    field[...] = field_in[...]
    p = lax.bitwise_xor(lax.axis_index("row"), k)
    add_drops(p, message, pan_own, links, holder, lanes, field)


def final_body(n_row, n_col, pan_own, links, holder, lanes, field_own, panels, *refs):
    arrived, field_in = refs[: n_row - 1], refs[n_row - 1 : n_row + n_col - 2]
    seg_out, pan_out, field, seg, pan, sems = refs[n_row + n_col - 2 :]
    seg_own, _, width = field.shape
    total = field_own[...]
    for x in field_in:
        total += x[...].astype(F32)
    field[...] = total
    p = lax.bitwise_xor(lax.axis_index("row"), 1)
    add_drops(p, arrived[0], pan_own, links, holder, lanes, field)
    for q in range(pan_own):
        total = panels[q]
        for x in arrived:
            total += x[q].astype(F32)
        pan[:, q * width : (q + 1) * width] = total.astype(BF16)
    chunks = sems.shape[0] - 1
    copies = [pltpu.make_async_copy(pan, pan_out, sems.at[chunks])]
    copies[0].start()
    size = seg_own // chunks
    for i in range(chunks):
        for k in range(i * size, (i + 1) * size):
            seg[:, k * width : (k + 1) * width] = field[k].astype(BF16)
        part = pl.ds(i * size * width, size * width)
        copies.append(pltpu.make_async_copy(seg.at[:, part], seg_out.at[:, part], sems.at[i]))
        copies[-1].start()
    for copy in copies:
        copy.wait()


def shards(
    current,
    charge,
    rhs_scale,
    induct_tiles,
    induct_rows,
    induct_slots,
    induct_needs,
    coeff_tiles,
    coeff_rows,
    coeff_slots,
    coeff_needs,
    link_needs,
    end_slots,
    end_offsets,
):
    n_row = lax.axis_size("row")
    n_col = lax.axis_size("col")
    width = induct_tiles.shape[1]
    rhs = current.shape[0]
    seg_own = current.shape[1] // width
    pan_own = charge.shape[1] // width
    seg_group, pan_group = seg_own * n_col, pan_own * n_col
    cap_l, cap_p, cap_k = induct_needs.shape[1], coeff_needs.shape[1], link_needs.shape[1]
    slots_t, off_t = end_slots.T, end_offsets.T

    partners = [*reversed(range(1, n_row))]
    partners[:2] = partners[1::-1]

    def like(blocks, dtype):
        return jax.ShapeDtypeStruct((blocks, rhs, width), dtype)

    charges = exchange_all(charge, [charge] * (n_col - 1), "col")
    cur = exchange_all(current, [current] * (n_col - 1), "col")
    (pack,) = call(
        functools.partial(pack_body, pan_own),
        "pack_charges",
        [like(pan_own + 1, BF16)],
        [VMEM] * 2,
        [pltpu.VMEM((rhs, width), jnp.int32)],
        moved=2**16,
    )(*in_hbm(charge, induct_needs))
    (pack,) = call(
        functools.partial(join_body, pan_own),
        "join_charges",
        [like(pan_group + 1, BF16)],
        [VMEM] * n_col,
        moved=2**16,
    )(pack, *charges[1:])
    packs = exchange_all(pack, [pack] * (n_row - 1), "row")

    rows_own = n_row * pan_own
    scalars = [slots_t, link_needs, coeff_slots, coeff_rows, coeff_needs, induct_slots, induct_rows, rhs_scale]
    moved = [*scalars, coeff_tiles]
    outs = call(
        functools.partial(ends_body, n_row, n_col, pan_own, cap_k, len(moved)),
        "end_sums",
        [pltpu.SMEM(x.shape, x.dtype) for x in scalars]
        + [jax.ShapeDtypeStruct(coeff_tiles.shape, BF16)]
        + [pltpu.SMEM((2 * seg_own,), jnp.int32), jax.ShapeDtypeStruct((2 * seg_own, width), jnp.int32)]
        + [like(seg_own, BF16), like(rows_own, F32)]
        + [like(rows_own, BF16)] * (n_col - 1),
        [ANY] * (len(moved) + 2),
        [
            pltpu.VMEM(current.shape, BF16),
            pltpu.VMEM(off_t.shape, jnp.int32),
            pltpu.VMEM((n_row * pan_group, rhs, width), F32),
            pltpu.SemaphoreType.DMA((len(moved) + 2,)),
        ],
        flops=5 * 10**8,
        moved=2**18,
        out_specs=[SMEM] * len(scalars) + [VMEM, SMEM] + [VMEM] * (2 + n_col),
    )(*in_hbm(current, off_t, *moved))
    _, links_s, coeff_slots, coeff_rows, coeff_needs, induct_slots, induct_rows, scale, coeff_tiles = outs[: len(moved)]
    holder, lanes, own_blocks, ends_own, *ends_out = outs[len(moved) :]

    part, *messages = call(
        functools.partial(coeff_body, n_row, n_col, pan_own, partners),
        "coeff_tiles",
        [like(pan_group, F32)] + [like(2 * pan_group + rows_own, BF16)] * (n_col - 1),
        [SMEM] * 3 + [VMEM] * (n_row + n_col),
        [
            pltpu.VMEM((n_row * pan_group, rhs, width), BF16),
            pltpu.SMEM((n_row * cap_p,), jnp.int32),
        ],
        flops=10**9,
        moved=coeff_tiles.size * 2,
    )(coeff_slots, coeff_rows, coeff_needs, *[packs[k] for k in partners], packs[0], *ends_out, coeff_tiles)
    parts = exchange_all(None, messages, "col")[1:]

    *picks, own_picks = call(
        functools.partial(pick_body, n_row, n_col, cap_l, partners),
        "pick_blocks",
        [like(cap_l, BF16)] * n_row,
        [ANY] + [VMEM] * (n_row + n_col),
        [pltpu.VMEM((n_row, width), jnp.int32)],
        moved=2**18,
    )(part, *[packs[k] for k in partners], packs[0], own_blocks, *cur[1:])
    got = exchange_all(own_picks, picks[::-1], "row")

    pot, end_keep, *row_messages = call(
        functools.partial(panels_body, n_row, n_col, pan_own),
        "panel_sums",
        [like(pan_group, BF16), like(pan_own, F32)] + [like(pan_own + pan_group, BF16)] * (n_row - 1),
        [VMEM] * (1 + n_col),
        flops=10**9,
        moved=2**18,
    )(part, ends_own, *parts)

    order = [*partners[1:], 0, partners[0]]
    field_own, *field_out = call(
        functools.partial(induct_body, n_row, n_col, seg_own, order),
        "induct_tiles",
        [like(seg_own, F32)] + [like(seg_own, BF16)] * (n_col - 1),
        [SMEM, SMEM, ANY] + [VMEM] * (n_row + 1),
        [
            pltpu.VMEM((n_row * cap_l, rhs, width), BF16),
            pltpu.VMEM((seg_group, rhs, width), F32),
        ],
        flops=10**8,
        moved=2**16,
    )(induct_slots, induct_rows, pot, *[got[k] for k in order], induct_tiles)
    field_in = exchange_all(None, field_out, "col")[1:]

    (row_messages[-1],) = call(
        hold_body,
        "hold_near",
        [like(pan_own + pan_group, BF16)],
        [ANY, VMEM],
        moved=2**16,
    )(field_own, row_messages[-1])
    arrived = exchange_all(None, row_messages[::-1], "row")[1:]

    field, panels, pot_out = call(
        functools.partial(base_body, pan_own),
        "base_sums",
        [like(seg_own, F32), like(pan_own, F32), jax.ShapeDtypeStruct(charge.shape, BF16)],
        [SMEM] * 3 + [VMEM] * 5,
        flops=0,
        moved=0,
    )(links_s, holder, scale, lanes, pack, field_own, end_keep, pot)

    for k in partners[:-1]:
        (field,) = call(
            functools.partial(drops_body, k, pan_own),
            "add_drops",
            [like(seg_own, F32)],
            [SMEM] * 2 + [VMEM] * 3,
            flops=11 * 10**8 if k == partners[-2] else 0,
            moved=0,
        )(links_s, holder, lanes, arrived[k - 1], field)

    seg_out, pan_out = call(
        functools.partial(final_body, n_row, n_col, pan_own),
        "outputs",
        [jax.ShapeDtypeStruct(x.shape, BF16) for x in (current, charge)],
        [SMEM] * 2 + [VMEM] * (1 + n_row + n_col),
        [
            pltpu.VMEM((seg_own, rhs, width), F32),
            pltpu.VMEM(current.shape, BF16),
            pltpu.VMEM(charge.shape, BF16),
            pltpu.SemaphoreType.DMA((3,)),
        ],
        flops=10**9,
        moved=2**20,
        out_specs=[ANY, ANY],
    )(links_s, holder, lanes, field, panels, *arrived, *field_in)
    return (seg_out, pan_out, pot_out)


def solution(mesh):
    blocks = P(("parts", "row", "col"))
    matrix = P(("parts", "row", "col"), None)
    tiles = P(("parts", "row", "col"), None, None)
    values = P("rhs", ("parts", "row", "col"))
    return jax.shard_map(
        shards,
        mesh=mesh,
        in_specs=(
            values,
            values,
            P(("parts", "rhs")),
            tiles,
            blocks,
            blocks,
            matrix,
            tiles,
            blocks,
            blocks,
            matrix,
            matrix,
            matrix,
            matrix,
        ),
        out_specs=(values, values, values),
        check_vma=False,
    )
```

```python
import functools

import jax
import jax.numpy as jnp
from jax import lax
from jax.experimental import pallas as pl
from jax.experimental.pallas import tpu as pltpu
from jax.sharding import PartitionSpec as P

F32 = jnp.float32
BF16 = jnp.bfloat16
VMEM = pl.BlockSpec(memory_space=pltpu.VMEM)
SMEM = pl.BlockSpec(memory_space=pltpu.SMEM)
ANY = pl.BlockSpec(memory_space=pl.ANY)


def exchange(x, axis, k):
    if k == 0:
        return x
    return lax.ppermute(x, axis, [(i, i ^ k) for i in range(lax.axis_size(axis))])


def exchange_all(first, others, axis):
    n = lax.axis_size(axis)
    got = {0: first}
    for k in reversed(range(1, n)):
        got[k] = exchange(others[k - 1], axis, k)
    return [got[k] for k in range(n)]


def call(body, name, out_shape, in_specs, scratch=(), flops=0, moved=0, out_specs=None):
    return pl.pallas_call(
        body,
        out_shape=out_shape,
        in_specs=in_specs,
        out_specs=out_specs or [VMEM] * len(out_shape),
        scratch_shapes=list(scratch),
        compiler_params=pltpu.CompilerParams(vmem_limit_bytes=16 * 2**20),
        cost_estimate=pl.CostEstimate(flops=flops, bytes_accessed=moved, transcendentals=0),
        name=name,
    )


def in_hbm(*arrays):
    return [pltpu.with_memory_space_constraint(x, pltpu.HBM) for x in arrays]


def pack_body(pan_own, charge, needs, message, wide):
    width = charge.shape[1] // pan_own
    for q in range(pan_own):
        message[q] = charge[:, q * width : (q + 1) * width]
    wide[...] = jnp.zeros_like(wide)
    wide[: needs.shape[0], : needs.shape[1]] = needs[...]
    message[pan_own] = wide[...].astype(F32).astype(BF16)


def join_body(pan_own, own, *refs):
    others, message = refs[:-1], refs[-1]
    c = lax.axis_index("col")
    width = own.shape[2]
    message[pl.ds(c * pan_own, pan_own)] = own[pl.ds(0, pan_own)]
    for j, x in enumerate(others):
        first = lax.bitwise_xor(c, j + 1) * pan_own
        for q in range(pan_own):
            message[first + q] = x[:, q * width : (q + 1) * width]
    message[message.shape[0] - 1] = own[pan_own]


STEP = 16


def list_size(count):
    return count + STEP


def first_run(count):
    return count // 2 // STEP * STEP


def sort_tiles(slots, rows, listed, seg_own, n_col, spare_slot):
    count = slots.shape[0]
    size, run = list_size(count), first_run(count)
    c = lax.axis_index("col")

    def put(at, tile, slot, row):
        listed[at] = tile
        listed[2 * size + at] = slot
        listed[4 * size + at] = row

    def step(i, found):
        away, here = found
        for u in range(8):
            t = i * 8 + u
            row = rows[t]
            mine = (lax.div(row, seg_own) == c).astype(jnp.int32)
            put(jnp.where(mine == 1, size + here, away), t, slots[t], row)
            away, here = away + 1 - mine, here + mine
        return away, here

    found = lax.fori_loop(0, count // 8, step, (jnp.int32(0), jnp.int32(0)))
    for half, n in enumerate(found):
        steps = lax.max(lax.div(n - run + STEP - 1, STEP), 0)
        spare_row = (lax.rem(c + 1 - half, n_col)) * seg_own

        def fill(i, carry, half=half, spare_row=spare_row):
            put(half * size + i, 0, spare_slot, spare_row)
            return carry

        lax.fori_loop(n, run + steps * STEP, fill, 0)
        listed[6 * size + half] = steps


def ends_body(n_row, n_col, pan_own, cap, n_moved, spare_slot, *refs):
    sources, targets = refs[: n_moved + 2], refs[n_moved + 2 : 2 * n_moved + 2]
    (holder, listed, lanes, blocks, own, *sends), (cur, off, acc, sems) = refs[2 * n_moved + 2 : -4], refs[-4:]
    copies = [
        pltpu.make_async_copy(source, target, sems.at[i])
        for i, (source, target) in enumerate(zip(sources, (cur, off, *targets)))
    ]
    for copy in copies:
        copy.start()
    slots, links = targets[:2]
    seg_own, _, width = blocks.shape
    pan_group = pan_own * n_col
    r, c = lax.axis_index("row"), lax.axis_index("col")
    acc[...] = jnp.zeros_like(acc)
    levels = lax.broadcasted_iota(jnp.int32, (width, width), 0)
    for copy in copies[:4]:
        copy.wait()

    def block(k):
        span = pl.ds(pl.multiple_of(k * width, width), width)
        for e in range(2):
            lanes[pl.ds(2 * k + e, 1), :] = off[e : e + 1, span]
        to_hot = jnp.where(levels == off[0:1, span], 1.0, 0.0).astype(BF16)
        from_hot = jnp.where(levels == off[1:2, span], -1.0, 0.0).astype(BF16)
        hot = jnp.concatenate([to_hot, from_hot], axis=0)
        value = cur[:, span]
        blocks[k] = value
        sums = lax.dot_general(value, hot, (((1,), (1,)), ((), ())), preferred_element_type=F32)
        return sums.astype(BF16).astype(F32)

    unroll = 16

    def step(i, carry):
        got = [block(i * unroll + u) for u in range(unroll)]
        for u in range(unroll):
            for e in range(2):
                slot = slots[e, i * unroll + u]
                holder[slot] = 2 * (i * unroll + u) + e
                p = lax.div(slot, cap)
                b = links[p, slot - p * cap]
                acc[lax.bitwise_xor(p, r) * pan_group + b] += got[u][:, e * width : (e + 1) * width]
        return carry

    lax.fori_loop(0, seg_own // unroll, step, 0)
    for k in range(n_row):
        here = pl.ds(k * pan_own, pan_own)
        own[here] = acc[pl.ds(k * pan_group + c * pan_own, pan_own)]
        for j in range(1, n_col):
            there = lax.bitwise_xor(c, j)
            sends[j - 1][here] = acc[pl.ds(k * pan_group + there * pan_own, pan_own)].astype(BF16)
    for copy in copies[4:]:
        copy.wait()
    sort_tiles(targets[5], targets[6], listed, seg_own, n_col, spare_slot)


def pick_body(n_row, n_col, cap, partners, _after, *refs):
    packs = {k: refs[i] for i, k in enumerate([*partners, 0])}
    own, peers = refs[n_row], refs[n_row + 1 : n_row + n_col]
    outs, asked = refs[n_row + n_col : -1], refs[-1]
    seg_own, rhs, width = own.shape
    r, c = lax.axis_index("row"), lax.axis_index("col")
    mine = lax.broadcasted_iota(jnp.int32, (rhs, width), 0) == r
    for k in range(n_row):
        needs = packs[k][packs[k].shape[0] - 1].astype(F32)
        asked[k : k + 1, :] = jnp.sum(jnp.where(mine, needs, 0.0), axis=0, keepdims=True).astype(jnp.int32)
    for k in range(n_row):
        for s in range(cap):
            b = asked[k, s]
            holder = lax.div(b, seg_own)
            b = b - holder * seg_own
            j = lax.bitwise_xor(holder, c)
            value = own[b]
            span = pl.ds(pl.multiple_of(b * width, width), width)
            for q, peer in enumerate(peers):
                value = jnp.where(j == q + 1, peer[:, span], value)
            outs[n_row - 1 - k][s] = value


def multiply(tiles, src, tile, source, row, acc, start, count):
    rhs, width = src.shape[1:]

    def products(first):
        got = []
        for i in (first, first + 2, first + 4, first + 6):
            left = jnp.concatenate([src[source(i)], src[source(i + 1)]], axis=0)
            right = jnp.concatenate([tiles[tile(i)], tiles[tile(i + 1)]], axis=1)
            both = jnp.dot(left, right, preferred_element_type=F32)
            got += [both[:rhs, :width], both[rhs:, width:]]
        return got

    def add(first, got):
        for u, value in enumerate(got):
            acc[row(first + u)] += value

    waiting = products(start)
    for first in range(8, count, 8):
        ahead = products(start + first)
        add(start + first - 8, waiting)
        waiting = ahead
    add(start + count - 8, waiting)


def coeff_body(n_row, n_col, pan_own, partners, slots, rows, needs, *refs):
    packs = {k: refs[i] for i, k in enumerate([*partners, 0])}
    ends = refs[n_row : n_row + n_col - 1]
    tiles, part, *messages = refs[n_row + n_col - 1 : -2]
    src, named = refs[-2:]
    r = lax.axis_index("row")
    pan_group = pan_own * n_col
    cap = needs.shape[1]
    for k in range(n_row):
        src[pl.ds(lax.bitwise_xor(r, k) * pan_group, pan_group)] = packs[k][pl.ds(0, pan_group)]
    for p in range(n_row):
        for s in range(cap):
            named[p * cap + s] = p * pan_group + needs[p, s]
    part[...] = jnp.zeros_like(part)
    multiply(tiles, src, lambda t: t, lambda t: named[slots[t]], lambda t: rows[t], part, 0, tiles.shape[0])
    high = part[...].astype(BF16)
    low = (part[...] - high.astype(F32)).astype(BF16)
    for message, sums in zip(messages, ends):
        message[pl.ds(0, pan_group)] = high
        message[pl.ds(pan_group, pan_group)] = low
        message[pl.ds(2 * pan_group, sums.shape[0])] = sums[...]


def induct_body(n_row, n_col, seg_own, order, half, listed, _after, *refs):
    got = {k: refs[i] for i, k in enumerate(order)}
    tiles = refs[n_row]
    outs, (src, acc) = refs[n_row + 1 : -2], refs[-2:]
    cap = got[0].shape[0]
    r, c = lax.axis_index("row"), lax.axis_index("col")
    for k in range(n_row):
        src[pl.ds(lax.bitwise_xor(r, k) * cap, cap)] = got[k][...]
    src[n_row * cap] = jnp.zeros(src.shape[1:], BF16)
    columns = range(1, n_col) if half == 0 else range(1)
    spans = [pl.ds(lax.bitwise_xor(c, j) * seg_own, seg_own) for j in columns]
    for span in spans:
        acc[span] = jnp.zeros((seg_own, *acc.shape[1:]), F32)
    size, run = list_size(tiles.shape[0]), first_run(tiles.shape[0])
    entry = [lambda i, at=kind * 2 * size + half * size: listed[at + i] for kind in range(3)]
    multiply(tiles, src, *entry, acc, 0, run)

    def step(i, carry):
        multiply(tiles, src, *entry, acc, run + i * STEP, STEP)
        return carry

    lax.fori_loop(0, listed[6 * size + half], step, 0)
    for out, span in zip(outs, spans):
        out[...] = acc[span].astype(out.dtype)


def panels_body(n_row, n_col, pan_own, part, ends_own, *refs):
    parts = refs[: n_col - 1]
    pot, end_keep, *messages = refs[n_col - 1 :]
    pan_group = part.shape[0]
    total = part[...]
    for x in parts:
        total += x[pl.ds(0, pan_group)].astype(F32) + x[pl.ds(pan_group, pan_group)].astype(F32)
    rounded = total.astype(BF16)
    pot[...] = rounded
    for k in range(n_row):
        sums = ends_own[pl.ds(k * pan_own, pan_own)]
        for x in parts:
            sums += x[pl.ds(2 * pan_group + k * pan_own, pan_own)].astype(F32)
        if k == 0:
            end_keep[...] = sums
        else:
            messages[n_row - 1 - k][pl.ds(0, pan_own)] = sums.astype(BF16)
            messages[n_row - 1 - k][pl.ds(pan_own, pan_group)] = rounded


def hold_body(_after, message, out):
    out[...] = message[...]


def add_drops(p, pots, first, links, holder, lanes, field):
    cap = links.shape[1]
    ends, drops = [], []
    for s in range(cap):
        j = holder[p * cap + s]
        values = pots[first + links[p, s]].astype(F32)
        at = jnp.broadcast_to(lanes[pl.ds(j, 1), :], values.shape)
        drop = jnp.take_along_axis(values, at, axis=1, mode="promise_in_bounds")
        k = lax.div(j, 2)
        drops.append(drop * (1 - 2 * (j - 2 * k)).astype(F32))
        ends.append(k)
    for k, drop in zip(ends, drops):
        field[k] += drop


def base_body(pan_own, links, holder, scale, lanes, pack, field_own, end_own, pot, field, panels, pot_out):
    rhs, width = pot.shape[1:]
    r, c = lax.axis_index("row"), lax.axis_index("col")
    field[...] = field_own[...]
    row = lax.broadcasted_iota(jnp.int32, (rhs, width), 0)
    factor = jnp.zeros((rhs, width), F32)
    for i in range(rhs):
        factor = jnp.where(row == i, scale[i], factor)
    for q in range(pan_own):
        panels[q] = factor * pack[c * pan_own + q].astype(F32) + end_own[q]
        pot_out[:, q * width : (q + 1) * width] = pot[c * pan_own + q]
    add_drops(r, pot, 0, links, holder, lanes, field)


def drops_body(k, pan_own, links, holder, lanes, message, field_in, field):
    field[...] = field_in[...]
    p = lax.bitwise_xor(lax.axis_index("row"), k)
    add_drops(p, message, pan_own, links, holder, lanes, field)


def final_body(n_row, n_col, pan_own, links, holder, lanes, field_own, panels, *refs):
    arrived, field_in = refs[: n_row - 1], refs[n_row - 1 : n_row + n_col - 2]
    seg_out, pan_out, field, seg, pan, sems = refs[n_row + n_col - 2 :]
    seg_own, _, width = field.shape
    total = field_own[...]
    for x in field_in:
        total += x[...].astype(F32)
    field[...] = total
    p = lax.bitwise_xor(lax.axis_index("row"), 1)
    add_drops(p, arrived[0], pan_own, links, holder, lanes, field)
    for q in range(pan_own):
        total = panels[q]
        for x in arrived:
            total += x[q].astype(F32)
        pan[:, q * width : (q + 1) * width] = total.astype(BF16)
    chunks = sems.shape[0] - 1
    copies = [pltpu.make_async_copy(pan, pan_out, sems.at[chunks])]
    copies[0].start()
    size = seg_own // chunks
    for i in range(chunks):
        for k in range(i * size, (i + 1) * size):
            seg[:, k * width : (k + 1) * width] = field[k].astype(BF16)
        part = pl.ds(i * size * width, size * width)
        copies.append(pltpu.make_async_copy(seg.at[:, part], seg_out.at[:, part], sems.at[i]))
        copies[-1].start()
    for copy in copies:
        copy.wait()


def shards(
    current,
    charge,
    rhs_scale,
    induct_tiles,
    induct_rows,
    induct_slots,
    induct_needs,
    coeff_tiles,
    coeff_rows,
    coeff_slots,
    coeff_needs,
    link_needs,
    end_slots,
    end_offsets,
):
    n_row = lax.axis_size("row")
    n_col = lax.axis_size("col")
    width = induct_tiles.shape[1]
    rhs = current.shape[0]
    seg_own = current.shape[1] // width
    pan_own = charge.shape[1] // width
    seg_group, pan_group = seg_own * n_col, pan_own * n_col
    cap_l, cap_p, cap_k = induct_needs.shape[1], coeff_needs.shape[1], link_needs.shape[1]
    slots_t, off_t = end_slots.T, end_offsets.T

    partners = [*reversed(range(1, n_row))]
    partners[:2] = partners[1::-1]

    def like(blocks, dtype):
        return jax.ShapeDtypeStruct((blocks, rhs, width), dtype)

    charges = exchange_all(charge, [charge] * (n_col - 1), "col")
    cur = exchange_all(current, [current] * (n_col - 1), "col")
    (pack,) = call(
        functools.partial(pack_body, pan_own),
        "pack_charges",
        [like(pan_own + 1, BF16)],
        [VMEM] * 2,
        [pltpu.VMEM((rhs, width), jnp.int32)],
        moved=2**16,
    )(*in_hbm(charge, induct_needs))
    (pack,) = call(
        functools.partial(join_body, pan_own),
        "join_charges",
        [like(pan_group + 1, BF16)],
        [VMEM] * n_col,
        moved=2**16,
    )(pack, *charges[1:])
    packs = exchange_all(pack, [pack] * (n_row - 1), "row")

    rows_own = n_row * pan_own
    scalars = [slots_t, link_needs, coeff_slots, coeff_rows, coeff_needs, induct_slots, induct_rows, rhs_scale]
    moved = [*scalars, coeff_tiles]
    outs = call(
        functools.partial(ends_body, n_row, n_col, pan_own, cap_k, len(moved), n_row * cap_l),
        "end_sums",
        [pltpu.SMEM(x.shape, x.dtype) for x in scalars]
        + [jax.ShapeDtypeStruct(coeff_tiles.shape, BF16)]
        + [pltpu.SMEM((2 * seg_own,), jnp.int32), pltpu.SMEM((6 * list_size(induct_rows.shape[0]) + 2,), jnp.int32)]
        + [jax.ShapeDtypeStruct((2 * seg_own, width), jnp.int32)]
        + [like(seg_own, BF16), like(rows_own, F32)]
        + [like(rows_own, BF16)] * (n_col - 1),
        [ANY] * (len(moved) + 2),
        [
            pltpu.VMEM(current.shape, BF16),
            pltpu.VMEM(off_t.shape, jnp.int32),
            pltpu.VMEM((n_row * pan_group, rhs, width), F32),
            pltpu.SemaphoreType.DMA((len(moved) + 2,)),
        ],
        flops=5 * 10**8,
        moved=2**18,
        out_specs=[SMEM] * len(scalars) + [VMEM, SMEM, SMEM] + [VMEM] * (2 + n_col),
    )(*in_hbm(current, off_t, *moved))
    _, links_s, coeff_slots, coeff_rows, coeff_needs, induct_slots, induct_rows, scale, coeff_tiles = outs[: len(moved)]
    holder, listed, lanes, own_blocks, ends_own, *ends_out = outs[len(moved) :]

    part, *messages = call(
        functools.partial(coeff_body, n_row, n_col, pan_own, partners),
        "coeff_tiles",
        [like(pan_group, F32)] + [like(2 * pan_group + rows_own, BF16)] * (n_col - 1),
        [SMEM] * 3 + [VMEM] * (n_row + n_col),
        [
            pltpu.VMEM((n_row * pan_group, rhs, width), BF16),
            pltpu.SMEM((n_row * cap_p,), jnp.int32),
        ],
        flops=10**9,
        moved=coeff_tiles.size * 2,
    )(coeff_slots, coeff_rows, coeff_needs, *[packs[k] for k in partners], packs[0], *ends_out, coeff_tiles)
    parts = exchange_all(None, messages, "col")[1:]

    *picks, own_picks = call(
        functools.partial(pick_body, n_row, n_col, cap_l, partners),
        "pick_blocks",
        [like(cap_l, BF16)] * n_row,
        [ANY] + [VMEM] * (n_row + n_col),
        [pltpu.VMEM((n_row, width), jnp.int32)],
        moved=2**18,
    )(part, *[packs[k] for k in partners], packs[0], own_blocks, *cur[1:])
    got = exchange_all(own_picks, picks[::-1], "row")

    pot, end_keep, *row_messages = call(
        functools.partial(panels_body, n_row, n_col, pan_own),
        "panel_sums",
        [like(pan_group, BF16), like(pan_own, F32)] + [like(pan_own + pan_group, BF16)] * (n_row - 1),
        [VMEM] * (1 + n_col),
        flops=10**9,
        moved=2**18,
    )(part, ends_own, *parts)

    order = [*partners[1:], 0, partners[0]]

    def induct(name, half, outs, after):
        return call(
            functools.partial(induct_body, n_row, n_col, seg_own, order, half),
            name,
            outs,
            [SMEM, ANY] + [VMEM] * (n_row + 1),
            [
                pltpu.VMEM((n_row * cap_l + 1, rhs, width), BF16),
                pltpu.VMEM((seg_group, rhs, width), F32),
            ],
            flops=10**8,
            moved=2**16,
        )(listed, after, *[got[k] for k in order], induct_tiles)

    field_out = induct("induct_away", 0, [like(seg_own, BF16)] * (n_col - 1), pot)
    field_in = exchange_all(None, field_out, "col")[1:]

    (row_messages[-1],) = call(
        hold_body,
        "hold_near",
        [like(pan_own + pan_group, BF16)],
        [ANY, VMEM],
        moved=2**16,
    )(field_out[0], row_messages[-1])
    arrived = exchange_all(None, row_messages[::-1], "row")[1:]
    (field_own,) = induct("induct_own", 1, [like(seg_own, F32)], row_messages[-1])

    field, panels, pot_out = call(
        functools.partial(base_body, pan_own),
        "base_sums",
        [like(seg_own, F32), like(pan_own, F32), jax.ShapeDtypeStruct(charge.shape, BF16)],
        [SMEM] * 3 + [VMEM] * 5,
        flops=0,
        moved=0,
    )(links_s, holder, scale, lanes, pack, field_own, end_keep, pot)

    for k in reversed(range(2, n_row)):
        (field,) = call(
            functools.partial(drops_body, k, pan_own),
            "add_drops",
            [like(seg_own, F32)],
            [SMEM] * 2 + [VMEM] * 3,
            flops=11 * 10**8 if k == 2 else 0,
            moved=0,
        )(links_s, holder, lanes, arrived[k - 1], field)

    seg_out, pan_out = call(
        functools.partial(final_body, n_row, n_col, pan_own),
        "outputs",
        [jax.ShapeDtypeStruct(x.shape, BF16) for x in (current, charge)],
        [SMEM] * 2 + [VMEM] * (1 + n_row + n_col),
        [
            pltpu.VMEM((seg_own, rhs, width), F32),
            pltpu.VMEM(current.shape, BF16),
            pltpu.VMEM(charge.shape, BF16),
            pltpu.SemaphoreType.DMA((3,)),
        ],
        flops=10**9,
        moved=2**20,
        out_specs=[ANY, ANY],
    )(links_s, holder, lanes, field, panels, *arrived, *field_in)
    return (seg_out, pan_out, pot_out)


def solution(mesh):
    blocks = P(("parts", "row", "col"))
    matrix = P(("parts", "row", "col"), None)
    tiles = P(("parts", "row", "col"), None, None)
    values = P("rhs", ("parts", "row", "col"))
    return jax.shard_map(
        shards,
        mesh=mesh,
        in_specs=(
            values,
            values,
            P(("parts", "rhs")),
            tiles,
            blocks,
            blocks,
            matrix,
            tiles,
            blocks,
            blocks,
            matrix,
            matrix,
            matrix,
            matrix,
        ),
        out_specs=(values, values, values),
        check_vma=False,
    )
```

```python
import functools

import jax
import jax.numpy as jnp
from jax import lax
from jax.experimental import pallas as pl
from jax.experimental.pallas import tpu as pltpu
from jax.sharding import PartitionSpec as P

F32 = jnp.float32
BF16 = jnp.bfloat16
VMEM = pl.BlockSpec(memory_space=pltpu.VMEM)
SMEM = pl.BlockSpec(memory_space=pltpu.SMEM)
ANY = pl.BlockSpec(memory_space=pl.ANY)


def exchange(x, axis, k):
    if k == 0:
        return x
    return lax.ppermute(x, axis, [(i, i ^ k) for i in range(lax.axis_size(axis))])


def exchange_all(first, others, axis):
    n = lax.axis_size(axis)
    got = {0: first}
    for k in reversed(range(1, n)):
        got[k] = exchange(others[k - 1], axis, k)
    return [got[k] for k in range(n)]


def call(body, name, out_shape, in_specs, scratch=(), flops=0, moved=0, out_specs=None):
    return pl.pallas_call(
        body,
        out_shape=out_shape,
        in_specs=in_specs,
        out_specs=out_specs or [VMEM] * len(out_shape),
        scratch_shapes=list(scratch),
        compiler_params=pltpu.CompilerParams(vmem_limit_bytes=16 * 2**20),
        cost_estimate=pl.CostEstimate(flops=flops, bytes_accessed=moved, transcendentals=0),
        name=name,
    )


def in_hbm(*arrays):
    return [pltpu.with_memory_space_constraint(x, pltpu.HBM) for x in arrays]


def pack_body(pan_own, charge, needs, message, wide):
    width = charge.shape[1] // pan_own
    for q in range(pan_own):
        message[q] = charge[:, q * width : (q + 1) * width]
    wide[...] = jnp.zeros_like(wide)
    wide[: needs.shape[0], : needs.shape[1]] = needs[...]
    message[pan_own] = wide[...].astype(F32).astype(BF16)


def join_body(pan_own, own, *refs):
    others, message = refs[:-1], refs[-1]
    c = lax.axis_index("col")
    width = own.shape[2]
    message[pl.ds(c * pan_own, pan_own)] = own[pl.ds(0, pan_own)]
    for j, x in enumerate(others):
        first = lax.bitwise_xor(c, j + 1) * pan_own
        for q in range(pan_own):
            message[first + q] = x[:, q * width : (q + 1) * width]
    message[message.shape[0] - 1] = own[pan_own]


STEP = 16


def list_size(count):
    return count + STEP


def first_run(count):
    return count // 2 // STEP * STEP


def sort_tiles(rows, listed, seg_own):
    count = rows.shape[0]
    size, run = list_size(count), first_run(count)
    base = lax.axis_index("col") * seg_own

    def step(i, here):
        for u in range(16):
            t = i * 16 + u
            inside = rows[t] - base
            mine = jnp.logical_and(inside >= 0, inside < seg_own)
            listed[jnp.where(mine, size + here, t - here)] = t
            here = here + mine.astype(jnp.int32)
        return here

    here = lax.fori_loop(0, count // 16, step, jnp.int32(0))
    for half, n in enumerate((count - here, here)):
        steps = lax.max(lax.div(n - run + STEP - 1, STEP), 0)

        def fill(i, carry, half=half):
            listed[half * size + i] = 0
            return carry

        lax.fori_loop(n, run + steps * STEP, fill, 0)
        listed[2 * size + half] = steps
        listed[2 * size + 2 + half] = n


def ends_body(n_row, n_col, pan_own, cap, n_moved, *refs):
    sources, targets = refs[: n_moved + 2], refs[n_moved + 2 : 2 * n_moved + 2]
    (holder, listed, lanes, blocks, own, *sends), (cur, off, acc, sems) = refs[2 * n_moved + 2 : -4], refs[-4:]
    copies = [
        pltpu.make_async_copy(source, target, sems.at[i])
        for i, (source, target) in enumerate(zip(sources, (cur, off, *targets)))
    ]
    for copy in copies:
        copy.start()
    slots, links = targets[:2]
    seg_own, _, width = blocks.shape
    pan_group = pan_own * n_col
    r, c = lax.axis_index("row"), lax.axis_index("col")
    acc[...] = jnp.zeros_like(acc)
    levels = lax.broadcasted_iota(jnp.int32, (width, width), 0)
    for copy in copies[:4]:
        copy.wait()

    def block(k):
        span = pl.ds(pl.multiple_of(k * width, width), width)
        for e in range(2):
            lanes[pl.ds(2 * k + e, 1), :] = off[e : e + 1, span]
        to_hot = jnp.where(levels == off[0:1, span], 1.0, 0.0).astype(BF16)
        from_hot = jnp.where(levels == off[1:2, span], -1.0, 0.0).astype(BF16)
        hot = jnp.concatenate([to_hot, from_hot], axis=0)
        value = cur[:, span]
        blocks[k] = value
        sums = lax.dot_general(value, hot, (((1,), (1,)), ((), ())), preferred_element_type=F32)
        return sums.astype(BF16).astype(F32)

    unroll = 16

    def step(i, carry):
        got = [block(i * unroll + u) for u in range(unroll)]
        for u in range(unroll):
            for e in range(2):
                slot = slots[e, i * unroll + u]
                holder[slot] = 2 * (i * unroll + u) + e
                p = lax.div(slot, cap)
                b = links[p, slot - p * cap]
                acc[lax.bitwise_xor(p, r) * pan_group + b] += got[u][:, e * width : (e + 1) * width]
        return carry

    lax.fori_loop(0, seg_own // unroll, step, 0)
    for k in range(n_row):
        here = pl.ds(k * pan_own, pan_own)
        own[here] = acc[pl.ds(k * pan_group + c * pan_own, pan_own)]
        for j in range(1, n_col):
            there = lax.bitwise_xor(c, j)
            sends[j - 1][here] = acc[pl.ds(k * pan_group + there * pan_own, pan_own)].astype(BF16)
    for copy in copies[4:]:
        copy.wait()
    sort_tiles(targets[6], listed, seg_own)


def pick_body(n_row, n_col, cap, partners, _after, *refs):
    packs = {k: refs[i] for i, k in enumerate([*partners, 0])}
    own, peers = refs[n_row], refs[n_row + 1 : n_row + n_col]
    outs, asked = refs[n_row + n_col : -1], refs[-1]
    seg_own, rhs, width = own.shape
    r, c = lax.axis_index("row"), lax.axis_index("col")
    mine = lax.broadcasted_iota(jnp.int32, (rhs, width), 0) == r
    for k in range(n_row):
        needs = packs[k][packs[k].shape[0] - 1].astype(F32)
        asked[k : k + 1, :] = jnp.sum(jnp.where(mine, needs, 0.0), axis=0, keepdims=True).astype(jnp.int32)
    for k in range(n_row):
        for s in range(cap):
            b = asked[k, s]
            holder = lax.div(b, seg_own)
            b = b - holder * seg_own
            j = lax.bitwise_xor(holder, c)
            value = own[b]
            span = pl.ds(pl.multiple_of(b * width, width), width)
            for q, peer in enumerate(peers):
                value = jnp.where(j == q + 1, peer[:, span], value)
            outs[n_row - 1 - k][s] = value


def multiply(tiles, src, tile, source, row, acc, start, count):
    rhs, width = src.shape[1:]

    def products(first):
        got = []
        for i in (first, first + 2, first + 4, first + 6):
            left = jnp.concatenate([src[source(i)], src[source(i + 1)]], axis=0)
            right = jnp.concatenate([tiles[tile(i)], tiles[tile(i + 1)]], axis=1)
            both = jnp.dot(left, right, preferred_element_type=F32)
            got += [both[:rhs, :width], both[rhs:, width:]]
        return got

    def add(first, got):
        for u, value in enumerate(got):
            acc[row(first + u)] += value

    waiting = products(start)
    for first in range(8, count, 8):
        ahead = products(start + first)
        add(start + first - 8, waiting)
        waiting = ahead
    add(start + count - 8, waiting)


def coeff_body(n_row, n_col, pan_own, partners, slots, rows, needs, *refs):
    packs = {k: refs[i] for i, k in enumerate([*partners, 0])}
    ends = refs[n_row : n_row + n_col - 1]
    tiles, part, *messages = refs[n_row + n_col - 1 : -2]
    src, named = refs[-2:]
    r = lax.axis_index("row")
    pan_group = pan_own * n_col
    cap = needs.shape[1]
    for k in range(n_row):
        src[pl.ds(lax.bitwise_xor(r, k) * pan_group, pan_group)] = packs[k][pl.ds(0, pan_group)]
    for p in range(n_row):
        for s in range(cap):
            named[p * cap + s] = p * pan_group + needs[p, s]
    part[...] = jnp.zeros_like(part)
    multiply(tiles, src, lambda t: t, lambda t: named[slots[t]], lambda t: rows[t], part, 0, tiles.shape[0])
    high = part[...].astype(BF16)
    low = (part[...] - high.astype(F32)).astype(BF16)
    for message, sums in zip(messages, ends):
        message[pl.ds(0, pan_group)] = high
        message[pl.ds(pan_group, pan_group)] = low
        message[pl.ds(2 * pan_group, sums.shape[0])] = sums[...]


def induct_body(n_row, n_col, seg_own, order, half, slots, rows, listed, _after, *refs):
    got = {k: refs[i] for i, k in enumerate(order)}
    tiles = refs[n_row]
    outs, (src, acc) = refs[n_row + 1 : -2], refs[-2:]
    cap = got[0].shape[0]
    r, c = lax.axis_index("row"), lax.axis_index("col")
    for k in range(n_row):
        src[pl.ds(lax.bitwise_xor(r, k) * cap, cap)] = got[k][...]
    src[n_row * cap] = jnp.zeros(src.shape[1:], BF16)
    columns = range(1, n_col) if half == 0 else range(1)
    spans = [pl.ds(lax.bitwise_xor(c, j) * seg_own, seg_own) for j in columns]
    for span in spans:
        acc[span] = jnp.zeros((seg_own, *acc.shape[1:]), F32)
    size, run = list_size(tiles.shape[0]), first_run(tiles.shape[0])
    length = listed[2 * size + 2 + half]

    def tile(i):
        return listed[half * size + i]

    def source(i):
        return jnp.where(i < length, slots[tile(i)], n_row * cap)

    def row(i):
        return rows[tile(i)]

    multiply(tiles, src, tile, source, row, acc, 0, run)

    def step(i, carry):
        multiply(tiles, src, tile, source, row, acc, run + i * STEP, STEP)
        return carry

    lax.fori_loop(0, listed[2 * size + half], step, 0)
    for out, span in zip(outs, spans):
        out[...] = acc[span].astype(out.dtype)


def panels_body(n_row, n_col, pan_own, part, ends_own, *refs):
    parts = refs[: n_col - 1]
    pot, end_keep, *messages = refs[n_col - 1 :]
    pan_group = part.shape[0]
    total = part[...]
    for x in parts:
        total += x[pl.ds(0, pan_group)].astype(F32) + x[pl.ds(pan_group, pan_group)].astype(F32)
    rounded = total.astype(BF16)
    pot[...] = rounded
    for k in range(n_row):
        sums = ends_own[pl.ds(k * pan_own, pan_own)]
        for x in parts:
            sums += x[pl.ds(2 * pan_group + k * pan_own, pan_own)].astype(F32)
        if k == 0:
            end_keep[...] = sums
        else:
            messages[n_row - 1 - k][pl.ds(0, pan_own)] = sums.astype(BF16)
            messages[n_row - 1 - k][pl.ds(pan_own, pan_group)] = rounded


def hold_body(_after, message, out):
    out[...] = message[...]


def add_drops(p, pots, first, links, holder, lanes, field):
    cap = links.shape[1]
    ends, drops = [], []
    for s in range(cap):
        j = holder[p * cap + s]
        values = pots[first + links[p, s]].astype(F32)
        at = jnp.broadcast_to(lanes[pl.ds(j, 1), :], values.shape)
        drop = jnp.take_along_axis(values, at, axis=1, mode="promise_in_bounds")
        k = lax.div(j, 2)
        drops.append(drop * (1 - 2 * (j - 2 * k)).astype(F32))
        ends.append(k)
    for k, drop in zip(ends, drops):
        field[k] += drop


def base_body(pan_own, links, holder, scale, lanes, pack, field_own, end_own, pot, field, panels, pot_out):
    rhs, width = pot.shape[1:]
    r, c = lax.axis_index("row"), lax.axis_index("col")
    field[...] = field_own[...]
    row = lax.broadcasted_iota(jnp.int32, (rhs, width), 0)
    factor = jnp.zeros((rhs, width), F32)
    for i in range(rhs):
        factor = jnp.where(row == i, scale[i], factor)
    for q in range(pan_own):
        panels[q] = factor * pack[c * pan_own + q].astype(F32) + end_own[q]
        pot_out[:, q * width : (q + 1) * width] = pot[c * pan_own + q]
    add_drops(r, pot, 0, links, holder, lanes, field)


def drops_body(k, pan_own, links, holder, lanes, message, field_in, field):
    field[...] = field_in[...]
    p = lax.bitwise_xor(lax.axis_index("row"), k)
    add_drops(p, message, pan_own, links, holder, lanes, field)


def final_body(n_row, n_col, pan_own, links, holder, lanes, field_own, panels, *refs):
    arrived, field_in = refs[: n_row - 1], refs[n_row - 1 : n_row + n_col - 2]
    seg_out, pan_out, field, seg, pan, sems = refs[n_row + n_col - 2 :]
    seg_own, _, width = field.shape
    total = field_own[...]
    for x in field_in:
        total += x[...].astype(F32)
    field[...] = total
    p = lax.bitwise_xor(lax.axis_index("row"), 1)
    add_drops(p, arrived[0], pan_own, links, holder, lanes, field)
    for q in range(pan_own):
        total = panels[q]
        for x in arrived:
            total += x[q].astype(F32)
        pan[:, q * width : (q + 1) * width] = total.astype(BF16)
    chunks = sems.shape[0] - 1
    copies = [pltpu.make_async_copy(pan, pan_out, sems.at[chunks])]
    copies[0].start()
    size = seg_own // chunks
    for i in range(chunks):
        for k in range(i * size, (i + 1) * size):
            seg[:, k * width : (k + 1) * width] = field[k].astype(BF16)
        part = pl.ds(i * size * width, size * width)
        copies.append(pltpu.make_async_copy(seg.at[:, part], seg_out.at[:, part], sems.at[i]))
        copies[-1].start()
    for copy in copies:
        copy.wait()


def shards(
    current,
    charge,
    rhs_scale,
    induct_tiles,
    induct_rows,
    induct_slots,
    induct_needs,
    coeff_tiles,
    coeff_rows,
    coeff_slots,
    coeff_needs,
    link_needs,
    end_slots,
    end_offsets,
):
    n_row = lax.axis_size("row")
    n_col = lax.axis_size("col")
    width = induct_tiles.shape[1]
    rhs = current.shape[0]
    seg_own = current.shape[1] // width
    pan_own = charge.shape[1] // width
    seg_group, pan_group = seg_own * n_col, pan_own * n_col
    cap_l, cap_p, cap_k = induct_needs.shape[1], coeff_needs.shape[1], link_needs.shape[1]
    slots_t, off_t = end_slots.T, end_offsets.T

    partners = [*reversed(range(1, n_row))]
    partners[:2] = partners[1::-1]

    def like(blocks, dtype):
        return jax.ShapeDtypeStruct((blocks, rhs, width), dtype)

    charges = exchange_all(charge, [charge] * (n_col - 1), "col")
    cur = exchange_all(current, [current] * (n_col - 1), "col")
    (pack,) = call(
        functools.partial(pack_body, pan_own),
        "pack_charges",
        [like(pan_own + 1, BF16)],
        [VMEM] * 2,
        [pltpu.VMEM((rhs, width), jnp.int32)],
        moved=2**16,
    )(*in_hbm(charge, induct_needs))
    (pack,) = call(
        functools.partial(join_body, pan_own),
        "join_charges",
        [like(pan_group + 1, BF16)],
        [VMEM] * n_col,
        moved=2**16,
    )(pack, *charges[1:])
    packs = exchange_all(pack, [pack] * (n_row - 1), "row")

    rows_own = n_row * pan_own
    scalars = [slots_t, link_needs, coeff_slots, coeff_rows, coeff_needs, induct_slots, induct_rows, rhs_scale]
    moved = [*scalars, coeff_tiles]
    outs = call(
        functools.partial(ends_body, n_row, n_col, pan_own, cap_k, len(moved)),
        "end_sums",
        [pltpu.SMEM(x.shape, x.dtype) for x in scalars]
        + [jax.ShapeDtypeStruct(coeff_tiles.shape, BF16)]
        + [pltpu.SMEM((2 * seg_own,), jnp.int32), pltpu.SMEM((2 * list_size(induct_rows.shape[0]) + 4,), jnp.int32)]
        + [jax.ShapeDtypeStruct((2 * seg_own, width), jnp.int32)]
        + [like(seg_own, BF16), like(rows_own, F32)]
        + [like(rows_own, BF16)] * (n_col - 1),
        [ANY] * (len(moved) + 2),
        [
            pltpu.VMEM(current.shape, BF16),
            pltpu.VMEM(off_t.shape, jnp.int32),
            pltpu.VMEM((n_row * pan_group, rhs, width), F32),
            pltpu.SemaphoreType.DMA((len(moved) + 2,)),
        ],
        flops=5 * 10**8,
        moved=2**18,
        out_specs=[SMEM] * len(scalars) + [VMEM, SMEM, SMEM] + [VMEM] * (2 + n_col),
    )(*in_hbm(current, off_t, *moved))
    _, links_s, coeff_slots, coeff_rows, coeff_needs, induct_slots, induct_rows, scale, coeff_tiles = outs[: len(moved)]
    holder, listed, lanes, own_blocks, ends_own, *ends_out = outs[len(moved) :]

    part, *messages = call(
        functools.partial(coeff_body, n_row, n_col, pan_own, partners),
        "coeff_tiles",
        [like(pan_group, F32)] + [like(2 * pan_group + rows_own, BF16)] * (n_col - 1),
        [SMEM] * 3 + [VMEM] * (n_row + n_col),
        [
            pltpu.VMEM((n_row * pan_group, rhs, width), BF16),
            pltpu.SMEM((n_row * cap_p,), jnp.int32),
        ],
        flops=10**9,
        moved=coeff_tiles.size * 2,
    )(coeff_slots, coeff_rows, coeff_needs, *[packs[k] for k in partners], packs[0], *ends_out, coeff_tiles)
    parts = exchange_all(None, messages, "col")[1:]

    *picks, own_picks = call(
        functools.partial(pick_body, n_row, n_col, cap_l, partners),
        "pick_blocks",
        [like(cap_l, BF16)] * n_row,
        [ANY] + [VMEM] * (n_row + n_col),
        [pltpu.VMEM((n_row, width), jnp.int32)],
        moved=2**18,
    )(part, *[packs[k] for k in partners], packs[0], own_blocks, *cur[1:])
    got = exchange_all(own_picks, picks[::-1], "row")

    pot, end_keep, *row_messages = call(
        functools.partial(panels_body, n_row, n_col, pan_own),
        "panel_sums",
        [like(pan_group, BF16), like(pan_own, F32)] + [like(pan_own + pan_group, BF16)] * (n_row - 1),
        [VMEM] * (1 + n_col),
        flops=10**9,
        moved=2**18,
    )(part, ends_own, *parts)

    order = [*partners[1:], 0, partners[0]]

    def induct(name, half, outs, after):
        return call(
            functools.partial(induct_body, n_row, n_col, seg_own, order, half),
            name,
            outs,
            [SMEM] * 3 + [ANY] + [VMEM] * (n_row + 1),
            [
                pltpu.VMEM((n_row * cap_l + 1, rhs, width), BF16),
                pltpu.VMEM((seg_group, rhs, width), F32),
            ],
            flops=10**8,
            moved=2**16,
        )(induct_slots, induct_rows, listed, after, *[got[k] for k in order], induct_tiles)

    field_out = induct("induct_away", 0, [like(seg_own, BF16)] * (n_col - 1), pot)
    field_in = exchange_all(None, field_out, "col")[1:]

    (row_messages[-1],) = call(
        hold_body,
        "hold_near",
        [like(pan_own + pan_group, BF16)],
        [ANY, VMEM],
        moved=2**16,
    )(field_out[0], row_messages[-1])
    arrived = exchange_all(None, row_messages[::-1], "row")[1:]
    (field_own,) = induct("induct_own", 1, [like(seg_own, F32)], row_messages[-1])

    field, panels, pot_out = call(
        functools.partial(base_body, pan_own),
        "base_sums",
        [like(seg_own, F32), like(pan_own, F32), jax.ShapeDtypeStruct(charge.shape, BF16)],
        [SMEM] * 3 + [VMEM] * 5,
        flops=0,
        moved=0,
    )(links_s, holder, scale, lanes, pack, field_own, end_keep, pot)

    for k in reversed(range(2, n_row)):
        (field,) = call(
            functools.partial(drops_body, k, pan_own),
            "add_drops",
            [like(seg_own, F32)],
            [SMEM] * 2 + [VMEM] * 3,
            flops=11 * 10**8 if k == 2 else 0,
            moved=0,
        )(links_s, holder, lanes, arrived[k - 1], field)

    seg_out, pan_out = call(
        functools.partial(final_body, n_row, n_col, pan_own),
        "outputs",
        [jax.ShapeDtypeStruct(x.shape, BF16) for x in (current, charge)],
        [SMEM] * 2 + [VMEM] * (1 + n_row + n_col),
        [
            pltpu.VMEM((seg_own, rhs, width), F32),
            pltpu.VMEM(current.shape, BF16),
            pltpu.VMEM(charge.shape, BF16),
            pltpu.SemaphoreType.DMA((3,)),
        ],
        flops=10**9,
        moved=2**20,
        out_specs=[ANY, ANY],
    )(links_s, holder, lanes, field, panels, *arrived, *field_in)
    return (seg_out, pan_out, pot_out)


def solution(mesh):
    blocks = P(("parts", "row", "col"))
    matrix = P(("parts", "row", "col"), None)
    tiles = P(("parts", "row", "col"), None, None)
    values = P("rhs", ("parts", "row", "col"))
    return jax.shard_map(
        shards,
        mesh=mesh,
        in_specs=(
            values,
            values,
            P(("parts", "rhs")),
            tiles,
            blocks,
            blocks,
            matrix,
            tiles,
            blocks,
            blocks,
            matrix,
            matrix,
            matrix,
            matrix,
        ),
        out_specs=(values, values, values),
        check_vma=False,
    )
```

```python
import functools

import jax
import jax.numpy as jnp
from jax import lax
from jax.experimental import pallas as pl
from jax.experimental.pallas import tpu as pltpu
from jax.sharding import PartitionSpec as P

F32 = jnp.float32
BF16 = jnp.bfloat16
VMEM = pl.BlockSpec(memory_space=pltpu.VMEM)
SMEM = pl.BlockSpec(memory_space=pltpu.SMEM)
ANY = pl.BlockSpec(memory_space=pl.ANY)


def exchange(x, axis, k):
    if k == 0:
        return x
    return lax.ppermute(x, axis, [(i, i ^ k) for i in range(lax.axis_size(axis))])


def exchange_all(first, others, axis):
    n = lax.axis_size(axis)
    got = {0: first}
    for k in reversed(range(1, n)):
        got[k] = exchange(others[k - 1], axis, k)
    return [got[k] for k in range(n)]


def call(body, name, out_shape, in_specs, scratch=(), flops=0, moved=0, out_specs=None):
    return pl.pallas_call(
        body,
        out_shape=out_shape,
        in_specs=in_specs,
        out_specs=out_specs or [VMEM] * len(out_shape),
        scratch_shapes=list(scratch),
        compiler_params=pltpu.CompilerParams(vmem_limit_bytes=16 * 2**20),
        cost_estimate=pl.CostEstimate(flops=flops, bytes_accessed=moved, transcendentals=0),
        name=name,
    )


def in_hbm(*arrays):
    return [pltpu.with_memory_space_constraint(x, pltpu.HBM) for x in arrays]


def pack_body(pan_own, seg_own, charge, needs, rows, message, listed, wide):
    width = charge.shape[1] // pan_own
    for q in range(pan_own):
        message[q] = charge[:, q * width : (q + 1) * width]
    wide[...] = jnp.zeros_like(wide)
    wide[: needs.shape[0], : needs.shape[1]] = needs[...]
    message[pan_own] = wide[...].astype(F32).astype(BF16)
    sort_tiles(rows, listed, seg_own)


def join_body(pan_own, own, *refs):
    others, message = refs[:-1], refs[-1]
    c = lax.axis_index("col")
    width = own.shape[2]
    message[pl.ds(c * pan_own, pan_own)] = own[pl.ds(0, pan_own)]
    for j, x in enumerate(others):
        first = lax.bitwise_xor(c, j + 1) * pan_own
        for q in range(pan_own):
            message[first + q] = x[:, q * width : (q + 1) * width]
    message[message.shape[0] - 1] = own[pan_own]


STEP = 16


def list_size(count):
    return count + STEP


def first_run(count):
    return count // 2 // STEP * STEP


def sort_tiles(rows, listed, seg_own):
    count = rows.shape[0]
    size, run = list_size(count), first_run(count)
    base = lax.axis_index("col") * seg_own

    def step(i, here):
        for u in range(16):
            t = i * 16 + u
            inside = rows[t] - base
            mine = jnp.logical_and(inside >= 0, inside < seg_own)
            listed[jnp.where(mine, size + here, t - here)] = t
            here = here + mine.astype(jnp.int32)
        return here

    here = lax.fori_loop(0, count // 16, step, jnp.int32(0))
    for half, n in enumerate((count - here, here)):
        steps = lax.max(lax.div(n - run + STEP - 1, STEP), 0)

        def fill(i, carry, half=half):
            listed[half * size + i] = 0
            return carry

        lax.fori_loop(n, run + steps * STEP, fill, 0)
        listed[2 * size + half] = steps
        listed[2 * size + 2 + half] = n


def ends_body(n_row, n_col, pan_own, cap, n_moved, *refs):
    sources, targets = refs[: n_moved + 2], refs[n_moved + 2 : 2 * n_moved + 2]
    (holder, lanes, blocks, own, *sends), (cur, off, acc, sems) = refs[2 * n_moved + 2 : -4], refs[-4:]
    copies = [
        pltpu.make_async_copy(source, target, sems.at[i])
        for i, (source, target) in enumerate(zip(sources, (cur, off, *targets)))
    ]
    for copy in copies:
        copy.start()
    slots, links = targets[:2]
    seg_own, _, width = blocks.shape
    pan_group = pan_own * n_col
    r, c = lax.axis_index("row"), lax.axis_index("col")
    acc[...] = jnp.zeros_like(acc)
    levels = lax.broadcasted_iota(jnp.int32, (width, width), 0)
    for copy in copies[:4]:
        copy.wait()

    def block(k):
        span = pl.ds(pl.multiple_of(k * width, width), width)
        for e in range(2):
            lanes[pl.ds(2 * k + e, 1), :] = off[e : e + 1, span]
        to_hot = jnp.where(levels == off[0:1, span], 1.0, 0.0).astype(BF16)
        from_hot = jnp.where(levels == off[1:2, span], -1.0, 0.0).astype(BF16)
        hot = jnp.concatenate([to_hot, from_hot], axis=0)
        value = cur[:, span]
        blocks[k] = value
        sums = lax.dot_general(value, hot, (((1,), (1,)), ((), ())), preferred_element_type=F32)
        return sums.astype(BF16).astype(F32)

    unroll = 16

    def step(i, carry):
        got = [block(i * unroll + u) for u in range(unroll)]
        for u in range(unroll):
            for e in range(2):
                slot = slots[e, i * unroll + u]
                holder[slot] = 2 * (i * unroll + u) + e
                p = lax.div(slot, cap)
                b = links[p, slot - p * cap]
                acc[lax.bitwise_xor(p, r) * pan_group + b] += got[u][:, e * width : (e + 1) * width]
        return carry

    lax.fori_loop(0, seg_own // unroll, step, 0)
    for k in range(n_row):
        here = pl.ds(k * pan_own, pan_own)
        own[here] = acc[pl.ds(k * pan_group + c * pan_own, pan_own)]
        for j in range(1, n_col):
            there = lax.bitwise_xor(c, j)
            sends[j - 1][here] = acc[pl.ds(k * pan_group + there * pan_own, pan_own)].astype(BF16)
    for copy in copies[4:]:
        copy.wait()


def pick_body(n_row, n_col, cap, partners, _after, *refs):
    packs = {k: refs[i] for i, k in enumerate([*partners, 0])}
    own, peers = refs[n_row], refs[n_row + 1 : n_row + n_col]
    outs, asked = refs[n_row + n_col : -1], refs[-1]
    seg_own, rhs, width = own.shape
    r, c = lax.axis_index("row"), lax.axis_index("col")
    mine = lax.broadcasted_iota(jnp.int32, (rhs, width), 0) == r
    for k in range(n_row):
        needs = packs[k][packs[k].shape[0] - 1].astype(F32)
        asked[k : k + 1, :] = jnp.sum(jnp.where(mine, needs, 0.0), axis=0, keepdims=True).astype(jnp.int32)
    for k in range(n_row):
        for s in range(cap):
            b = asked[k, s]
            holder = lax.div(b, seg_own)
            b = b - holder * seg_own
            j = lax.bitwise_xor(holder, c)
            value = own[b]
            span = pl.ds(pl.multiple_of(b * width, width), width)
            for q, peer in enumerate(peers):
                value = jnp.where(j == q + 1, peer[:, span], value)
            outs[n_row - 1 - k][s] = value


def multiply(tiles, src, tile, source, row, acc, start, count):
    rhs, width = src.shape[1:]

    def products(first):
        got = []
        for i in (first, first + 2, first + 4, first + 6):
            left = jnp.concatenate([src[source(i)], src[source(i + 1)]], axis=0)
            right = jnp.concatenate([tiles[tile(i)], tiles[tile(i + 1)]], axis=1)
            both = jnp.dot(left, right, preferred_element_type=F32)
            got += [both[:rhs, :width], both[rhs:, width:]]
        return got

    def add(first, got):
        for u, value in enumerate(got):
            acc[row(first + u)] += value

    waiting = products(start)
    for first in range(8, count, 8):
        ahead = products(start + first)
        add(start + first - 8, waiting)
        waiting = ahead
    add(start + count - 8, waiting)


def coeff_body(n_row, n_col, pan_own, partners, slots, rows, needs, *refs):
    packs = {k: refs[i] for i, k in enumerate([*partners, 0])}
    ends = refs[n_row : n_row + n_col - 1]
    tiles, part, *messages = refs[n_row + n_col - 1 : -2]
    src, named = refs[-2:]
    r = lax.axis_index("row")
    pan_group = pan_own * n_col
    cap = needs.shape[1]
    for k in range(n_row):
        src[pl.ds(lax.bitwise_xor(r, k) * pan_group, pan_group)] = packs[k][pl.ds(0, pan_group)]
    for p in range(n_row):
        for s in range(cap):
            named[p * cap + s] = p * pan_group + needs[p, s]
    part[...] = jnp.zeros_like(part)
    multiply(tiles, src, lambda t: t, lambda t: named[slots[t]], lambda t: rows[t], part, 0, tiles.shape[0])
    high = part[...].astype(BF16)
    low = (part[...] - high.astype(F32)).astype(BF16)
    for message, sums in zip(messages, ends):
        message[pl.ds(0, pan_group)] = high
        message[pl.ds(pan_group, pan_group)] = low
        message[pl.ds(2 * pan_group, sums.shape[0])] = sums[...]


def induct_body(n_row, n_col, seg_own, order, half, slots, rows, listed, _after, *refs):
    got = {k: refs[i] for i, k in enumerate(order)}
    tiles = refs[n_row]
    outs, (src, acc) = refs[n_row + 1 : -2], refs[-2:]
    cap = got[0].shape[0]
    r, c = lax.axis_index("row"), lax.axis_index("col")
    for k in range(n_row):
        src[pl.ds(lax.bitwise_xor(r, k) * cap, cap)] = got[k][...]
    src[n_row * cap] = jnp.zeros(src.shape[1:], BF16)
    columns = range(1, n_col) if half == 0 else range(1)
    spans = [pl.ds(lax.bitwise_xor(c, j) * seg_own, seg_own) for j in columns]
    for span in spans:
        acc[span] = jnp.zeros((seg_own, *acc.shape[1:]), F32)
    size, run = list_size(tiles.shape[0]), first_run(tiles.shape[0])
    length = listed[2 * size + 2 + half]

    def tile(i):
        return listed[half * size + i]

    def source(i):
        return jnp.where(i < length, slots[tile(i)], n_row * cap)

    def row(i):
        return rows[tile(i)]

    multiply(tiles, src, tile, source, row, acc, 0, run)

    def step(i, carry):
        multiply(tiles, src, tile, source, row, acc, run + i * STEP, STEP)
        return carry

    lax.fori_loop(0, listed[2 * size + half], step, 0)
    for out, span in zip(outs, spans):
        out[...] = acc[span].astype(out.dtype)


def panels_body(n_row, n_col, pan_own, part, ends_own, *refs):
    parts = refs[: n_col - 1]
    pot, end_keep, *messages = refs[n_col - 1 :]
    pan_group = part.shape[0]
    total = part[...]
    for x in parts:
        total += x[pl.ds(0, pan_group)].astype(F32) + x[pl.ds(pan_group, pan_group)].astype(F32)
    rounded = total.astype(BF16)
    pot[...] = rounded
    for k in range(n_row):
        sums = ends_own[pl.ds(k * pan_own, pan_own)]
        for x in parts:
            sums += x[pl.ds(2 * pan_group + k * pan_own, pan_own)].astype(F32)
        if k == 0:
            end_keep[...] = sums
        else:
            messages[n_row - 1 - k][pl.ds(0, pan_own)] = sums.astype(BF16)
            messages[n_row - 1 - k][pl.ds(pan_own, pan_group)] = rounded


def hold_body(_after, message, out):
    out[...] = message[...]


def add_drops(p, pots, first, links, holder, lanes, field):
    cap = links.shape[1]
    ends, drops = [], []
    for s in range(cap):
        j = holder[p * cap + s]
        values = pots[first + links[p, s]].astype(F32)
        at = jnp.broadcast_to(lanes[pl.ds(j, 1), :], values.shape)
        drop = jnp.take_along_axis(values, at, axis=1, mode="promise_in_bounds")
        k = lax.div(j, 2)
        drops.append(drop * (1 - 2 * (j - 2 * k)).astype(F32))
        ends.append(k)
    for k, drop in zip(ends, drops):
        field[k] += drop


def base_body(pan_own, links, holder, scale, lanes, pack, field_own, end_own, pot, field, panels, pot_out):
    rhs, width = pot.shape[1:]
    r, c = lax.axis_index("row"), lax.axis_index("col")
    field[...] = field_own[...]
    row = lax.broadcasted_iota(jnp.int32, (rhs, width), 0)
    factor = jnp.zeros((rhs, width), F32)
    for i in range(rhs):
        factor = jnp.where(row == i, scale[i], factor)
    for q in range(pan_own):
        panels[q] = factor * pack[c * pan_own + q].astype(F32) + end_own[q]
        pot_out[:, q * width : (q + 1) * width] = pot[c * pan_own + q]
    add_drops(r, pot, 0, links, holder, lanes, field)


def drops_body(k, pan_own, links, holder, lanes, message, field_in, field):
    field[...] = field_in[...]
    p = lax.bitwise_xor(lax.axis_index("row"), k)
    add_drops(p, message, pan_own, links, holder, lanes, field)


def final_body(n_row, n_col, pan_own, links, holder, lanes, field_own, panels, *refs):
    arrived, field_in = refs[: n_row - 1], refs[n_row - 1 : n_row + n_col - 2]
    seg_out, pan_out, field, seg, pan, sems = refs[n_row + n_col - 2 :]
    seg_own, _, width = field.shape
    total = field_own[...]
    for x in field_in:
        total += x[...].astype(F32)
    field[...] = total
    p = lax.bitwise_xor(lax.axis_index("row"), 1)
    add_drops(p, arrived[0], pan_own, links, holder, lanes, field)
    for q in range(pan_own):
        total = panels[q]
        for x in arrived:
            total += x[q].astype(F32)
        pan[:, q * width : (q + 1) * width] = total.astype(BF16)
    chunks = sems.shape[0] - 1
    copies = [pltpu.make_async_copy(pan, pan_out, sems.at[chunks])]
    copies[0].start()
    size = seg_own // chunks
    for i in range(chunks):
        for k in range(i * size, (i + 1) * size):
            seg[:, k * width : (k + 1) * width] = field[k].astype(BF16)
        part = pl.ds(i * size * width, size * width)
        copies.append(pltpu.make_async_copy(seg.at[:, part], seg_out.at[:, part], sems.at[i]))
        copies[-1].start()
    for copy in copies:
        copy.wait()


def shards(
    current,
    charge,
    rhs_scale,
    induct_tiles,
    induct_rows,
    induct_slots,
    induct_needs,
    coeff_tiles,
    coeff_rows,
    coeff_slots,
    coeff_needs,
    link_needs,
    end_slots,
    end_offsets,
):
    n_row = lax.axis_size("row")
    n_col = lax.axis_size("col")
    width = induct_tiles.shape[1]
    rhs = current.shape[0]
    seg_own = current.shape[1] // width
    pan_own = charge.shape[1] // width
    seg_group, pan_group = seg_own * n_col, pan_own * n_col
    cap_l, cap_p, cap_k = induct_needs.shape[1], coeff_needs.shape[1], link_needs.shape[1]
    slots_t, off_t = end_slots.T, end_offsets.T

    partners = [*reversed(range(1, n_row))]
    partners[:2] = partners[1::-1]

    def like(blocks, dtype):
        return jax.ShapeDtypeStruct((blocks, rhs, width), dtype)

    charges = exchange_all(charge, [charge] * (n_col - 1), "col")
    cur = exchange_all(current, [current] * (n_col - 1), "col")
    pack, listed = call(
        functools.partial(pack_body, pan_own, seg_own),
        "pack_charges",
        [like(pan_own + 1, BF16), pltpu.SMEM((2 * list_size(induct_rows.shape[0]) + 4,), jnp.int32)],
        [VMEM, VMEM, SMEM],
        [pltpu.VMEM((rhs, width), jnp.int32)],
        moved=2**16,
        out_specs=[VMEM, SMEM],
    )(*in_hbm(charge, induct_needs, induct_rows))
    (pack,) = call(
        functools.partial(join_body, pan_own),
        "join_charges",
        [like(pan_group + 1, BF16)],
        [VMEM] * n_col,
        moved=2**16,
    )(pack, *charges[1:])
    packs = exchange_all(pack, [pack] * (n_row - 1), "row")

    rows_own = n_row * pan_own
    scalars = [slots_t, link_needs, coeff_slots, coeff_rows, coeff_needs, induct_slots, induct_rows, rhs_scale]
    moved = [*scalars, coeff_tiles]
    outs = call(
        functools.partial(ends_body, n_row, n_col, pan_own, cap_k, len(moved)),
        "end_sums",
        [pltpu.SMEM(x.shape, x.dtype) for x in scalars]
        + [jax.ShapeDtypeStruct(coeff_tiles.shape, BF16)]
        + [pltpu.SMEM((2 * seg_own,), jnp.int32)]
        + [jax.ShapeDtypeStruct((2 * seg_own, width), jnp.int32)]
        + [like(seg_own, BF16), like(rows_own, F32)]
        + [like(rows_own, BF16)] * (n_col - 1),
        [ANY] * (len(moved) + 2),
        [
            pltpu.VMEM(current.shape, BF16),
            pltpu.VMEM(off_t.shape, jnp.int32),
            pltpu.VMEM((n_row * pan_group, rhs, width), F32),
            pltpu.SemaphoreType.DMA((len(moved) + 2,)),
        ],
        flops=5 * 10**8,
        moved=2**18,
        out_specs=[SMEM] * len(scalars) + [VMEM, SMEM] + [VMEM] * (2 + n_col),
    )(*in_hbm(current, off_t, *moved))
    _, links_s, coeff_slots, coeff_rows, coeff_needs, induct_slots, induct_rows, scale, coeff_tiles = outs[: len(moved)]
    holder, lanes, own_blocks, ends_own, *ends_out = outs[len(moved) :]

    part, *messages = call(
        functools.partial(coeff_body, n_row, n_col, pan_own, partners),
        "coeff_tiles",
        [like(pan_group, F32)] + [like(2 * pan_group + rows_own, BF16)] * (n_col - 1),
        [SMEM] * 3 + [VMEM] * (n_row + n_col),
        [
            pltpu.VMEM((n_row * pan_group, rhs, width), BF16),
            pltpu.SMEM((n_row * cap_p,), jnp.int32),
        ],
        flops=10**9,
        moved=coeff_tiles.size * 2,
    )(coeff_slots, coeff_rows, coeff_needs, *[packs[k] for k in partners], packs[0], *ends_out, coeff_tiles)
    parts = exchange_all(None, messages, "col")[1:]

    *picks, own_picks = call(
        functools.partial(pick_body, n_row, n_col, cap_l, partners),
        "pick_blocks",
        [like(cap_l, BF16)] * n_row,
        [ANY] + [VMEM] * (n_row + n_col),
        [pltpu.VMEM((n_row, width), jnp.int32)],
        moved=2**18,
    )(part, *[packs[k] for k in partners], packs[0], own_blocks, *cur[1:])
    got = exchange_all(own_picks, picks[::-1], "row")

    pot, end_keep, *row_messages = call(
        functools.partial(panels_body, n_row, n_col, pan_own),
        "panel_sums",
        [like(pan_group, BF16), like(pan_own, F32)] + [like(pan_own + pan_group, BF16)] * (n_row - 1),
        [VMEM] * (1 + n_col),
        flops=10**9,
        moved=2**18,
    )(part, ends_own, *parts)

    order = [*partners[1:], 0, partners[0]]

    def induct(name, half, outs, after):
        return call(
            functools.partial(induct_body, n_row, n_col, seg_own, order, half),
            name,
            outs,
            [SMEM] * 3 + [ANY] + [VMEM] * (n_row + 1),
            [
                pltpu.VMEM((n_row * cap_l + 1, rhs, width), BF16),
                pltpu.VMEM((seg_group, rhs, width), F32),
            ],
            flops=10**8,
            moved=2**16,
        )(induct_slots, induct_rows, listed, after, *[got[k] for k in order], induct_tiles)

    field_out = induct("induct_away", 0, [like(seg_own, BF16)] * (n_col - 1), pot)
    field_in = exchange_all(None, field_out, "col")[1:]

    (row_messages[-1],) = call(
        hold_body,
        "hold_near",
        [like(pan_own + pan_group, BF16)],
        [ANY, VMEM],
        moved=2**16,
    )(field_out[0], row_messages[-1])
    arrived = exchange_all(None, row_messages[::-1], "row")[1:]
    (field_own,) = induct("induct_own", 1, [like(seg_own, F32)], row_messages[-1])

    field, panels, pot_out = call(
        functools.partial(base_body, pan_own),
        "base_sums",
        [like(seg_own, F32), like(pan_own, F32), jax.ShapeDtypeStruct(charge.shape, BF16)],
        [SMEM] * 3 + [VMEM] * 5,
        flops=0,
        moved=0,
    )(links_s, holder, scale, lanes, pack, field_own, end_keep, pot)

    for k in reversed(range(2, n_row)):
        (field,) = call(
            functools.partial(drops_body, k, pan_own),
            "add_drops",
            [like(seg_own, F32)],
            [SMEM] * 2 + [VMEM] * 3,
            flops=11 * 10**8 if k == 2 else 0,
            moved=0,
        )(links_s, holder, lanes, arrived[k - 1], field)

    seg_out, pan_out = call(
        functools.partial(final_body, n_row, n_col, pan_own),
        "outputs",
        [jax.ShapeDtypeStruct(x.shape, BF16) for x in (current, charge)],
        [SMEM] * 2 + [VMEM] * (1 + n_row + n_col),
        [
            pltpu.VMEM((seg_own, rhs, width), F32),
            pltpu.VMEM(current.shape, BF16),
            pltpu.VMEM(charge.shape, BF16),
            pltpu.SemaphoreType.DMA((3,)),
        ],
        flops=10**9,
        moved=2**20,
        out_specs=[ANY, ANY],
    )(links_s, holder, lanes, field, panels, *arrived, *field_in)
    return (seg_out, pan_out, pot_out)


def solution(mesh):
    blocks = P(("parts", "row", "col"))
    matrix = P(("parts", "row", "col"), None)
    tiles = P(("parts", "row", "col"), None, None)
    values = P("rhs", ("parts", "row", "col"))
    return jax.shard_map(
        shards,
        mesh=mesh,
        in_specs=(
            values,
            values,
            P(("parts", "rhs")),
            tiles,
            blocks,
            blocks,
            matrix,
            tiles,
            blocks,
            blocks,
            matrix,
            matrix,
            matrix,
            matrix,
        ),
        out_specs=(values, values, values),
        check_vma=False,
    )
```

```python
import functools

import jax
import jax.numpy as jnp
from jax import lax
from jax.experimental import pallas as pl
from jax.experimental.pallas import tpu as pltpu
from jax.sharding import PartitionSpec as P

F32 = jnp.float32
BF16 = jnp.bfloat16
VMEM = pl.BlockSpec(memory_space=pltpu.VMEM)
SMEM = pl.BlockSpec(memory_space=pltpu.SMEM)
ANY = pl.BlockSpec(memory_space=pl.ANY)


def exchange(x, axis, k):
    if k == 0:
        return x
    return lax.ppermute(x, axis, [(i, i ^ k) for i in range(lax.axis_size(axis))])


def exchange_all(first, others, axis):
    n = lax.axis_size(axis)
    got = {0: first}
    for k in reversed(range(1, n)):
        got[k] = exchange(others[k - 1], axis, k)
    return [got[k] for k in range(n)]


def call(body, name, out_shape, in_specs, scratch=(), flops=0, moved=0, out_specs=None):
    return pl.pallas_call(
        body,
        out_shape=out_shape,
        in_specs=in_specs,
        out_specs=out_specs or [VMEM] * len(out_shape),
        scratch_shapes=list(scratch),
        compiler_params=pltpu.CompilerParams(vmem_limit_bytes=16 * 2**20),
        cost_estimate=pl.CostEstimate(flops=flops, bytes_accessed=moved, transcendentals=0),
        name=name,
    )


def in_hbm(*arrays):
    return [pltpu.with_memory_space_constraint(x, pltpu.HBM) for x in arrays]


def pack_body(pan_own, seg_own, charge, needs, rows, message, listed, wide):
    width = charge.shape[1] // pan_own
    for q in range(pan_own):
        message[q] = charge[:, q * width : (q + 1) * width]
    wide[...] = jnp.zeros_like(wide)
    wide[: needs.shape[0], : needs.shape[1]] = needs[...]
    message[pan_own] = wide[...].astype(F32).astype(BF16)
    sort_tiles(rows, listed, seg_own)


def join_body(pan_own, own, *refs):
    others, message = refs[:-1], refs[-1]
    c = lax.axis_index("col")
    width = own.shape[2]
    message[pl.ds(c * pan_own, pan_own)] = own[pl.ds(0, pan_own)]
    for j, x in enumerate(others):
        first = lax.bitwise_xor(c, j + 1) * pan_own
        for q in range(pan_own):
            message[first + q] = x[:, q * width : (q + 1) * width]
    message[message.shape[0] - 1] = own[pan_own]


STEP = 16


def list_size(count):
    return count + STEP


def first_run(count):
    return count * 7 // 12 // STEP * STEP


def sort_tiles(rows, listed, seg_own):
    count = rows.shape[0]
    size, run = list_size(count), first_run(count)
    base = lax.axis_index("col") * seg_own

    def step(i, here):
        for u in range(16):
            t = i * 16 + u
            inside = rows[t] - base
            mine = jnp.logical_and(inside >= 0, inside < seg_own)
            listed[jnp.where(mine, size + here, t - here)] = t
            here = here + mine.astype(jnp.int32)
        return here

    here = lax.fori_loop(0, count // 16, step, jnp.int32(0))
    for half, n in enumerate((count - here, here)):
        steps = lax.max(lax.div(n - run + STEP - 1, STEP), 0)

        def fill(i, carry, half=half):
            listed[half * size + i] = 0
            return carry

        lax.fori_loop(n, run + steps * STEP, fill, 0)
        listed[2 * size + half] = steps
        listed[2 * size + 2 + half] = n


def ends_body(n_row, n_col, pan_own, cap, n_moved, *refs):
    sources, targets = refs[: n_moved + 2], refs[n_moved + 2 : 2 * n_moved + 2]
    (holder, named, lanes, blocks, own, *sends), (cur, off, acc, sems) = refs[2 * n_moved + 2 : -4], refs[-4:]
    copies = [
        pltpu.make_async_copy(source, target, sems.at[i])
        for i, (source, target) in enumerate(zip(sources, (cur, off, *targets)))
    ]
    for copy in copies:
        copy.start()
    slots, links = targets[:2]
    seg_own, _, width = blocks.shape
    pan_group = pan_own * n_col
    r, c = lax.axis_index("row"), lax.axis_index("col")
    acc[...] = jnp.zeros_like(acc)
    levels = lax.broadcasted_iota(jnp.int32, (width, width), 0)
    for copy in copies[:4]:
        copy.wait()

    def block(k):
        span = pl.ds(pl.multiple_of(k * width, width), width)
        for e in range(2):
            lanes[pl.ds(2 * k + e, 1), :] = off[e : e + 1, span]
        to_hot = jnp.where(levels == off[0:1, span], 1.0, 0.0).astype(BF16)
        from_hot = jnp.where(levels == off[1:2, span], -1.0, 0.0).astype(BF16)
        hot = jnp.concatenate([to_hot, from_hot], axis=0)
        value = cur[:, span]
        blocks[k] = value
        sums = lax.dot_general(value, hot, (((1,), (1,)), ((), ())), preferred_element_type=F32)
        return sums.astype(BF16).astype(F32)

    unroll = 16

    def step(i, carry):
        got = [block(i * unroll + u) for u in range(unroll)]
        for u in range(unroll):
            for e in range(2):
                slot = slots[e, i * unroll + u]
                holder[slot] = 2 * (i * unroll + u) + e
                p = lax.div(slot, cap)
                b = links[p, slot - p * cap]
                acc[lax.bitwise_xor(p, r) * pan_group + b] += got[u][:, e * width : (e + 1) * width]
        return carry

    lax.fori_loop(0, seg_own // unroll, step, 0)
    for k in range(n_row):
        here = pl.ds(k * pan_own, pan_own)
        own[here] = acc[pl.ds(k * pan_group + c * pan_own, pan_own)]
        for j in range(1, n_col):
            there = lax.bitwise_xor(c, j)
            sends[j - 1][here] = acc[pl.ds(k * pan_group + there * pan_own, pan_own)].astype(BF16)
    for copy in copies[4:]:
        copy.wait()
    needs = targets[4]
    for p in range(n_row):
        for s in range(needs.shape[1]):
            named[p * needs.shape[1] + s] = p * pan_group + needs[p, s]


def pick_body(n_row, n_col, cap, partners, _after, *refs):
    packs = {k: refs[i] for i, k in enumerate([*partners, 0])}
    own, peers = refs[n_row], refs[n_row + 1 : n_row + n_col]
    outs, asked = refs[n_row + n_col : -1], refs[-1]
    seg_own, rhs, width = own.shape
    r, c = lax.axis_index("row"), lax.axis_index("col")
    mine = lax.broadcasted_iota(jnp.int32, (rhs, width), 0) == r
    for k in range(n_row):
        needs = packs[k][packs[k].shape[0] - 1].astype(F32)
        asked[k : k + 1, :] = jnp.sum(jnp.where(mine, needs, 0.0), axis=0, keepdims=True).astype(jnp.int32)
    for k in range(n_row):
        for s in range(cap):
            b = asked[k, s]
            holder = lax.div(b, seg_own)
            b = b - holder * seg_own
            j = lax.bitwise_xor(holder, c)
            value = own[b]
            span = pl.ds(pl.multiple_of(b * width, width), width)
            for q, peer in enumerate(peers):
                value = jnp.where(j == q + 1, peer[:, span], value)
            outs[n_row - 1 - k][s] = value


def multiply(tiles, src, tile, source, row, acc, start, count):
    rhs, width = src.shape[1:]

    def products(first):
        got = []
        for i in (first, first + 2, first + 4, first + 6):
            left = jnp.concatenate([src[source(i)], src[source(i + 1)]], axis=0)
            right = jnp.concatenate([tiles[tile(i)], tiles[tile(i + 1)]], axis=1)
            both = jnp.dot(left, right, preferred_element_type=F32)
            got += [both[:rhs, :width], both[rhs:, width:]]
        return got

    def add(first, got):
        for u, value in enumerate(got):
            acc[row(first + u)] += value

    waiting = products(start)
    for first in range(8, count, 8):
        ahead = products(start + first)
        add(start + first - 8, waiting)
        waiting = ahead
    add(start + count - 8, waiting)


def coeff_body(n_row, n_col, pan_own, partners, slots, rows, named, *refs):
    packs = {k: refs[i] for i, k in enumerate([*partners, 0])}
    ends = refs[n_row : n_row + n_col - 1]
    tiles, part, *messages = refs[n_row + n_col - 1 : -1]
    src = refs[-1]
    r = lax.axis_index("row")
    pan_group = pan_own * n_col
    for k in range(n_row):
        src[pl.ds(lax.bitwise_xor(r, k) * pan_group, pan_group)] = packs[k][pl.ds(0, pan_group)]
    part[...] = jnp.zeros_like(part)
    multiply(tiles, src, lambda t: t, lambda t: named[slots[t]], lambda t: rows[t], part, 0, tiles.shape[0])
    high = part[...].astype(BF16)
    low = (part[...] - high.astype(F32)).astype(BF16)
    for message, sums in zip(messages, ends):
        message[pl.ds(0, pan_group)] = high
        message[pl.ds(pan_group, pan_group)] = low
        message[pl.ds(2 * pan_group, sums.shape[0])] = sums[...]


def induct_body(n_row, n_col, seg_own, order, half, slots, rows, listed, _after, *refs):
    got = {k: refs[i] for i, k in enumerate(order)}
    tiles = refs[n_row]
    outs, (src, acc) = refs[n_row + 1 : -2], refs[-2:]
    cap = got[0].shape[0]
    r, c = lax.axis_index("row"), lax.axis_index("col")
    for k in range(n_row):
        src[pl.ds(lax.bitwise_xor(r, k) * cap, cap)] = got[k][...]
    src[n_row * cap] = jnp.zeros(src.shape[1:], BF16)
    columns = range(1, n_col) if half == 0 else range(1)
    spans = [pl.ds(lax.bitwise_xor(c, j) * seg_own, seg_own) for j in columns]
    for span in spans:
        acc[span] = jnp.zeros((seg_own, *acc.shape[1:]), F32)
    size, run = list_size(tiles.shape[0]), first_run(tiles.shape[0])
    length = listed[2 * size + 2 + half]

    def tile(i):
        return listed[half * size + i]

    def source(i):
        return jnp.where(i < length, slots[tile(i)], n_row * cap)

    def row(i):
        return rows[tile(i)]

    multiply(tiles, src, tile, source, row, acc, 0, run)

    def step(i, carry):
        multiply(tiles, src, tile, source, row, acc, run + i * STEP, STEP)
        return carry

    lax.fori_loop(0, listed[2 * size + half], step, 0)
    for out, span in zip(outs, spans):
        out[...] = acc[span].astype(out.dtype)


def panels_body(n_row, n_col, pan_own, part, ends_own, *refs):
    parts = refs[: n_col - 1]
    pot, end_keep, *messages = refs[n_col - 1 :]
    pan_group = part.shape[0]
    total = part[...]
    for x in parts:
        total += x[pl.ds(0, pan_group)].astype(F32) + x[pl.ds(pan_group, pan_group)].astype(F32)
    rounded = total.astype(BF16)
    pot[...] = rounded
    for k in range(n_row):
        sums = ends_own[pl.ds(k * pan_own, pan_own)]
        for x in parts:
            sums += x[pl.ds(2 * pan_group + k * pan_own, pan_own)].astype(F32)
        if k == 0:
            end_keep[...] = sums
        else:
            messages[n_row - 1 - k][pl.ds(0, pan_own)] = sums.astype(BF16)
            messages[n_row - 1 - k][pl.ds(pan_own, pan_group)] = rounded


def hold_body(_after, message, out):
    out[...] = message[...]


def add_drops(p, pots, first, links, holder, lanes, field):
    cap = links.shape[1]
    ends, drops = [], []
    for s in range(cap):
        j = holder[p * cap + s]
        values = pots[first + links[p, s]].astype(F32)
        at = jnp.broadcast_to(lanes[pl.ds(j, 1), :], values.shape)
        drop = jnp.take_along_axis(values, at, axis=1, mode="promise_in_bounds")
        k = lax.div(j, 2)
        drops.append(drop * (1 - 2 * (j - 2 * k)).astype(F32))
        ends.append(k)
    for k, drop in zip(ends, drops):
        field[k] += drop


def base_body(pan_own, links, holder, scale, lanes, pack, field_own, end_own, pot, field, panels, pot_out):
    rhs, width = pot.shape[1:]
    r, c = lax.axis_index("row"), lax.axis_index("col")
    field[...] = field_own[...]
    row = lax.broadcasted_iota(jnp.int32, (rhs, width), 0)
    factor = jnp.zeros((rhs, width), F32)
    for i in range(rhs):
        factor = jnp.where(row == i, scale[i], factor)
    for q in range(pan_own):
        panels[q] = factor * pack[c * pan_own + q].astype(F32) + end_own[q]
        pot_out[:, q * width : (q + 1) * width] = pot[c * pan_own + q]
    add_drops(r, pot, 0, links, holder, lanes, field)


def drops_body(k, pan_own, links, holder, lanes, message, field_in, field):
    field[...] = field_in[...]
    p = lax.bitwise_xor(lax.axis_index("row"), k)
    add_drops(p, message, pan_own, links, holder, lanes, field)


def final_body(n_row, n_col, pan_own, links, holder, lanes, field_own, panels, *refs):
    arrived, field_in = refs[: n_row - 1], refs[n_row - 1 : n_row + n_col - 2]
    seg_out, pan_out, field, seg, pan, sems = refs[n_row + n_col - 2 :]
    seg_own, _, width = field.shape
    total = field_own[...]
    for x in field_in:
        total += x[...].astype(F32)
    field[...] = total
    p = lax.bitwise_xor(lax.axis_index("row"), 1)
    add_drops(p, arrived[0], pan_own, links, holder, lanes, field)
    for q in range(pan_own):
        total = panels[q]
        for x in arrived:
            total += x[q].astype(F32)
        pan[:, q * width : (q + 1) * width] = total.astype(BF16)
    chunks = sems.shape[0] - 1
    copies = [pltpu.make_async_copy(pan, pan_out, sems.at[chunks])]
    copies[0].start()
    size = seg_own // chunks
    for i in range(chunks):
        for k in range(i * size, (i + 1) * size):
            seg[:, k * width : (k + 1) * width] = field[k].astype(BF16)
        part = pl.ds(i * size * width, size * width)
        copies.append(pltpu.make_async_copy(seg.at[:, part], seg_out.at[:, part], sems.at[i]))
        copies[-1].start()
    for copy in copies:
        copy.wait()


def shards(
    current,
    charge,
    rhs_scale,
    induct_tiles,
    induct_rows,
    induct_slots,
    induct_needs,
    coeff_tiles,
    coeff_rows,
    coeff_slots,
    coeff_needs,
    link_needs,
    end_slots,
    end_offsets,
):
    n_row = lax.axis_size("row")
    n_col = lax.axis_size("col")
    width = induct_tiles.shape[1]
    rhs = current.shape[0]
    seg_own = current.shape[1] // width
    pan_own = charge.shape[1] // width
    seg_group, pan_group = seg_own * n_col, pan_own * n_col
    cap_l, cap_p, cap_k = induct_needs.shape[1], coeff_needs.shape[1], link_needs.shape[1]
    slots_t, off_t = end_slots.T, end_offsets.T

    partners = [*reversed(range(1, n_row))]
    partners[:2] = partners[1::-1]

    def like(blocks, dtype):
        return jax.ShapeDtypeStruct((blocks, rhs, width), dtype)

    charges = exchange_all(charge, [charge] * (n_col - 1), "col")
    cur = exchange_all(current, [current] * (n_col - 1), "col")
    pack, listed = call(
        functools.partial(pack_body, pan_own, seg_own),
        "pack_charges",
        [like(pan_own + 1, BF16), pltpu.SMEM((2 * list_size(induct_rows.shape[0]) + 4,), jnp.int32)],
        [VMEM, VMEM, SMEM],
        [pltpu.VMEM((rhs, width), jnp.int32)],
        moved=2**16,
        out_specs=[VMEM, SMEM],
    )(*in_hbm(charge, induct_needs, induct_rows))
    (pack,) = call(
        functools.partial(join_body, pan_own),
        "join_charges",
        [like(pan_group + 1, BF16)],
        [VMEM] * n_col,
        moved=2**16,
    )(pack, *charges[1:])
    packs = exchange_all(pack, [pack] * (n_row - 1), "row")

    rows_own = n_row * pan_own
    scalars = [slots_t, link_needs, coeff_slots, coeff_rows, coeff_needs, induct_slots, induct_rows, rhs_scale]
    moved = [*scalars, coeff_tiles]
    outs = call(
        functools.partial(ends_body, n_row, n_col, pan_own, cap_k, len(moved)),
        "end_sums",
        [pltpu.SMEM(x.shape, x.dtype) for x in scalars]
        + [jax.ShapeDtypeStruct(coeff_tiles.shape, BF16)]
        + [pltpu.SMEM((2 * seg_own,), jnp.int32), pltpu.SMEM((n_row * cap_p,), jnp.int32)]
        + [jax.ShapeDtypeStruct((2 * seg_own, width), jnp.int32)]
        + [like(seg_own, BF16), like(rows_own, F32)]
        + [like(rows_own, BF16)] * (n_col - 1),
        [ANY] * (len(moved) + 2),
        [
            pltpu.VMEM(current.shape, BF16),
            pltpu.VMEM(off_t.shape, jnp.int32),
            pltpu.VMEM((n_row * pan_group, rhs, width), F32),
            pltpu.SemaphoreType.DMA((len(moved) + 2,)),
        ],
        flops=5 * 10**8,
        moved=2**18,
        out_specs=[SMEM] * len(scalars) + [VMEM, SMEM, SMEM] + [VMEM] * (2 + n_col),
    )(*in_hbm(current, off_t, *moved))
    _, links_s, coeff_slots, coeff_rows, coeff_needs, induct_slots, induct_rows, scale, coeff_tiles = outs[: len(moved)]
    holder, named, lanes, own_blocks, ends_own, *ends_out = outs[len(moved) :]

    part, *messages = call(
        functools.partial(coeff_body, n_row, n_col, pan_own, partners),
        "coeff_tiles",
        [like(pan_group, F32)] + [like(2 * pan_group + rows_own, BF16)] * (n_col - 1),
        [SMEM] * 3 + [VMEM] * (n_row + n_col),
        [pltpu.VMEM((n_row * pan_group, rhs, width), BF16)],
        flops=10**9,
        moved=coeff_tiles.size * 2,
    )(coeff_slots, coeff_rows, named, *[packs[k] for k in partners], packs[0], *ends_out, coeff_tiles)
    parts = exchange_all(None, messages, "col")[1:]

    *picks, own_picks = call(
        functools.partial(pick_body, n_row, n_col, cap_l, partners),
        "pick_blocks",
        [like(cap_l, BF16)] * n_row,
        [ANY] + [VMEM] * (n_row + n_col),
        [pltpu.VMEM((n_row, width), jnp.int32)],
        moved=2**18,
    )(part, *[packs[k] for k in partners], packs[0], own_blocks, *cur[1:])
    got = exchange_all(own_picks, picks[::-1], "row")

    pot, end_keep, *row_messages = call(
        functools.partial(panels_body, n_row, n_col, pan_own),
        "panel_sums",
        [like(pan_group, BF16), like(pan_own, F32)] + [like(pan_own + pan_group, BF16)] * (n_row - 1),
        [VMEM] * (1 + n_col),
        flops=10**9,
        moved=2**18,
    )(part, ends_own, *parts)

    order = [*partners[1:], 0, partners[0]]

    def induct(name, half, outs, after):
        return call(
            functools.partial(induct_body, n_row, n_col, seg_own, order, half),
            name,
            outs,
            [SMEM] * 3 + [ANY] + [VMEM] * (n_row + 1),
            [
                pltpu.VMEM((n_row * cap_l + 1, rhs, width), BF16),
                pltpu.VMEM((seg_group, rhs, width), F32),
            ],
            flops=10**8,
            moved=2**16,
        )(induct_slots, induct_rows, listed, after, *[got[k] for k in order], induct_tiles)

    field_out = induct("induct_away", 0, [like(seg_own, BF16)] * (n_col - 1), pot)
    field_in = exchange_all(None, field_out, "col")[1:]

    (row_messages[-1],) = call(
        hold_body,
        "hold_near",
        [like(pan_own + pan_group, BF16)],
        [ANY, VMEM],
        moved=2**16,
    )(field_out[0], row_messages[-1])
    arrived = exchange_all(None, row_messages[::-1], "row")[1:]
    (field_own,) = induct("induct_own", 1, [like(seg_own, F32)], row_messages[-1])

    field, panels, pot_out = call(
        functools.partial(base_body, pan_own),
        "base_sums",
        [like(seg_own, F32), like(pan_own, F32), jax.ShapeDtypeStruct(charge.shape, BF16)],
        [SMEM] * 3 + [VMEM] * 5,
        flops=0,
        moved=0,
    )(links_s, holder, scale, lanes, pack, field_own, end_keep, pot)

    for k in reversed(range(2, n_row)):
        (field,) = call(
            functools.partial(drops_body, k, pan_own),
            "add_drops",
            [like(seg_own, F32)],
            [SMEM] * 2 + [VMEM] * 3,
            flops=11 * 10**8 if k == 2 else 0,
            moved=0,
        )(links_s, holder, lanes, arrived[k - 1], field)

    seg_out, pan_out = call(
        functools.partial(final_body, n_row, n_col, pan_own),
        "outputs",
        [jax.ShapeDtypeStruct(x.shape, BF16) for x in (current, charge)],
        [SMEM] * 2 + [VMEM] * (1 + n_row + n_col),
        [
            pltpu.VMEM((seg_own, rhs, width), F32),
            pltpu.VMEM(current.shape, BF16),
            pltpu.VMEM(charge.shape, BF16),
            pltpu.SemaphoreType.DMA((3,)),
        ],
        flops=10**9,
        moved=2**20,
        out_specs=[ANY, ANY],
    )(links_s, holder, lanes, field, panels, *arrived, *field_in)
    return (seg_out, pan_out, pot_out)


def solution(mesh):
    blocks = P(("parts", "row", "col"))
    matrix = P(("parts", "row", "col"), None)
    tiles = P(("parts", "row", "col"), None, None)
    values = P("rhs", ("parts", "row", "col"))
    return jax.shard_map(
        shards,
        mesh=mesh,
        in_specs=(
            values,
            values,
            P(("parts", "rhs")),
            tiles,
            blocks,
            blocks,
            matrix,
            tiles,
            blocks,
            blocks,
            matrix,
            matrix,
            matrix,
            matrix,
        ),
        out_specs=(values, values, values),
        check_vma=False,
    )
```

```python
import functools

import jax
import jax.numpy as jnp
from jax import lax
from jax.experimental import pallas as pl
from jax.experimental.pallas import tpu as pltpu
from jax.sharding import PartitionSpec as P

F32 = jnp.float32
BF16 = jnp.bfloat16
VMEM = pl.BlockSpec(memory_space=pltpu.VMEM)
SMEM = pl.BlockSpec(memory_space=pltpu.SMEM)
ANY = pl.BlockSpec(memory_space=pl.ANY)


def exchange(x, axis, k):
    if k == 0:
        return x
    return lax.ppermute(x, axis, [(i, i ^ k) for i in range(lax.axis_size(axis))])


def exchange_all(first, others, axis):
    n = lax.axis_size(axis)
    got = {0: first}
    for k in reversed(range(1, n)):
        got[k] = exchange(others[k - 1], axis, k)
    return [got[k] for k in range(n)]


def call(body, name, out_shape, in_specs, scratch=(), flops=0, moved=0, out_specs=None):
    return pl.pallas_call(
        body,
        out_shape=out_shape,
        in_specs=in_specs,
        out_specs=out_specs or [VMEM] * len(out_shape),
        scratch_shapes=list(scratch),
        compiler_params=pltpu.CompilerParams(vmem_limit_bytes=16 * 2**20),
        cost_estimate=pl.CostEstimate(flops=flops, bytes_accessed=moved, transcendentals=0),
        name=name,
    )


def in_hbm(*arrays):
    return [pltpu.with_memory_space_constraint(x, pltpu.HBM) for x in arrays]


def pack_body(pan_own, seg_own, charge, needs, rows, message, listed, wide):
    width = charge.shape[1] // pan_own
    for q in range(pan_own):
        message[q] = charge[:, q * width : (q + 1) * width]
    wide[...] = jnp.zeros_like(wide)
    wide[: needs.shape[0], : needs.shape[1]] = needs[...]
    message[pan_own] = wide[...].astype(F32).astype(BF16)
    sort_tiles(rows, listed, seg_own)


def join_body(pan_own, own, *refs):
    others, message = refs[:-1], refs[-1]
    c = lax.axis_index("col")
    width = own.shape[2]
    message[pl.ds(c * pan_own, pan_own)] = own[pl.ds(0, pan_own)]
    for j, x in enumerate(others):
        first = lax.bitwise_xor(c, j + 1) * pan_own
        for q in range(pan_own):
            message[first + q] = x[:, q * width : (q + 1) * width]
    message[message.shape[0] - 1] = own[pan_own]


STEP = 16


def list_size(count):
    return count + STEP


def first_run(count):
    return count * 7 // 12 // STEP * STEP


def sort_tiles(rows, listed, seg_own):
    count = rows.shape[0]
    size, run = list_size(count), first_run(count)
    base = lax.axis_index("col") * seg_own

    def step(i, here):
        for u in range(16):
            t = i * 16 + u
            inside = rows[t] - base
            mine = jnp.logical_and(inside >= 0, inside < seg_own)
            listed[jnp.where(mine, size + here, t - here)] = t
            here = here + mine.astype(jnp.int32)
        return here

    here = lax.fori_loop(0, count // 16, step, jnp.int32(0))
    for half, n in enumerate((count - here, here)):
        steps = lax.max(lax.div(n - run + STEP - 1, STEP), 0)

        def fill(i, carry, half=half):
            listed[half * size + i] = 0
            return carry

        lax.fori_loop(n, run + steps * STEP, fill, 0)
        listed[2 * size + half] = steps
        listed[2 * size + 2 + half] = n


def ends_body(n_row, n_col, pan_own, cap, n_moved, *refs):
    sources, targets = refs[: n_moved + 2], refs[n_moved + 2 : 2 * n_moved + 2]
    (holder, named, lanes, blocks, own, *sends), (cur, off, acc, sems) = refs[2 * n_moved + 2 : -4], refs[-4:]
    copies = [
        pltpu.make_async_copy(source, target, sems.at[i])
        for i, (source, target) in enumerate(zip(sources, (cur, off, *targets)))
    ]
    for copy in copies:
        copy.start()
    slots, links = targets[:2]
    seg_own, _, width = blocks.shape
    pan_group = pan_own * n_col
    r, c = lax.axis_index("row"), lax.axis_index("col")
    acc[...] = jnp.zeros_like(acc)
    levels = lax.broadcasted_iota(jnp.int32, (width, width), 0)
    for copy in copies[:4]:
        copy.wait()

    def block(k):
        span = pl.ds(pl.multiple_of(k * width, width), width)
        for e in range(2):
            lanes[pl.ds(2 * k + e, 1), :] = off[e : e + 1, span]
        to_hot = jnp.where(levels == off[0:1, span], 1.0, 0.0).astype(BF16)
        from_hot = jnp.where(levels == off[1:2, span], -1.0, 0.0).astype(BF16)
        hot = jnp.concatenate([to_hot, from_hot], axis=0)
        value = cur[:, span]
        blocks[k] = value
        sums = lax.dot_general(value, hot, (((1,), (1,)), ((), ())), preferred_element_type=F32)
        return sums.astype(BF16).astype(F32)

    unroll = 16

    def step(i, carry):
        got = [block(i * unroll + u) for u in range(unroll)]
        for u in range(unroll):
            for e in range(2):
                slot = slots[e, i * unroll + u]
                holder[slot] = 2 * (i * unroll + u) + e
                p = lax.div(slot, cap)
                b = links[p, slot - p * cap]
                acc[lax.bitwise_xor(p, r) * pan_group + b] += got[u][:, e * width : (e + 1) * width]
        return carry

    lax.fori_loop(0, seg_own // unroll, step, 0)
    for k in range(n_row):
        here = pl.ds(k * pan_own, pan_own)
        own[here] = acc[pl.ds(k * pan_group + c * pan_own, pan_own)]
        for j in range(1, n_col):
            there = lax.bitwise_xor(c, j)
            sends[j - 1][here] = acc[pl.ds(k * pan_group + there * pan_own, pan_own)].astype(BF16)
    for copy in copies[4:]:
        copy.wait()
    needs = targets[4]
    for p in range(n_row):
        for s in range(needs.shape[1]):
            named[p * needs.shape[1] + s] = p * pan_group + needs[p, s]


def pick_body(n_row, n_col, cap, partners, _after, *refs):
    packs = {k: refs[i] for i, k in enumerate([*partners, 0])}
    own, peers = refs[n_row], refs[n_row + 1 : n_row + n_col]
    outs, asked = refs[n_row + n_col : -1], refs[-1]
    seg_own, rhs, width = own.shape
    r, c = lax.axis_index("row"), lax.axis_index("col")
    mine = lax.broadcasted_iota(jnp.int32, (rhs, width), 0) == r
    for k in range(n_row):
        needs = packs[k][packs[k].shape[0] - 1].astype(F32)
        asked[k : k + 1, :] = jnp.sum(jnp.where(mine, needs, 0.0), axis=0, keepdims=True).astype(jnp.int32)
    for k in range(n_row):
        for s in range(cap):
            b = asked[k, s]
            holder = lax.div(b, seg_own)
            b = b - holder * seg_own
            j = lax.bitwise_xor(holder, c)
            value = own[b]
            span = pl.ds(pl.multiple_of(b * width, width), width)
            for q, peer in enumerate(peers):
                value = jnp.where(j == q + 1, peer[:, span], value)
            outs[n_row - 1 - k][s] = value


def multiply(tiles, src, tile, source, row, acc, start, count):
    rhs, width = src.shape[1:]

    def products(first):
        got = []
        for i in (first, first + 2, first + 4, first + 6):
            left = jnp.concatenate([src[source(i)], src[source(i + 1)]], axis=0)
            right = jnp.concatenate([tiles[tile(i)], tiles[tile(i + 1)]], axis=1)
            both = jnp.dot(left, right, preferred_element_type=F32)
            got += [both[:rhs, :width], both[rhs:, width:]]
        return got

    def add(first, got):
        for u, value in enumerate(got):
            acc[row(first + u)] += value

    waiting = products(start)
    for first in range(8, count, 8):
        ahead = products(start + first)
        add(start + first - 8, waiting)
        waiting = ahead
    add(start + count - 8, waiting)


def coeff_body(n_row, n_col, pan_own, partners, slots, rows, named, *refs):
    packs = {k: refs[i] for i, k in enumerate([*partners, 0])}
    ends = refs[n_row : n_row + n_col - 1]
    tiles, part, *messages = refs[n_row + n_col - 1 : -1]
    src = refs[-1]
    r = lax.axis_index("row")
    pan_group = pan_own * n_col
    for k in range(n_row):
        src[pl.ds(lax.bitwise_xor(r, k) * pan_group, pan_group)] = packs[k][pl.ds(0, pan_group)]
    part[...] = jnp.zeros_like(part)
    multiply(tiles, src, lambda t: t, lambda t: named[slots[t]], lambda t: rows[t], part, 0, tiles.shape[0])
    high = part[...].astype(BF16)
    low = (part[...] - high.astype(F32)).astype(BF16)
    for message, sums in zip(messages, ends):
        message[pl.ds(0, pan_group)] = high
        message[pl.ds(pan_group, pan_group)] = low
        message[pl.ds(2 * pan_group, sums.shape[0])] = sums[...]


def induct_body(n_row, n_col, seg_own, order, half, slots, rows, listed, _after, *refs):
    got = {k: refs[i] for i, k in enumerate(order)}
    tiles = refs[n_row]
    outs, (src, acc) = refs[n_row + 1 : -2], refs[-2:]
    cap = got[0].shape[0]
    r, c = lax.axis_index("row"), lax.axis_index("col")
    for k in range(n_row):
        src[pl.ds(lax.bitwise_xor(r, k) * cap, cap)] = got[k][...]
    src[n_row * cap] = jnp.zeros(src.shape[1:], BF16)
    columns = range(1, n_col) if half == 0 else range(1)
    spans = [pl.ds(lax.bitwise_xor(c, j) * seg_own, seg_own) for j in columns]
    for span in spans:
        acc[span] = jnp.zeros((seg_own, *acc.shape[1:]), F32)
    size, run = list_size(tiles.shape[0]), first_run(tiles.shape[0])
    length = listed[2 * size + 2 + half]

    def tile(i):
        return listed[half * size + i]

    def source(i):
        return jnp.where(i < length, slots[tile(i)], n_row * cap)

    def row(i):
        return rows[tile(i)]

    multiply(tiles, src, tile, source, row, acc, 0, run)

    def step(i, carry):
        multiply(tiles, src, tile, source, row, acc, run + i * STEP, STEP)
        return carry

    lax.fori_loop(0, listed[2 * size + half], step, 0)
    for out, span in zip(outs, spans):
        out[...] = acc[span].astype(out.dtype)


def panels_body(n_row, n_col, pan_own, part, ends_own, *refs):
    parts = refs[: n_col - 1]
    pot, end_keep, *messages = refs[n_col - 1 :]
    pan_group = part.shape[0]
    total = part[...]
    for x in parts:
        total += x[pl.ds(0, pan_group)].astype(F32) + x[pl.ds(pan_group, pan_group)].astype(F32)
    rounded = total.astype(BF16)
    pot[...] = rounded
    for k in range(n_row):
        sums = ends_own[pl.ds(k * pan_own, pan_own)]
        for x in parts:
            sums += x[pl.ds(2 * pan_group + k * pan_own, pan_own)].astype(F32)
        if k == 0:
            end_keep[...] = sums
        else:
            messages[n_row - 1 - k][pl.ds(0, pan_own)] = sums.astype(BF16)
            messages[n_row - 1 - k][pl.ds(pan_own, pan_group)] = rounded


def hold_body(_after, message, out):
    out[...] = message[...]


def add_drops(p, pots, first, links, holder, lanes, field):
    cap = links.shape[1]
    ends, drops = [], []
    for s in range(cap):
        j = holder[p * cap + s]
        values = pots[first + links[p, s]].astype(F32)
        at = jnp.broadcast_to(lanes[pl.ds(j, 1), :], values.shape)
        drop = jnp.take_along_axis(values, at, axis=1, mode="promise_in_bounds")
        k = lax.div(j, 2)
        drops.append(drop * (1 - 2 * (j - 2 * k)).astype(F32))
        ends.append(k)
    for k, drop in zip(ends, drops):
        field[k] += drop


def base_body(pan_own, links, holder, scale, lanes, pack, field_own, end_own, pot, field, panels, pot_out):
    rhs, width = pot.shape[1:]
    r, c = lax.axis_index("row"), lax.axis_index("col")
    field[...] = field_own[...]
    row = lax.broadcasted_iota(jnp.int32, (rhs, width), 0)
    factor = jnp.zeros((rhs, width), F32)
    for i in range(rhs):
        factor = jnp.where(row == i, scale[i], factor)
    for q in range(pan_own):
        panels[q] = factor * pack[c * pan_own + q].astype(F32) + end_own[q]
        pot_out[:, q * width : (q + 1) * width] = pot[c * pan_own + q]
    add_drops(r, pot, 0, links, holder, lanes, field)


def drops_body(k, pan_own, links, holder, lanes, message, field_in, field):
    field[...] = field_in[...]
    p = lax.bitwise_xor(lax.axis_index("row"), k)
    add_drops(p, message, pan_own, links, holder, lanes, field)


def final_body(n_row, n_col, pan_own, links, holder, lanes, field_own, panels, *refs):
    arrived, field_in = refs[: n_row - 1], refs[n_row - 1 : n_row + n_col - 2]
    seg_out, pan_out, field, seg, pan, sems = refs[n_row + n_col - 2 :]
    seg_own, _, width = field.shape
    total = field_own[...]
    for x in field_in:
        total += x[...].astype(F32)
    field[...] = total
    p = lax.bitwise_xor(lax.axis_index("row"), 1)
    add_drops(p, arrived[0], pan_own, links, holder, lanes, field)
    for q in range(pan_own):
        total = panels[q]
        for x in arrived:
            total += x[q].astype(F32)
        pan[:, q * width : (q + 1) * width] = total.astype(BF16)
    chunks = sems.shape[0] - 1
    copies = [pltpu.make_async_copy(pan, pan_out, sems.at[chunks])]
    copies[0].start()
    size = seg_own // chunks
    for i in range(chunks):
        for k in range(i * size, (i + 1) * size):
            seg[:, k * width : (k + 1) * width] = field[k].astype(BF16)
        part = pl.ds(i * size * width, size * width)
        copies.append(pltpu.make_async_copy(seg.at[:, part], seg_out.at[:, part], sems.at[i]))
        copies[-1].start()
    for copy in copies:
        copy.wait()


def shards(
    current,
    charge,
    rhs_scale,
    induct_tiles,
    induct_rows,
    induct_slots,
    induct_needs,
    coeff_tiles,
    coeff_rows,
    coeff_slots,
    coeff_needs,
    link_needs,
    end_slots,
    end_offsets,
):
    n_row = lax.axis_size("row")
    n_col = lax.axis_size("col")
    width = induct_tiles.shape[1]
    rhs = current.shape[0]
    seg_own = current.shape[1] // width
    pan_own = charge.shape[1] // width
    seg_group, pan_group = seg_own * n_col, pan_own * n_col
    cap_l, cap_p, cap_k = induct_needs.shape[1], coeff_needs.shape[1], link_needs.shape[1]
    slots_t, off_t = end_slots.T, end_offsets.T

    partners = [*reversed(range(1, n_row))]
    partners[:2] = partners[1::-1]

    def like(blocks, dtype):
        return jax.ShapeDtypeStruct((blocks, rhs, width), dtype)

    charges = exchange_all(charge, [charge] * (n_col - 1), "col")
    cur = exchange_all(current, [current] * (n_col - 1), "col")
    pack, listed = call(
        functools.partial(pack_body, pan_own, seg_own),
        "pack_charges",
        [like(pan_own + 1, BF16), pltpu.SMEM((2 * list_size(induct_rows.shape[0]) + 4,), jnp.int32)],
        [VMEM, VMEM, SMEM],
        [pltpu.VMEM((rhs, width), jnp.int32)],
        moved=2**16,
        out_specs=[VMEM, SMEM],
    )(*in_hbm(charge, induct_needs, induct_rows))
    (pack,) = call(
        functools.partial(join_body, pan_own),
        "join_charges",
        [like(pan_group + 1, BF16)],
        [VMEM] * n_col,
        moved=2**16,
    )(pack, *charges[1:])
    packs = exchange_all(pack, [pack] * (n_row - 1), "row")

    rows_own = n_row * pan_own
    scalars = [slots_t, link_needs, coeff_slots, coeff_rows, coeff_needs, induct_slots, induct_rows, rhs_scale]
    moved = [*scalars, coeff_tiles]
    outs = call(
        functools.partial(ends_body, n_row, n_col, pan_own, cap_k, len(moved)),
        "end_sums",
        [pltpu.SMEM(x.shape, x.dtype) for x in scalars]
        + [jax.ShapeDtypeStruct(coeff_tiles.shape, BF16)]
        + [pltpu.SMEM((2 * seg_own,), jnp.int32), pltpu.SMEM((n_row * cap_p,), jnp.int32)]
        + [jax.ShapeDtypeStruct((2 * seg_own, width), jnp.int32)]
        + [like(seg_own, BF16), like(rows_own, F32)]
        + [like(rows_own, BF16)] * (n_col - 1),
        [ANY] * (len(moved) + 2),
        [
            pltpu.VMEM(current.shape, BF16),
            pltpu.VMEM(off_t.shape, jnp.int32),
            pltpu.VMEM((n_row * pan_group, rhs, width), F32),
            pltpu.SemaphoreType.DMA((len(moved) + 2,)),
        ],
        flops=5 * 10**8,
        moved=2**18,
        out_specs=[SMEM] * len(scalars) + [VMEM, SMEM, SMEM] + [VMEM] * (2 + n_col),
    )(*in_hbm(current, off_t, *moved))
    _, links_s, coeff_slots, coeff_rows, coeff_needs, induct_slots, induct_rows, scale, coeff_tiles = outs[: len(moved)]
    holder, named, lanes, own_blocks, ends_own, *ends_out = outs[len(moved) :]

    part, *messages = call(
        functools.partial(coeff_body, n_row, n_col, pan_own, partners),
        "coeff_tiles",
        [like(pan_group, F32)] + [like(2 * pan_group + rows_own, BF16)] * (n_col - 1),
        [SMEM] * 3 + [VMEM] * (n_row + n_col),
        [pltpu.VMEM((n_row * pan_group, rhs, width), BF16)],
        flops=10**9,
        moved=coeff_tiles.size * 2,
    )(coeff_slots, coeff_rows, named, *[packs[k] for k in partners], packs[0], *ends_out, coeff_tiles)
    parts = exchange_all(None, messages, "col")[1:]

    *picks, own_picks = call(
        functools.partial(pick_body, n_row, n_col, cap_l, partners),
        "pick_blocks",
        [like(cap_l, BF16)] * n_row,
        [ANY] + [VMEM] * (n_row + n_col),
        [pltpu.VMEM((n_row, width), jnp.int32)],
        moved=2**18,
    )(part, *[packs[k] for k in partners], packs[0], own_blocks, *cur[1:])
    got = exchange_all(own_picks, picks[::-1], "row")

    pot, end_keep, *row_messages = call(
        functools.partial(panels_body, n_row, n_col, pan_own),
        "panel_sums",
        [like(pan_group, BF16), like(pan_own, F32)] + [like(pan_own + pan_group, BF16)] * (n_row - 1),
        [VMEM] * (1 + n_col),
        flops=10**9,
        moved=2**18,
    )(part, ends_own, *parts)

    order = [*range(n_row - 2, -1, -1), n_row - 1]

    def induct(name, half, outs, after):
        return call(
            functools.partial(induct_body, n_row, n_col, seg_own, order, half),
            name,
            outs,
            [SMEM] * 3 + [ANY] + [VMEM] * (n_row + 1),
            [
                pltpu.VMEM((n_row * cap_l + 1, rhs, width), BF16),
                pltpu.VMEM((seg_group, rhs, width), F32),
            ],
            flops=10**8,
            moved=2**16,
        )(induct_slots, induct_rows, listed, after, *[got[k] for k in order], induct_tiles)

    field_out = induct("induct_away", 0, [like(seg_own, BF16)] * (n_col - 1), pot)
    field_in = exchange_all(None, field_out, "col")[1:]

    (row_messages[-1],) = call(
        hold_body,
        "hold_near",
        [like(pan_own + pan_group, BF16)],
        [ANY, VMEM],
        moved=2**16,
    )(field_out[0], row_messages[-1])
    arrived = exchange_all(None, row_messages[::-1], "row")[1:]
    (field_own,) = induct("induct_own", 1, [like(seg_own, F32)], row_messages[-1])

    field, panels, pot_out = call(
        functools.partial(base_body, pan_own),
        "base_sums",
        [like(seg_own, F32), like(pan_own, F32), jax.ShapeDtypeStruct(charge.shape, BF16)],
        [SMEM] * 3 + [VMEM] * 5,
        flops=0,
        moved=0,
    )(links_s, holder, scale, lanes, pack, field_own, end_keep, pot)

    for k in partners[:-1]:
        (field,) = call(
            functools.partial(drops_body, k, pan_own),
            "add_drops",
            [like(seg_own, F32)],
            [SMEM] * 2 + [VMEM] * 3,
            flops=11 * 10**8 if k == partners[-2] else 0,
            moved=0,
        )(links_s, holder, lanes, arrived[k - 1], field)

    seg_out, pan_out = call(
        functools.partial(final_body, n_row, n_col, pan_own),
        "outputs",
        [jax.ShapeDtypeStruct(x.shape, BF16) for x in (current, charge)],
        [SMEM] * 2 + [VMEM] * (1 + n_row + n_col),
        [
            pltpu.VMEM((seg_own, rhs, width), F32),
            pltpu.VMEM(current.shape, BF16),
            pltpu.VMEM(charge.shape, BF16),
            pltpu.SemaphoreType.DMA((3,)),
        ],
        flops=10**9,
        moved=2**20,
        out_specs=[ANY, ANY],
    )(links_s, holder, lanes, field, panels, *arrived, *field_in)
    return (seg_out, pan_out, pot_out)


def solution(mesh):
    blocks = P(("parts", "row", "col"))
    matrix = P(("parts", "row", "col"), None)
    tiles = P(("parts", "row", "col"), None, None)
    values = P("rhs", ("parts", "row", "col"))
    return jax.shard_map(
        shards,
        mesh=mesh,
        in_specs=(
            values,
            values,
            P(("parts", "rhs")),
            tiles,
            blocks,
            blocks,
            matrix,
            tiles,
            blocks,
            blocks,
            matrix,
            matrix,
            matrix,
            matrix,
        ),
        out_specs=(values, values, values),
        check_vma=False,
    )
```

```python
import functools

import jax
import jax.numpy as jnp
from jax import lax
from jax.experimental import pallas as pl
from jax.experimental.pallas import tpu as pltpu
from jax.sharding import PartitionSpec as P

F32 = jnp.float32
BF16 = jnp.bfloat16
VMEM = pl.BlockSpec(memory_space=pltpu.VMEM)
SMEM = pl.BlockSpec(memory_space=pltpu.SMEM)
ANY = pl.BlockSpec(memory_space=pl.ANY)


def exchange(x, axis, k):
    if k == 0:
        return x
    return lax.ppermute(x, axis, [(i, i ^ k) for i in range(lax.axis_size(axis))])


def exchange_all(first, others, axis):
    n = lax.axis_size(axis)
    got = {0: first}
    for k in reversed(range(1, n)):
        got[k] = exchange(others[k - 1], axis, k)
    return [got[k] for k in range(n)]


def call(body, name, out_shape, in_specs, scratch=(), flops=0, moved=0, out_specs=None):
    return pl.pallas_call(
        body,
        out_shape=out_shape,
        in_specs=in_specs,
        out_specs=out_specs or [VMEM] * len(out_shape),
        scratch_shapes=list(scratch),
        compiler_params=pltpu.CompilerParams(vmem_limit_bytes=16 * 2**20),
        cost_estimate=pl.CostEstimate(flops=flops, bytes_accessed=moved, transcendentals=0),
        name=name,
    )


def in_hbm(*arrays):
    return [pltpu.with_memory_space_constraint(x, pltpu.HBM) for x in arrays]


def pack_body(pan_own, seg_own, charge, needs, rows, message, listed, wide):
    width = charge.shape[1] // pan_own
    for q in range(pan_own):
        message[q] = charge[:, q * width : (q + 1) * width]
    wide[...] = jnp.zeros_like(wide)
    wide[: needs.shape[0], : needs.shape[1]] = needs[...]
    message[pan_own] = wide[...].astype(F32).astype(BF16)
    sort_tiles(rows, listed, seg_own)


def join_body(pan_own, own, *refs):
    others, message = refs[:-1], refs[-1]
    c = lax.axis_index("col")
    width = own.shape[2]
    message[pl.ds(c * pan_own, pan_own)] = own[pl.ds(0, pan_own)]
    for j, x in enumerate(others):
        first = lax.bitwise_xor(c, j + 1) * pan_own
        for q in range(pan_own):
            message[first + q] = x[:, q * width : (q + 1) * width]
    message[message.shape[0] - 1] = own[pan_own]


STEP = 16


def list_size(count):
    return count + STEP


def first_run(count):
    return count * 7 // 12 // STEP * STEP


def sort_tiles(rows, listed, seg_own):
    count = rows.shape[0]
    size, run = list_size(count), first_run(count)
    base = lax.axis_index("col") * seg_own

    def step(i, here):
        for u in range(16):
            t = i * 16 + u
            inside = rows[t] - base
            mine = jnp.logical_and(inside >= 0, inside < seg_own)
            listed[jnp.where(mine, size + here, t - here)] = t
            here = here + mine.astype(jnp.int32)
        return here

    here = lax.fori_loop(0, count // 16, step, jnp.int32(0))
    for half, n in enumerate((count - here, here)):
        steps = lax.max(lax.div(n - run + STEP - 1, STEP), 0)

        def fill(i, carry, half=half):
            listed[half * size + i] = 0
            return carry

        lax.fori_loop(n, run + steps * STEP, fill, 0)
        listed[2 * size + half] = steps
        listed[2 * size + 2 + half] = n


def ends_body(n_row, n_col, pan_own, cap, n_moved, *refs):
    sources, targets = refs[: n_moved + 2], refs[n_moved + 2 : 2 * n_moved + 2]
    (holder, named, lanes, blocks, own, *sends), (cur, off, acc, sems) = refs[2 * n_moved + 2 : -4], refs[-4:]
    copies = [
        pltpu.make_async_copy(source, target, sems.at[i])
        for i, (source, target) in enumerate(zip(sources, (cur, off, *targets)))
    ]
    for copy in copies:
        copy.start()
    slots, links = targets[:2]
    seg_own, _, width = blocks.shape
    pan_group = pan_own * n_col
    r, c = lax.axis_index("row"), lax.axis_index("col")
    acc[...] = jnp.zeros_like(acc)
    levels = lax.broadcasted_iota(jnp.int32, (width, width), 0)
    for copy in copies[:4]:
        copy.wait()

    def block(k):
        span = pl.ds(pl.multiple_of(k * width, width), width)
        for e in range(2):
            lanes[pl.ds(2 * k + e, 1), :] = off[e : e + 1, span]
        to_hot = jnp.where(levels == off[0:1, span], 1.0, 0.0).astype(BF16)
        from_hot = jnp.where(levels == off[1:2, span], -1.0, 0.0).astype(BF16)
        hot = jnp.concatenate([to_hot, from_hot], axis=0)
        value = cur[:, span]
        blocks[k] = value
        sums = lax.dot_general(value, hot, (((1,), (1,)), ((), ())), preferred_element_type=F32)
        return sums.astype(BF16).astype(F32)

    unroll = 16

    def step(i, carry):
        got = [block(i * unroll + u) for u in range(unroll)]
        for u in range(unroll):
            for e in range(2):
                slot = slots[e, i * unroll + u]
                holder[slot] = 2 * (i * unroll + u) + e
                p = lax.div(slot, cap)
                b = links[p, slot - p * cap]
                acc[lax.bitwise_xor(p, r) * pan_group + b] += got[u][:, e * width : (e + 1) * width]
        return carry

    lax.fori_loop(0, seg_own // unroll, step, 0)
    for k in range(n_row):
        here = pl.ds(k * pan_own, pan_own)
        own[here] = acc[pl.ds(k * pan_group + c * pan_own, pan_own)]
        for j in range(1, n_col):
            there = lax.bitwise_xor(c, j)
            sends[j - 1][here] = acc[pl.ds(k * pan_group + there * pan_own, pan_own)].astype(BF16)
    for copy in copies[4:]:
        copy.wait()
    needs = targets[4]
    for p in range(n_row):
        for s in range(needs.shape[1]):
            named[p * needs.shape[1] + s] = p * pan_group + needs[p, s]


def pick_body(n_row, n_col, cap, partners, _after, *refs):
    packs = {k: refs[i] for i, k in enumerate([*partners, 0])}
    own, peers = refs[n_row], refs[n_row + 1 : n_row + n_col]
    outs, asked = refs[n_row + n_col : -1], refs[-1]
    seg_own, rhs, width = own.shape
    r, c = lax.axis_index("row"), lax.axis_index("col")
    mine = lax.broadcasted_iota(jnp.int32, (rhs, width), 0) == r
    for k in range(n_row):
        needs = packs[k][packs[k].shape[0] - 1].astype(F32)
        asked[k : k + 1, :] = jnp.sum(jnp.where(mine, needs, 0.0), axis=0, keepdims=True).astype(jnp.int32)
    for k in range(n_row):
        for s in range(cap):
            b = asked[k, s]
            holder = lax.div(b, seg_own)
            b = b - holder * seg_own
            j = lax.bitwise_xor(holder, c)
            value = own[b]
            span = pl.ds(pl.multiple_of(b * width, width), width)
            for q, peer in enumerate(peers):
                value = jnp.where(j == q + 1, peer[:, span], value)
            outs[n_row - 1 - k][s] = value


def multiply(tiles, src, tile, source, row, acc, start, count):
    rhs, width = src.shape[1:]

    def products(first):
        got = []
        for i in (first, first + 2, first + 4, first + 6):
            left = jnp.concatenate([src[source(i)], src[source(i + 1)]], axis=0)
            right = jnp.concatenate([tiles[tile(i)], tiles[tile(i + 1)]], axis=1)
            both = jnp.dot(left, right, preferred_element_type=F32)
            got += [both[:rhs, :width], both[rhs:, width:]]
        return got

    def add(first, got):
        for u, value in enumerate(got):
            acc[row(first + u)] += value

    waiting = products(start)
    for first in range(8, count, 8):
        ahead = products(start + first)
        add(start + first - 8, waiting)
        waiting = ahead
    add(start + count - 8, waiting)


def coeff_body(n_row, n_col, pan_own, partners, slots, rows, named, *refs):
    packs = {k: refs[i] for i, k in enumerate([*partners, 0])}
    ends = refs[n_row : n_row + n_col - 1]
    tiles, part, *messages = refs[n_row + n_col - 1 : -1]
    src = refs[-1]
    r = lax.axis_index("row")
    pan_group = pan_own * n_col
    for k in range(n_row):
        src[pl.ds(lax.bitwise_xor(r, k) * pan_group, pan_group)] = packs[k][pl.ds(0, pan_group)]
    part[...] = jnp.zeros_like(part)
    multiply(tiles, src, lambda t: t, lambda t: named[slots[t]], lambda t: rows[t], part, 0, tiles.shape[0])
    high = part[...].astype(BF16)
    low = (part[...] - high.astype(F32)).astype(BF16)
    for message, sums in zip(messages, ends):
        message[pl.ds(0, pan_group)] = high
        message[pl.ds(pan_group, pan_group)] = low
        message[pl.ds(2 * pan_group, sums.shape[0])] = sums[...]


def induct_body(n_row, n_col, seg_own, order, half, slots, rows, listed, _after, *refs):
    got = {k: refs[i] for i, k in enumerate(order)}
    tiles = refs[n_row]
    outs, (src, acc) = refs[n_row + 1 : -2], refs[-2:]
    cap = got[0].shape[0]
    r, c = lax.axis_index("row"), lax.axis_index("col")
    for k in range(n_row):
        src[pl.ds(lax.bitwise_xor(r, k) * cap, cap)] = got[k][...]
    src[n_row * cap] = jnp.zeros(src.shape[1:], BF16)
    columns = range(1, n_col) if half == 0 else range(1)
    spans = [pl.ds(lax.bitwise_xor(c, j) * seg_own, seg_own) for j in columns]
    for span in spans:
        acc[span] = jnp.zeros((seg_own, *acc.shape[1:]), F32)
    size, run = list_size(tiles.shape[0]), first_run(tiles.shape[0])
    length = listed[2 * size + 2 + half]

    def tile(i):
        return listed[half * size + i]

    def source(i):
        return jnp.where(i < length, slots[tile(i)], n_row * cap)

    def row(i):
        return rows[tile(i)]

    multiply(tiles, src, tile, source, row, acc, 0, run)

    def step(i, carry):
        multiply(tiles, src, tile, source, row, acc, run + i * STEP, STEP)
        return carry

    lax.fori_loop(0, listed[2 * size + half], step, 0)
    for out, span in zip(outs, spans):
        out[...] = acc[span].astype(out.dtype)


def panels_body(n_row, n_col, pan_own, part, ends_own, *refs):
    parts = refs[: n_col - 1]
    pot, end_keep, *messages = refs[n_col - 1 :]
    pan_group = part.shape[0]
    total = part[...]
    for x in parts:
        total += x[pl.ds(0, pan_group)].astype(F32) + x[pl.ds(pan_group, pan_group)].astype(F32)
    rounded = total.astype(BF16)
    pot[...] = rounded
    for k in range(n_row):
        sums = ends_own[pl.ds(k * pan_own, pan_own)]
        for x in parts:
            sums += x[pl.ds(2 * pan_group + k * pan_own, pan_own)].astype(F32)
        if k == 0:
            end_keep[...] = sums
        else:
            messages[n_row - 1 - k][pl.ds(0, pan_own)] = sums.astype(BF16)
            messages[n_row - 1 - k][pl.ds(pan_own, pan_group)] = rounded


def hold_body(_after, message, out):
    out[...] = message[...]


def add_drops(p, pots, first, links, holder, lanes, field):
    cap = links.shape[1]
    ends, drops = [], []
    for s in range(cap):
        j = holder[p * cap + s]
        values = pots[first + links[p, s]].astype(F32)
        at = jnp.broadcast_to(lanes[pl.ds(j, 1), :], values.shape)
        drop = jnp.take_along_axis(values, at, axis=1, mode="promise_in_bounds")
        k = lax.div(j, 2)
        drops.append(drop * (1 - 2 * (j - 2 * k)).astype(F32))
        ends.append(k)
    for k, drop in zip(ends, drops):
        field[k] += drop


def base_body(pan_own, links, holder, scale, lanes, pack, field_own, end_own, pot, field, panels, pot_out):
    rhs, width = pot.shape[1:]
    r, c = lax.axis_index("row"), lax.axis_index("col")
    field[...] = field_own[...]
    row = lax.broadcasted_iota(jnp.int32, (rhs, width), 0)
    factor = jnp.zeros((rhs, width), F32)
    for i in range(rhs):
        factor = jnp.where(row == i, scale[i], factor)
    for q in range(pan_own):
        panels[q] = factor * pack[c * pan_own + q].astype(F32) + end_own[q]
        pot_out[:, q * width : (q + 1) * width] = pot[c * pan_own + q]
    add_drops(r, pot, 0, links, holder, lanes, field)


def drops_body(k, pan_own, links, holder, lanes, message, field_in, field):
    field[...] = field_in[...]
    p = lax.bitwise_xor(lax.axis_index("row"), k)
    add_drops(p, message, pan_own, links, holder, lanes, field)


def final_body(n_row, n_col, pan_own, links, holder, lanes, field_own, panels, *refs):
    arrived, field_in = refs[: n_row - 1], refs[n_row - 1 : n_row + n_col - 2]
    seg_out, pan_out, field, seg, pan, sems = refs[n_row + n_col - 2 :]
    seg_own, _, width = field.shape
    total = field_own[...]
    for x in field_in:
        total += x[...].astype(F32)
    field[...] = total
    p = lax.bitwise_xor(lax.axis_index("row"), 1)
    add_drops(p, arrived[0], pan_own, links, holder, lanes, field)
    for q in range(pan_own):
        total = panels[q]
        for x in arrived:
            total += x[q].astype(F32)
        pan[:, q * width : (q + 1) * width] = total.astype(BF16)
    chunks = sems.shape[0] - 1
    copies = [pltpu.make_async_copy(pan, pan_out, sems.at[chunks])]
    copies[0].start()
    size = seg_own // chunks
    for i in range(chunks):
        for k in range(i * size, (i + 1) * size):
            seg[:, k * width : (k + 1) * width] = field[k].astype(BF16)
        part = pl.ds(i * size * width, size * width)
        copies.append(pltpu.make_async_copy(seg.at[:, part], seg_out.at[:, part], sems.at[i]))
        copies[-1].start()
    for copy in copies:
        copy.wait()


def shards(
    current,
    charge,
    rhs_scale,
    induct_tiles,
    induct_rows,
    induct_slots,
    induct_needs,
    coeff_tiles,
    coeff_rows,
    coeff_slots,
    coeff_needs,
    link_needs,
    end_slots,
    end_offsets,
):
    n_row = lax.axis_size("row")
    n_col = lax.axis_size("col")
    width = induct_tiles.shape[1]
    rhs = current.shape[0]
    seg_own = current.shape[1] // width
    pan_own = charge.shape[1] // width
    seg_group, pan_group = seg_own * n_col, pan_own * n_col
    cap_l, cap_p, cap_k = induct_needs.shape[1], coeff_needs.shape[1], link_needs.shape[1]
    slots_t, off_t = end_slots.T, end_offsets.T

    partners = [*reversed(range(1, n_row))]
    partners[:2] = partners[1::-1]

    def like(blocks, dtype):
        return jax.ShapeDtypeStruct((blocks, rhs, width), dtype)

    charges = exchange_all(charge, [charge] * (n_col - 1), "col")
    cur = exchange_all(current, [current] * (n_col - 1), "col")
    pack, listed = call(
        functools.partial(pack_body, pan_own, seg_own),
        "pack_charges",
        [like(pan_own + 1, BF16), pltpu.SMEM((2 * list_size(induct_rows.shape[0]) + 4,), jnp.int32)],
        [VMEM, VMEM, SMEM],
        [pltpu.VMEM((rhs, width), jnp.int32)],
        moved=2**16,
        out_specs=[VMEM, SMEM],
    )(*in_hbm(charge, induct_needs, induct_rows))
    (pack,) = call(
        functools.partial(join_body, pan_own),
        "join_charges",
        [like(pan_group + 1, BF16)],
        [VMEM] * n_col,
        moved=2**16,
    )(pack, *charges[1:])
    packs = exchange_all(pack, [pack] * (n_row - 1), "row")

    rows_own = n_row * pan_own
    scalars = [slots_t, link_needs, coeff_slots, coeff_rows, coeff_needs, induct_slots, induct_rows, rhs_scale]
    moved = [*scalars, coeff_tiles]
    outs = call(
        functools.partial(ends_body, n_row, n_col, pan_own, cap_k, len(moved)),
        "end_sums",
        [pltpu.SMEM(x.shape, x.dtype) for x in scalars]
        + [jax.ShapeDtypeStruct(coeff_tiles.shape, BF16)]
        + [pltpu.SMEM((2 * seg_own,), jnp.int32), pltpu.SMEM((n_row * cap_p,), jnp.int32)]
        + [jax.ShapeDtypeStruct((2 * seg_own, width), jnp.int32)]
        + [like(seg_own, BF16), like(rows_own, F32)]
        + [like(rows_own, BF16)] * (n_col - 1),
        [ANY] * (len(moved) + 2),
        [
            pltpu.VMEM(current.shape, BF16),
            pltpu.VMEM(off_t.shape, jnp.int32),
            pltpu.VMEM((n_row * pan_group, rhs, width), F32),
            pltpu.SemaphoreType.DMA((len(moved) + 2,)),
        ],
        flops=5 * 10**8,
        moved=2**18,
        out_specs=[SMEM] * len(scalars) + [VMEM, SMEM, SMEM] + [VMEM] * (2 + n_col),
    )(*in_hbm(current, off_t, *moved))
    _, links_s, coeff_slots, coeff_rows, coeff_needs, induct_slots, induct_rows, scale, coeff_tiles = outs[: len(moved)]
    holder, named, lanes, own_blocks, ends_own, *ends_out = outs[len(moved) :]

    part, *messages = call(
        functools.partial(coeff_body, n_row, n_col, pan_own, partners),
        "coeff_tiles",
        [like(pan_group, F32)] + [like(2 * pan_group + rows_own, BF16)] * (n_col - 1),
        [SMEM] * 3 + [VMEM] * (n_row + n_col),
        [pltpu.VMEM((n_row * pan_group, rhs, width), BF16)],
        flops=10**9,
        moved=coeff_tiles.size * 2,
    )(coeff_slots, coeff_rows, named, *[packs[k] for k in partners], packs[0], *ends_out, coeff_tiles)
    parts = exchange_all(None, messages, "col")[1:]

    *picks, own_picks = call(
        functools.partial(pick_body, n_row, n_col, cap_l, partners),
        "pick_blocks",
        [like(cap_l, BF16)] * n_row,
        [ANY] + [VMEM] * (n_row + n_col),
        [pltpu.VMEM((n_row, width), jnp.int32)],
        moved=2**18,
    )(part, *[packs[k] for k in partners], packs[0], own_blocks, *cur[1:])
    got = exchange_all(own_picks, picks[::-1], "row")

    pot, end_keep, *row_messages = call(
        functools.partial(panels_body, n_row, n_col, pan_own),
        "panel_sums",
        [like(pan_group, BF16), like(pan_own, F32)] + [like(pan_own + pan_group, BF16)] * (n_row - 1),
        [VMEM] * (1 + n_col),
        flops=10**9,
        moved=2**18,
    )(part, ends_own, *parts)

    order = [*partners[1:], 0, partners[0]]

    def induct(name, half, outs, after):
        return call(
            functools.partial(induct_body, n_row, n_col, seg_own, order, half),
            name,
            outs,
            [SMEM] * 3 + [ANY] + [VMEM] * (n_row + 1),
            [
                pltpu.VMEM((n_row * cap_l + 1, rhs, width), BF16),
                pltpu.VMEM((seg_group, rhs, width), F32),
            ],
            flops=10**8,
            moved=2**16,
        )(induct_slots, induct_rows, listed, after, *[got[k] for k in order], induct_tiles)

    field_out = induct("induct_away", 0, [like(seg_own, BF16)] * (n_col - 1), pot)
    field_in = exchange_all(None, field_out, "col")[1:]

    (row_messages[-1],) = call(
        hold_body,
        "hold_near",
        [like(pan_own + pan_group, BF16)],
        [ANY, VMEM],
        moved=2**16,
    )(field_out[0], row_messages[-1])
    arrived = exchange_all(None, row_messages[::-1], "row")[1:]
    (field_own,) = induct("induct_own", 1, [like(seg_own, F32)], row_messages[-1])

    field, panels, pot_out = call(
        functools.partial(base_body, pan_own),
        "base_sums",
        [like(seg_own, F32), like(pan_own, F32), jax.ShapeDtypeStruct(charge.shape, BF16)],
        [SMEM] * 3 + [VMEM] * 5,
        flops=0,
        moved=0,
    )(links_s, holder, scale, lanes, pack, field_own, end_keep, pot)

    for k in reversed(range(2, n_row)):
        (field,) = call(
            functools.partial(drops_body, k, pan_own),
            "add_drops",
            [like(seg_own, F32)],
            [SMEM] * 2 + [VMEM] * 3,
            flops=11 * 10**8 if k == 2 else 0,
            moved=0,
        )(links_s, holder, lanes, arrived[k - 1], field)

    seg_out, pan_out = call(
        functools.partial(final_body, n_row, n_col, pan_own),
        "outputs",
        [jax.ShapeDtypeStruct(x.shape, BF16) for x in (current, charge)],
        [SMEM] * 2 + [VMEM] * (1 + n_row + n_col),
        [
            pltpu.VMEM((seg_own, rhs, width), F32),
            pltpu.VMEM(current.shape, BF16),
            pltpu.VMEM(charge.shape, BF16),
            pltpu.SemaphoreType.DMA((5,)),
        ],
        flops=10**9,
        moved=2**20,
        out_specs=[ANY, ANY],
    )(links_s, holder, lanes, field, panels, *arrived, *field_in)
    return (seg_out, pan_out, pot_out)


def solution(mesh):
    blocks = P(("parts", "row", "col"))
    matrix = P(("parts", "row", "col"), None)
    tiles = P(("parts", "row", "col"), None, None)
    values = P("rhs", ("parts", "row", "col"))
    return jax.shard_map(
        shards,
        mesh=mesh,
        in_specs=(
            values,
            values,
            P(("parts", "rhs")),
            tiles,
            blocks,
            blocks,
            matrix,
            tiles,
            blocks,
            blocks,
            matrix,
            matrix,
            matrix,
            matrix,
        ),
        out_specs=(values, values, values),
        check_vma=False,
    )
```
